32 devices in a mesh: seq: 2 (over x), row: 4 (over z), col: 4 (over y, core).
Axes of the slice: x: 2, y: 2, z: 4, core: 2. Of those that a mesh axis runs over, the one named last changes fastest.
Arguments:
- alignment_input: bfloat16 [64, 256, 64], P('seq', ('row', 'col')), may hold values from -30 to 30
- pair_input: bfloat16 [256, 256, 128], P('row', 'col'), may hold values from -60 to 60
- token_valid_mask: int32 [256], replicated, may hold values from 0 to 1, as said below
- first_factor_weights: bfloat16 [64, 32], replicated, may hold values from -0.75 to 0.75
- second_factor_weights: bfloat16 [64, 32], replicated, may hold values from -0.75 to 0.75
- content_weights_grid: bfloat16 [64, 256], replicated, may hold values from -0.75 to 0.75
- sigmoid_weights_grid: bfloat16 [64, 256], replicated, may hold values from -0.75 to 0.75
- outer_matrix: float32 [1024, 128], replicated, may hold values from -0.0234375 to 0.0234375
- score_matrix: float32 [128, 8], replicated, may hold values from -20 to 20
- final_mixing_weights: bfloat16 [256, 64], replicated, may hold values from -0.375 to 0.375
- adjoint_of_rowset: bfloat16 [64, 256, 64], P('seq', ('row', 'col')), may hold values from -48 to 48
Outputs:
- alignment_output: bfloat16 [64, 256, 64], P('seq', ('row', 'col'))
- pair_output: bfloat16 [256, 256, 128], P('row', 'col')
- pair_gradient: bfloat16 [256, 256, 128], P('row', 'col')
The draws below stay inside these ranges and needn't reach their ends.
Inputs may be any that keep to these rules, and one draw needn't show every extreme that they name: `token_valid_mask`: the mask is 1 on a first run of more than half of the 256 tokens and 0 on the rest.
All inputs are finite; a program needn't handle non-finite values.
Results may differ from the reference program's by a relative error of at most 0.028.
The reference program's roundings to bfloat16 on the way count: a program that leaves them out, or rounds other values in their place, can miss the bound.
Values may be sent and summed in bfloat16 or wider, within the bound.
No kernel may reach another device: no remote copies, remote signals or barrier semaphores. Data moves between devices by JAX's collectives and lax.ppermute only.
A program may use at most 64 MiB of HBM per device.

```python
import math
import jax
import jax.numpy as jnp
from jax import lax

FEATURE_WIDTH = 64
CZ = 128
FACTOR_WIDTH = 32
ATTENTION_HEADS = 8
HEAD_WIDTH = 32
ROW_TOTAL_NUM = 64
RESIDUE_NUMBER = 256


def score_base(key):
    return jax.random.normal(jax.random.fold_in(key, 101), (CZ, ATTENTION_HEADS), jnp.float32)


def draw_score_matrix(key, part):
    base = score_base(key)
    key = jax.random.fold_in(key, 7)
    head_scale = jnp.exp(jax.random.uniform(key, (1, ATTENTION_HEADS), jnp.float32, math.log(0.6), math.log(2.4)))
    return base * head_scale / math.sqrt(CZ)


def draw_pair_input(key, part):
    key = jax.random.fold_in(key, 11)
    perturbation_seed, multiplier_seed = jax.random.split(key, 2)
    feature_multiplier = jnp.exp(jax.random.uniform(multiplier_seed, (CZ,), jnp.float32, math.log(0.3), math.log(3.0)))
    random_perturbation = jax.random.normal(perturbation_seed, (RESIDUE_NUMBER, RESIDUE_NUMBER, CZ), jnp.float32)
    return (random_perturbation * feature_multiplier).astype(jnp.bfloat16)


def draw_alignment_input(key, part):
    key = jax.random.fold_in(key, 23)
    perturbation_seed, multiplier_seed = jax.random.split(key)
    feature_multiplier = jnp.exp(jax.random.uniform(multiplier_seed, (FEATURE_WIDTH,), jnp.float32, math.log(0.3), math.log(3.0)))
    random_perturbation = jax.random.normal(perturbation_seed, (ROW_TOTAL_NUM, RESIDUE_NUMBER, FEATURE_WIDTH), jnp.float32)
    return (random_perturbation * feature_multiplier).astype(jnp.bfloat16)


def draw_token_valid_mask(key, part):
    key = jax.random.fold_in(key, 31)
    length = jax.random.randint(key, (), RESIDUE_NUMBER // 2 + 1, RESIDUE_NUMBER + 1)
    return (jnp.arange(RESIDUE_NUMBER, dtype=jnp.int32) < length).astype(jnp.int32)


def level_of(rng, extent, pieces, least, high):
    def one(dim, blocks):
        draws = jax.random.uniform(jax.random.fold_in(jax.random.fold_in(rng, 6), dim), (blocks,), jnp.float32, least / len(pieces), high / len(pieces))
        return jnp.repeat(jnp.exp(draws), extent[dim] // blocks).reshape((-1,) + (1,) * (len(extent) - dim - 1))

    gain = one(*pieces[0])
    for cut in pieces[1:]:
        gain = gain * one(*cut)
    return gain


def noise(stream_key, shape, spread, limit, cuts=(), kind=jnp.bfloat16):
    drawn = spread * jax.random.normal(stream_key, shape, jnp.float32)
    if cuts:
        drawn = drawn * level_of(stream_key, shape, cuts, -0.22, 0.18)
    return jnp.clip(drawn, -limit, limit).astype(kind)


def setup_inputs(seed: int = 0) -> dict:
    splits = jax.random.split(jax.random.key(seed), 12)
    return {
        "alignment_input": draw_alignment_input(jax.random.fold_in(splits[11], 71), 0),
        "pair_input": draw_pair_input(jax.random.fold_in(splits[11], 71), 0),
        "token_valid_mask": draw_token_valid_mask(jax.random.fold_in(splits[11], 71), 0),
        "first_factor_weights": noise(splits[3], (FEATURE_WIDTH, FACTOR_WIDTH), FEATURE_WIDTH ** -0.5, 0.75),
        "second_factor_weights": noise(splits[4], (FEATURE_WIDTH, FACTOR_WIDTH), FEATURE_WIDTH ** -0.5, 0.75),
        "content_weights_grid": noise(splits[5], (FEATURE_WIDTH, ATTENTION_HEADS * HEAD_WIDTH), FEATURE_WIDTH ** -0.5, 0.75),
        "sigmoid_weights_grid": noise(splits[6], (FEATURE_WIDTH, ATTENTION_HEADS * HEAD_WIDTH), FEATURE_WIDTH ** -0.5, 0.75),
        "outer_matrix": noise(splits[7], (FACTOR_WIDTH * FACTOR_WIDTH, CZ), (FACTOR_WIDTH * FACTOR_WIDTH * ROW_TOTAL_NUM) ** -0.5, 0.0234375, (), jnp.float32),
        "score_matrix": draw_score_matrix(jax.random.fold_in(splits[11], 71), 0),
        "final_mixing_weights": noise(splits[9], (ATTENTION_HEADS * HEAD_WIDTH, FEATURE_WIDTH), (ATTENTION_HEADS * HEAD_WIDTH) ** -0.5, 0.375),
        "adjoint_of_rowset": noise(splits[10], (ROW_TOTAL_NUM, RESIDUE_NUMBER, FEATURE_WIDTH), 8.0, 48.0, ((0, 2), (1, 16))),
    }


epsilon = 1e-05
far_below = -1e+30

def layer_normalize(inputs):
    center = inputs - lax.optimization_barrier(jnp.mean(inputs, axis=-1, keepdims=True))
    inverse = lax.rsqrt(lax.optimization_barrier(jnp.mean(center * center, axis=-1, keepdims=True)) + epsilon)
    return (center * inverse, inverse)

def reference(alignment_input, pair_input, token_valid_mask, first_factor_weights, second_factor_weights, content_weights_grid, sigmoid_weights_grid, outer_matrix, score_matrix, final_mixing_weights, adjoint_of_rowset):
    highest = lax.Precision.HIGHEST
    mask_float = token_valid_mask.astype(jnp.float32)
    normalized_pair = layer_normalize(alignment_input.astype(jnp.float32))[0].astype(jnp.bfloat16)
    left_proj = (jnp.dot(normalized_pair, first_factor_weights, preferred_element_type=jnp.float32) * mask_float[None, :, None]).astype(jnp.bfloat16)
    right_proj = (jnp.dot(normalized_pair, second_factor_weights, preferred_element_type=jnp.float32) * mask_float[None, :, None]).astype(jnp.bfloat16)
    values = jnp.dot(normalized_pair, content_weights_grid, preferred_element_type=jnp.float32).astype(jnp.bfloat16)
    gating = jax.nn.sigmoid(jnp.dot(normalized_pair, sigmoid_weights_grid, preferred_element_type=jnp.float32))
    left_float = left_proj.astype(jnp.float32)
    right_float = right_proj.astype(jnp.float32)
    block_rows = math.gcd(RESIDUE_NUMBER, 16)

    def rows_update(number):
        row_start = (number * block_rows).astype(jnp.int32)
        rows_part = lax.dynamic_slice_in_dim(left_float, row_start, block_rows, 1)
        products = jnp.einsum('sic,sjd->ijcd', rows_part, right_float).reshape(block_rows, RESIDUE_NUMBER, FACTOR_WIDTH * FACTOR_WIDTH)
        return jnp.dot(products, outer_matrix, precision=highest, preferred_element_type=jnp.float32)
    update = lax.map(rows_update, jnp.arange(RESIDUE_NUMBER // block_rows, dtype=jnp.int32)).reshape(RESIDUE_NUMBER, RESIDUE_NUMBER, CZ)
    pair_output = (pair_input.astype(jnp.float32) + update).astype(jnp.bfloat16)
    normal_pair, inverse_pair = layer_normalize(pair_output.astype(jnp.float32))
    logits = jnp.dot(normal_pair, score_matrix, precision=highest, preferred_element_type=jnp.float32)
    valid_cols = mask_float[None, :, None] > 0
    masked = jnp.where(valid_cols, logits, far_below)
    row_max = lax.optimization_barrier(jnp.max(masked, axis=1, keepdims=True))
    scaled = jnp.exp(masked - row_max) * mask_float[None, :, None]
    probabilities = scaled / lax.optimization_barrier(jnp.sum(scaled, axis=1, keepdims=True))
    weights = probabilities.astype(jnp.bfloat16)
    head_values = values.astype(jnp.float32).reshape(ROW_TOTAL_NUM, RESIDUE_NUMBER, ATTENTION_HEADS, HEAD_WIDTH)
    averaged = jnp.einsum('ijh,sjhk->sihk', weights.astype(jnp.float32), head_values).reshape(ROW_TOTAL_NUM, RESIDUE_NUMBER, ATTENTION_HEADS * HEAD_WIDTH)
    gated_values = (gating * averaged).astype(jnp.bfloat16)
    alignment_output = (alignment_input.astype(jnp.float32) + jnp.dot(gated_values, final_mixing_weights, preferred_element_type=jnp.float32)).astype(jnp.bfloat16)
    gated_gradient = jnp.dot(adjoint_of_rowset, final_mixing_weights.T, preferred_element_type=jnp.float32)
    grad_avg = (gated_gradient * gating).astype(jnp.bfloat16)
    grad_heads = grad_avg.astype(jnp.float32).reshape(ROW_TOTAL_NUM, RESIDUE_NUMBER, ATTENTION_HEADS, HEAD_WIDTH)
    grad_weights = jnp.einsum('sihk,sjhk->ijh', grad_heads, head_values)
    inner_sum = lax.optimization_barrier(jnp.sum(probabilities * grad_weights, axis=1, keepdims=True))
    grad_logits = probabilities * (grad_weights - inner_sum)
    grad_normal = jnp.dot(grad_logits, score_matrix.T, precision=highest, preferred_element_type=jnp.float32)
    centered_grad = grad_normal - lax.optimization_barrier(jnp.mean(grad_normal, axis=-1, keepdims=True))
    along = lax.optimization_barrier(jnp.mean(grad_normal * normal_pair, axis=-1, keepdims=True))
    pair_gradient = (inverse_pair * (centered_grad - normal_pair * along)).astype(jnp.bfloat16)
    return (alignment_output, pair_output, pair_gradient)
```

```python
import functools

import jax
import jax.numpy as jnp
from jax import lax
from jax.experimental import pallas as pl
from jax.experimental.pallas import tpu as pltpu
from jax.sharding import PartitionSpec as P

epsilon = 1e-05
far_below = -1e30
vmem_bytes = 48 * 1024 * 1024
pack = 4

f32 = jnp.float32
bf16 = jnp.bfloat16


def nt_dot(a, b):
    return lax.dot_general(a, b, (((1,), (1,)), ((), ())), preferred_element_type=f32)


def nn_dot(a, b):
    return jnp.dot(a, b, preferred_element_type=f32)


def high_low(x):
    high = x.astype(bf16)
    return high, (x - high.astype(f32)).astype(bf16)


def split3(x):
    a = lax.reduce_precision(x, 8, 7)
    b = lax.reduce_precision(x - a, 8, 7)
    c = lax.reduce_precision(x - a - b, 8, 7)
    return a.astype(bf16), b.astype(bf16), c.astype(bf16)


def call(kernel, out_shape, scratch=(), smem=0, flops=0, nbytes=0):
    count = None

    def run(*args):
        specs = [pl.BlockSpec(memory_space=pltpu.SMEM)] * smem
        specs += [pl.BlockSpec(memory_space=pltpu.VMEM)] * (len(args) - smem)
        return pl.pallas_call(
            kernel,
            out_shape=out_shape,
            in_specs=specs,
            out_specs=jax.tree.map(lambda _: pl.BlockSpec(memory_space=pltpu.VMEM), out_shape),
            scratch_shapes=list(scratch),
            compiler_params=pltpu.CompilerParams(vmem_limit_bytes=vmem_bytes),
            cost_estimate=pl.CostEstimate(flops=flops, bytes_accessed=nbytes, transcendentals=0),
        )(*args)

    return run


def prepare_kernel(x_ref, xt_ref, adj_ref, w1_ref, mask_ref, norm_ref, both_ref, left_ref):
    def normalize(x):
        x = x.astype(f32)
        center = x - jnp.mean(x, axis=-1, keepdims=True)
        inverse = lax.rsqrt(jnp.mean(center * center, axis=-1, keepdims=True) + epsilon)
        return (center * inverse).astype(bf16)

    seqs, tokens, width = x_ref.shape
    normed = normalize(x_ref[...])
    norm_ref[...] = normed
    both_ref[...] = jnp.concatenate([normed, adj_ref[...]], axis=-1)
    turned = normalize(xt_ref[...]).reshape(tokens * seqs, width)
    left_ref[...] = (nt_dot(w1_ref[...], turned) * mask_ref[...]).astype(bf16)


def update_kernel(
    left_ref,
    xc_ref,
    w2_ref,
    maskj_ref,
    mt_ref,
    st_ref,
    pair_ref,
    pout_ref,
    pout_t_ref,
    logits_ref,
    rr_ref,
    lm_ref,
    oh_ref,
    ol_ref,
):
    nq, nk, fc, _ = left_ref.shape
    seqs, tokens = xc_ref.shape[2], xc_ref.shape[3]
    tile_j = nk * tokens
    width_d = w2_ref.shape[0]
    groups = pair_ref.shape[0] // (pack * tile_j)
    per_k = groups // nk
    lanes = pack * tile_j
    wk = pack * seqs
    z = pair_ref.shape[1]

    w2 = w2_ref[...]
    maskj = maskj_ref[...]

    def right_of(q, carry):
        for s in range(seqs):
            x = jnp.concatenate([xc_ref[q, k, s] for k in range(nk)], axis=0)
            res = nt_dot(w2, jnp.concatenate([x, x], axis=0)) * maskj
            rr_ref[q, :, s, :] = res
        return carry

    lax.fori_loop(0, nq, right_of, 0)

    for q in range(nq):
        for k in range(nk):
            for g in range(per_k):
                row = (k * per_k + g) * fc
                lm_ref[row : row + fc, q * wk : (q + 1) * wk] = left_ref[
                    q, k, :, g * wk : (g + 1) * wk
                ]

    first = lax.broadcasted_iota(jnp.int32, (seqs, 2 * tile_j), 1) < tile_j

    def outer_of(d, carry):
        empty = jnp.zeros((seqs, 2 * tile_j), bf16)
        rows = []
        for q in range(nq):
            both = rr_ref[q, d]
            part = (
                jnp.where(first, both, 0.0).astype(bf16),
                jnp.where(first, 0.0, both).astype(bf16),
            )
            for i in range(pack):
                pieces = [empty] * (pack // 2)
                pieces[i // 2] = part[i % 2]
                rows.append(jnp.concatenate(pieces, axis=1))
        block = jnp.concatenate(rows, axis=0)
        out = nn_dot(lm_ref[...], block)
        high, low = high_low(out)
        at = pl.ds(pl.multiple_of(d * fc, fc), fc)
        oh_ref[:, at, :] = high.reshape(groups, fc, lanes)
        ol_ref[:, at, :] = low.reshape(groups, fc, lanes)
        return carry

    lax.fori_loop(0, width_d, outer_of, 0, unroll=2)

    maskl = jnp.concatenate([maskj] * (pack // 2), axis=1) > 0

    def finish(g, carry):
        mt = mt_ref[...]
        two = nn_dot(mt, oh_ref[g])
        update = two[:z] + two[z:] + nn_dot(mt[:z], ol_ref[g])
        at = pl.ds(pl.multiple_of(g * lanes, lanes), lanes)
        before = pair_ref[at, :].astype(f32).T
        result = (before + update).astype(bf16)
        pout_t_ref[g] = result
        x = result.astype(f32)
        pout_ref[at, :] = x.T.astype(bf16)
        center = x - jnp.mean(x, axis=0, keepdims=True)
        inverse = lax.rsqrt(jnp.mean(center * center, axis=0, keepdims=True) + epsilon)
        high, low = high_low(center * inverse)
        scores = nn_dot(st_ref[...], jnp.concatenate([high, low], axis=0))
        heads = logits_ref.shape[1]
        logits = scores[:heads] + scores[heads : 2 * heads] + scores[2 * heads : 3 * heads]
        logits_ref[g] = jnp.where(maskl, logits, far_below)
        return carry

    lax.fori_loop(0, groups, finish, 0, unroll=2)


def weights_kernel(
    col_ref,
    xc_ref,
    rows_ref,
    wv_ref,
    wga_ref,
    logits_ref,
    maskj_ref,
    gw_ref,
    own_ref,
    pay1_ref,
    pay2_ref,
    pay3_ref,
    acc_ref,
):
    nq, nk, seqs, tokens, _ = xc_ref.shape
    tile = nk * tokens
    groups, heads, lanes = logits_ref.shape
    chans = wv_ref.shape[1]
    head_width = chans // heads
    wv = wv_ref[...]
    wga = wga_ref[...]
    owner = lax.broadcasted_iota(jnp.int32, (tile, chans), 1) // head_width
    step = 4

    acc_ref[...] = jnp.zeros_like(acc_ref)

    def some(n, carry):
        q = n // (seqs // step)
        s0 = (n % (seqs // step)) * step
        vs, gs = [], []
        for ds in range(step):
            x = jnp.concatenate([xc_ref[q, k, s0 + ds] for k in range(nk)], axis=0)
            v = nn_dot(x, wv).astype(bf16)
            vs.append(jnp.concatenate([v, v], axis=0))
            r = jnp.concatenate([rows_ref[q, k, s0 + ds] for k in range(nk)], axis=0)
            both = nn_dot(r, wga)
            gs.append((both[:, chans:] * jax.nn.sigmoid(both[:, :chans])).astype(bf16))
        spread = [
            jnp.concatenate(
                [jnp.where(owner == h, g, jnp.zeros_like(g)) for h in range(heads)], axis=0
            )
            for g in gs
        ]
        acc_ref[...] += nt_dot(jnp.concatenate(spread, axis=1), jnp.concatenate(vs, axis=1))
        return carry

    lax.fori_loop(0, nq * (seqs // step), some, 0)

    first = lax.broadcasted_iota(jnp.int32, (groups, 2 * tile), 1) < tile
    for h in range(heads):
        for half in range(pack // 2):
            a = acc_ref[pl.ds(h * tile + 2 * half, groups, stride=pack), :]
            b = acc_ref[pl.ds(h * tile + 2 * half + 1, groups, stride=pack), :]
            gw_ref[:, h, half * 2 * tile : (half + 1) * 2 * tile] = jnp.where(first, a, b)

    rows = groups * heads
    lane = lax.broadcasted_iota(jnp.int32, (rows, 2 * tile), 1)
    low = lane < tile
    maskj = maskj_ref[...]
    stats = jnp.zeros((rows, 2 * tile), f32)
    for half in range(pack // 2):
        cut = slice(half * 2 * tile, (half + 1) * 2 * tile)
        lg = logits_ref[:, :, cut].reshape(rows, 2 * tile)
        gw = gw_ref[:, :, cut].reshape(rows, 2 * tile)
        m0 = jnp.max(jnp.where(low, lg, far_below), axis=1, keepdims=True)
        m1 = jnp.max(jnp.where(low, far_below, lg), axis=1, keepdims=True)
        p = jnp.exp(lg - jnp.where(low, m0, m1)) * maskj
        pg = p * gw
        for e, m in ((0, m0), (1, m1)):
            mine = low if e == 0 else jnp.logical_not(low)
            i = 2 * half + e
            total = jnp.sum(jnp.where(mine, p, 0.0), axis=1, keepdims=True)
            inner = jnp.sum(jnp.where(mine, pg, 0.0), axis=1, keepdims=True)
            stats = jnp.where(lane == i, m, stats)
            stats = jnp.where(lane == pack + i, total, stats)
            stats = jnp.where(lane == 2 * pack + i, inner, stats)
    turned = stats.T[:16]
    col = col_ref[0]
    per = groups // nk
    for shift, pay in enumerate((own_ref, pay1_ref, pay2_ref, pay3_ref)):
        dest = lax.rem(col + shift, nk)
        pay[0] = turned[:8]
        pay[1] = turned[8:]
        for g in range(per):
            piece = logits_ref[dest * per + g]
            for half in range(pack // 2):
                pay[2 + g * (pack // 2) + half] = piece[:, half * 2 * tile : (half + 1) * 2 * tile]


def values_kernel(all_ref, wv_ref, norm_ref, wg_ref, v_ref, gate_ref):
    owners, seqs, tokens, width = all_ref.shape
    wv = wv_ref[...]
    for s in range(seqs):
        x = jnp.concatenate([all_ref[k, s] for k in range(owners)], axis=0)
        v_ref[s] = nn_dot(x, wv).astype(bf16)
    gate_ref[...] = jax.nn.sigmoid(
        nn_dot(norm_ref[...].reshape(seqs * tokens, width), wg_ref[...])
    )


def gradient_kernel(
    own_ref, r1_ref, r2_ref, r3_ref, logits_ref, gw_ref, pout_t_ref, sk_ref, out_ref, stat_ref
):
    groups, heads, lanes = logits_ref.shape
    rows = groups * heads
    pays = (own_ref, r1_ref, r2_ref, r3_ref)
    ms = [p[0][:pack] for p in pays]
    ls = [p[0][pack : 2 * pack] for p in pays]
    ns = [p[1][:pack] for p in pays]
    top = functools.reduce(jnp.maximum, ms)
    scales = [jnp.exp(m - top) for m in ms]
    total = sum(a * b for a, b in zip(ls, scales))
    inner = sum(a * b for a, b in zip(ns, scales)) / total
    stacked = jnp.concatenate([top, total, inner, jnp.zeros((rows - 3 * pack, rows), f32)], axis=0)
    stat_ref[...] = stacked.T

    tile = lanes // pack
    low = lax.broadcasted_iota(jnp.int32, (heads, 2 * tile), 1) < tile

    def one(g, carry):
        st = stat_ref[pl.ds(pl.multiple_of(g * heads, heads), heads), :]

        def spread(base):
            halves = [
                jnp.where(
                    low,
                    st[:, base + 2 * half : base + 2 * half + 1],
                    st[:, base + 2 * half + 1 : base + 2 * half + 2],
                )
                for half in range(pack // 2)
            ]
            return jnp.concatenate(halves, axis=1)

        prob = jnp.exp(logits_ref[g] - spread(0)) / spread(pack)
        gl = prob * (gw_ref[g] - spread(2 * pack))
        g1 = gl.astype(bf16).astype(f32)
        g2 = (gl - g1).astype(bf16).astype(f32)
        g3 = gl - g1 - g2
        stack = jnp.concatenate([g1, g2, g3, g1, g2, g1], axis=0).astype(bf16)
        grad = nn_dot(sk_ref[...], stack)
        x = pout_t_ref[g].astype(f32)
        center = x - jnp.mean(x, axis=0, keepdims=True)
        inverse = lax.rsqrt(jnp.mean(center * center, axis=0, keepdims=True) + epsilon)
        normal = center * inverse
        centered = grad - jnp.mean(grad, axis=0, keepdims=True)
        along = jnp.mean(grad * normal, axis=0, keepdims=True)
        result = inverse * (centered - normal * along)
        out_ref[pl.ds(pl.multiple_of(g * lanes, lanes), lanes), :] = result.T.astype(bf16)
        return carry

    lax.fori_loop(0, groups, one, 0, unroll=2)


def alignment_kernel(
    col_ref,
    own_ref,
    r1_ref,
    r2_ref,
    r3_ref,
    v_ref,
    gate_ref,
    x_ref,
    wf_ref,
    out_ref,
    w_ref,
    gated_ref,
):
    pays = (own_ref, r1_ref, r2_ref, r3_ref)
    nk = len(pays)
    heads = own_ref.shape[1]
    wide = own_ref.shape[2]
    tile = wide // 2
    pieces = own_ref.shape[0] - 2
    rows = pieces * heads
    seqs, all_tokens, chans = v_ref.shape
    tokens = pieces * 2
    head_width = chans // heads
    col = col_ref[0]

    low = lax.broadcasted_iota(jnp.int32, (rows, wide), 1) < tile
    lgs = [p[2:].reshape(rows, wide) for p in pays]
    peak = functools.reduce(jnp.maximum, lgs)
    m0 = jnp.max(jnp.where(low, peak, far_below), axis=1, keepdims=True)
    m1 = jnp.max(jnp.where(low, far_below, peak), axis=1, keepdims=True)
    top = jnp.where(low, m0, m1)
    ps = [jnp.exp(lg - top) for lg in lgs]
    every = sum(ps)
    t0 = jnp.sum(jnp.where(low, every, 0.0), axis=1, keepdims=True)
    t1 = jnp.sum(jnp.where(low, 0.0, every), axis=1, keepdims=True)
    total = jnp.where(low, t0, t1)
    for shift, p in enumerate(ps):
        source = lax.rem(col + nk - shift, nk)
        weight = p / total
        rolled = pltpu.roll(weight, tile, 1)
        for n in range(pieces):
            w_ref[source, :, 2 * n, :] = weight[n * heads : (n + 1) * heads]
            w_ref[source, :, 2 * n + 1, :] = rolled[n * heads : (n + 1) * heads]
    w = jnp.concatenate(
        [w_ref[k].reshape(heads * tokens, wide)[:, :tile] for k in range(nk)], axis=1
    ).astype(bf16)

    owner = lax.broadcasted_iota(jnp.int32, (tokens, chans), 1) // head_width

    def one(s, carry):
        full = nn_dot(w, v_ref[s])
        mean = jnp.zeros((tokens, chans), f32)
        for h in range(heads):
            mean = jnp.where(owner == h, full[h * tokens : (h + 1) * tokens], mean)
        at = pl.ds(pl.multiple_of(s * tokens, tokens), tokens)
        gated_ref[at, :] = (gate_ref[at, :] * mean).astype(bf16)
        return carry

    lax.fori_loop(0, seqs, one, 0, unroll=4)
    out_ref[...] = (x_ref[...].astype(f32) + nn_dot(gated_ref[...], wf_ref[...])).astype(bf16)


def on_device(
    counts,
    alignment_input,
    pair_input,
    token_valid_mask,
    first_factor_weights,
    second_factor_weights,
    content_weights_grid,
    sigmoid_weights_grid,
    outer_matrix,
    score_matrix,
    final_mixing_weights,
    adjoint_of_rowset,
):
    nq, nr, nk = counts
    row_index = lax.axis_index("row")
    col_index = lax.axis_index("col")
    seqs, tokens, width = alignment_input.shape
    tile_i, tile_j, z = pair_input.shape
    fc = first_factor_weights.shape[1]
    fd = second_factor_weights.shape[1]
    heads = score_matrix.shape[1]
    chans = content_weights_grid.shape[1]
    groups = tile_i // pack
    lanes = pack * tile_j
    sds = jax.ShapeDtypeStruct

    maskf = token_valid_mask.astype(f32)
    own_start = (row_index * nk + col_index) * tokens
    own_mask = lax.dynamic_slice_in_dim(maskf, own_start, tokens)
    own_mask = jnp.broadcast_to(own_mask[:, None], (tokens, seqs)).reshape(1, tokens * seqs)
    col_mask = lax.dynamic_slice_in_dim(maskf, col_index * tile_j, tile_j)
    col_mask = jnp.concatenate([col_mask, col_mask]).reshape(1, 2 * tile_j)
    col_scalar = col_index.astype(jnp.int32).reshape(1)

    normed, both, left = call(
        prepare_kernel,
        (
            sds((seqs, tokens, width), bf16),
            sds((seqs, tokens, 2 * width), bf16),
            sds((fc, tokens * seqs), bf16),
        ),
    )(
        alignment_input,
        jnp.swapaxes(alignment_input, 0, 1),
        adjoint_of_rowset,
        first_factor_weights.T,
        own_mask,
    )

    turn = [(r * nk + c, c * nk + r) for r in range(nr) for c in range(nk)]
    crossed = lax.ppermute(normed, ("row", "col"), turn)
    lefts = lax.all_gather(left, ("seq", "col"), axis=0).reshape(nq, nk, fc, tokens * seqs)
    cols = lax.all_gather(crossed, ("seq", "row"), axis=0).reshape(nq, nk, seqs, tokens, width)
    rows = lax.all_gather(both, ("seq", "col"), axis=0).reshape(nq, nk, seqs, tokens, 2 * width)
    every = lax.all_gather(normed, ("row", "col"), axis=0)

    m3 = outer_matrix.reshape(fc, fd, z).transpose(2, 1, 0).reshape(z, fd * fc)
    m_high = lax.reduce_precision(m3, 8, 7)
    mt = jnp.concatenate([m_high, m3 - m_high], axis=0).astype(bf16)
    s1, s2, s3 = split3(score_matrix)
    none = jnp.zeros((heads, z), bf16)
    st = jnp.concatenate(
        [
            jnp.concatenate([s1.T, s1.T], axis=1),
            jnp.concatenate([s2.T, s2.T], axis=1),
            jnp.concatenate([s3.T, none], axis=1),
            jnp.concatenate([none, none], axis=1),
        ],
        axis=0,
    )
    sk = jnp.concatenate([s1, s1, s1, s2, s2, s3], axis=1)
    blank = jnp.zeros((width, chans), bf16)
    wga = jnp.concatenate(
        [
            jnp.concatenate([sigmoid_weights_grid, blank], axis=1),
            jnp.concatenate([blank, final_mixing_weights.T], axis=1),
        ],
        axis=0,
    )

    pair_out, pair_t, logits = call(
        update_kernel,
        (
            sds((tile_i * tile_j, z), bf16),
            sds((groups, z, lanes), bf16),
            sds((groups, heads, lanes), f32),
        ),
        scratch=(
            pltpu.VMEM((nq, fd, seqs, 2 * tile_j), f32),
            pltpu.VMEM((groups * fc, nq * pack * seqs), bf16),
            pltpu.VMEM((groups, fd * fc, lanes), bf16),
            pltpu.VMEM((groups, fd * fc, lanes), bf16),
        ),
        flops=14_000_000_000,
        nbytes=5_000_000,
    )(
        lefts,
        cols,
        second_factor_weights.T,
        col_mask,
        mt,
        st,
        pair_input.reshape(tile_i * tile_j, z),
    )

    payload = sds((2 + groups // nk * (pack // 2), heads, 2 * tile_j), f32)
    gw, pay0, pay1, pay2, pay3 = call(
        weights_kernel,
        (sds((groups, heads, lanes), f32), payload, payload, payload, payload),
        scratch=(pltpu.VMEM((heads * tile_i, 2 * tile_j), f32),),
        smem=1,
        flops=6_000_000_000,
        nbytes=3_000_000,
    )(col_scalar, cols, rows, content_weights_grid, wga, logits, col_mask)

    got = [
        lax.ppermute(pay, "col", [(c, (c + shift) % nk) for c in range(nk)])
        for shift, pay in ((1, pay1), (2, pay2), (3, pay3))
    ]

    values, gating = call(
        values_kernel,
        (sds((seqs, nr * nk * tokens, chans), bf16), sds((seqs * tokens, chans), f32)),
        flops=4_000_000_000,
        nbytes=6_000_000,
    )(every, content_weights_grid, normed, sigmoid_weights_grid)

    gradient = call(
        gradient_kernel,
        sds((tile_i * tile_j, z), bf16),
        scratch=(pltpu.VMEM((groups * heads, groups * heads), f32),),
        flops=4_000_000_000,
        nbytes=3_000_000,
    )(pay0, *got, logits, gw, pair_t, sk)

    aligned = call(
        alignment_kernel,
        sds((seqs * tokens, width), bf16),
        scratch=(
            pltpu.VMEM((nk, heads, tokens, 2 * tile_j), f32),
            pltpu.VMEM((seqs * tokens, chans), bf16),
        ),
        smem=1,
        flops=3_000_000_000,
        nbytes=5_000_000,
    )(
        col_scalar,
        pay0,
        *got,
        values,
        gating,
        alignment_input.reshape(seqs * tokens, width),
        final_mixing_weights,
    )
    return (
        aligned.reshape(seqs, tokens, width),
        pair_out.reshape(tile_i, tile_j, z),
        gradient.reshape(tile_i, tile_j, z),
    )


def solution(mesh):
    counts = (mesh.shape["seq"], mesh.shape["row"], mesh.shape["col"])
    in_specs = (
        P("seq", ("row", "col"), None),
        P("row", "col", None),
        P(),
        P(),
        P(),
        P(),
        P(),
        P(),
        P(),
        P(),
        P("seq", ("row", "col"), None),
    )
    out_specs = (P("seq", ("row", "col"), None), P("row", "col", None), P("row", "col", None))
    return jax.shard_map(
        functools.partial(on_device, counts),
        mesh=mesh,
        in_specs=in_specs,
        out_specs=out_specs,
        check_vma=False,
    )
```

```python
import functools

import jax
import jax.numpy as jnp
from jax import lax
from jax.experimental import pallas as pl
from jax.experimental.pallas import tpu as pltpu
from jax.sharding import PartitionSpec as P

epsilon = 1e-05
far_below = -1e30
vmem_bytes = 48 * 1024 * 1024
pack = 4

f32 = jnp.float32
bf16 = jnp.bfloat16


def nt_dot(a, b):
    return lax.dot_general(a, b, (((1,), (1,)), ((), ())), preferred_element_type=f32)


def nn_dot(a, b):
    return jnp.dot(a, b, preferred_element_type=f32)


def high_low(x):
    high = x.astype(bf16)
    return high, (x - high.astype(f32)).astype(bf16)


def call(kernel, out_shape, scratch=(), smem=0, flops=0, nbytes=0, vmem=vmem_bytes):
    count = None

    def run(*args):
        specs = [pl.BlockSpec(memory_space=pltpu.SMEM)] * smem
        specs += [pl.BlockSpec(memory_space=pltpu.VMEM)] * (len(args) - smem)
        return pl.pallas_call(
            kernel,
            out_shape=out_shape,
            in_specs=specs,
            out_specs=jax.tree.map(lambda _: pl.BlockSpec(memory_space=pltpu.VMEM), out_shape),
            scratch_shapes=list(scratch),
            compiler_params=pltpu.CompilerParams(vmem_limit_bytes=vmem),
            cost_estimate=pl.CostEstimate(flops=flops, bytes_accessed=nbytes, transcendentals=0),
        )(*args)

    return run


def valid_count(mask_ref):
    return jnp.sum(mask_ref[...].astype(f32), axis=1, keepdims=True)


def column_mask(mask_ref, col, tile, copies):
    lane = lax.broadcasted_iota(jnp.int32, (1, copies * tile), 1)
    token = (lax.rem(lane, tile) + col * tile).astype(f32)
    return (token < valid_count(mask_ref)).astype(f32)


def twice(w):
    none = jnp.zeros_like(w)
    return jnp.concatenate(
        [jnp.concatenate([w, none], axis=1), jnp.concatenate([none, w], axis=1)], axis=0
    )


def prepare_kernel(own_ref, x_ref, adj_ref, w1_ref, mask_ref, norm_ref, both_ref, left_ref, turn_ref):
    seqs, tokens, width = x_ref.shape
    half = seqs // 2
    x = x_ref[...].astype(f32)
    center = x - jnp.mean(x, axis=-1, keepdims=True)
    inverse = lax.rsqrt(jnp.mean(center * center, axis=-1, keepdims=True) + epsilon)
    normed = center * inverse
    packed = jnp.concatenate([normed[:half], normed[half:]], axis=-1).astype(bf16)
    norm_ref[...] = packed
    both_ref[0] = packed
    adj = adj_ref[...].astype(f32)
    both_ref[1] = jnp.concatenate([adj[:half], adj[half:]], axis=-1).astype(bf16)
    for s in range(seqs):
        turn_ref[:, s, :] = normed[s]
    token = lax.broadcasted_iota(jnp.int32, (tokens, seqs, width), 0) + own_ref[0]
    count = valid_count(mask_ref).reshape(1, 1, 1)
    turned = jnp.where(token.astype(f32) < count, turn_ref[...], 0.0).astype(bf16)
    left_ref[...] = nt_dot(w1_ref[...], turned.reshape(tokens * seqs, width)).astype(bf16)


def update_kernel(
    col_ref,
    left_ref,
    xc_ref,
    w2_ref,
    mask_ref,
    m_ref,
    score_ref,
    pair_ref,
    pout_ref,
    pout_t_ref,
    logits_ref,
    rr_ref,
    lm_ref,
    mt_ref,
    oh_ref,
    ol_ref,
):
    nq, nk, fc, _ = left_ref.shape
    half, tokens = xc_ref.shape[2], xc_ref.shape[3]
    seqs = 2 * half
    tile_j = nk * tokens
    width_d = w2_ref.shape[0]
    groups = pair_ref.shape[0] // (pack * tile_j)
    per_k = groups // nk
    lanes = pack * tile_j
    wk = pack * seqs
    z = pair_ref.shape[1]
    heads = logits_ref.shape[1]

    w2 = twice(w2_ref[...])
    maskj = column_mask(mask_ref, col_ref[0], tile_j, 2)

    def right_of(q, carry):
        for s in range(half):
            x = jnp.concatenate([xc_ref[q, k, s] for k in range(nk)], axis=0)
            res = nt_dot(w2, jnp.concatenate([x, x], axis=0)) * maskj
            rr_ref[q, :, s, :] = res[:width_d]
            rr_ref[q, :, s + half, :] = res[width_d:]
        return carry

    lax.fori_loop(0, nq, right_of, 0)

    for q in range(nq):
        for k in range(nk):
            for g in range(per_k):
                row = (k * per_k + g) * fc
                lm_ref[row : row + fc, q * wk : (q + 1) * wk] = left_ref[
                    q, k, :, g * wk : (g + 1) * wk
                ]

    some = z // fc
    for n in range(width_d // some):
        block = jnp.concatenate(
            [m_ref[pl.ds(n * some + e, fc, stride=width_d), :] for e in range(some)], axis=0
        ).T
        high, low = high_low(block)
        mt_ref[:z, n * z : (n + 1) * z] = high
        mt_ref[z:, n * z : (n + 1) * z] = low

    first = lax.broadcasted_iota(jnp.int32, (seqs, 2 * tile_j), 1) < tile_j
    chunk = 4

    def outer_of(d, carry):
        empty = jnp.zeros((seqs, 2 * tile_j), bf16)
        rows = []
        for q in range(nq):
            both = rr_ref[q, d]
            part = (
                jnp.where(first, both, 0.0).astype(bf16),
                jnp.where(first, 0.0, both).astype(bf16),
            )
            for i in range(pack):
                pieces = [empty] * (pack // 2)
                pieces[i // 2] = part[i % 2]
                rows.append(jnp.concatenate(pieces, axis=1))
        block = jnp.concatenate(rows, axis=0)
        at = pl.ds(pl.multiple_of(d * fc, fc), fc)
        for n in range(groups // chunk):
            out = nn_dot(lm_ref[n * chunk * fc : (n + 1) * chunk * fc, :], block)
            high, low = high_low(out)
            oh_ref[n * chunk : (n + 1) * chunk, at, :] = high.reshape(chunk, fc, lanes)
            ol_ref[n * chunk : (n + 1) * chunk, at, :] = low.reshape(chunk, fc, lanes)
        return carry

    lax.fori_loop(0, width_d, outer_of, 0, unroll=2)

    maskl = jnp.concatenate([maskj] * (pack // 2), axis=1) > 0
    score = score_ref[...]
    s1 = score.astype(bf16).astype(f32)
    s2 = (score - s1).astype(bf16).astype(f32)
    s3 = score - s1 - s2
    none = jnp.zeros_like(s1)
    st = jnp.concatenate(
        [
            jnp.concatenate([s1, s2, s3, none], axis=0),
            jnp.concatenate([s1, s2, none, none], axis=0),
        ],
        axis=1,
    ).astype(bf16)

    def finish(g, carry):
        two = nn_dot(mt_ref[...], oh_ref[g])
        update = two[:z] + two[z:] + nn_dot(mt_ref[:z, :], ol_ref[g])
        at = pl.ds(pl.multiple_of(g * lanes, lanes), lanes)
        before = pair_ref[at, :].astype(f32).T
        result = (before + update).astype(bf16)
        pout_t_ref[g] = result
        x = result.astype(f32)
        pout_ref[at, :] = x.T.astype(bf16)
        center = x - jnp.mean(x, axis=0, keepdims=True)
        inverse = lax.rsqrt(jnp.mean(center * center, axis=0, keepdims=True) + epsilon)
        high, low = high_low(center * inverse)
        scores = nn_dot(st, jnp.concatenate([high, low], axis=0))
        logits = scores[:heads] + scores[heads : 2 * heads] + scores[2 * heads : 3 * heads]
        logits_ref[g] = jnp.where(maskl, logits, far_below)
        return carry

    lax.fori_loop(0, groups, finish, 0, unroll=2)


def by_heads(w, heads, out_ref):
    width, chans = w.shape
    hw = chans // heads
    block = 4 * hw
    slot = lax.broadcasted_iota(jnp.int32, (width, block), 1) // hw
    w = w.astype(f32)
    for t in range(chans // block):
        part = w[:, t * block : (t + 1) * block]
        turns = [part] + [pltpu.roll(part, n * hw, 1) for n in range(1, 4)]
        for e in range(4):
            h = t * 4 + e
            for s in range(4):
                out_ref[s * width : (s + 1) * width, h * block : (h + 1) * block] = jnp.where(
                    slot == s, turns[(s - e) % 4], 0.0
                ).astype(bf16)


def weights_kernel(
    col_ref,
    xc_ref,
    rows_ref,
    wv_ref,
    wg_ref,
    wf_ref,
    logits_ref,
    mask_ref,
    gw_ref,
    own_ref,
    pay1_ref,
    pay2_ref,
    pay3_ref,
    acc_ref,
    bv_ref,
    bg_ref,
    bf_ref,
    gs_ref,
    vs_ref,
):
    nq, nk, half, tokens, _ = xc_ref.shape
    tile = nk * tokens
    groups, heads, lanes = logits_ref.shape
    col = col_ref[0]
    by_heads(wv_ref[...], heads, bv_ref)
    by_heads(wg_ref[...], heads, bg_ref)
    by_heads(wf_ref[...], heads, bf_ref)
    acc_ref[...] = jnp.zeros_like(acc_ref)
    block = bv_ref.shape[1] // heads

    def four(read, n):
        return jnp.concatenate(
            [
                jnp.concatenate(
                    [
                        jnp.concatenate([read(k, 2 * (2 * n + e) + p) for k in range(nk)], axis=0)
                        for p in range(2)
                    ],
                    axis=1,
                )
                for e in range(2)
            ],
            axis=0,
        )

    def some(q, carry):
        for hp in range(heads // 2):
            cut = slice(hp * 2 * block, (hp + 1) * 2 * block)
            for n in range(half // 4):
                v = nn_dot(four(lambda k, s: xc_ref[q, k, s], n), bv_ref[:, cut]).astype(bf16)
                gate = nn_dot(four(lambda k, s: rows_ref[q, k, 0, s], n), bg_ref[:, cut])
                grad = nn_dot(four(lambda k, s: rows_ref[q, k, 1, s], n), bf_ref[:, cut])
                g = (grad * jax.nn.sigmoid(gate)).astype(bf16)
                for e in range(2):
                    to = slice((2 * n + e) * block, (2 * n + e + 1) * block)
                    for o in range(2):
                        mine = slice(o * block, (o + 1) * block)
                        ve = v[e * tile : (e + 1) * tile, mine]
                        vs_ref[2 * hp + o, :tile, to] = ve
                        vs_ref[2 * hp + o, tile:, to] = ve
                        gs_ref[2 * hp + o, :, to] = g[e * tile : (e + 1) * tile, mine]
        for h in range(heads):
            acc_ref[h * tile : (h + 1) * tile, :] += nt_dot(gs_ref[h], vs_ref[h])
        return carry

    lax.fori_loop(0, nq, some, 0)

    first = lax.broadcasted_iota(jnp.int32, (groups, 2 * tile), 1) < tile
    for h in range(heads):
        for part in range(pack // 2):
            a = acc_ref[pl.ds(h * tile + 2 * part, groups, stride=pack), :]
            b = acc_ref[pl.ds(h * tile + 2 * part + 1, groups, stride=pack), :]
            gw_ref[:, h, part * 2 * tile : (part + 1) * 2 * tile] = jnp.where(first, a, b)

    rows = groups * heads
    lane = lax.broadcasted_iota(jnp.int32, (rows, 2 * tile), 1)
    low = lane < tile
    maskj = column_mask(mask_ref, col, tile, 2)
    stats = jnp.zeros((rows, 2 * tile), f32)
    for part in range(pack // 2):
        cut = slice(part * 2 * tile, (part + 1) * 2 * tile)
        lg = logits_ref[:, :, cut].reshape(rows, 2 * tile)
        gw = gw_ref[:, :, cut].reshape(rows, 2 * tile)
        m0 = jnp.max(jnp.where(low, lg, far_below), axis=1, keepdims=True)
        m1 = jnp.max(jnp.where(low, far_below, lg), axis=1, keepdims=True)
        p = jnp.exp(lg - jnp.where(low, m0, m1)) * maskj
        pg = p * gw
        for e, m in ((0, m0), (1, m1)):
            mine = low if e == 0 else jnp.logical_not(low)
            i = 2 * part + e
            total = jnp.sum(jnp.where(mine, p, 0.0), axis=1, keepdims=True)
            inner = jnp.sum(jnp.where(mine, pg, 0.0), axis=1, keepdims=True)
            stats = jnp.where(lane == i, m, stats)
            stats = jnp.where(lane == pack + i, total, stats)
            stats = jnp.where(lane == 2 * pack + i, inner, stats)
    turned = stats.T[:16]
    per = groups // nk
    for shift, pay in enumerate((own_ref, pay1_ref, pay2_ref, pay3_ref)):
        dest = lax.rem(col + shift, nk)
        pay[0] = turned[:8]
        pay[1] = turned[8:]
        for g in range(per):
            piece = logits_ref[dest * per + g]
            for part in range(pack // 2):
                pay[2 + g * (pack // 2) + part] = piece[:, part * 2 * tile : (part + 1) * 2 * tile]


def values_kernel(all_ref, wv_ref, norm_ref, wg_ref, v_ref, gate_ref):
    owners, half, tokens, wide = all_ref.shape
    chans = wv_ref.shape[1]
    wv = twice(wv_ref[...])
    for s in range(half):
        x = jnp.concatenate([all_ref[k, s] for k in range(owners)], axis=0)
        v = nn_dot(x, wv).astype(bf16)
        v_ref[s] = v[:, :chans]
        v_ref[s + half] = v[:, chans:]
    gate = jax.nn.sigmoid(nn_dot(norm_ref[...].reshape(half * tokens, wide), twice(wg_ref[...])))
    gate_ref[: half * tokens] = gate[:, :chans]
    gate_ref[half * tokens :] = gate[:, chans:]


def gradient_kernel(
    own_ref, r1_ref, r2_ref, r3_ref, logits_ref, gw_ref, pout_t_ref, score_ref, out_ref, stat_ref
):
    groups, heads, lanes = logits_ref.shape
    rows = groups * heads
    score = score_ref[...]
    z = score.shape[1]
    s1 = score.astype(bf16).astype(f32)
    s2 = (score - s1).astype(bf16).astype(f32)
    s3 = score - s1 - s2
    parts = [s1, s1, s1, s2, s2, s3, jnp.zeros((z - 6 * heads, z), f32)]
    sk = jnp.concatenate(parts, axis=0).T[:, : 6 * heads].astype(bf16)
    pays = (own_ref, r1_ref, r2_ref, r3_ref)
    ms = [p[0][:pack] for p in pays]
    ls = [p[0][pack : 2 * pack] for p in pays]
    ns = [p[1][:pack] for p in pays]
    top = functools.reduce(jnp.maximum, ms)
    scales = [jnp.exp(m - top) for m in ms]
    total = sum(a * b for a, b in zip(ls, scales))
    inner = sum(a * b for a, b in zip(ns, scales)) / total
    stacked = jnp.concatenate([top, total, inner, jnp.zeros((rows - 3 * pack, rows), f32)], axis=0)
    stat_ref[...] = stacked.T

    tile = lanes // pack
    low = lax.broadcasted_iota(jnp.int32, (heads, 2 * tile), 1) < tile

    def one(g, carry):
        st = stat_ref[pl.ds(pl.multiple_of(g * heads, heads), heads), :]

        def spread(base):
            halves = [
                jnp.where(
                    low,
                    st[:, base + 2 * half : base + 2 * half + 1],
                    st[:, base + 2 * half + 1 : base + 2 * half + 2],
                )
                for half in range(pack // 2)
            ]
            return jnp.concatenate(halves, axis=1)

        prob = jnp.exp(logits_ref[g] - spread(0)) / spread(pack)
        gl = prob * (gw_ref[g] - spread(2 * pack))
        g1 = gl.astype(bf16).astype(f32)
        g2 = (gl - g1).astype(bf16).astype(f32)
        g3 = gl - g1 - g2
        stack = jnp.concatenate([g1, g2, g3, g1, g2, g1], axis=0).astype(bf16)
        grad = nn_dot(sk, stack)
        x = pout_t_ref[g].astype(f32)
        center = x - jnp.mean(x, axis=0, keepdims=True)
        inverse = lax.rsqrt(jnp.mean(center * center, axis=0, keepdims=True) + epsilon)
        normal = center * inverse
        centered = grad - jnp.mean(grad, axis=0, keepdims=True)
        along = jnp.mean(grad * normal, axis=0, keepdims=True)
        result = inverse * (centered - normal * along)
        out_ref[pl.ds(pl.multiple_of(g * lanes, lanes), lanes), :] = result.T.astype(bf16)
        return carry

    lax.fori_loop(0, groups, one, 0, unroll=2)


def alignment_kernel(
    col_ref,
    own_ref,
    r1_ref,
    r2_ref,
    r3_ref,
    v_ref,
    gate_ref,
    x_ref,
    wf_ref,
    out_ref,
    w_ref,
    gated_ref,
):
    pays = (own_ref, r1_ref, r2_ref, r3_ref)
    nk = len(pays)
    heads = own_ref.shape[1]
    wide = own_ref.shape[2]
    tile = wide // 2
    pieces = own_ref.shape[0] - 2
    rows = pieces * heads
    seqs, all_tokens, chans = v_ref.shape
    tokens = pieces * 2
    head_width = chans // heads
    col = col_ref[0]

    low = lax.broadcasted_iota(jnp.int32, (rows, wide), 1) < tile
    lgs = [p[2:].reshape(rows, wide) for p in pays]
    peak = functools.reduce(jnp.maximum, lgs)
    m0 = jnp.max(jnp.where(low, peak, far_below), axis=1, keepdims=True)
    m1 = jnp.max(jnp.where(low, far_below, peak), axis=1, keepdims=True)
    top = jnp.where(low, m0, m1)
    ps = [jnp.exp(lg - top) for lg in lgs]
    every = sum(ps)
    t0 = jnp.sum(jnp.where(low, every, 0.0), axis=1, keepdims=True)
    t1 = jnp.sum(jnp.where(low, 0.0, every), axis=1, keepdims=True)
    total = jnp.where(low, t0, t1)
    for shift, p in enumerate(ps):
        source = lax.rem(col + nk - shift, nk)
        weight = p / total
        rolled = pltpu.roll(weight, tile, 1)
        for n in range(pieces):
            w_ref[source, :, 2 * n, :] = weight[n * heads : (n + 1) * heads]
            w_ref[source, :, 2 * n + 1, :] = rolled[n * heads : (n + 1) * heads]
    w = jnp.concatenate(
        [w_ref[k].reshape(heads * tokens, wide)[:, :tile] for k in range(nk)], axis=1
    ).astype(bf16)

    owner = lax.broadcasted_iota(jnp.int32, (tokens, chans), 1) // head_width

    def one(s, carry):
        full = nn_dot(w, v_ref[s])
        mean = jnp.zeros((tokens, chans), f32)
        for h in range(heads):
            mean = jnp.where(owner == h, full[h * tokens : (h + 1) * tokens], mean)
        at = pl.ds(pl.multiple_of(s * tokens, tokens), tokens)
        gated_ref[at, :] = (gate_ref[at, :] * mean).astype(bf16)
        return carry

    lax.fori_loop(0, seqs, one, 0, unroll=4)
    out_ref[...] = (x_ref[...].astype(f32) + nt_dot(gated_ref[...], wf_ref[...])).astype(bf16)


def on_device(
    counts,
    alignment_input,
    pair_input,
    token_valid_mask,
    first_factor_weights,
    second_factor_weights,
    content_weights_grid,
    sigmoid_weights_grid,
    outer_matrix,
    score_matrix,
    final_mixing_weights,
    adjoint_of_rowset,
):
    nq, nr, nk = counts
    row_index = lax.axis_index("row")
    col_index = lax.axis_index("col")
    seqs, tokens, width = alignment_input.shape
    tile_i, tile_j, z = pair_input.shape
    fc = first_factor_weights.shape[1]
    fd = second_factor_weights.shape[1]
    heads = score_matrix.shape[1]
    chans = content_weights_grid.shape[1]
    groups = tile_i // pack
    lanes = pack * tile_j
    sds = jax.ShapeDtypeStruct

    mask = token_valid_mask.reshape(1, -1)
    own_start = ((row_index * nk + col_index) * tokens).astype(jnp.int32).reshape(1)
    col_scalar = col_index.astype(jnp.int32).reshape(1)
    half = seqs // 2

    normed, both, left = call(
        prepare_kernel,
        (
            sds((half, tokens, 2 * width), bf16),
            sds((2, half, tokens, 2 * width), bf16),
            sds((fc, tokens * seqs), bf16),
        ),
        scratch=(pltpu.VMEM((tokens, seqs, width), f32),),
        smem=1,
        vmem=60 * 1024 * 1024,
    )(own_start, alignment_input, adjoint_of_rowset, first_factor_weights.T, mask)

    turn = [(r * nk + c, c * nk + r) for r in range(nr) for c in range(nk)]
    crossed = lax.ppermute(normed, ("row", "col"), turn)
    lefts = lax.all_gather(left, ("seq", "col"), axis=0).reshape(nq, nk, fc, tokens * seqs)
    cols = lax.all_gather(crossed, ("seq", "row"), axis=0).reshape(
        nq, nk, half, tokens, 2 * width
    )
    both, after, lefts, cols = lax.optimization_barrier((both, normed, lefts, cols))
    rows = lax.all_gather(both, ("seq", "col"), axis=0).reshape(
        nq, nk, 2, half, tokens, 2 * width
    )
    every = lax.all_gather(after, ("row", "col"), axis=0)

    pair_out, pair_t, logits = call(
        update_kernel,
        (
            sds((tile_i * tile_j, z), bf16),
            sds((groups, z, lanes), bf16),
            sds((groups, heads, lanes), f32),
        ),
        scratch=(
            pltpu.VMEM((nq, fd, seqs, 2 * tile_j), f32),
            pltpu.VMEM((groups * fc, nq * pack * seqs), bf16),
            pltpu.VMEM((2 * z, fd * fc), bf16),
            pltpu.VMEM((groups, fd * fc, lanes), bf16),
            pltpu.VMEM((groups, fd * fc, lanes), bf16),
        ),
        smem=1,
        flops=14_000_000_000,
        nbytes=5_000_000,
    )(
        col_scalar,
        lefts,
        cols,
        second_factor_weights.T,
        mask,
        outer_matrix,
        score_matrix.T,
        pair_input.reshape(tile_i * tile_j, z),
    )

    payload = sds((2 + groups // nk * (pack // 2), heads, 2 * tile_j), f32)
    gw, pay0, pay1, pay2, pay3 = call(
        weights_kernel,
        (sds((groups, heads, lanes), f32), payload, payload, payload, payload),
        scratch=(
            pltpu.VMEM((heads * tile_i, 2 * tile_j), f32),
            pltpu.VMEM((4 * width, 4 * chans), bf16),
            pltpu.VMEM((4 * width, 4 * chans), bf16),
            pltpu.VMEM((4 * width, 4 * chans), bf16),
            pltpu.VMEM((heads, tile_i, seqs * chans // heads), bf16),
            pltpu.VMEM((heads, 2 * tile_j, seqs * chans // heads), bf16),
        ),
        smem=1,
        flops=6_000_000_000,
        nbytes=3_000_000,
    )(
        col_scalar,
        cols,
        rows,
        content_weights_grid,
        sigmoid_weights_grid,
        final_mixing_weights.T,
        logits,
        mask,
    )

    got = [
        lax.ppermute(pay, "col", [(c, (c + shift) % nk) for c in range(nk)])
        for shift, pay in ((1, pay1), (2, pay2), (3, pay3))
    ]

    values, gating = call(
        values_kernel,
        (sds((seqs, nr * nk * tokens, chans), bf16), sds((seqs * tokens, chans), f32)),
        flops=4_000_000_000,
        nbytes=6_000_000,
    )(every, content_weights_grid, normed, sigmoid_weights_grid)

    gradient = call(
        gradient_kernel,
        sds((tile_i * tile_j, z), bf16),
        scratch=(pltpu.VMEM((groups * heads, groups * heads), f32),),
        flops=4_000_000_000,
        nbytes=3_000_000,
    )(pay0, *got, logits, gw, pair_t, score_matrix.T)

    aligned = call(
        alignment_kernel,
        sds((seqs * tokens, width), bf16),
        scratch=(
            pltpu.VMEM((nk, heads, tokens, 2 * tile_j), f32),
            pltpu.VMEM((seqs * tokens, chans), bf16),
        ),
        smem=1,
        flops=3_000_000_000,
        nbytes=5_000_000,
    )(
        col_scalar,
        pay0,
        *got,
        values,
        gating,
        alignment_input.reshape(seqs * tokens, width),
        final_mixing_weights.T,
    )
    return (
        aligned.reshape(seqs, tokens, width),
        pair_out.reshape(tile_i, tile_j, z),
        gradient.reshape(tile_i, tile_j, z),
    )


def solution(mesh):
    counts = (mesh.shape["seq"], mesh.shape["row"], mesh.shape["col"])
    in_specs = (
        P("seq", ("row", "col"), None),
        P("row", "col", None),
        P(),
        P(),
        P(),
        P(),
        P(),
        P(),
        P(),
        P(),
        P("seq", ("row", "col"), None),
    )
    out_specs = (P("seq", ("row", "col"), None), P("row", "col", None), P("row", "col", None))
    return jax.shard_map(
        functools.partial(on_device, counts),
        mesh=mesh,
        in_specs=in_specs,
        out_specs=out_specs,
        check_vma=False,
    )
```

```python
import functools

import jax
import jax.numpy as jnp
from jax import lax
from jax.experimental import pallas as pl
from jax.experimental.pallas import tpu as pltpu
from jax.sharding import PartitionSpec as P

epsilon = 1e-05
far_below = -1e30
vmem_bytes = 48 * 1024 * 1024
pack = 4

f32 = jnp.float32
bf16 = jnp.bfloat16


def nt_dot(a, b):
    return lax.dot_general(a, b, (((1,), (1,)), ((), ())), preferred_element_type=f32)


def nn_dot(a, b):
    return jnp.dot(a, b, preferred_element_type=f32)


def high_low(x):
    high = x.astype(bf16)
    return high, (x - high.astype(f32)).astype(bf16)


def call(kernel, out_shape, scratch=(), smem=0, flops=0, nbytes=0, vmem=vmem_bytes, far=(), far_out=()):
    count = None

    def run(*args):
        specs = [pl.BlockSpec(memory_space=pltpu.SMEM)] * smem
        specs += [pl.BlockSpec(memory_space=pltpu.VMEM)] * (len(args) - smem)
        return pl.pallas_call(
            kernel,
            out_shape=out_shape,
            in_specs=[
                pl.BlockSpec(memory_space=pl.ANY) if n in far else spec
                for n, spec in enumerate(specs)
            ],
            out_specs=[
                pl.BlockSpec(memory_space=pl.ANY if n in far_out else pltpu.VMEM)
                for n in range(len(out_shape))
            ],
            scratch_shapes=list(scratch),
            compiler_params=pltpu.CompilerParams(vmem_limit_bytes=vmem),
            cost_estimate=pl.CostEstimate(flops=flops, bytes_accessed=nbytes, transcendentals=0),
        )(*args)

    return run


def valid_count(mask_ref):
    return jnp.sum(mask_ref[...].astype(f32), axis=1, keepdims=True)


def column_mask(mask_ref, col, tile, copies):
    lane = lax.broadcasted_iota(jnp.int32, (1, copies * tile), 1)
    token = (lax.rem(lane, tile) + col * tile).astype(f32)
    return (token < valid_count(mask_ref)).astype(f32)


def twice(w):
    none = jnp.zeros_like(w)
    return jnp.concatenate(
        [jnp.concatenate([w, none], axis=1), jnp.concatenate([none, w], axis=1)], axis=0
    )


def prepare_kernel(own_ref, x_ref, adj_ref, w1_ref, mask_ref, norm_ref, both_ref, left_ref, turn_ref):
    seqs, tokens, width = x_ref.shape
    half = seqs // 2
    x = x_ref[...].astype(f32)
    center = x - jnp.mean(x, axis=-1, keepdims=True)
    inverse = lax.rsqrt(jnp.mean(center * center, axis=-1, keepdims=True) + epsilon)
    normed = center * inverse
    packed = jnp.concatenate([normed[:half], normed[half:]], axis=-1).astype(bf16)
    norm_ref[...] = packed
    both_ref[0] = packed
    adj = adj_ref[...].astype(f32)
    both_ref[1] = jnp.concatenate([adj[:half], adj[half:]], axis=-1).astype(bf16)
    for s in range(seqs):
        turn_ref[:, s, :] = normed[s]
    token = lax.broadcasted_iota(jnp.int32, (tokens, seqs, width), 0) + own_ref[0]
    count = valid_count(mask_ref).reshape(1, 1, 1)
    turned = jnp.where(token.astype(f32) < count, turn_ref[...], 0.0).astype(bf16)
    left_ref[...] = nt_dot(w1_ref[...], turned.reshape(tokens * seqs, width)).astype(bf16)


def update_kernel(
    place_ref,
    left0_ref,
    left1_ref,
    left2_ref,
    left3_ref,
    tok0_ref,
    tok1_ref,
    tok2_ref,
    tok3_ref,
    w2_ref,
    mask_ref,
    m_hbm,
    score_ref,
    pair_hbm,
    pout_hbm,
    pout_t_ref,
    logits_ref,
    xc_ref,
    m_ref,
    pair_ref,
    pout_ref,
    in_sem,
    out_sem,
    rr_ref,
    lm_ref,
    mt_ref,
    oh_ref,
    ol_ref,
):
    fetch_m = pltpu.make_async_copy(m_hbm, m_ref, in_sem.at[0])
    fetch_pair = pltpu.make_async_copy(pair_hbm, pair_ref, in_sem.at[1])
    fetch_m.start()
    fetch_pair.start()
    nk, nq, half, tokens, _ = xc_ref.shape
    fc = left0_ref.shape[1]
    row, col = place_ref[0], place_ref[1]
    seqs = 2 * half
    tile_j = nk * tokens
    width_d = w2_ref.shape[0]
    groups = pair_ref.shape[0] // (pack * tile_j)
    per_k = groups // nk
    lanes = pack * tile_j
    wk = pack * seqs
    z = pair_ref.shape[1]
    heads = logits_ref.shape[1]

    w2 = twice(w2_ref[...])
    maskj = column_mask(mask_ref, col, tile_j, 2)

    for t, ref in enumerate((tok0_ref, tok1_ref, tok2_ref, tok3_ref)):
        xc_ref[lax.rem(row + nk - t, nk)] = ref[...]

    def right_of(q, carry):
        for s in range(half):
            x = jnp.concatenate([xc_ref[k, q, s] for k in range(nk)], axis=0)
            res = nt_dot(w2, jnp.concatenate([x, x], axis=0)) * maskj
            rr_ref[q, :, s, :] = res[:width_d]
            rr_ref[q, :, s + half, :] = res[width_d:]
        return carry

    lax.fori_loop(0, nq, right_of, 0)

    for t, ref in enumerate((left0_ref, left1_ref, left2_ref, left3_ref)):
        k = lax.rem(col + nk - t, nk)
        for g in range(per_k):
            at = pl.ds(pl.multiple_of((k * per_k + g) * fc, fc), fc)
            for q in range(nq):
                lm_ref[at, q * wk : (q + 1) * wk] = ref[q, :, g * wk : (g + 1) * wk]

    first = lax.broadcasted_iota(jnp.int32, (seqs, 2 * tile_j), 1) < tile_j
    chunk = 4

    def outer_of(d, carry):
        empty = jnp.zeros((seqs, 2 * tile_j), bf16)
        rows = []
        for q in range(nq):
            both = rr_ref[q, d]
            part = (
                jnp.where(first, both, 0.0).astype(bf16),
                jnp.where(first, 0.0, both).astype(bf16),
            )
            for i in range(pack):
                pieces = [empty] * (pack // 2)
                pieces[i // 2] = part[i % 2]
                rows.append(jnp.concatenate(pieces, axis=1))
        block = jnp.concatenate(rows, axis=0)
        at = pl.ds(pl.multiple_of(d * fc, fc), fc)
        for n in range(groups // chunk):
            out = nn_dot(lm_ref[n * chunk * fc : (n + 1) * chunk * fc, :], block)
            high, low = high_low(out)
            oh_ref[n * chunk : (n + 1) * chunk, at, :] = high.reshape(chunk, fc, lanes)
            ol_ref[n * chunk : (n + 1) * chunk, at, :] = low.reshape(chunk, fc, lanes)
        return carry

    lax.fori_loop(0, width_d, outer_of, 0, unroll=4)

    fetch_m.wait()
    some = z // fc
    for n in range(width_d // some):
        block = jnp.concatenate(
            [m_ref[pl.ds(n * some + e, fc, stride=width_d), :] for e in range(some)], axis=0
        ).T
        high, low = high_low(block)
        mt_ref[:z, n * z : (n + 1) * z] = high
        mt_ref[z:, n * z : (n + 1) * z] = low
    fetch_pair.wait()

    maskl = jnp.concatenate([maskj] * (pack // 2), axis=1) > 0
    score = score_ref[...]
    s1 = score.astype(bf16).astype(f32)
    s2 = (score - s1).astype(bf16).astype(f32)
    s3 = score - s1 - s2
    none = jnp.zeros_like(s1)
    st = jnp.concatenate(
        [
            jnp.concatenate([s1, s2, s3, none], axis=0),
            jnp.concatenate([s1, s2, none, none], axis=0),
        ],
        axis=1,
    ).astype(bf16)

    def finish(g, carry):
        two = nn_dot(mt_ref[...], oh_ref[g])
        update = two[:z] + two[z:] + nn_dot(mt_ref[:z, :], ol_ref[g])
        at = pl.ds(pl.multiple_of(g * lanes, lanes), lanes)
        before = pair_ref[at, :].astype(f32).T
        result = (before + update).astype(bf16)
        pout_t_ref[g] = result
        x = result.astype(f32)
        pout_ref[at, :] = x.T.astype(bf16)
        pltpu.make_async_copy(pout_ref.at[at], pout_hbm.at[at], out_sem.at[g]).start()
        center = x - jnp.mean(x, axis=0, keepdims=True)
        inverse = lax.rsqrt(jnp.mean(center * center, axis=0, keepdims=True) + epsilon)
        high, low = high_low(center * inverse)
        scores = nn_dot(st, jnp.concatenate([high, low], axis=0))
        logits = scores[:heads] + scores[heads : 2 * heads] + scores[2 * heads : 3 * heads]
        logits_ref[g] = jnp.where(maskl, logits, far_below)
        return carry

    lax.fori_loop(0, groups, finish, 0, unroll=4)
    for g in range(groups):
        at = pl.ds(g * lanes, lanes)
        pltpu.make_async_copy(pout_ref.at[at], pout_hbm.at[at], out_sem.at[g]).wait()


def by_heads(w, heads, out_ref):
    width, chans = w.shape
    hw = chans // heads
    block = 4 * hw
    slot = lax.broadcasted_iota(jnp.int32, (width, block), 1) // hw
    w = w.astype(f32)
    for t in range(chans // block):
        part = w[:, t * block : (t + 1) * block]
        turns = [part] + [pltpu.roll(part, n * hw, 1) for n in range(1, 4)]
        for e in range(4):
            h = t * 4 + e
            for s in range(4):
                out_ref[s * width : (s + 1) * width, h * block : (h + 1) * block] = jnp.where(
                    slot == s, turns[(s - e) % 4], 0.0
                ).astype(bf16)


def weights_kernel(
    col_ref,
    xc_ref,
    rows_ref,
    wv_ref,
    wg_ref,
    wf_ref,
    logits_ref,
    mask_ref,
    gw_ref,
    own_ref,
    pay1_ref,
    pay2_ref,
    pay3_ref,
    acc_ref,
    bv_ref,
    bg_ref,
    bf_ref,
    gs_ref,
    vs_ref,
):
    nk, nq, half, tokens, _ = xc_ref.shape
    tile = nk * tokens
    groups, heads, lanes = logits_ref.shape
    col = col_ref[0]
    by_heads(wv_ref[...], heads, bv_ref)
    by_heads(wg_ref[...], heads, bg_ref)
    by_heads(wf_ref[...], heads, bf_ref)
    acc_ref[...] = jnp.zeros_like(acc_ref)
    block = bv_ref.shape[1] // heads

    def four(read, n):
        return jnp.concatenate(
            [
                jnp.concatenate(
                    [
                        jnp.concatenate([read(k, 2 * (2 * n + e) + p) for k in range(nk)], axis=0)
                        for p in range(2)
                    ],
                    axis=1,
                )
                for e in range(2)
            ],
            axis=0,
        )

    def some(q, carry):
        for hp in range(heads // 2):
            cut = slice(hp * 2 * block, (hp + 1) * 2 * block)
            for n in range(half // 4):
                v = nn_dot(four(lambda k, s: xc_ref[k, q, s], n), bv_ref[:, cut]).astype(bf16)
                gate = nn_dot(four(lambda k, s: rows_ref[q, k, 0, s], n), bg_ref[:, cut])
                grad = nn_dot(four(lambda k, s: rows_ref[q, k, 1, s], n), bf_ref[:, cut])
                g = (grad * jax.nn.sigmoid(gate)).astype(bf16)
                for e in range(2):
                    to = slice((2 * n + e) * block, (2 * n + e + 1) * block)
                    for o in range(2):
                        mine = slice(o * block, (o + 1) * block)
                        ve = v[e * tile : (e + 1) * tile, mine]
                        vs_ref[2 * hp + o, :tile, to] = ve
                        vs_ref[2 * hp + o, tile:, to] = ve
                        gs_ref[2 * hp + o, :, to] = g[e * tile : (e + 1) * tile, mine]
        for h in range(heads):
            acc_ref[h * tile : (h + 1) * tile, :] += nt_dot(gs_ref[h], vs_ref[h])
        return carry

    lax.fori_loop(0, nq, some, 0)

    first = lax.broadcasted_iota(jnp.int32, (groups, 2 * tile), 1) < tile
    for h in range(heads):
        for part in range(pack // 2):
            a = acc_ref[pl.ds(h * tile + 2 * part, groups, stride=pack), :]
            b = acc_ref[pl.ds(h * tile + 2 * part + 1, groups, stride=pack), :]
            gw_ref[:, h, part * 2 * tile : (part + 1) * 2 * tile] = jnp.where(first, a, b)

    rows = groups * heads
    lane = lax.broadcasted_iota(jnp.int32, (rows, 2 * tile), 1)
    low = lane < tile
    maskj = column_mask(mask_ref, col, tile, 2)
    stats = jnp.zeros((rows, 2 * tile), f32)
    for part in range(pack // 2):
        cut = slice(part * 2 * tile, (part + 1) * 2 * tile)
        lg = logits_ref[:, :, cut].reshape(rows, 2 * tile)
        gw = gw_ref[:, :, cut].reshape(rows, 2 * tile)
        m0 = jnp.max(jnp.where(low, lg, far_below), axis=1, keepdims=True)
        m1 = jnp.max(jnp.where(low, far_below, lg), axis=1, keepdims=True)
        p = jnp.exp(lg - jnp.where(low, m0, m1)) * maskj
        pg = p * gw
        for e, m in ((0, m0), (1, m1)):
            mine = low if e == 0 else jnp.logical_not(low)
            i = 2 * part + e
            total = jnp.sum(jnp.where(mine, p, 0.0), axis=1, keepdims=True)
            inner = jnp.sum(jnp.where(mine, pg, 0.0), axis=1, keepdims=True)
            stats = jnp.where(lane == i, m, stats)
            stats = jnp.where(lane == pack + i, total, stats)
            stats = jnp.where(lane == 2 * pack + i, inner, stats)
    turned = stats.T[:16]
    per = groups // nk
    for shift, pay in enumerate((own_ref, pay1_ref, pay2_ref, pay3_ref)):
        dest = lax.rem(col + shift, nk)
        pay[0] = turned[:8]
        pay[1] = turned[8:]
        for g in range(per):
            piece = logits_ref[dest * per + g]
            for part in range(pack // 2):
                pay[2 + g * (pack // 2) + part] = piece[:, part * 2 * tile : (part + 1) * 2 * tile]


def values_kernel(all_ref, wv_ref, norm_ref, wg_ref, v_ref, gate_ref):
    owners, half, tokens, wide = all_ref.shape
    chans = wv_ref.shape[1]
    wv = twice(wv_ref[...])
    for s in range(half):
        x = jnp.concatenate([all_ref[k, s] for k in range(owners)], axis=0)
        v = nn_dot(x, wv).astype(bf16)
        v_ref[s] = v[:, :chans]
        v_ref[s + half] = v[:, chans:]
    gate = jax.nn.sigmoid(nn_dot(norm_ref[...].reshape(half * tokens, wide), twice(wg_ref[...])))
    gate_ref[: half * tokens] = gate[:, :chans]
    gate_ref[half * tokens :] = gate[:, chans:]


def gradient_kernel(
    own_ref, r1_ref, r2_ref, r3_ref, logits_ref, gw_ref, pout_t_ref, score_ref, out_ref, stat_ref
):
    groups, heads, lanes = logits_ref.shape
    rows = groups * heads
    score = score_ref[...]
    z = score.shape[1]
    s1 = score.astype(bf16).astype(f32)
    s2 = (score - s1).astype(bf16).astype(f32)
    s3 = score - s1 - s2
    parts = [s1, s1, s1, s2, s2, s3, jnp.zeros((z - 6 * heads, z), f32)]
    sk = jnp.concatenate(parts, axis=0).T[:, : 6 * heads].astype(bf16)
    pays = (own_ref, r1_ref, r2_ref, r3_ref)
    ms = [p[0][:pack] for p in pays]
    ls = [p[0][pack : 2 * pack] for p in pays]
    ns = [p[1][:pack] for p in pays]
    top = functools.reduce(jnp.maximum, ms)
    scales = [jnp.exp(m - top) for m in ms]
    total = sum(a * b for a, b in zip(ls, scales))
    inner = sum(a * b for a, b in zip(ns, scales)) / total
    stacked = jnp.concatenate([top, total, inner, jnp.zeros((rows - 3 * pack, rows), f32)], axis=0)
    stat_ref[...] = stacked.T

    tile = lanes // pack
    low = lax.broadcasted_iota(jnp.int32, (heads, 2 * tile), 1) < tile

    def one(g, carry):
        st = stat_ref[pl.ds(pl.multiple_of(g * heads, heads), heads), :]

        def spread(base):
            halves = [
                jnp.where(
                    low,
                    st[:, base + 2 * half : base + 2 * half + 1],
                    st[:, base + 2 * half + 1 : base + 2 * half + 2],
                )
                for half in range(pack // 2)
            ]
            return jnp.concatenate(halves, axis=1)

        prob = jnp.exp(logits_ref[g] - spread(0)) / spread(pack)
        gl = prob * (gw_ref[g] - spread(2 * pack))
        g1 = gl.astype(bf16).astype(f32)
        g2 = (gl - g1).astype(bf16).astype(f32)
        g3 = gl - g1 - g2
        stack = jnp.concatenate([g1, g2, g3, g1, g2, g1], axis=0).astype(bf16)
        grad = nn_dot(sk, stack)
        x = pout_t_ref[g].astype(f32)
        center = x - jnp.mean(x, axis=0, keepdims=True)
        inverse = lax.rsqrt(jnp.mean(center * center, axis=0, keepdims=True) + epsilon)
        normal = center * inverse
        centered = grad - jnp.mean(grad, axis=0, keepdims=True)
        along = jnp.mean(grad * normal, axis=0, keepdims=True)
        result = inverse * (centered - normal * along)
        out_ref[pl.ds(pl.multiple_of(g * lanes, lanes), lanes), :] = result.T.astype(bf16)
        return carry

    lax.fori_loop(0, groups, one, 0, unroll=4)


def alignment_kernel(
    col_ref,
    own_ref,
    r1_ref,
    r2_ref,
    r3_ref,
    v_ref,
    gate_ref,
    x_ref,
    wf_ref,
    out_ref,
    w_ref,
    gated_ref,
):
    pays = (own_ref, r1_ref, r2_ref, r3_ref)
    nk = len(pays)
    heads = own_ref.shape[1]
    wide = own_ref.shape[2]
    tile = wide // 2
    pieces = own_ref.shape[0] - 2
    rows = pieces * heads
    seqs, all_tokens, chans = v_ref.shape
    tokens = pieces * 2
    head_width = chans // heads
    col = col_ref[0]

    low = lax.broadcasted_iota(jnp.int32, (rows, wide), 1) < tile
    lgs = [p[2:].reshape(rows, wide) for p in pays]
    peak = functools.reduce(jnp.maximum, lgs)
    m0 = jnp.max(jnp.where(low, peak, far_below), axis=1, keepdims=True)
    m1 = jnp.max(jnp.where(low, far_below, peak), axis=1, keepdims=True)
    top = jnp.where(low, m0, m1)
    ps = [jnp.exp(lg - top) for lg in lgs]
    every = sum(ps)
    t0 = jnp.sum(jnp.where(low, every, 0.0), axis=1, keepdims=True)
    t1 = jnp.sum(jnp.where(low, 0.0, every), axis=1, keepdims=True)
    total = jnp.where(low, t0, t1)
    for shift, p in enumerate(ps):
        source = lax.rem(col + nk - shift, nk)
        weight = p / total
        rolled = pltpu.roll(weight, tile, 1)
        for n in range(pieces):
            w_ref[source, :, 2 * n, :] = weight[n * heads : (n + 1) * heads]
            w_ref[source, :, 2 * n + 1, :] = rolled[n * heads : (n + 1) * heads]
    w = jnp.concatenate(
        [w_ref[k].reshape(heads * tokens, wide)[:, :tile] for k in range(nk)], axis=1
    ).astype(bf16)

    owner = lax.broadcasted_iota(jnp.int32, (tokens, chans), 1) // head_width

    def one(s, carry):
        full = nn_dot(w, v_ref[s])
        mean = jnp.zeros((tokens, chans), f32)
        for h in range(heads):
            mean = jnp.where(owner == h, full[h * tokens : (h + 1) * tokens], mean)
        at = pl.ds(pl.multiple_of(s * tokens, tokens), tokens)
        gated_ref[at, :] = (gate_ref[at, :] * mean).astype(bf16)
        return carry

    lax.fori_loop(0, seqs, one, 0, unroll=4)
    out_ref[...] = (x_ref[...].astype(f32) + nt_dot(gated_ref[...], wf_ref[...])).astype(bf16)


def on_device(
    counts,
    alignment_input,
    pair_input,
    token_valid_mask,
    first_factor_weights,
    second_factor_weights,
    content_weights_grid,
    sigmoid_weights_grid,
    outer_matrix,
    score_matrix,
    final_mixing_weights,
    adjoint_of_rowset,
):
    nq, nr, nk = counts
    row_index = lax.axis_index("row")
    col_index = lax.axis_index("col")
    seqs, tokens, width = alignment_input.shape
    tile_i, tile_j, z = pair_input.shape
    fc = first_factor_weights.shape[1]
    fd = second_factor_weights.shape[1]
    heads = score_matrix.shape[1]
    chans = content_weights_grid.shape[1]
    groups = tile_i // pack
    lanes = pack * tile_j
    sds = jax.ShapeDtypeStruct

    mask = token_valid_mask.reshape(1, -1)
    own_start = ((row_index * nk + col_index) * tokens).astype(jnp.int32).reshape(1)
    place = jnp.stack([row_index, col_index]).astype(jnp.int32)
    col_scalar = col_index.astype(jnp.int32).reshape(1)
    half = seqs // 2

    normed, both, left = call(
        prepare_kernel,
        (
            sds((half, tokens, 2 * width), bf16),
            sds((2, half, tokens, 2 * width), bf16),
            sds((fc, tokens * seqs), bf16),
        ),
        scratch=(pltpu.VMEM((tokens, seqs, width), f32),),
        smem=1,
        vmem=60 * 1024 * 1024,
    )(own_start, alignment_input, adjoint_of_rowset, first_factor_weights.T, mask)

    rows = lax.all_gather(both, ("seq", "col"), axis=0).reshape(
        nq, nk, 2, half, tokens, 2 * width
    )
    every = lax.all_gather(normed, ("row", "col"), axis=0)
    toks = lax.all_gather(normed, "seq", axis=0)
    lefts = lax.all_gather(left, "seq", axis=0)

    all_lefts = [lefts] + [
        lax.ppermute(lefts, "col", [(c, (c + t) % nk) for c in range(nk)]) for t in range(1, nk)
    ]
    all_toks = [
        lax.ppermute(
            toks,
            ("row", "col"),
            [(r * nk + c, (c + t) % nr * nk + r) for r in range(nr) for c in range(nk)],
        )
        for t in range(nr)
    ]

    pair_out, pair_t, logits, cols = call(
        update_kernel,
        (
            sds((tile_i * tile_j, z), bf16),
            sds((groups, z, lanes), bf16),
            sds((groups, heads, lanes), f32),
            sds((nk, nq, half, tokens, 2 * width), bf16),
        ),
        scratch=(
            pltpu.VMEM((fc * fd, z), f32),
            pltpu.VMEM((tile_i * tile_j, z), bf16),
            pltpu.VMEM((tile_i * tile_j, z), bf16),
            pltpu.SemaphoreType.DMA((2,)),
            pltpu.SemaphoreType.DMA((groups,)),
            pltpu.VMEM((nq, fd, seqs, 2 * tile_j), f32),
            pltpu.VMEM((groups * fc, nq * pack * seqs), bf16),
            pltpu.VMEM((2 * z, fd * fc), bf16),
            pltpu.VMEM((groups, fd * fc, lanes), bf16),
            pltpu.VMEM((groups, fd * fc, lanes), bf16),
        ),
        smem=1,
        flops=14_000_000_000,
        nbytes=5_000_000,
        vmem=60 * 1024 * 1024,
        far=(11, 13),
        far_out=(0,),
    )(
        place,
        *all_lefts,
        *all_toks,
        second_factor_weights.T,
        mask,
        outer_matrix,
        score_matrix.T,
        pair_input.reshape(tile_i * tile_j, z),
    )

    payload = sds((2 + groups // nk * (pack // 2), heads, 2 * tile_j), f32)
    gw, pay0, pay1, pay2, pay3 = call(
        weights_kernel,
        (sds((groups, heads, lanes), f32), payload, payload, payload, payload),
        scratch=(
            pltpu.VMEM((heads * tile_i, 2 * tile_j), f32),
            pltpu.VMEM((4 * width, 4 * chans), bf16),
            pltpu.VMEM((4 * width, 4 * chans), bf16),
            pltpu.VMEM((4 * width, 4 * chans), bf16),
            pltpu.VMEM((heads, tile_i, seqs * chans // heads), bf16),
            pltpu.VMEM((heads, 2 * tile_j, seqs * chans // heads), bf16),
        ),
        smem=1,
        flops=6_000_000_000,
        nbytes=3_000_000,
    )(
        col_scalar,
        cols,
        rows,
        content_weights_grid,
        sigmoid_weights_grid,
        final_mixing_weights.T,
        logits,
        mask,
    )

    got = [
        lax.ppermute(pay, "col", [(c, (c + shift) % nk) for c in range(nk)])
        for shift, pay in ((1, pay1), (2, pay2), (3, pay3))
    ]

    values, gating = call(
        values_kernel,
        (sds((seqs, nr * nk * tokens, chans), bf16), sds((seqs * tokens, chans), f32)),
        flops=4_000_000_000,
        nbytes=6_000_000,
    )(every, content_weights_grid, normed, sigmoid_weights_grid)

    (gradient,) = call(
        gradient_kernel,
        (sds((tile_i * tile_j, z), bf16),),
        scratch=(pltpu.VMEM((groups * heads, groups * heads), f32),),
        flops=4_000_000_000,
        nbytes=3_000_000,
    )(pay0, *got, logits, gw, pair_t, score_matrix.T)

    (aligned,) = call(
        alignment_kernel,
        (sds((seqs * tokens, width), bf16),),
        scratch=(
            pltpu.VMEM((nk, heads, tokens, 2 * tile_j), f32),
            pltpu.VMEM((seqs * tokens, chans), bf16),
        ),
        smem=1,
        flops=3_000_000_000,
        nbytes=5_000_000,
    )(
        col_scalar,
        pay0,
        *got,
        values,
        gating,
        alignment_input.reshape(seqs * tokens, width),
        final_mixing_weights.T,
    )
    return (
        aligned.reshape(seqs, tokens, width),
        pair_out.reshape(tile_i, tile_j, z),
        gradient.reshape(tile_i, tile_j, z),
    )


def solution(mesh):
    counts = (mesh.shape["seq"], mesh.shape["row"], mesh.shape["col"])
    in_specs = (
        P("seq", ("row", "col"), None),
        P("row", "col", None),
        P(),
        P(),
        P(),
        P(),
        P(),
        P(),
        P(),
        P(),
        P("seq", ("row", "col"), None),
    )
    out_specs = (P("seq", ("row", "col"), None), P("row", "col", None), P("row", "col", None))
    return jax.shard_map(
        functools.partial(on_device, counts),
        mesh=mesh,
        in_specs=in_specs,
        out_specs=out_specs,
        check_vma=False,
    )
```

```python
import functools

import jax
import jax.numpy as jnp
from jax import lax
from jax.experimental import pallas as pl
from jax.experimental.pallas import tpu as pltpu
from jax.sharding import PartitionSpec as P

epsilon = 1e-05
far_below = -1e30
vmem_bytes = 48 * 1024 * 1024
pack = 4

f32 = jnp.float32
bf16 = jnp.bfloat16


def nt_dot(a, b):
    return lax.dot_general(a, b, (((1,), (1,)), ((), ())), preferred_element_type=f32)


def nn_dot(a, b):
    return jnp.dot(a, b, preferred_element_type=f32)


def high_low(x):
    high = x.astype(bf16)
    return high, (x - high.astype(f32)).astype(bf16)


def call(kernel, out_shape, scratch=(), smem=0, flops=0, nbytes=0, vmem=vmem_bytes, far=(), far_out=()):
    count = None

    def run(*args):
        specs = [pl.BlockSpec(memory_space=pltpu.SMEM)] * smem
        specs += [pl.BlockSpec(memory_space=pltpu.VMEM)] * (len(args) - smem)
        return pl.pallas_call(
            kernel,
            out_shape=out_shape,
            in_specs=[
                pl.BlockSpec(memory_space=pl.ANY) if n in far else spec
                for n, spec in enumerate(specs)
            ],
            out_specs=[
                pl.BlockSpec(memory_space=pl.ANY if n in far_out else pltpu.VMEM)
                for n in range(len(out_shape))
            ],
            scratch_shapes=list(scratch),
            compiler_params=pltpu.CompilerParams(vmem_limit_bytes=vmem),
            cost_estimate=pl.CostEstimate(flops=flops, bytes_accessed=nbytes, transcendentals=0),
        )(*args)

    return run


def valid_count(mask_ref):
    return jnp.sum(mask_ref[...].astype(f32), axis=1, keepdims=True)


def column_mask(mask_ref, col, tile, copies):
    lane = lax.broadcasted_iota(jnp.int32, (1, copies * tile), 1)
    token = (lax.rem(lane, tile) + col * tile).astype(f32)
    return (token < valid_count(mask_ref)).astype(f32)


def twice(w):
    none = jnp.zeros_like(w)
    return jnp.concatenate(
        [jnp.concatenate([w, none], axis=1), jnp.concatenate([none, w], axis=1)], axis=0
    )


def prepare_kernel(
    own_ref, x_ref, adj_ref, w1_ref, w2_ref, mask_ref, both_ref, sides_ref, turn_ref, right_ref
):
    seqs, tokens, width = x_ref.shape
    half = seqs // 2
    fd = w2_ref.shape[0]
    x = x_ref[...].astype(f32)
    center = x - jnp.mean(x, axis=-1, keepdims=True)
    inverse = lax.rsqrt(jnp.mean(center * center, axis=-1, keepdims=True) + epsilon)
    normed = center * inverse
    rows = half * tokens
    packed = jnp.concatenate([normed[:half], normed[half:]], axis=-1)
    both_ref[:rows] = packed.reshape(rows, 2 * width).astype(bf16)
    adj = adj_ref[...].astype(f32)
    packed = jnp.concatenate([adj[:half], adj[half:]], axis=-1)
    both_ref[rows:] = packed.reshape(rows, 2 * width).astype(bf16)
    token = lax.broadcasted_iota(jnp.int32, (seqs, tokens, width), 1) + own_ref[0]
    count = valid_count(mask_ref).reshape(1, 1, 1)
    real = jnp.where(token.astype(f32) < count, normed, 0.0)
    for s in range(seqs):
        turn_ref[:, s, :] = real[s]
    turned = turn_ref[...].astype(bf16).reshape(tokens * seqs, width)
    left = nt_dot(w1_ref[...], turned).astype(bf16)
    fc = w1_ref.shape[0]
    wk = pack * seqs
    for g in range(tokens // pack):
        sides_ref[g * fc : (g + 1) * fc, :] = left[:, g * wk : (g + 1) * wk]
    size = 128 // tokens
    real = real.astype(bf16)
    w2 = w2_ref[...]
    d = lax.broadcasted_iota(jnp.int32, (fd, 128), 0)
    lane = lax.broadcasted_iota(jnp.int32, (fd, 128), 1)
    mine = lax.rem(d, size) == lane // tokens
    for s in range(seqs):
        res = nt_dot(w2, jnp.concatenate([real[s]] * size, axis=0))
        res = jnp.where(mine, res, 0.0).reshape(fd // size, size, 128)
        right_ref[:, s, :] = jnp.sum(res, axis=1)
    base = tokens // pack * fc
    sides_ref[base:, :] = right_ref[...].reshape(fd // size * seqs, 128).astype(bf16)


def update_kernel(
    place_ref,
    left0_ref,
    left1_ref,
    left2_ref,
    left3_ref,
    right0_ref,
    right1_ref,
    right2_ref,
    right3_ref,
    mask_ref,
    m_hbm,
    score_ref,
    pair_hbm,
    pout_hbm,
    pout_t_ref,
    logits_ref,
    m_ref,
    pair_ref,
    pout_ref,
    in_sem,
    out_sem,
    rk_ref,
    rab_ref,
    lm_ref,
    mt_ref,
    oh_ref,
    ol_ref,
):
    fetch_m = pltpu.make_async_copy(m_hbm, m_ref, in_sem.at[0])
    fetch_pair = pltpu.make_async_copy(pair_hbm, pair_ref, in_sem.at[1])
    fetch_m.start()
    fetch_pair.start()
    nk = rk_ref.shape[0]
    width_d, pair_rows, _ = rab_ref.shape
    nq = right0_ref.shape[0]
    seqs = pair_rows // nq
    row, col = place_ref[0], place_ref[1]
    z = pair_ref.shape[1]
    groups, heads, lanes = logits_ref.shape
    tile_j = lanes // pack
    tokens = tile_j // nk
    per_k = groups // nk
    fc = lm_ref.shape[0] // groups
    wk = pack * seqs
    maskj = column_mask(mask_ref, col, tile_j, 2)

    for t, ref in enumerate((right0_ref, right1_ref, right2_ref, right3_ref)):
        rk_ref[lax.rem(row + nk - t, nk)] = ref[...].reshape(rk_ref.shape[1:])
    size = 128 // tokens
    right = jnp.concatenate([rk_ref[k] for k in range(nk)], axis=1)
    source = lax.broadcasted_iota(jnp.int32, (nk * 128, 4 * tile_j), 0)
    target = lax.broadcasted_iota(jnp.int32, (nk * 128, 4 * tile_j), 1)
    used = jnp.logical_or(target < tile_j, target >= 3 * tile_j)
    j = lax.rem(target, tile_j)
    offset = jnp.where(used, source - (j // tokens * 128 + lax.rem(j, tokens)), -1)
    blocks = width_d // size
    for e in range(size):
        pick = jnp.where(offset == e * tokens, 1.0, 0.0).astype(bf16)
        res = nn_dot(right, pick).astype(bf16)
        for q in range(nq):
            for n in range(blocks):
                at = (q * blocks + n) * seqs
                rab_ref[n * size + e, q * seqs : (q + 1) * seqs, :] = res[at : at + seqs]

    for t, ref in enumerate((left0_ref, left1_ref, left2_ref, left3_ref)):
        k = lax.rem(col + nk - t, nk)
        for g in range(per_k):
            at = pl.ds(pl.multiple_of((k * per_k + g) * fc, fc), fc)
            for q in range(nq):
                from_row = (q * per_k + g) * fc
                lm_ref[at, q * wk : (q + 1) * wk] = ref[from_row : from_row + fc, :]

    chunk = 4

    def outer_of(d, carry):
        empty = jnp.zeros((seqs, 2 * tile_j), bf16)
        rows = []
        for q in range(nq):
            both = rab_ref[d, q * seqs : (q + 1) * seqs, :]
            part = both[:, : 2 * tile_j], both[:, 2 * tile_j :]
            for i in range(pack):
                pieces = [empty] * (pack // 2)
                pieces[i // 2] = part[i % 2]
                rows.append(jnp.concatenate(pieces, axis=1))
        block = jnp.concatenate(rows, axis=0)
        at = pl.ds(pl.multiple_of(d * fc, fc), fc)
        for n in range(groups // chunk):
            out = nn_dot(lm_ref[n * chunk * fc : (n + 1) * chunk * fc, :], block)
            high, low = high_low(out)
            oh_ref[n * chunk : (n + 1) * chunk, at, :] = high.reshape(chunk, fc, lanes)
            ol_ref[n * chunk : (n + 1) * chunk, at, :] = low.reshape(chunk, fc, lanes)
        return carry

    lax.fori_loop(0, width_d, outer_of, 0, unroll=4)

    fetch_m.wait()
    some = z // fc
    for n in range(width_d // some):
        block = jnp.concatenate(
            [m_ref[pl.ds(n * some + e, fc, stride=width_d), :] for e in range(some)], axis=0
        ).T
        high, low = high_low(block)
        mt_ref[:z, n * z : (n + 1) * z] = high
        mt_ref[z:, n * z : (n + 1) * z] = low
    fetch_pair.wait()

    maskl = jnp.concatenate([maskj] * (pack // 2), axis=1) > 0
    score = score_ref[...]
    s1 = score.astype(bf16).astype(f32)
    s2 = (score - s1).astype(bf16).astype(f32)
    s3 = score - s1 - s2
    none = jnp.zeros_like(s1)
    st = jnp.concatenate(
        [
            jnp.concatenate([s1, s2, s3, none], axis=0),
            jnp.concatenate([s1, s2, none, none], axis=0),
        ],
        axis=1,
    ).astype(bf16)

    def finish(g, carry):
        two = nn_dot(mt_ref[...], oh_ref[g])
        update = two[:z] + two[z:] + nn_dot(mt_ref[:z, :], ol_ref[g])
        at = pl.ds(pl.multiple_of(g * lanes, lanes), lanes)
        before = pair_ref[at, :].astype(f32).T
        result = (before + update).astype(bf16)
        pout_t_ref[g] = result
        x = result.astype(f32)
        pout_ref[at, :] = x.T.astype(bf16)
        pltpu.make_async_copy(pout_ref.at[at], pout_hbm.at[at], out_sem.at[g]).start()
        center = x - jnp.mean(x, axis=0, keepdims=True)
        inverse = lax.rsqrt(jnp.mean(center * center, axis=0, keepdims=True) + epsilon)
        high, low = high_low(center * inverse)
        scores = nn_dot(st, jnp.concatenate([high, low], axis=0))
        logits = scores[:heads] + scores[heads : 2 * heads] + scores[2 * heads : 3 * heads]
        logits_ref[g] = jnp.where(maskl, logits, far_below)
        return carry

    lax.fori_loop(0, groups, finish, 0, unroll=4)
    for g in range(groups):
        at = pl.ds(g * lanes, lanes)
        pltpu.make_async_copy(pout_ref.at[at], pout_hbm.at[at], out_sem.at[g]).wait()


def by_heads(w, heads, out_ref):
    width, chans = w.shape
    hw = chans // heads
    block = 4 * hw
    slot = lax.broadcasted_iota(jnp.int32, (width, block), 1) // hw
    w = w.astype(f32)
    for t in range(chans // block):
        part = w[:, t * block : (t + 1) * block]
        turns = [part] + [pltpu.roll(part, n * hw, 1) for n in range(1, 4)]
        for e in range(4):
            h = t * 4 + e
            for s in range(4):
                out_ref[s * width : (s + 1) * width, h * block : (h + 1) * block] = jnp.where(
                    slot == s, turns[(s - e) % 4], 0.0
                ).astype(bf16)


def weights_kernel(
    col_ref,
    ev_ref,
    side0_ref,
    side1_ref,
    side2_ref,
    side3_ref,
    wv_ref,
    wg_ref,
    wf_ref,
    gw_ref,
    acc_ref,
    bv_ref,
    bg_ref,
    bf_ref,
    rows_ref,
    gs_ref,
    vs_ref,
):
    _, nk, half, tokens, _ = ev_ref.shape
    tile = nk * tokens
    groups, heads, lanes = gw_ref.shape
    col = col_ref[0]
    count = rows_ref.shape[1] * rows_ref.shape[2] * tokens
    for t, ref in enumerate((side0_ref, side1_ref, side2_ref, side3_ref)):
        start = ref.shape[0] - count
        rows_ref[lax.rem(col + nk - t, nk)] = ref[start:, :].reshape(rows_ref.shape[1:])
    by_heads(wv_ref[...], heads, bv_ref)
    by_heads(wg_ref[...], heads, bg_ref)
    by_heads(wf_ref[...], heads, bf_ref)
    block = bv_ref.shape[1] // heads

    def four(read, n):
        return jnp.concatenate(
            [
                jnp.concatenate(
                    [
                        jnp.concatenate([read(k, 2 * (2 * n + e) + p) for k in range(nk)], axis=0)
                        for p in range(2)
                    ],
                    axis=1,
                )
                for e in range(2)
            ],
            axis=0,
        )

    slots = [lax.rem(col + nk - k, nk) for k in range(nk)]
    for hp in range(heads // 2):
        cut = slice(hp * 2 * block, (hp + 1) * 2 * block)
        for n in range(half // 4):
            v = nn_dot(four(lambda k, s: ev_ref[col, slots[k], s], n), bv_ref[:, cut]).astype(bf16)
            gate = nn_dot(four(lambda k, s: rows_ref[k, 0, s], n), bg_ref[:, cut])
            grad = nn_dot(four(lambda k, s: rows_ref[k, 1, s], n), bf_ref[:, cut])
            g = (grad * jax.nn.sigmoid(gate)).astype(bf16)
            for e in range(2):
                to = slice((2 * n + e) * block, (2 * n + e + 1) * block)
                for o in range(2):
                    mine = slice(o * block, (o + 1) * block)
                    ve = v[e * tile : (e + 1) * tile, mine]
                    vs_ref[2 * hp + o, :tile, to] = ve
                    vs_ref[2 * hp + o, tile:, to] = ve
                    gs_ref[2 * hp + o, :, to] = g[e * tile : (e + 1) * tile, mine]
    for h in range(heads):
        acc_ref[h * tile : (h + 1) * tile, :] = nt_dot(gs_ref[h], vs_ref[h])

    first = lax.broadcasted_iota(jnp.int32, (groups, 2 * tile), 1) < tile
    for h in range(heads):
        for part in range(pack // 2):
            a = acc_ref[pl.ds(h * tile + 2 * part, groups, stride=pack), :]
            b = acc_ref[pl.ds(h * tile + 2 * part + 1, groups, stride=pack), :]
            gw_ref[:, h, part * 2 * tile : (part + 1) * 2 * tile] = jnp.where(first, a, b)


def softmax_kernel(
    col_ref,
    logits_ref,
    gwa_ref,
    gwb_ref,
    mask_ref,
    gw_ref,
    own_ref,
    pay1_ref,
    pay2_ref,
    pay3_ref,
):
    groups, heads, lanes = logits_ref.shape
    tile = lanes // pack
    nk = 4
    rows = groups * heads
    col = col_ref[0]
    gw_ref[...] = gwa_ref[...] + gwb_ref[...]
    lane = lax.broadcasted_iota(jnp.int32, (rows, 2 * tile), 1)
    low = lane < tile
    maskj = column_mask(mask_ref, col, tile, 2)
    stats = jnp.zeros((rows, 2 * tile), f32)
    for part in range(pack // 2):
        cut = slice(part * 2 * tile, (part + 1) * 2 * tile)
        lg = logits_ref[:, :, cut].reshape(rows, 2 * tile)
        gw = gw_ref[:, :, cut].reshape(rows, 2 * tile)
        m0 = jnp.max(jnp.where(low, lg, far_below), axis=1, keepdims=True)
        m1 = jnp.max(jnp.where(low, far_below, lg), axis=1, keepdims=True)
        p = jnp.exp(lg - jnp.where(low, m0, m1)) * maskj
        pg = p * gw
        for e, m in ((0, m0), (1, m1)):
            mine = low if e == 0 else jnp.logical_not(low)
            i = 2 * part + e
            total = jnp.sum(jnp.where(mine, p, 0.0), axis=1, keepdims=True)
            inner = jnp.sum(jnp.where(mine, pg, 0.0), axis=1, keepdims=True)
            stats = jnp.where(lane == i, m, stats)
            stats = jnp.where(lane == pack + i, total, stats)
            stats = jnp.where(lane == 2 * pack + i, inner, stats)
    turned = stats.T[:16]
    per = groups // nk
    for shift, pay in enumerate((own_ref, pay1_ref, pay2_ref, pay3_ref)):
        dest = lax.rem(col + shift, nk)
        pay[0] = turned[:8]
        pay[1] = turned[8:]
        for g in range(per):
            piece = logits_ref[dest * per + g]
            for part in range(pack // 2):
                pay[2 + g * (pack // 2) + part] = piece[:, part * 2 * tile : (part + 1) * 2 * tile]


def values_kernel(col_ref, ev_ref, wv_ref, both_ref, wg_ref, v_ref, gate_ref):
    nr, nk, half, tokens, wide = ev_ref.shape
    chans = wv_ref.shape[1]
    wv = twice(wv_ref[...])
    slots = [lax.rem(col_ref[0] + nk - k, nk) for k in range(nk)]
    for s in range(half):
        x = jnp.concatenate([ev_ref[r, slots[k], s] for r in range(nr) for k in range(nk)], axis=0)
        v = nn_dot(x, wv).astype(bf16)
        v_ref[s] = v[:, :chans]
        v_ref[s + half] = v[:, chans:]
    gate = jax.nn.sigmoid(nn_dot(both_ref[: half * tokens, :], twice(wg_ref[...])))
    gate_ref[: half * tokens] = gate[:, :chans]
    gate_ref[half * tokens :] = gate[:, chans:]


def gradient_kernel(
    own_ref, r1_ref, r2_ref, r3_ref, logits_ref, gw_ref, pout_t_ref, score_ref, out_ref, stat_ref
):
    groups, heads, lanes = logits_ref.shape
    rows = groups * heads
    score = score_ref[...]
    z = score.shape[1]
    s1 = score.astype(bf16).astype(f32)
    s2 = (score - s1).astype(bf16).astype(f32)
    s3 = score - s1 - s2
    parts = [s1, s1, s1, s2, s2, s3, jnp.zeros((z - 6 * heads, z), f32)]
    sk = jnp.concatenate(parts, axis=0).T[:, : 6 * heads].astype(bf16)
    pays = (own_ref, r1_ref, r2_ref, r3_ref)
    ms = [p[0][:pack] for p in pays]
    ls = [p[0][pack : 2 * pack] for p in pays]
    ns = [p[1][:pack] for p in pays]
    top = functools.reduce(jnp.maximum, ms)
    scales = [jnp.exp(m - top) for m in ms]
    total = sum(a * b for a, b in zip(ls, scales))
    inner = sum(a * b for a, b in zip(ns, scales)) / total
    stacked = jnp.concatenate([top, total, inner, jnp.zeros((rows - 3 * pack, rows), f32)], axis=0)
    stat_ref[...] = stacked.T

    tile = lanes // pack
    low = lax.broadcasted_iota(jnp.int32, (heads, 2 * tile), 1) < tile

    def one(g, carry):
        st = stat_ref[pl.ds(pl.multiple_of(g * heads, heads), heads), :]

        def spread(base):
            halves = [
                jnp.where(
                    low,
                    st[:, base + 2 * half : base + 2 * half + 1],
                    st[:, base + 2 * half + 1 : base + 2 * half + 2],
                )
                for half in range(pack // 2)
            ]
            return jnp.concatenate(halves, axis=1)

        prob = jnp.exp(logits_ref[g] - spread(0)) / spread(pack)
        gl = prob * (gw_ref[g] - spread(2 * pack))
        g1 = gl.astype(bf16).astype(f32)
        g2 = (gl - g1).astype(bf16).astype(f32)
        g3 = gl - g1 - g2
        stack = jnp.concatenate([g1, g2, g3, g1, g2, g1], axis=0).astype(bf16)
        grad = nn_dot(sk, stack)
        x = pout_t_ref[g].astype(f32)
        center = x - jnp.mean(x, axis=0, keepdims=True)
        inverse = lax.rsqrt(jnp.mean(center * center, axis=0, keepdims=True) + epsilon)
        normal = center * inverse
        centered = grad - jnp.mean(grad, axis=0, keepdims=True)
        along = jnp.mean(grad * normal, axis=0, keepdims=True)
        result = inverse * (centered - normal * along)
        out_ref[pl.ds(pl.multiple_of(g * lanes, lanes), lanes), :] = result.T.astype(bf16)
        return carry

    lax.fori_loop(0, groups, one, 0, unroll=4)


def alignment_kernel(
    col_ref,
    own_ref,
    r1_ref,
    r2_ref,
    r3_ref,
    v_ref,
    gate_ref,
    x_ref,
    wf_ref,
    out_ref,
    w_ref,
    gated_ref,
):
    pays = (own_ref, r1_ref, r2_ref, r3_ref)
    nk = len(pays)
    heads = own_ref.shape[1]
    wide = own_ref.shape[2]
    tile = wide // 2
    pieces = own_ref.shape[0] - 2
    rows = pieces * heads
    seqs, all_tokens, chans = v_ref.shape
    tokens = pieces * 2
    head_width = chans // heads
    col = col_ref[0]

    low = lax.broadcasted_iota(jnp.int32, (rows, wide), 1) < tile
    lgs = [p[2:].reshape(rows, wide) for p in pays]
    peak = functools.reduce(jnp.maximum, lgs)
    m0 = jnp.max(jnp.where(low, peak, far_below), axis=1, keepdims=True)
    m1 = jnp.max(jnp.where(low, far_below, peak), axis=1, keepdims=True)
    top = jnp.where(low, m0, m1)
    ps = [jnp.exp(lg - top) for lg in lgs]
    every = sum(ps)
    t0 = jnp.sum(jnp.where(low, every, 0.0), axis=1, keepdims=True)
    t1 = jnp.sum(jnp.where(low, 0.0, every), axis=1, keepdims=True)
    total = jnp.where(low, t0, t1)
    for shift, p in enumerate(ps):
        source = lax.rem(col + nk - shift, nk)
        weight = p / total
        rolled = pltpu.roll(weight, tile, 1)
        for n in range(pieces):
            w_ref[source, :, 2 * n, :] = weight[n * heads : (n + 1) * heads]
            w_ref[source, :, 2 * n + 1, :] = rolled[n * heads : (n + 1) * heads]
    w = jnp.concatenate(
        [w_ref[k].reshape(heads * tokens, wide)[:, :tile] for k in range(nk)], axis=1
    ).astype(bf16)

    owner = lax.broadcasted_iota(jnp.int32, (tokens, chans), 1) // head_width

    def one(s, carry):
        full = nn_dot(w, v_ref[s])
        mean = jnp.zeros((tokens, chans), f32)
        for h in range(heads):
            mean = jnp.where(owner == h, full[h * tokens : (h + 1) * tokens], mean)
        at = pl.ds(pl.multiple_of(s * tokens, tokens), tokens)
        gated_ref[at, :] = (gate_ref[at, :] * mean).astype(bf16)
        return carry

    lax.fori_loop(0, seqs, one, 0, unroll=4)
    out_ref[...] = (x_ref[...].astype(f32) + nt_dot(gated_ref[...], wf_ref[...])).astype(bf16)


def on_device(
    counts,
    alignment_input,
    pair_input,
    token_valid_mask,
    first_factor_weights,
    second_factor_weights,
    content_weights_grid,
    sigmoid_weights_grid,
    outer_matrix,
    score_matrix,
    final_mixing_weights,
    adjoint_of_rowset,
):
    nq, nr, nk = counts
    row_index = lax.axis_index("row")
    col_index = lax.axis_index("col")
    seqs, tokens, width = alignment_input.shape
    tile_i, tile_j, z = pair_input.shape
    fc = first_factor_weights.shape[1]
    fd = second_factor_weights.shape[1]
    heads = score_matrix.shape[1]
    chans = content_weights_grid.shape[1]
    groups = tile_i // pack
    lanes = pack * tile_j
    sds = jax.ShapeDtypeStruct

    mask = token_valid_mask.reshape(1, -1)
    own_start = ((row_index * nk + col_index) * tokens).astype(jnp.int32).reshape(1)
    place = jnp.stack([row_index, col_index]).astype(jnp.int32)
    col_scalar = col_index.astype(jnp.int32).reshape(1)
    half = seqs // 2

    sides_left = tokens // pack * fc
    sides_rows = sides_left + fd * tokens // 128 * seqs
    both, sides = call(
        prepare_kernel,
        (sds((2 * half * tokens, 2 * width), bf16), sds((sides_rows, 128), bf16)),
        scratch=(
            pltpu.VMEM((tokens, seqs, width), f32),
            pltpu.VMEM((fd * tokens // 128, seqs, 128), f32),
        ),
        smem=1,
        vmem=60 * 1024 * 1024,
    )(
        own_start,
        alignment_input,
        adjoint_of_rowset,
        first_factor_weights.T,
        second_factor_weights.T,
        mask,
    )

    sides = lax.all_gather(sides, "seq", axis=0)
    lefts = jnp.concatenate([sides[:, :sides_left].reshape(nq * sides_left, 128), both], axis=0)
    rights = sides[:, sides_left:]
    all_rights = [
        lax.ppermute(
            rights,
            ("row", "col"),
            [(r * nk + c, (c + t) % nr * nk + r) for r in range(nr) for c in range(nk)],
        )
        for t in range(nr)
    ]
    all_lefts = [lefts] + [
        lax.ppermute(lefts, "col", [(c, (c + t) % nk) for c in range(nk)]) for t in range(1, nk)
    ]
    start = nq * sides_left
    block_rows = jnp.stack([x[start : start + half * tokens] for x in all_lefts])
    every = lax.all_gather(block_rows, "row", axis=0).reshape(nr, nk, half, tokens, 2 * width)

    pair_out, pair_t, logits = call(
        update_kernel,
        (
            sds((tile_i * tile_j, z), bf16),
            sds((groups, z, lanes), bf16),
            sds((groups, heads, lanes), f32),
        ),
        scratch=(
            pltpu.VMEM((fc * fd, z), f32),
            pltpu.VMEM((tile_i * tile_j, z), bf16),
            pltpu.VMEM((tile_i * tile_j, z), bf16),
            pltpu.SemaphoreType.DMA((2,)),
            pltpu.SemaphoreType.DMA((groups,)),
            pltpu.VMEM((nk, nq * (sides_rows - sides_left), 128), bf16),
            pltpu.VMEM((fd, nq * seqs, 4 * tile_j), bf16),
            pltpu.VMEM((groups * fc, nq * pack * seqs), bf16),
            pltpu.VMEM((2 * z, fd * fc), bf16),
            pltpu.VMEM((groups, fd * fc, lanes), bf16),
            pltpu.VMEM((groups, fd * fc, lanes), bf16),
        ),
        smem=1,
        flops=14_000_000_000,
        nbytes=5_000_000,
        vmem=60 * 1024 * 1024,
        far=(10, 12),
        far_out=(0,),
    )(
        place,
        *all_lefts,
        *all_rights,
        mask,
        outer_matrix,
        score_matrix.T,
        pair_input.reshape(tile_i * tile_j, z),
    )

    head_lanes = seqs * chans // heads
    (gw_own,) = call(
        weights_kernel,
        (sds((groups, heads, lanes), f32),),
        scratch=(
            pltpu.VMEM((heads * tile_i, 2 * tile_j), f32),
            pltpu.VMEM((4 * width, 4 * chans), bf16),
            pltpu.VMEM((4 * width, 4 * chans), bf16),
            pltpu.VMEM((4 * width, 4 * chans), bf16),
            pltpu.VMEM((nk, 2, half, tokens, 2 * width), bf16),
            pltpu.VMEM((heads, tile_i, head_lanes), bf16),
            pltpu.VMEM((heads, 2 * tile_j, head_lanes), bf16),
        ),
        smem=1,
        flops=3_000_000_000,
        nbytes=3_000_000,
    )(
        col_scalar,
        every,
        *all_lefts,
        content_weights_grid,
        sigmoid_weights_grid,
        final_mixing_weights.T,
    )
    if nq == 2:
        gw_other = lax.ppermute(gw_own, "seq", [(0, 1), (1, 0)])
    else:
        gw_own, gw_other = lax.psum(gw_own, "seq"), jnp.zeros_like(gw_own)

    values, gating = call(
        values_kernel,
        (sds((seqs, nr * nk * tokens, chans), bf16), sds((seqs * tokens, chans), f32)),
        smem=1,
        flops=4_000_000_000,
        nbytes=6_000_000,
    )(col_scalar, every, content_weights_grid, both, sigmoid_weights_grid)

    payload = sds((2 + groups // nk * (pack // 2), heads, 2 * tile_j), f32)
    gw, pay0, pay1, pay2, pay3 = call(
        softmax_kernel,
        (sds((groups, heads, lanes), f32), payload, payload, payload, payload),
        smem=1,
    )(col_scalar, logits, gw_own, gw_other, mask)

    got = [
        lax.ppermute(pay, "col", [(c, (c + shift) % nk) for c in range(nk)])
        for shift, pay in ((1, pay1), (2, pay2), (3, pay3))
    ]

    (gradient,) = call(
        gradient_kernel,
        (sds((tile_i * tile_j, z), bf16),),
        scratch=(pltpu.VMEM((groups * heads, groups * heads), f32),),
        flops=4_000_000_000,
        nbytes=3_000_000,
    )(pay0, *got, logits, gw, pair_t, score_matrix.T)

    (aligned,) = call(
        alignment_kernel,
        (sds((seqs * tokens, width), bf16),),
        scratch=(
            pltpu.VMEM((nk, heads, tokens, 2 * tile_j), f32),
            pltpu.VMEM((seqs * tokens, chans), bf16),
        ),
        smem=1,
        flops=3_000_000_000,
        nbytes=5_000_000,
    )(
        col_scalar,
        pay0,
        *got,
        values,
        gating,
        alignment_input.reshape(seqs * tokens, width),
        final_mixing_weights.T,
    )
    return (
        aligned.reshape(seqs, tokens, width),
        pair_out.reshape(tile_i, tile_j, z),
        gradient.reshape(tile_i, tile_j, z),
    )


def solution(mesh):
    counts = (mesh.shape["seq"], mesh.shape["row"], mesh.shape["col"])
    in_specs = (
        P("seq", ("row", "col"), None),
        P("row", "col", None),
        P(),
        P(),
        P(),
        P(),
        P(),
        P(),
        P(),
        P(),
        P("seq", ("row", "col"), None),
    )
    out_specs = (P("seq", ("row", "col"), None), P("row", "col", None), P("row", "col", None))
    return jax.shard_map(
        functools.partial(on_device, counts),
        mesh=mesh,
        in_specs=in_specs,
        out_specs=out_specs,
        check_vma=False,
    )
```

```python
import functools

import jax
import jax.numpy as jnp
from jax import lax
from jax.experimental import pallas as pl
from jax.experimental.pallas import tpu as pltpu
from jax.sharding import PartitionSpec as P

epsilon = 1e-05
far_below = -1e30
vmem_bytes = 48 * 1024 * 1024
pack = 4

f32 = jnp.float32
bf16 = jnp.bfloat16


def nt_dot(a, b):
    return lax.dot_general(a, b, (((1,), (1,)), ((), ())), preferred_element_type=f32)


def nn_dot(a, b):
    return jnp.dot(a, b, preferred_element_type=f32)


def high_low(x):
    high = x.astype(bf16)
    return high, (x - high.astype(f32)).astype(bf16)


def call(kernel, out_shape, scratch=(), smem=0, flops=0, nbytes=0, vmem=vmem_bytes, far=(), far_out=()):
    count = None

    def run(*args):
        specs = [pl.BlockSpec(memory_space=pltpu.SMEM)] * smem
        specs += [pl.BlockSpec(memory_space=pltpu.VMEM)] * (len(args) - smem)
        return pl.pallas_call(
            kernel,
            out_shape=out_shape,
            in_specs=[
                pl.BlockSpec(memory_space=pl.ANY) if n in far else spec
                for n, spec in enumerate(specs)
            ],
            out_specs=[
                pl.BlockSpec(memory_space=pl.ANY if n in far_out else pltpu.VMEM)
                for n in range(len(out_shape))
            ],
            scratch_shapes=list(scratch),
            compiler_params=pltpu.CompilerParams(vmem_limit_bytes=vmem),
            cost_estimate=pl.CostEstimate(flops=flops, bytes_accessed=nbytes, transcendentals=0),
        )(*args)

    return run


def valid_count(mask_ref):
    return jnp.sum(mask_ref[...].astype(f32), axis=1, keepdims=True)


def column_mask(mask_ref, col, tile, copies):
    lane = lax.broadcasted_iota(jnp.int32, (1, copies * tile), 1)
    token = (lax.rem(lane, tile) + col * tile).astype(f32)
    return (token < valid_count(mask_ref)).astype(f32)


def twice(w):
    none = jnp.zeros_like(w)
    return jnp.concatenate(
        [jnp.concatenate([w, none], axis=1), jnp.concatenate([none, w], axis=1)], axis=0
    )


def prepare_kernel(
    own_ref, x_ref, adj_ref, w1_ref, w2_ref, mask_ref, norm_ref, adj_out_ref, sides_ref, turn_ref, right_ref
):
    seqs, tokens, width = x_ref.shape
    half = seqs // 2
    fd = w2_ref.shape[0]
    x = x_ref[...].astype(f32)
    center = x - jnp.mean(x, axis=-1, keepdims=True)
    inverse = lax.rsqrt(jnp.mean(center * center, axis=-1, keepdims=True) + epsilon)
    normed = center * inverse
    rows = half * tokens
    packed = jnp.concatenate([normed[:half], normed[half:]], axis=-1)
    norm_ref[...] = packed.reshape(rows, 2 * width).astype(bf16)
    adj = adj_ref[...].astype(f32)
    packed = jnp.concatenate([adj[:half], adj[half:]], axis=-1)
    adj_out_ref[...] = packed.reshape(rows, 2 * width).astype(bf16)
    token = lax.broadcasted_iota(jnp.int32, (seqs, tokens, width), 1) + own_ref[0]
    count = valid_count(mask_ref).reshape(1, 1, 1)
    real = jnp.where(token.astype(f32) < count, normed, 0.0)
    for s in range(seqs):
        turn_ref[:, s, :] = real[s]
    turned = turn_ref[...].astype(bf16).reshape(tokens * seqs, width)
    left = nt_dot(w1_ref[...], turned).astype(bf16)
    fc = w1_ref.shape[0]
    wk = pack * seqs
    for g in range(tokens // pack):
        sides_ref[g * fc : (g + 1) * fc, :] = left[:, g * wk : (g + 1) * wk]
    size = 128 // tokens
    real = real.astype(bf16)
    w2 = w2_ref[...]
    d = lax.broadcasted_iota(jnp.int32, (fd, 128), 0)
    lane = lax.broadcasted_iota(jnp.int32, (fd, 128), 1)
    mine = lax.rem(d, size) == lane // tokens
    for s in range(seqs):
        res = nt_dot(w2, jnp.concatenate([real[s]] * size, axis=0))
        res = jnp.where(mine, res, 0.0).reshape(fd // size, size, 128)
        right_ref[:, s, :] = jnp.sum(res, axis=1)
    base = tokens // pack * fc
    sides_ref[base:, :] = right_ref[...].reshape(fd // size * seqs, 128).astype(bf16)


def update_kernel(
    place_ref,
    left0_ref,
    left1_ref,
    left2_ref,
    left3_ref,
    right0_ref,
    right1_ref,
    right2_ref,
    right3_ref,
    mask_ref,
    m_hbm,
    score_ref,
    pair_hbm,
    pout_hbm,
    pout_t_ref,
    logits_ref,
    m_ref,
    pair_ref,
    pout_ref,
    in_sem,
    out_sem,
    rk_ref,
    rab_ref,
    lm_ref,
    mt_ref,
    oh_ref,
    ol_ref,
):
    fetch_m = pltpu.make_async_copy(m_hbm, m_ref, in_sem.at[0])
    fetch_pair = pltpu.make_async_copy(pair_hbm, pair_ref, in_sem.at[1])
    fetch_m.start()
    fetch_pair.start()
    nk = rk_ref.shape[0]
    width_d, pair_rows, _ = rab_ref.shape
    row, col = place_ref[0], place_ref[1]
    z = pair_ref.shape[1]
    groups, heads, lanes = logits_ref.shape
    tile_j = lanes // pack
    tokens = tile_j // nk
    per_k = groups // nk
    fc = lm_ref.shape[0] // groups
    seqs = 128 // pack
    nq = pair_rows // seqs
    wk = pack * seqs
    maskj = column_mask(mask_ref, col, tile_j, 2)

    for t, ref in enumerate((right0_ref, right1_ref, right2_ref, right3_ref)):
        rk_ref[lax.rem(row + nk - t, nk)] = ref[: rk_ref.shape[1], :]
    size = 128 // tokens
    right = jnp.concatenate([rk_ref[k] for k in range(nk)], axis=1)
    source = lax.broadcasted_iota(jnp.int32, (nk * 128, 4 * tile_j), 0)
    target = lax.broadcasted_iota(jnp.int32, (nk * 128, 4 * tile_j), 1)
    used = jnp.logical_or(target < tile_j, target >= 3 * tile_j)
    j = lax.rem(target, tile_j)
    offset = jnp.where(used, source - (j // tokens * 128 + lax.rem(j, tokens)), -1)
    blocks = width_d // size
    for e in range(size):
        pick = jnp.where(offset == e * tokens, 1.0, 0.0).astype(bf16)
        res = nn_dot(right, pick).astype(bf16)
        for q in range(nq):
            for n in range(blocks):
                at = (q * blocks + n) * seqs
                rab_ref[n * size + e, q * seqs : (q + 1) * seqs, :] = res[at : at + seqs]

    for t, ref in enumerate((left0_ref, left1_ref, left2_ref, left3_ref)):
        k = jnp.bitwise_xor(col, t)
        for g in range(per_k):
            at = pl.ds(pl.multiple_of((k * per_k + g) * fc, fc), fc)
            for q in range(nq):
                from_row = (q * per_k + g) * fc
                lm_ref[at, q * wk : (q + 1) * wk] = ref[from_row : from_row + fc, :]

    chunk = 4
    empty = jnp.zeros((seqs, 2 * tile_j), bf16)

    def block_of(d):
        rows = []
        for q in range(nq):
            both = rab_ref[d, q * seqs : (q + 1) * seqs, :]
            part = both[:, : 2 * tile_j], both[:, 2 * tile_j :]
            for i in range(pack):
                pieces = [empty] * (pack // 2)
                pieces[i // 2] = part[i % 2]
                rows.append(jnp.concatenate(pieces, axis=1))
        return jnp.concatenate(rows, axis=0)

    def outer_of(n, carry):
        block = jnp.concatenate([block_of(2 * n), block_of(2 * n + 1)], axis=1)
        for m in range(groups // chunk):
            out = nn_dot(lm_ref[m * chunk * fc : (m + 1) * chunk * fc, :], block)
            high, low = high_low(out)
            for e in range(2):
                at = pl.ds(pl.multiple_of((2 * n + e) * fc, fc), fc)
                for g in range(chunk):
                    group = m * chunk + g
                    to = slice(group % 2 * lanes, (group % 2 + 1) * lanes)
                    cut = slice(g * fc, (g + 1) * fc), slice(e * lanes, (e + 1) * lanes)
                    oh_ref[group // 2, at, to] = high[cut]
                    ol_ref[group // 2, at, to] = low[cut]
        return carry

    lax.fori_loop(0, width_d // 2, outer_of, 0, unroll=2)

    fetch_m.wait()
    some = z // fc
    for n in range(width_d // some):
        block = jnp.concatenate(
            [m_ref[pl.ds(n * some + e, fc, stride=width_d), :] for e in range(some)], axis=0
        ).T
        high, low = high_low(block)
        mt_ref[:z, n * z : (n + 1) * z] = high
        mt_ref[z:, n * z : (n + 1) * z] = low
    fetch_pair.wait()

    maskl = jnp.concatenate([maskj] * pack, axis=1) > 0
    score = score_ref[...]
    s1 = score.astype(bf16).astype(f32)
    s2 = (score - s1).astype(bf16).astype(f32)
    s3 = score - s1 - s2
    none = jnp.zeros_like(s1)
    st = jnp.concatenate(
        [
            jnp.concatenate([s1, s2, s3, none], axis=0),
            jnp.concatenate([s1, s2, none, none], axis=0),
        ],
        axis=1,
    ).astype(bf16)

    def finish(n, carry):
        two = nn_dot(mt_ref[...], oh_ref[n])
        update = two[:z] + two[z:] + nn_dot(mt_ref[:z, :], ol_ref[n])
        at = pl.ds(pl.multiple_of(n * 2 * lanes, 2 * lanes), 2 * lanes)
        before = pair_ref[at, :].astype(f32).T
        result = (before + update).astype(bf16)
        pout_t_ref[2 * n] = result[:, :lanes]
        pout_t_ref[2 * n + 1] = result[:, lanes:]
        x = result.astype(f32)
        pout_ref[at, :] = x.T.astype(bf16)
        pltpu.make_async_copy(pout_ref.at[at], pout_hbm.at[at], out_sem.at[n]).start()
        center = x - jnp.mean(x, axis=0, keepdims=True)
        inverse = lax.rsqrt(jnp.mean(center * center, axis=0, keepdims=True) + epsilon)
        high, low = high_low(center * inverse)
        scores = nn_dot(st, jnp.concatenate([high, low], axis=0))
        logits = scores[:heads] + scores[heads : 2 * heads] + scores[2 * heads : 3 * heads]
        logits = jnp.where(maskl, logits, far_below)
        logits_ref[2 * n] = logits[:, :lanes]
        logits_ref[2 * n + 1] = logits[:, lanes:]
        return carry

    lax.fori_loop(0, groups // 2, finish, 0, unroll=2)
    for n in range(groups // 2):
        at = pl.ds(n * 2 * lanes, 2 * lanes)
        pltpu.make_async_copy(pout_ref.at[at], pout_hbm.at[at], out_sem.at[n]).wait()


def by_heads(w, heads, out_ref):
    width, chans = w.shape
    hw = chans // heads
    block = 4 * hw
    slot = lax.broadcasted_iota(jnp.int32, (width, block), 1) // hw
    w = w.astype(f32)
    for t in range(chans // block):
        part = w[:, t * block : (t + 1) * block]
        turns = [part] + [pltpu.roll(part, n * hw, 1) for n in range(1, 4)]
        for e in range(4):
            h = t * 4 + e
            for s in range(4):
                out_ref[s * width : (s + 1) * width, h * block : (h + 1) * block] = jnp.where(
                    slot == s, turns[(s - e) % 4], 0.0
                ).astype(bf16)


def weights_kernel(
    place_ref,
    side0_ref,
    side1_ref,
    side2_ref,
    side3_ref,
    cols0_ref,
    cols1_ref,
    cols2_ref,
    cols3_ref,
    wv_ref,
    wg_ref,
    wf_ref,
    gw_ref,
    acc_ref,
    bv_ref,
    bg_ref,
    bf_ref,
    rows_ref,
    cols_ref,
    gs_ref,
    vs_ref,
):
    nk, half, tokens, _ = cols_ref.shape
    tile = nk * tokens
    groups, heads, lanes = gw_ref.shape
    row, col = place_ref[0], place_ref[1]
    count = half * tokens
    for t, ref in enumerate((side0_ref, side1_ref, side2_ref, side3_ref)):
        start = ref.shape[0] - 2 * count
        rows_ref[jnp.bitwise_xor(col, t)] = ref[start:, :].reshape(rows_ref.shape[1:])
    for t, ref in enumerate((cols0_ref, cols1_ref, cols2_ref, cols3_ref)):
        start = ref.shape[0] - count
        cols_ref[lax.rem(row + nk - t, nk)] = ref[start:, :].reshape(cols_ref.shape[1:])
    by_heads(wv_ref[...], heads, bv_ref)
    by_heads(wg_ref[...], heads, bg_ref)
    by_heads(wf_ref[...], heads, bf_ref)
    block = bv_ref.shape[1] // heads

    def four(read, n):
        return jnp.concatenate(
            [
                jnp.concatenate(
                    [
                        jnp.concatenate([read(k, 2 * (2 * n + e) + p) for k in range(nk)], axis=0)
                        for p in range(2)
                    ],
                    axis=1,
                )
                for e in range(2)
            ],
            axis=0,
        )

    for hp in range(heads // 2):
        cut = slice(hp * 2 * block, (hp + 1) * 2 * block)
        for n in range(half // 4):
            v = nn_dot(four(lambda k, s: cols_ref[k, s], n), bv_ref[:, cut]).astype(bf16)
            gate = nn_dot(four(lambda k, s: rows_ref[k, 0, s], n), bg_ref[:, cut])
            grad = nn_dot(four(lambda k, s: rows_ref[k, 1, s], n), bf_ref[:, cut])
            g = (grad * jax.nn.sigmoid(gate)).astype(bf16)
            for e in range(2):
                to = slice((2 * n + e) * block, (2 * n + e + 1) * block)
                for o in range(2):
                    mine = slice(o * block, (o + 1) * block)
                    ve = v[e * tile : (e + 1) * tile, mine]
                    vs_ref[2 * hp + o, :tile, to] = ve
                    vs_ref[2 * hp + o, tile:, to] = ve
                    gs_ref[2 * hp + o, :, to] = g[e * tile : (e + 1) * tile, mine]
    for h in range(heads):
        acc_ref[h * tile : (h + 1) * tile, :] = nt_dot(gs_ref[h], vs_ref[h])

    first = lax.broadcasted_iota(jnp.int32, (groups, 2 * tile), 1) < tile
    for h in range(heads):
        for part in range(pack // 2):
            a = acc_ref[pl.ds(h * tile + 2 * part, groups, stride=pack), :]
            b = acc_ref[pl.ds(h * tile + 2 * part + 1, groups, stride=pack), :]
            gw_ref[:, h, part * 2 * tile : (part + 1) * 2 * tile] = jnp.where(first, a, b)


def softmax_kernel(
    col_ref,
    logits_ref,
    gwa_ref,
    gwb_ref,
    mask_ref,
    gw_ref,
    own_ref,
    pay1_ref,
    pay2_ref,
    pay3_ref,
):
    groups, heads, lanes = logits_ref.shape
    tile = lanes // pack
    nk = 4
    rows = groups * heads
    col = col_ref[0]
    gw_ref[...] = gwa_ref[...] + gwb_ref[...]
    lane = lax.broadcasted_iota(jnp.int32, (rows, 2 * tile), 1)
    low = lane < tile
    maskj = column_mask(mask_ref, col, tile, 2)
    stats = jnp.zeros((rows, 2 * tile), f32)
    for part in range(pack // 2):
        cut = slice(part * 2 * tile, (part + 1) * 2 * tile)
        lg = logits_ref[:, :, cut].reshape(rows, 2 * tile)
        gw = gw_ref[:, :, cut].reshape(rows, 2 * tile)
        m0 = jnp.max(jnp.where(low, lg, far_below), axis=1, keepdims=True)
        m1 = jnp.max(jnp.where(low, far_below, lg), axis=1, keepdims=True)
        p = jnp.exp(lg - jnp.where(low, m0, m1)) * maskj
        pg = p * gw
        for e, m in ((0, m0), (1, m1)):
            mine = low if e == 0 else jnp.logical_not(low)
            i = 2 * part + e
            total = jnp.sum(jnp.where(mine, p, 0.0), axis=1, keepdims=True)
            inner = jnp.sum(jnp.where(mine, pg, 0.0), axis=1, keepdims=True)
            stats = jnp.where(lane == i, m, stats)
            stats = jnp.where(lane == pack + i, total, stats)
            stats = jnp.where(lane == 2 * pack + i, inner, stats)
    turned = stats.T[:16]
    per = groups // nk
    for shift, pay in enumerate((own_ref, pay1_ref, pay2_ref, pay3_ref)):
        dest = lax.rem(col + shift, nk)
        pay[0] = turned[:8]
        pay[1] = turned[8:]
        for g in range(per):
            piece = logits_ref[dest * per + g]
            for part in range(pack // 2):
                pay[2 + g * (pack // 2) + part] = piece[:, part * 2 * tile : (part + 1) * 2 * tile]


def values_kernel(ev_ref, wv_ref, norm_ref, wg_ref, v_ref, gate_ref):
    owners, half, tokens, wide = ev_ref.shape
    chans = wv_ref.shape[1]
    wv = twice(wv_ref[...])
    for s in range(half):
        x = jnp.concatenate([ev_ref[k, s] for k in range(owners)], axis=0)
        v = nn_dot(x, wv).astype(bf16)
        v_ref[s] = v[:, :chans]
        v_ref[s + half] = v[:, chans:]
    gate = jax.nn.sigmoid(nn_dot(norm_ref[...], twice(wg_ref[...])))
    gate_ref[: half * tokens] = gate[:, :chans]
    gate_ref[half * tokens :] = gate[:, chans:]


def gradient_kernel(
    own_ref, r1_ref, r2_ref, r3_ref, logits_ref, gw_ref, pout_t_ref, score_ref, out_ref, stat_ref
):
    groups, heads, lanes = logits_ref.shape
    rows = groups * heads
    score = score_ref[...]
    z = score.shape[1]
    s1 = score.astype(bf16).astype(f32)
    s2 = (score - s1).astype(bf16).astype(f32)
    s3 = score - s1 - s2
    parts = [s1, s1, s1, s2, s2, s3, jnp.zeros((z - 6 * heads, z), f32)]
    sk = jnp.concatenate(parts, axis=0).T[:, : 6 * heads].astype(bf16)
    pays = (own_ref, r1_ref, r2_ref, r3_ref)
    ms = [p[0][:pack] for p in pays]
    ls = [p[0][pack : 2 * pack] for p in pays]
    ns = [p[1][:pack] for p in pays]
    top = functools.reduce(jnp.maximum, ms)
    scales = [jnp.exp(m - top) for m in ms]
    total = sum(a * b for a, b in zip(ls, scales))
    inner = sum(a * b for a, b in zip(ns, scales)) / total
    stacked = jnp.concatenate([top, total, inner, jnp.zeros((rows - 3 * pack, rows), f32)], axis=0)
    stat_ref[...] = stacked.T

    tile = lanes // pack
    low = lax.broadcasted_iota(jnp.int32, (heads, 2 * tile), 1) < tile

    def one(g, carry):
        st = stat_ref[pl.ds(pl.multiple_of(g * heads, heads), heads), :]

        def spread(base):
            halves = [
                jnp.where(
                    low,
                    st[:, base + 2 * half : base + 2 * half + 1],
                    st[:, base + 2 * half + 1 : base + 2 * half + 2],
                )
                for half in range(pack // 2)
            ]
            return jnp.concatenate(halves, axis=1)

        prob = jnp.exp(logits_ref[g] - spread(0)) / spread(pack)
        gl = prob * (gw_ref[g] - spread(2 * pack))
        g1 = gl.astype(bf16).astype(f32)
        g2 = (gl - g1).astype(bf16).astype(f32)
        g3 = gl - g1 - g2
        stack = jnp.concatenate([g1, g2, g3, g1, g2, g1], axis=0).astype(bf16)
        grad = nn_dot(sk, stack)
        x = pout_t_ref[g].astype(f32)
        center = x - jnp.mean(x, axis=0, keepdims=True)
        inverse = lax.rsqrt(jnp.mean(center * center, axis=0, keepdims=True) + epsilon)
        normal = center * inverse
        centered = grad - jnp.mean(grad, axis=0, keepdims=True)
        along = jnp.mean(grad * normal, axis=0, keepdims=True)
        result = inverse * (centered - normal * along)
        out_ref[pl.ds(pl.multiple_of(g * lanes, lanes), lanes), :] = result.T.astype(bf16)
        return carry

    lax.fori_loop(0, groups, one, 0, unroll=4)


def alignment_kernel(
    col_ref,
    own_ref,
    r1_ref,
    r2_ref,
    r3_ref,
    v_ref,
    gate_ref,
    x_ref,
    wf_ref,
    out_ref,
    w_ref,
    gated_ref,
):
    pays = (own_ref, r1_ref, r2_ref, r3_ref)
    nk = len(pays)
    heads = own_ref.shape[1]
    wide = own_ref.shape[2]
    tile = wide // 2
    pieces = own_ref.shape[0] - 2
    rows = pieces * heads
    seqs, all_tokens, chans = v_ref.shape
    tokens = pieces * 2
    head_width = chans // heads
    col = col_ref[0]

    low = lax.broadcasted_iota(jnp.int32, (rows, wide), 1) < tile
    lgs = [p[2:].reshape(rows, wide) for p in pays]
    peak = functools.reduce(jnp.maximum, lgs)
    m0 = jnp.max(jnp.where(low, peak, far_below), axis=1, keepdims=True)
    m1 = jnp.max(jnp.where(low, far_below, peak), axis=1, keepdims=True)
    top = jnp.where(low, m0, m1)
    ps = [jnp.exp(lg - top) for lg in lgs]
    every = sum(ps)
    t0 = jnp.sum(jnp.where(low, every, 0.0), axis=1, keepdims=True)
    t1 = jnp.sum(jnp.where(low, 0.0, every), axis=1, keepdims=True)
    total = jnp.where(low, t0, t1)
    for shift, p in enumerate(ps):
        source = lax.rem(col + nk - shift, nk)
        weight = p / total
        rolled = pltpu.roll(weight, tile, 1)
        for n in range(pieces):
            w_ref[source, :, 2 * n, :] = weight[n * heads : (n + 1) * heads]
            w_ref[source, :, 2 * n + 1, :] = rolled[n * heads : (n + 1) * heads]
    w = jnp.concatenate(
        [w_ref[k].reshape(heads * tokens, wide)[:, :tile] for k in range(nk)], axis=1
    ).astype(bf16)

    owner = lax.broadcasted_iota(jnp.int32, (tokens, chans), 1) // head_width

    def one(s, carry):
        full = nn_dot(w, v_ref[s])
        mean = jnp.zeros((tokens, chans), f32)
        for h in range(heads):
            mean = jnp.where(owner == h, full[h * tokens : (h + 1) * tokens], mean)
        at = pl.ds(pl.multiple_of(s * tokens, tokens), tokens)
        gated_ref[at, :] = (gate_ref[at, :] * mean).astype(bf16)
        return carry

    lax.fori_loop(0, seqs, one, 0, unroll=4)
    out_ref[...] = (x_ref[...].astype(f32) + nt_dot(gated_ref[...], wf_ref[...])).astype(bf16)


def on_device(
    counts,
    alignment_input,
    pair_input,
    token_valid_mask,
    first_factor_weights,
    second_factor_weights,
    content_weights_grid,
    sigmoid_weights_grid,
    outer_matrix,
    score_matrix,
    final_mixing_weights,
    adjoint_of_rowset,
):
    nq, nr, nk = counts
    row_index = lax.axis_index("row")
    col_index = lax.axis_index("col")
    seqs, tokens, width = alignment_input.shape
    tile_i, tile_j, z = pair_input.shape
    fc = first_factor_weights.shape[1]
    fd = second_factor_weights.shape[1]
    heads = score_matrix.shape[1]
    chans = content_weights_grid.shape[1]
    groups = tile_i // pack
    lanes = pack * tile_j
    sds = jax.ShapeDtypeStruct

    mask = token_valid_mask.reshape(1, -1)
    own_start = ((row_index * nk + col_index) * tokens).astype(jnp.int32).reshape(1)
    place = jnp.stack([row_index, col_index]).astype(jnp.int32)
    col_scalar = col_index.astype(jnp.int32).reshape(1)
    half = seqs // 2

    sides_left = tokens // pack * fc
    sides_rows = sides_left + fd * tokens // 128 * seqs
    normed, adjoint, sides = call(
        prepare_kernel,
        (
            sds((half * tokens, 2 * width), bf16),
            sds((half * tokens, 2 * width), bf16),
            sds((sides_rows, 128), bf16),
        ),
        scratch=(
            pltpu.VMEM((tokens, seqs, width), f32),
            pltpu.VMEM((fd * tokens // 128, seqs, 128), f32),
        ),
        smem=1,
        vmem=60 * 1024 * 1024,
    )(
        own_start,
        alignment_input,
        adjoint_of_rowset,
        first_factor_weights.T,
        second_factor_weights.T,
        mask,
    )

    every = lax.all_gather(normed, ("row", "col"), axis=0).reshape(
        nr * nk, half, tokens, 2 * width
    )
    sides = lax.all_gather(sides, "seq", axis=0)
    rights = sides[:, sides_left:].reshape(nq * (sides_rows - sides_left), 128)
    rights = jnp.concatenate([rights, normed], axis=0)
    all_rights = [
        lax.ppermute(
            rights,
            ("row", "col"),
            [(r * nk + c, (c + t) % nr * nk + r) for r in range(nr) for c in range(nk)],
        )
        for t in range(nr)
    ]
    lefts = sides[:, :sides_left].reshape(nq * sides_left, 128)
    lefts = jnp.concatenate([lefts, normed, adjoint], axis=0)

    def exchange(x, bit):
        return lax.ppermute(x, "col", [(c, c ^ bit) for c in range(nk)])

    across = exchange(lefts, 2)
    all_lefts = [lefts, exchange(lefts, 1), across, exchange(across, 1)]

    head_lanes = seqs * chans // heads
    (gw_own,) = call(
        weights_kernel,
        (sds((groups, heads, lanes), f32),),
        scratch=(
            pltpu.VMEM((heads * tile_i, 2 * tile_j), f32),
            pltpu.VMEM((4 * width, 4 * chans), bf16),
            pltpu.VMEM((4 * width, 4 * chans), bf16),
            pltpu.VMEM((4 * width, 4 * chans), bf16),
            pltpu.VMEM((nk, 2, half, tokens, 2 * width), bf16),
            pltpu.VMEM((nk, half, tokens, 2 * width), bf16),
            pltpu.VMEM((heads, tile_i, head_lanes), bf16),
            pltpu.VMEM((heads, 2 * tile_j, head_lanes), bf16),
        ),
        smem=1,
        flops=3_000_000_000,
        nbytes=3_000_000,
    )(
        place,
        *all_lefts,
        *all_rights,
        content_weights_grid,
        sigmoid_weights_grid,
        final_mixing_weights.T,
    )
    if nq == 2:
        gw_other = lax.ppermute(gw_own, "seq", [(0, 1), (1, 0)])
    else:
        gw_own, gw_other = lax.psum(gw_own, "seq"), jnp.zeros_like(gw_own)

    pair_out, pair_t, logits = call(
        update_kernel,
        (
            sds((tile_i * tile_j, z), bf16),
            sds((groups, z, lanes), bf16),
            sds((groups, heads, lanes), f32),
        ),
        scratch=(
            pltpu.VMEM((fc * fd, z), f32),
            pltpu.VMEM((tile_i * tile_j, z), bf16),
            pltpu.VMEM((tile_i * tile_j, z), bf16),
            pltpu.SemaphoreType.DMA((2,)),
            pltpu.SemaphoreType.DMA((groups // 2,)),
            pltpu.VMEM((nk, nq * (sides_rows - sides_left), 128), bf16),
            pltpu.VMEM((fd, nq * seqs, 4 * tile_j), bf16),
            pltpu.VMEM((groups * fc, nq * pack * seqs), bf16),
            pltpu.VMEM((2 * z, fd * fc), bf16),
            pltpu.VMEM((groups // 2, fd * fc, 2 * lanes), bf16),
            pltpu.VMEM((groups // 2, fd * fc, 2 * lanes), bf16),
        ),
        smem=1,
        flops=14_000_000_000,
        nbytes=5_000_000,
        vmem=60 * 1024 * 1024,
        far=(10, 12),
        far_out=(0,),
    )(
        place,
        *all_lefts,
        *all_rights,
        mask,
        outer_matrix,
        score_matrix.T,
        pair_input.reshape(tile_i * tile_j, z),
    )

    values, gating = call(
        values_kernel,
        (sds((seqs, nr * nk * tokens, chans), bf16), sds((seqs * tokens, chans), f32)),
        flops=4_000_000_000,
        nbytes=6_000_000,
    )(every, content_weights_grid, normed, sigmoid_weights_grid)

    payload = sds((2 + groups // nk * (pack // 2), heads, 2 * tile_j), f32)
    gw, pay0, pay1, pay2, pay3 = call(
        softmax_kernel,
        (sds((groups, heads, lanes), f32), payload, payload, payload, payload),
        smem=1,
    )(col_scalar, logits, gw_own, gw_other, mask)

    got = [
        lax.ppermute(pay, "col", [(c, (c + shift) % nk) for c in range(nk)])
        for shift, pay in ((1, pay1), (2, pay2), (3, pay3))
    ]

    (gradient,) = call(
        gradient_kernel,
        (sds((tile_i * tile_j, z), bf16),),
        scratch=(pltpu.VMEM((groups * heads, groups * heads), f32),),
        flops=4_000_000_000,
        nbytes=3_000_000,
    )(pay0, *got, logits, gw, pair_t, score_matrix.T)

    (aligned,) = call(
        alignment_kernel,
        (sds((seqs * tokens, width), bf16),),
        scratch=(
            pltpu.VMEM((nk, heads, tokens, 2 * tile_j), f32),
            pltpu.VMEM((seqs * tokens, chans), bf16),
        ),
        smem=1,
        flops=3_000_000_000,
        nbytes=5_000_000,
    )(
        col_scalar,
        pay0,
        *got,
        values,
        gating,
        alignment_input.reshape(seqs * tokens, width),
        final_mixing_weights.T,
    )
    return (
        aligned.reshape(seqs, tokens, width),
        pair_out.reshape(tile_i, tile_j, z),
        gradient.reshape(tile_i, tile_j, z),
    )


def solution(mesh):
    counts = (mesh.shape["seq"], mesh.shape["row"], mesh.shape["col"])
    in_specs = (
        P("seq", ("row", "col"), None),
        P("row", "col", None),
        P(),
        P(),
        P(),
        P(),
        P(),
        P(),
        P(),
        P(),
        P("seq", ("row", "col"), None),
    )
    out_specs = (P("seq", ("row", "col"), None), P("row", "col", None), P("row", "col", None))
    return jax.shard_map(
        functools.partial(on_device, counts),
        mesh=mesh,
        in_specs=in_specs,
        out_specs=out_specs,
        check_vma=False,
    )
```

```python
import functools

import jax
import jax.numpy as jnp
from jax import lax
from jax.experimental import pallas as pl
from jax.experimental.pallas import tpu as pltpu
from jax.sharding import PartitionSpec as P

epsilon = 1e-05
far_below = -1e30
vmem_bytes = 32 * 1024 * 1024
pack = 4

f32 = jnp.float32
bf16 = jnp.bfloat16


def nt_dot(a, b):
    return lax.dot_general(a, b, (((1,), (1,)), ((), ())), preferred_element_type=f32)


def nn_dot(a, b):
    return jnp.dot(a, b, preferred_element_type=f32)


def high_low(x):
    high = x.astype(bf16)
    return high, (x - high.astype(f32)).astype(bf16)


def call(
    kernel, out_shape, scratch=(), smem=0, flops=0, nbytes=0, vmem=vmem_bytes, far=(), far_out=()
):
    def run(*args):
        count = len(args)
        in_specs = [
            pl.BlockSpec(memory_space=pltpu.SMEM if n < smem else pltpu.VMEM) for n in range(count)
        ]
        for n in far:
            in_specs[n] = pl.BlockSpec(memory_space=pltpu.HBM)
        landing = [pltpu.VMEM(args[n].shape, args[n].dtype) for n in far]
        if far:
            landing.append(pltpu.SemaphoreType.DMA((len(far),)))

        def body(*refs):
            inputs = list(refs[:count])
            extra = refs[len(refs) - len(landing) :]
            rest = refs[count : len(refs) - len(landing)]
            copies = []
            for i, n in enumerate(far):
                copies.append(pltpu.make_async_copy(inputs[n], extra[i], extra[-1].at[i]))
                copies[-1].start()
                inputs[n] = extra[i]

            def ready():
                for copy in copies:
                    copy.wait()

            kernel(ready, *inputs, *rest)

        return pl.pallas_call(
            body,
            out_shape=out_shape,
            in_specs=in_specs,
            out_specs=[
                pl.BlockSpec(memory_space=pltpu.HBM if n in far_out else pltpu.VMEM)
                for n in range(len(out_shape))
            ],
            scratch_shapes=list(scratch) + landing,
            compiler_params=pltpu.CompilerParams(vmem_limit_bytes=vmem),
            cost_estimate=pl.CostEstimate(flops=flops, bytes_accessed=nbytes, transcendentals=0),
        )(*args)

    return run


def valid_count(mask_ref):
    return jnp.sum(mask_ref[...].astype(f32), axis=1, keepdims=True)


def column_mask(mask_ref, col, tile, copies):
    lane = lax.broadcasted_iota(jnp.int32, (1, copies * tile), 1)
    token = (lax.rem(lane, tile) + col * tile).astype(f32)
    return (token < valid_count(mask_ref)).astype(f32)


def twice(w):
    none = jnp.zeros_like(w)
    return jnp.concatenate(
        [jnp.concatenate([w, none], axis=1), jnp.concatenate([none, w], axis=1)], axis=0
    )


def prepare_kernel(
    ready,
    own_ref,
    x_ref,
    adj_ref,
    w1_ref,
    w2_ref,
    mask_ref,
    rows_ref,
    cols_ref,
    left_ref,
    right_ref,
    norm_ref,
    turn_ref,
    place_ref,
):
    seqs, tokens, width = x_ref.shape
    half = seqs // 2
    fd = w2_ref.shape[0]
    x = x_ref[...].astype(f32)
    center = x - jnp.mean(x, axis=-1, keepdims=True)
    inverse = lax.rsqrt(jnp.mean(center * center, axis=-1, keepdims=True) + epsilon)
    normed = center * inverse
    rows = half * tokens
    adj = adj_ref[...].astype(f32)

    def two(x):
        x = jnp.concatenate([x[:half], x[half:]], axis=-1)
        return x.reshape(rows, 2 * width).astype(bf16)

    packed = two(normed)
    norm_ref[...] = packed
    rows_ref[-2 * rows : -rows, :] = packed
    rows_ref[-rows:, :] = two(adj)
    cols_ref[-rows:, :] = packed
    token = lax.broadcasted_iota(jnp.int32, (seqs, tokens, width), 1) + own_ref[0]
    count = valid_count(mask_ref).reshape(1, 1, 1)
    real = jnp.where(token.astype(f32) < count, normed, 0.0)
    for s in range(seqs):
        turn_ref[:, s, :] = real[s]
    turned = turn_ref[...].astype(bf16).reshape(tokens * seqs, width)
    left = nt_dot(w1_ref[...], turned).astype(bf16)
    fc = w1_ref.shape[0]
    wk = pack * seqs
    for g in range(tokens // pack):
        left_ref[g * fc : (g + 1) * fc, :] = left[:, g * wk : (g + 1) * wk]
    rows_ref[: -2 * rows, :] = left_ref[...]
    size = 128 // tokens
    real = real.astype(bf16)
    w2 = w2_ref[...]
    d = lax.broadcasted_iota(jnp.int32, (fd, 128), 0)
    lane = lax.broadcasted_iota(jnp.int32, (fd, 128), 1)
    mine = lax.rem(d, size) == lane // tokens
    for s in range(seqs):
        res = nt_dot(w2, jnp.concatenate([real[s]] * size, axis=0))
        res = jnp.where(mine, res, 0.0).reshape(fd // size, size, 128)
        place_ref[:, s, :] = jnp.sum(res, axis=1)
    right = place_ref[...].reshape(fd // size * seqs, 128).astype(bf16)
    right_ref[...] = right
    cols_ref[:-rows, :] = right


def update_kernel(
    ready,
    place_ref,
    left0_ref,
    left1_ref,
    left2_ref,
    left3_ref,
    right0_ref,
    right1_ref,
    right2_ref,
    right3_ref,
    far_left0_ref,
    far_left1_ref,
    far_left2_ref,
    far_left3_ref,
    far_right0_ref,
    far_right1_ref,
    far_right2_ref,
    far_right3_ref,
    mask_ref,
    m_ref,
    score_ref,
    pair_ref,
    pout_hbm,
    pout_t_ref,
    logits_ref,
    pout_ref,
    out_sem,
    rk_ref,
    rab_ref,
    lm_ref,
    mt_ref,
    oh_ref,
    ol_ref,
):
    nk = rk_ref.shape[0]
    width_d, pair_rows, _ = rab_ref.shape
    row, col, seq = place_ref[0], place_ref[1], place_ref[2]
    z = pair_ref.shape[1]
    groups, heads, lanes = logits_ref.shape
    tile_j = lanes // pack
    tokens = tile_j // nk
    per_k = groups // nk
    fc = lm_ref.shape[0] // groups
    seqs = 128 // pack
    nq = pair_rows // seqs
    wk = pack * seqs

    rights = (right0_ref, right1_ref, right2_ref, right3_ref)
    far_rights = (far_right0_ref, far_right1_ref, far_right2_ref, far_right3_ref)
    lefts = (left0_ref, left1_ref, left2_ref, left3_ref)
    far_lefts = (far_left0_ref, far_left1_ref, far_left2_ref, far_left3_ref)
    r_rows = rk_ref.shape[1] // nq
    l_rows = per_k * fc
    if nq == 2:
        sources = ((seq, 0, rights, lefts), (1 - seq, 0, far_rights, far_lefts))
    else:
        sources = tuple((q, q, far_rights, far_lefts) for q in range(nq))
    for q, slot, from_rights, from_lefts in sources:
        for t in range(nk):
            at = pl.ds(pl.multiple_of(q * r_rows, r_rows), r_rows)
            part = from_rights[t][slot * r_rows : (slot + 1) * r_rows, :]
            rk_ref[lax.rem(row + nk - t, nk), at, :] = part
            k = jnp.bitwise_xor(col, t)
            at = pl.ds(pl.multiple_of(k * l_rows, l_rows), l_rows)
            for g in range(per_k):
                from_row = slot * l_rows + g * fc
                at = pl.ds(pl.multiple_of((k * per_k + g) * fc, fc), fc)
                to = pl.ds(pl.multiple_of(q * wk, wk), wk)
                lm_ref[at, to] = from_lefts[t][from_row : from_row + fc, :]
    size = 128 // tokens
    right = jnp.concatenate([rk_ref[k] for k in range(nk)], axis=1)
    source = lax.broadcasted_iota(jnp.int32, (nk * 128, 4 * tile_j), 0)
    target = lax.broadcasted_iota(jnp.int32, (nk * 128, 4 * tile_j), 1)
    used = jnp.logical_or(target < tile_j, target >= 3 * tile_j)
    j = lax.rem(target, tile_j)
    offset = jnp.where(used, source - (j // tokens * 128 + lax.rem(j, tokens)), -1)
    blocks = width_d // size
    for e in range(size):
        pick = jnp.where(offset == e * tokens, 1.0, 0.0).astype(bf16)
        res = nn_dot(right, pick).astype(bf16)
        for q in range(nq):
            for n in range(blocks):
                at = (q * blocks + n) * seqs
                rab_ref[n * size + e, q * seqs : (q + 1) * seqs, :] = res[at : at + seqs]

    chunk = 4
    many = 4
    empty = jnp.zeros((seqs, 2 * tile_j), bf16)

    def block_of(d):
        rows = []
        for q in range(nq):
            both = rab_ref[d, q * seqs : (q + 1) * seqs, :]
            part = both[:, : 2 * tile_j], both[:, 2 * tile_j :]
            for i in range(pack):
                pieces = [empty] * (pack // 2)
                pieces[i // 2] = part[i % 2]
                rows.append(jnp.concatenate(pieces, axis=1))
        return jnp.concatenate(rows, axis=0)

    def outer_of(n, carry):
        block = jnp.concatenate([block_of(many * n + e) for e in range(many)], axis=1)
        for m in range(groups // chunk):
            out = nn_dot(lm_ref[m * chunk * fc : (m + 1) * chunk * fc, :], block)
            high, low = high_low(out)
            for e in range(many):
                at = pl.ds(pl.multiple_of((many * n + e) * fc, fc), fc)
                for g in range(chunk):
                    group = m * chunk + g
                    to = slice(group % 2 * lanes, (group % 2 + 1) * lanes)
                    cut = slice(g * fc, (g + 1) * fc), slice(e * lanes, (e + 1) * lanes)
                    oh_ref[group // 2, at, to] = high[cut]
                    ol_ref[group // 2, at, to] = low[cut]
        return carry

    lax.fori_loop(0, width_d // many, outer_of, 0)

    ready()
    some = z // fc
    for n in range(width_d // some):
        block = jnp.concatenate(
            [m_ref[pl.ds(n * some + e, fc, stride=width_d), :] for e in range(some)], axis=0
        ).T
        high, low = high_low(block)
        mt_ref[:z, n * z : (n + 1) * z] = high
        mt_ref[z:, n * z : (n + 1) * z] = low
    maskj = column_mask(mask_ref, col, tile_j, 2)

    maskl = jnp.concatenate([maskj] * pack, axis=1) > 0
    score = score_ref[...]
    s1 = score.astype(bf16).astype(f32)
    s2 = (score - s1).astype(bf16).astype(f32)
    s3 = score - s1 - s2
    none = jnp.zeros_like(s1)
    st = jnp.concatenate(
        [
            jnp.concatenate([s1, s2, s3, none], axis=0),
            jnp.concatenate([s1, s2, none, none], axis=0),
        ],
        axis=1,
    ).astype(bf16)

    def finish(n, carry):
        two = nn_dot(mt_ref[...], oh_ref[n])
        update = two[:z] + two[z:] + nn_dot(mt_ref[:z, :], ol_ref[n])
        at = pl.ds(pl.multiple_of(n * 2 * lanes, 2 * lanes), 2 * lanes)
        before = pair_ref[at, :].astype(f32).T
        result = (before + update).astype(bf16)
        pout_t_ref[2 * n] = result[:, :lanes]
        pout_t_ref[2 * n + 1] = result[:, lanes:]
        x = result.astype(f32)
        pout_ref[at, :] = x.T.astype(bf16)
        pltpu.make_async_copy(pout_ref.at[at], pout_hbm.at[at], out_sem.at[n]).start()
        center = x - jnp.mean(x, axis=0, keepdims=True)
        inverse = lax.rsqrt(jnp.mean(center * center, axis=0, keepdims=True) + epsilon)
        high, low = high_low(center * inverse)
        scores = nn_dot(st, jnp.concatenate([high, low], axis=0))
        logits = scores[:heads] + scores[heads : 2 * heads] + scores[2 * heads : 3 * heads]
        logits = jnp.where(maskl, logits, far_below)
        logits_ref[2 * n] = logits[:, :lanes]
        logits_ref[2 * n + 1] = logits[:, lanes:]
        return carry

    lax.fori_loop(0, groups // 2, finish, 0, unroll=2)
    for n in range(groups // 2):
        at = pl.ds(n * 2 * lanes, 2 * lanes)
        pltpu.make_async_copy(pout_ref.at[at], pout_hbm.at[at], out_sem.at[n]).wait()


def by_heads(w, heads, out_ref):
    width, chans = w.shape
    hw = chans // heads
    block = 4 * hw
    slot = lax.broadcasted_iota(jnp.int32, (width, block), 1) // hw
    w = w.astype(f32)
    for t in range(chans // block):
        part = w[:, t * block : (t + 1) * block]
        turns = [part] + [pltpu.roll(part, n * hw, 1) for n in range(1, 4)]
        for e in range(4):
            h = t * 4 + e
            for s in range(4):
                out_ref[s * width : (s + 1) * width, h * block : (h + 1) * block] = jnp.where(
                    slot == s, turns[(s - e) % 4], 0.0
                ).astype(bf16)


def weights_kernel(
    ready,
    place_ref,
    side0_ref,
    side1_ref,
    side2_ref,
    side3_ref,
    cols0_ref,
    cols1_ref,
    cols2_ref,
    cols3_ref,
    wv_ref,
    wg_ref,
    wf_ref,
    gw_ref,
    acc_ref,
    bv_ref,
    bg_ref,
    bf_ref,
    rows_ref,
    cols_ref,
    gs_ref,
    vs_ref,
):
    nk, half, tokens, _ = cols_ref.shape
    tile = nk * tokens
    groups, heads, lanes = gw_ref.shape
    row, col = place_ref[0], place_ref[1]
    count = half * tokens
    for t, ref in enumerate((side0_ref, side1_ref, side2_ref, side3_ref)):
        start = ref.shape[0] - 2 * count
        rows_ref[jnp.bitwise_xor(col, t)] = ref[start:, :].reshape(rows_ref.shape[1:])
    for t, ref in enumerate((cols0_ref, cols1_ref, cols2_ref, cols3_ref)):
        start = ref.shape[0] - count
        cols_ref[lax.rem(row + nk - t, nk)] = ref[start:, :].reshape(cols_ref.shape[1:])
    ready()
    by_heads(wv_ref[...], heads, bv_ref)
    by_heads(wg_ref[...], heads, bg_ref)
    by_heads(wf_ref[...], heads, bf_ref)
    block = bv_ref.shape[1] // heads

    def four(read, n):
        return jnp.concatenate(
            [
                jnp.concatenate(
                    [
                        jnp.concatenate([read(k, 2 * (2 * n + e) + p) for k in range(nk)], axis=0)
                        for p in range(2)
                    ],
                    axis=1,
                )
                for e in range(2)
            ],
            axis=0,
        )

    for hp in range(heads // 2):
        cut = slice(hp * 2 * block, (hp + 1) * 2 * block)
        for n in range(half // 4):
            v = nn_dot(four(lambda k, s: cols_ref[k, s], n), bv_ref[:, cut]).astype(bf16)
            gate = nn_dot(four(lambda k, s: rows_ref[k, 0, s], n), bg_ref[:, cut])
            grad = nn_dot(four(lambda k, s: rows_ref[k, 1, s], n), bf_ref[:, cut])
            g = (grad * jax.nn.sigmoid(gate)).astype(bf16)
            for e in range(2):
                to = slice((2 * n + e) * block, (2 * n + e + 1) * block)
                for o in range(2):
                    mine = slice(o * block, (o + 1) * block)
                    ve = v[e * tile : (e + 1) * tile, mine]
                    vs_ref[2 * hp + o, :tile, to] = ve
                    vs_ref[2 * hp + o, tile:, to] = ve
                    gs_ref[2 * hp + o, :, to] = g[e * tile : (e + 1) * tile, mine]
    for h in range(heads):
        acc_ref[h * tile : (h + 1) * tile, :] = nt_dot(gs_ref[h], vs_ref[h])

    first = lax.broadcasted_iota(jnp.int32, (groups, 2 * tile), 1) < tile
    for h in range(heads):
        for part in range(pack // 2):
            a = acc_ref[pl.ds(h * tile + 2 * part, groups, stride=pack), :]
            b = acc_ref[pl.ds(h * tile + 2 * part + 1, groups, stride=pack), :]
            gw_ref[:, h, part * 2 * tile : (part + 1) * 2 * tile] = jnp.where(first, a, b)


def softmax_kernel(
    ready,
    col_ref,
    logits_ref,
    gwa_ref,
    gwb_ref,
    mask_ref,
    gw_ref,
    own_ref,
    pay1_ref,
    pay2_ref,
    pay3_ref,
):
    groups, heads, lanes = logits_ref.shape
    tile = lanes // pack
    nk = 4
    rows = groups * heads
    col = col_ref[0]
    gw_ref[...] = gwa_ref[...] + gwb_ref[...]
    lane = lax.broadcasted_iota(jnp.int32, (rows, 2 * tile), 1)
    low = lane < tile
    maskj = column_mask(mask_ref, col, tile, 2)
    stats = jnp.zeros((rows, 2 * tile), f32)
    for part in range(pack // 2):
        cut = slice(part * 2 * tile, (part + 1) * 2 * tile)
        lg = logits_ref[:, :, cut].reshape(rows, 2 * tile)
        gw = gw_ref[:, :, cut].reshape(rows, 2 * tile)
        m0 = jnp.max(jnp.where(low, lg, far_below), axis=1, keepdims=True)
        m1 = jnp.max(jnp.where(low, far_below, lg), axis=1, keepdims=True)
        p = jnp.exp(lg - jnp.where(low, m0, m1)) * maskj
        pg = p * gw
        for e, m in ((0, m0), (1, m1)):
            mine = low if e == 0 else jnp.logical_not(low)
            i = 2 * part + e
            total = jnp.sum(jnp.where(mine, p, 0.0), axis=1, keepdims=True)
            inner = jnp.sum(jnp.where(mine, pg, 0.0), axis=1, keepdims=True)
            stats = jnp.where(lane == i, m, stats)
            stats = jnp.where(lane == pack + i, total, stats)
            stats = jnp.where(lane == 2 * pack + i, inner, stats)
    turned = stats.T[:16]
    per = groups // nk
    for shift, pay in enumerate((own_ref, pay1_ref, pay2_ref, pay3_ref)):
        dest = lax.rem(col + shift, nk)
        pay[0] = turned[:8]
        pay[1] = turned[8:]
        for g in range(per):
            piece = logits_ref[dest * per + g]
            for part in range(pack // 2):
                pay[2 + g * (pack // 2) + part] = piece[:, part * 2 * tile : (part + 1) * 2 * tile]


def values_kernel(ready, ev_ref, wv_ref, norm_ref, wg_ref, v_ref, gate_ref):
    owners, half, tokens, wide = ev_ref.shape
    chans = wv_ref.shape[1]
    gate = jax.nn.sigmoid(nn_dot(norm_ref[...], twice(wg_ref[...])))
    gate_ref[: half * tokens] = gate[:, :chans]
    gate_ref[half * tokens :] = gate[:, chans:]
    wv = twice(wv_ref[...])
    ready()
    for s in range(half):
        x = jnp.concatenate([ev_ref[k, s] for k in range(owners)], axis=0)
        v = nn_dot(x, wv).astype(bf16)
        v_ref[s] = v[:, :chans]
        v_ref[s + half] = v[:, chans:]


def gradient_kernel(
    ready,
    own_ref, r1_ref, r2_ref, r3_ref, logits_ref, gw_ref, pout_t_ref, score_ref, out_ref, stat_ref
):
    groups, heads, lanes = logits_ref.shape
    rows = groups * heads
    score = score_ref[...]
    z = score.shape[1]
    s1 = score.astype(bf16).astype(f32)
    s2 = (score - s1).astype(bf16).astype(f32)
    s3 = score - s1 - s2
    parts = [s1, s1, s1, s2, s2, s3, jnp.zeros((z - 6 * heads, z), f32)]
    sk = jnp.concatenate(parts, axis=0).T[:, : 6 * heads].astype(bf16)
    pays = (own_ref, r1_ref, r2_ref, r3_ref)
    ms = [p[0][:pack] for p in pays]
    ls = [p[0][pack : 2 * pack] for p in pays]
    ns = [p[1][:pack] for p in pays]
    top = functools.reduce(jnp.maximum, ms)
    scales = [jnp.exp(m - top) for m in ms]
    total = sum(a * b for a, b in zip(ls, scales))
    inner = sum(a * b for a, b in zip(ns, scales)) / total
    stacked = jnp.concatenate([top, total, inner, jnp.zeros((rows - 3 * pack, rows), f32)], axis=0)
    stat_ref[...] = stacked.T

    tile = lanes // pack
    low = lax.broadcasted_iota(jnp.int32, (heads, 2 * tile), 1) < tile

    def one(g, carry):
        st = stat_ref[pl.ds(pl.multiple_of(g * heads, heads), heads), :]

        def spread(base):
            halves = [
                jnp.where(
                    low,
                    st[:, base + 2 * half : base + 2 * half + 1],
                    st[:, base + 2 * half + 1 : base + 2 * half + 2],
                )
                for half in range(pack // 2)
            ]
            return jnp.concatenate(halves, axis=1)

        prob = jnp.exp(logits_ref[g] - spread(0)) / spread(pack)
        gl = prob * (gw_ref[g] - spread(2 * pack))
        g1 = gl.astype(bf16).astype(f32)
        g2 = (gl - g1).astype(bf16).astype(f32)
        g3 = gl - g1 - g2
        stack = jnp.concatenate([g1, g2, g3, g1, g2, g1], axis=0).astype(bf16)
        grad = nn_dot(sk, stack)
        x = pout_t_ref[g].astype(f32)
        center = x - jnp.mean(x, axis=0, keepdims=True)
        inverse = lax.rsqrt(jnp.mean(center * center, axis=0, keepdims=True) + epsilon)
        normal = center * inverse
        centered = grad - jnp.mean(grad, axis=0, keepdims=True)
        along = jnp.mean(grad * normal, axis=0, keepdims=True)
        result = inverse * (centered - normal * along)
        out_ref[pl.ds(pl.multiple_of(g * lanes, lanes), lanes), :] = result.T.astype(bf16)
        return carry

    lax.fori_loop(0, groups, one, 0, unroll=4)


def alignment_kernel(
    ready,
    col_ref,
    own_ref,
    r1_ref,
    r2_ref,
    r3_ref,
    v_ref,
    gate_ref,
    x_ref,
    wf_ref,
    out_ref,
    w_ref,
    gated_ref,
):
    pays = (own_ref, r1_ref, r2_ref, r3_ref)
    nk = len(pays)
    heads = own_ref.shape[1]
    wide = own_ref.shape[2]
    tile = wide // 2
    pieces = own_ref.shape[0] - 2
    rows = pieces * heads
    seqs, all_tokens, chans = v_ref.shape
    tokens = pieces * 2
    head_width = chans // heads
    col = col_ref[0]

    low = lax.broadcasted_iota(jnp.int32, (rows, wide), 1) < tile
    lgs = [p[2:].reshape(rows, wide) for p in pays]
    peak = functools.reduce(jnp.maximum, lgs)
    m0 = jnp.max(jnp.where(low, peak, far_below), axis=1, keepdims=True)
    m1 = jnp.max(jnp.where(low, far_below, peak), axis=1, keepdims=True)
    top = jnp.where(low, m0, m1)
    ps = [jnp.exp(lg - top) for lg in lgs]
    every = sum(ps)
    t0 = jnp.sum(jnp.where(low, every, 0.0), axis=1, keepdims=True)
    t1 = jnp.sum(jnp.where(low, 0.0, every), axis=1, keepdims=True)
    total = jnp.where(low, t0, t1)
    for shift, p in enumerate(ps):
        source = lax.rem(col + nk - shift, nk)
        weight = p / total
        rolled = pltpu.roll(weight, tile, 1)
        for n in range(pieces):
            w_ref[source, :, 2 * n, :] = weight[n * heads : (n + 1) * heads]
            w_ref[source, :, 2 * n + 1, :] = rolled[n * heads : (n + 1) * heads]
    w = jnp.concatenate(
        [w_ref[k].reshape(heads * tokens, wide)[:, :tile] for k in range(nk)], axis=1
    ).astype(bf16)

    owner = lax.broadcasted_iota(jnp.int32, (tokens, chans), 1) // head_width

    def one(s, carry):
        full = nn_dot(w, v_ref[s])
        mean = jnp.zeros((tokens, chans), f32)
        for h in range(heads):
            mean = jnp.where(owner == h, full[h * tokens : (h + 1) * tokens], mean)
        at = pl.ds(pl.multiple_of(s * tokens, tokens), tokens)
        gated_ref[at, :] = (gate_ref[at, :] * mean).astype(bf16)
        return carry

    lax.fori_loop(0, seqs, one, 0, unroll=4)
    out_ref[...] = (x_ref[...].astype(f32) + nt_dot(gated_ref[...], wf_ref[...])).astype(bf16)


def on_device(
    counts,
    alignment_input,
    pair_input,
    token_valid_mask,
    first_factor_weights,
    second_factor_weights,
    content_weights_grid,
    sigmoid_weights_grid,
    outer_matrix,
    score_matrix,
    final_mixing_weights,
    adjoint_of_rowset,
):
    nq, nr, nk = counts
    row_index = lax.axis_index("row")
    col_index = lax.axis_index("col")
    seqs, tokens, width = alignment_input.shape
    tile_i, tile_j, z = pair_input.shape
    fc = first_factor_weights.shape[1]
    fd = second_factor_weights.shape[1]
    heads = score_matrix.shape[1]
    chans = content_weights_grid.shape[1]
    groups = tile_i // pack
    lanes = pack * tile_j
    sds = jax.ShapeDtypeStruct

    mask = token_valid_mask.reshape(1, -1)
    own_start = ((row_index * nk + col_index) * tokens).astype(jnp.int32).reshape(1)
    seq_index = lax.axis_index("seq")
    place = jnp.stack([row_index, col_index, seq_index]).astype(jnp.int32)
    col_scalar = col_index.astype(jnp.int32).reshape(1)
    half = seqs // 2

    l_rows = tokens // pack * fc
    r_rows = fd * tokens // 128 * seqs
    n_rows = half * tokens
    rows, cols, left, right, normed = call(
        prepare_kernel,
        (
            sds((l_rows + 2 * n_rows, 128), bf16),
            sds((r_rows + n_rows, 128), bf16),
            sds((l_rows, 128), bf16),
            sds((r_rows, 128), bf16),
            sds((n_rows, 128), bf16),
        ),
        scratch=(
            pltpu.VMEM((tokens, seqs, width), f32),
            pltpu.VMEM((fd * tokens // 128, seqs, 128), f32),
        ),
        smem=1,
        vmem=60 * 1024 * 1024,
    )(
        own_start,
        alignment_input,
        adjoint_of_rowset,
        first_factor_weights.T,
        second_factor_weights.T,
        mask,
    )

    every = lax.all_gather(normed, ("row", "col"), axis=0).reshape(
        nr * nk, half, tokens, 2 * width
    )
    def to_columns(x, t, flip):
        pairs = [
            ((s * nr + r) * nk + c, ((s ^ flip) * nr + (c + t) % nr) * nk + r)
            for s in range(nq)
            for r in range(nr)
            for c in range(nk)
        ]
        return lax.ppermute(x, ("seq", "row", "col"), pairs)

    def to_rows(x, t, flip):
        pairs = [
            ((s * nr + r) * nk + c, ((s ^ flip) * nr + r) * nk + (c ^ t))
            for s in range(nq)
            for r in range(nr)
            for c in range(nk)
        ]
        return lax.ppermute(x, ("seq", "row", "col"), pairs)

    all_cols = [to_columns(cols, t, 0) for t in range(nr)]
    across = to_rows(rows, 2, 0)
    all_rows = [rows, to_rows(rows, 1, 0), across, to_rows(across, 1, 0)]
    if nq == 2:
        far_rights = [to_columns(right, t, 1) for t in range(nr)]
        far_lefts = [to_rows(left, t, 1) for t in range(nk)]
    else:
        right = lax.all_gather(right, "seq", axis=0, tiled=True)
        left = lax.all_gather(left, "seq", axis=0, tiled=True)
        far_rights = [to_columns(right, t, 0) for t in range(nr)]
        far_lefts = [left] + [to_rows(left, t, 0) for t in range(1, nk)]

    head_lanes = seqs * chans // heads
    (gw_own,) = call(
        weights_kernel,
        (sds((groups, heads, lanes), f32),),
        scratch=(
            pltpu.VMEM((heads * tile_i, 2 * tile_j), f32),
            pltpu.VMEM((4 * width, 4 * chans), bf16),
            pltpu.VMEM((4 * width, 4 * chans), bf16),
            pltpu.VMEM((4 * width, 4 * chans), bf16),
            pltpu.VMEM((nk, 2, half, tokens, 2 * width), bf16),
            pltpu.VMEM((nk, half, tokens, 2 * width), bf16),
            pltpu.VMEM((heads, tile_i, head_lanes), bf16),
            pltpu.VMEM((heads, 2 * tile_j, head_lanes), bf16),
        ),
        smem=1,
        flops=3_000_000_000,
        nbytes=3_000_000,
        far=(9, 10, 11),
    )(
        place,
        *all_rows,
        *all_cols,
        content_weights_grid,
        sigmoid_weights_grid,
        final_mixing_weights.T,
    )
    if nq == 2:
        gw_other = lax.ppermute(gw_own, "seq", [(0, 1), (1, 0)])
    else:
        gw_own, gw_other = lax.psum(gw_own, "seq"), jnp.zeros_like(gw_own)

    pair_out, pair_t, logits = call(
        update_kernel,
        (
            sds((tile_i * tile_j, z), bf16),
            sds((groups, z, lanes), bf16),
            sds((groups, heads, lanes), f32),
        ),
        scratch=(
            pltpu.VMEM((tile_i * tile_j, z), bf16),
            pltpu.SemaphoreType.DMA((groups // 2,)),
            pltpu.VMEM((nk, nq * r_rows, 128), bf16),
            pltpu.VMEM((fd, nq * seqs, 4 * tile_j), bf16),
            pltpu.VMEM((groups * fc, nq * pack * seqs), bf16),
            pltpu.VMEM((2 * z, fd * fc), bf16),
            pltpu.VMEM((groups // 2, fd * fc, 2 * lanes), bf16),
            pltpu.VMEM((groups // 2, fd * fc, 2 * lanes), bf16),
        ),
        smem=1,
        flops=14_000_000_000,
        nbytes=5_000_000,
        vmem=44 * 1024 * 1024,
        far=(17, 18, 19, 20),
        far_out=(0,),
    )(
        place,
        *all_rows,
        *all_cols,
        *far_lefts,
        *far_rights,
        mask,
        outer_matrix,
        score_matrix.T,
        pair_input.reshape(tile_i * tile_j, z),
    )

    values, gating = call(
        values_kernel,
        (sds((seqs, nr * nk * tokens, chans), bf16), sds((seqs * tokens, chans), f32)),
        flops=4_000_000_000,
        nbytes=6_000_000,
        far=(0,),
    )(every, content_weights_grid, normed, sigmoid_weights_grid)

    payload = sds((2 + groups // nk * (pack // 2), heads, 2 * tile_j), f32)
    gw, pay0, pay1, pay2, pay3 = call(
        softmax_kernel,
        (sds((groups, heads, lanes), f32), payload, payload, payload, payload),
        smem=1,
    )(col_scalar, logits, gw_own, gw_other, mask)

    got = [
        lax.ppermute(pay, "col", [(c, (c + shift) % nk) for c in range(nk)])
        for shift, pay in ((1, pay1), (2, pay2), (3, pay3))
    ]

    got, values, gating = lax.optimization_barrier((got, values, gating))

    (gradient,) = call(
        gradient_kernel,
        (sds((tile_i * tile_j, z), bf16),),
        scratch=(pltpu.VMEM((groups * heads, groups * heads), f32),),
        flops=4_000_000_000,
        nbytes=3_000_000,
    )(pay0, *got, logits, gw, pair_t, score_matrix.T)

    (aligned,) = call(
        alignment_kernel,
        (sds((seqs * tokens, width), bf16),),
        scratch=(
            pltpu.VMEM((nk, heads, tokens, 2 * tile_j), f32),
            pltpu.VMEM((seqs * tokens, chans), bf16),
        ),
        smem=1,
        flops=3_000_000_000,
        nbytes=5_000_000,
    )(
        col_scalar,
        pay0,
        *got,
        values,
        gating,
        alignment_input.reshape(seqs * tokens, width),
        final_mixing_weights.T,
    )
    return (
        aligned.reshape(seqs, tokens, width),
        pair_out.reshape(tile_i, tile_j, z),
        gradient.reshape(tile_i, tile_j, z),
    )


def solution(mesh):
    counts = (mesh.shape["seq"], mesh.shape["row"], mesh.shape["col"])
    in_specs = (
        P("seq", ("row", "col"), None),
        P("row", "col", None),
        P(),
        P(),
        P(),
        P(),
        P(),
        P(),
        P(),
        P(),
        P("seq", ("row", "col"), None),
    )
    out_specs = (P("seq", ("row", "col"), None), P("row", "col", None), P("row", "col", None))
    return jax.shard_map(
        functools.partial(on_device, counts),
        mesh=mesh,
        in_specs=in_specs,
        out_specs=out_specs,
        check_vma=False,
    )
```

```python
import functools

import jax
import jax.numpy as jnp
from jax import lax
from jax.experimental import pallas as pl
from jax.experimental.pallas import tpu as pltpu
from jax.sharding import PartitionSpec as P

epsilon = 1e-05
far_below = -1e30
vmem_bytes = 32 * 1024 * 1024
pack = 4

f32 = jnp.float32
bf16 = jnp.bfloat16


def nt_dot(a, b):
    return lax.dot_general(a, b, (((1,), (1,)), ((), ())), preferred_element_type=f32)


def nn_dot(a, b):
    return jnp.dot(a, b, preferred_element_type=f32)


def high_low(x):
    high = x.astype(bf16)
    return high, (x - high.astype(f32)).astype(bf16)


def call(
    kernel, out_shape, scratch=(), smem=0, flops=0, nbytes=0, vmem=vmem_bytes, far=(), far_out=()
):
    def run(*args):
        count = len(args)
        in_specs = [
            pl.BlockSpec(memory_space=pltpu.SMEM if n < smem else pltpu.VMEM) for n in range(count)
        ]
        for n in far:
            in_specs[n] = pl.BlockSpec(memory_space=pltpu.HBM)
        landing = [pltpu.VMEM(args[n].shape, args[n].dtype) for n in far]
        if far:
            landing.append(pltpu.SemaphoreType.DMA((len(far),)))

        def body(*refs):
            inputs = list(refs[:count])
            extra = refs[len(refs) - len(landing) :]
            rest = refs[count : len(refs) - len(landing)]
            copies = []
            for i, n in enumerate(far):
                copies.append(pltpu.make_async_copy(inputs[n], extra[i], extra[-1].at[i]))
                copies[-1].start()
                inputs[n] = extra[i]

            def ready():
                for copy in copies:
                    copy.wait()

            kernel(ready, *inputs, *rest)

        return pl.pallas_call(
            body,
            out_shape=out_shape,
            in_specs=in_specs,
            out_specs=[
                pl.BlockSpec(memory_space=pltpu.HBM if n in far_out else pltpu.VMEM)
                for n in range(len(out_shape))
            ],
            scratch_shapes=list(scratch) + landing,
            compiler_params=pltpu.CompilerParams(vmem_limit_bytes=vmem),
            cost_estimate=pl.CostEstimate(flops=flops, bytes_accessed=nbytes, transcendentals=0),
        )(*args)

    return run


def valid_count(mask_ref):
    return jnp.sum(mask_ref[...].astype(f32), axis=1, keepdims=True)


def column_mask(mask_ref, col, tile, copies):
    lane = lax.broadcasted_iota(jnp.int32, (1, copies * tile), 1)
    token = (lax.rem(lane, tile) + col * tile).astype(f32)
    return (token < valid_count(mask_ref)).astype(f32)


def twice(w):
    none = jnp.zeros_like(w)
    return jnp.concatenate(
        [jnp.concatenate([w, none], axis=1), jnp.concatenate([none, w], axis=1)], axis=0
    )


def prepare_kernel(
    ready,
    own_ref,
    x_ref,
    adj_ref,
    w1_ref,
    w2_ref,
    mask_ref,
    rows_ref,
    cols_ref,
    norm_ref,
    turn_ref,
    place_ref,
):
    seqs, tokens, width = x_ref.shape
    half = seqs // 2
    fd = w2_ref.shape[0]
    x = x_ref[...].astype(f32)
    center = x - jnp.mean(x, axis=-1, keepdims=True)
    inverse = lax.rsqrt(jnp.mean(center * center, axis=-1, keepdims=True) + epsilon)
    normed = center * inverse
    rows = half * tokens
    adj = adj_ref[...].astype(f32)

    def two(x):
        x = jnp.concatenate([x[:half], x[half:]], axis=-1)
        return x.reshape(rows, 2 * width).astype(bf16)

    packed = two(normed)
    norm_ref[...] = packed
    rows_ref[-2 * rows : -rows, :] = packed
    rows_ref[-rows:, :] = two(adj)
    cols_ref[-rows:, :] = packed
    token = lax.broadcasted_iota(jnp.int32, (seqs, tokens, width), 1) + own_ref[0]
    count = valid_count(mask_ref).reshape(1, 1, 1)
    real = jnp.where(token.astype(f32) < count, normed, 0.0)
    for s in range(seqs):
        turn_ref[:, s, :] = real[s]
    turned = turn_ref[...].astype(bf16).reshape(tokens * seqs, width)
    left = nt_dot(w1_ref[...], turned).astype(bf16)
    fc = w1_ref.shape[0]
    wk = pack * seqs
    for g in range(tokens // pack):
        rows_ref[g * fc : (g + 1) * fc, :] = left[:, g * wk : (g + 1) * wk]
    size = 128 // tokens
    real = real.astype(bf16)
    w2 = w2_ref[...]
    d = lax.broadcasted_iota(jnp.int32, (fd, 128), 0)
    lane = lax.broadcasted_iota(jnp.int32, (fd, 128), 1)
    mine = lax.rem(d, size) == lane // tokens
    for s in range(seqs):
        res = nt_dot(w2, jnp.concatenate([real[s]] * size, axis=0))
        res = jnp.where(mine, res, 0.0).reshape(fd // size, size, 128)
        place_ref[:, s, :] = jnp.sum(res, axis=1)
    cols_ref[:-rows, :] = place_ref[...].reshape(fd // size * seqs, 128).astype(bf16)


def join_kernel(
    ready,
    place_ref,
    rows0_ref,
    rows1_ref,
    rows2_ref,
    rows3_ref,
    cols0_ref,
    cols1_ref,
    cols2_ref,
    cols3_ref,
    out_ref,
):
    nk = 4
    row, col = place_ref[0], place_ref[1]
    r_rows = l_rows = out_ref.shape[0] // (2 * nk)
    for t, ref in enumerate((cols0_ref, cols1_ref, cols2_ref, cols3_ref)):
        at = pl.ds(pl.multiple_of(lax.rem(row + nk - t, nk) * r_rows, r_rows), r_rows)
        out_ref[at, :] = ref[:r_rows, :]
    for t, ref in enumerate((rows0_ref, rows1_ref, rows2_ref, rows3_ref)):
        start = nk * r_rows + jnp.bitwise_xor(col, t) * l_rows
        at = pl.ds(pl.multiple_of(start, l_rows), l_rows)
        out_ref[at, :] = ref[:l_rows, :]


def update_kernel(
    ready,
    place_ref,
    sides_ref,
    far_sides_ref,
    mask_ref,
    m_ref,
    score_ref,
    pair_ref,
    pout_hbm,
    pout_t_ref,
    logits_ref,
    pout_ref,
    out_sem,
    rk_ref,
    rab_ref,
    lm_ref,
    mt_ref,
    oh_ref,
    ol_ref,
    update_ref,
):
    nk = rk_ref.shape[0]
    width_d, pair_rows, _ = rab_ref.shape
    col, seq = place_ref[1], place_ref[2]
    z = pair_ref.shape[1]
    groups, heads, lanes = logits_ref.shape
    tile_j = lanes // pack
    tokens = tile_j // nk
    fc = lm_ref.shape[0] // groups
    seqs = 128 // pack
    nq = pair_rows // seqs
    wk = pack * seqs

    r_rows = rk_ref.shape[1] // nq
    l_rows = groups * fc
    if nq == 2:
        sources = ((seq, 0, sides_ref), (1 - seq, 0, far_sides_ref))
    else:
        sources = tuple((q, q, far_sides_ref) for q in range(nq))
    for q, slot, ref in sources:
        base = slot * (nk * r_rows + l_rows)
        at = pl.ds(pl.multiple_of(q * r_rows, r_rows), r_rows)
        for k in range(nk):
            rk_ref[k, at, :] = ref[base + k * r_rows : base + (k + 1) * r_rows, :]
        base = base + nk * r_rows
        to = pl.ds(pl.multiple_of(q * wk, wk), wk)
        lm_ref[:, to] = ref[base : base + l_rows, :]
    size = 128 // tokens
    right = jnp.concatenate([rk_ref[k] for k in range(nk)], axis=1)
    source = lax.broadcasted_iota(jnp.int32, (nk * 128, 4 * tile_j), 0)
    target = lax.broadcasted_iota(jnp.int32, (nk * 128, 4 * tile_j), 1)
    used = jnp.logical_or(target < tile_j, target >= 3 * tile_j)
    j = lax.rem(target, tile_j)
    offset = jnp.where(used, source - (j // tokens * 128 + lax.rem(j, tokens)), -1)
    blocks = width_d // size
    for e in range(size):
        pick = jnp.where(offset == e * tokens, 1.0, 0.0).astype(bf16)
        res = nn_dot(right, pick).astype(bf16)
        for q in range(nq):
            for n in range(blocks):
                at = (q * blocks + n) * seqs
                rab_ref[n * size + e, q * seqs : (q + 1) * seqs, :] = res[at : at + seqs]

    chunk = 4
    many = 4
    wide = oh_ref.shape[2] // lanes
    empty = jnp.zeros((seqs, 2 * tile_j), bf16)

    def block_of(d):
        rows = []
        for q in range(nq):
            both = rab_ref[d, q * seqs : (q + 1) * seqs, :]
            part = both[:, : 2 * tile_j], both[:, 2 * tile_j :]
            for i in range(pack):
                pieces = [empty] * (pack // 2)
                pieces[i // 2] = part[i % 2]
                rows.append(jnp.concatenate(pieces, axis=1))
        return jnp.concatenate(rows, axis=0)

    def outer_of(n, carry):
        block = jnp.concatenate([block_of(many * n + e) for e in range(many)], axis=1)
        for m in range(groups // chunk):
            out = nn_dot(lm_ref[m * chunk * fc : (m + 1) * chunk * fc, :], block)
            high, low = high_low(out)
            for e in range(many):
                at = pl.ds(pl.multiple_of((many * n + e) * fc, fc), fc)
                for g in range(chunk):
                    group = m * chunk + g
                    to = slice(group % wide * lanes, (group % wide + 1) * lanes)
                    cut = slice(g * fc, (g + 1) * fc), slice(e * lanes, (e + 1) * lanes)
                    oh_ref[group // wide, at, to] = high[cut]
                    ol_ref[group // wide, at, to] = low[cut]
        return carry

    lax.fori_loop(0, width_d // many, outer_of, 0)

    ready()
    some = z // fc
    for n in range(width_d // some):
        block = jnp.concatenate(
            [m_ref[pl.ds(n * some + e, fc, stride=width_d), :] for e in range(some)], axis=0
        ).T
        high, low = high_low(block)
        mt_ref[:z, n * z : (n + 1) * z] = high
        mt_ref[z:, n * z : (n + 1) * z] = low
    maskj = column_mask(mask_ref, col, tile_j, 2)

    maskl = jnp.concatenate([maskj] * (pack // 2), axis=1) > 0
    score = score_ref[...]
    s1 = score.astype(bf16).astype(f32)
    s2 = (score - s1).astype(bf16).astype(f32)
    s3 = score - s1 - s2
    none = jnp.zeros_like(s1)
    st = jnp.concatenate(
        [
            jnp.concatenate([s1, s2, s3, none], axis=0),
            jnp.concatenate([s1, s2, none, none], axis=0),
        ],
        axis=1,
    ).astype(bf16)

    def finish(n, carry):
        two = nn_dot(mt_ref[...], oh_ref[n])
        update_ref[...] = two[:z] + two[z:] + nn_dot(mt_ref[:z, :], ol_ref[n])
        for e in range(wide):
            g = n * wide + e
            at = pl.ds(pl.multiple_of(g * lanes, lanes), lanes)
            before = pair_ref[at, :].astype(f32).T
            result = (before + update_ref[:, e * lanes : (e + 1) * lanes]).astype(bf16)
            pout_t_ref[g] = result
            x = result.astype(f32)
            pout_ref[at, :] = x.T.astype(bf16)
            center = x - jnp.mean(x, axis=0, keepdims=True)
            inverse = lax.rsqrt(jnp.mean(center * center, axis=0, keepdims=True) + epsilon)
            high, low = high_low(center * inverse)
            scores = nn_dot(st, jnp.concatenate([high, low], axis=0))
            logits = scores[:heads] + scores[heads : 2 * heads] + scores[2 * heads : 3 * heads]
            logits_ref[g] = jnp.where(maskl, logits, far_below)
        at = pl.ds(pl.multiple_of(n * wide * lanes, wide * lanes), wide * lanes)
        pltpu.make_async_copy(pout_ref.at[at], pout_hbm.at[at], out_sem.at[n]).start()
        return carry

    lax.fori_loop(0, groups // wide, finish, 0)
    for n in range(groups // wide):
        at = pl.ds(n * wide * lanes, wide * lanes)
        pltpu.make_async_copy(pout_ref.at[at], pout_hbm.at[at], out_sem.at[n]).wait()


def by_heads(w, heads, out_ref):
    width, chans = w.shape
    hw = chans // heads
    block = 4 * hw
    slot = lax.broadcasted_iota(jnp.int32, (width, block), 1) // hw
    w = w.astype(f32)
    for t in range(chans // block):
        part = w[:, t * block : (t + 1) * block]
        turns = [part] + [pltpu.roll(part, n * hw, 1) for n in range(1, 4)]
        for e in range(4):
            h = t * 4 + e
            for s in range(4):
                out_ref[s * width : (s + 1) * width, h * block : (h + 1) * block] = jnp.where(
                    slot == s, turns[(s - e) % 4], 0.0
                ).astype(bf16)


def weights_kernel(
    ready,
    place_ref,
    side0_ref,
    side1_ref,
    side2_ref,
    side3_ref,
    cols0_ref,
    cols1_ref,
    cols2_ref,
    cols3_ref,
    wv_ref,
    wg_ref,
    wf_ref,
    gw_ref,
    acc_ref,
    bv_ref,
    bg_ref,
    bf_ref,
    rows_ref,
    cols_ref,
    gs_ref,
    vs_ref,
):
    nk, half, tokens, _ = cols_ref.shape
    tile = nk * tokens
    groups, heads, lanes = gw_ref.shape
    row, col = place_ref[0], place_ref[1]
    count = half * tokens
    for t, ref in enumerate((side0_ref, side1_ref, side2_ref, side3_ref)):
        start = ref.shape[0] - 2 * count
        rows_ref[jnp.bitwise_xor(col, t)] = ref[start:, :].reshape(rows_ref.shape[1:])
    for t, ref in enumerate((cols0_ref, cols1_ref, cols2_ref, cols3_ref)):
        start = ref.shape[0] - count
        cols_ref[lax.rem(row + nk - t, nk)] = ref[start:, :].reshape(cols_ref.shape[1:])
    ready()
    by_heads(wv_ref[...], heads, bv_ref)
    by_heads(wg_ref[...], heads, bg_ref)
    by_heads(wf_ref[...], heads, bf_ref)
    block = bv_ref.shape[1] // heads

    def four(read, n):
        return jnp.concatenate(
            [
                jnp.concatenate(
                    [
                        jnp.concatenate([read(k, 2 * (2 * n + e) + p) for k in range(nk)], axis=0)
                        for p in range(2)
                    ],
                    axis=1,
                )
                for e in range(2)
            ],
            axis=0,
        )

    for hp in range(heads // 2):
        cut = slice(hp * 2 * block, (hp + 1) * 2 * block)
        for n in range(half // 4):
            v = nn_dot(four(lambda k, s: cols_ref[k, s], n), bv_ref[:, cut]).astype(bf16)
            gate = nn_dot(four(lambda k, s: rows_ref[k, 0, s], n), bg_ref[:, cut])
            grad = nn_dot(four(lambda k, s: rows_ref[k, 1, s], n), bf_ref[:, cut])
            g = (grad * jax.nn.sigmoid(gate)).astype(bf16)
            for e in range(2):
                to = slice((2 * n + e) * block, (2 * n + e + 1) * block)
                for o in range(2):
                    mine = slice(o * block, (o + 1) * block)
                    ve = v[e * tile : (e + 1) * tile, mine]
                    vs_ref[2 * hp + o, :tile, to] = ve
                    vs_ref[2 * hp + o, tile:, to] = ve
                    gs_ref[2 * hp + o, :, to] = g[e * tile : (e + 1) * tile, mine]
    for h in range(heads):
        acc_ref[h * tile : (h + 1) * tile, :] = nt_dot(gs_ref[h], vs_ref[h])

    first = lax.broadcasted_iota(jnp.int32, (groups, 2 * tile), 1) < tile
    for h in range(heads):
        for part in range(pack // 2):
            a = acc_ref[pl.ds(h * tile + 2 * part, groups, stride=pack), :]
            b = acc_ref[pl.ds(h * tile + 2 * part + 1, groups, stride=pack), :]
            gw_ref[:, h, part * 2 * tile : (part + 1) * 2 * tile] = jnp.where(first, a, b)


def softmax_kernel(
    ready,
    col_ref,
    logits_ref,
    gwa_ref,
    gwb_ref,
    mask_ref,
    gw_ref,
    own_ref,
    pay1_ref,
    pay2_ref,
    pay3_ref,
):
    groups, heads, lanes = logits_ref.shape
    tile = lanes // pack
    nk = 4
    rows = groups * heads
    col = col_ref[0]
    gw_ref[...] = gwa_ref[...] + gwb_ref[...]
    lane = lax.broadcasted_iota(jnp.int32, (rows, 2 * tile), 1)
    low = lane < tile
    maskj = column_mask(mask_ref, col, tile, 2)
    stats = jnp.zeros((rows, 2 * tile), f32)
    for part in range(pack // 2):
        cut = slice(part * 2 * tile, (part + 1) * 2 * tile)
        lg = logits_ref[:, :, cut].reshape(rows, 2 * tile)
        gw = gw_ref[:, :, cut].reshape(rows, 2 * tile)
        m0 = jnp.max(jnp.where(low, lg, far_below), axis=1, keepdims=True)
        m1 = jnp.max(jnp.where(low, far_below, lg), axis=1, keepdims=True)
        p = jnp.exp(lg - jnp.where(low, m0, m1)) * maskj
        pg = p * gw
        for e, m in ((0, m0), (1, m1)):
            mine = low if e == 0 else jnp.logical_not(low)
            i = 2 * part + e
            total = jnp.sum(jnp.where(mine, p, 0.0), axis=1, keepdims=True)
            inner = jnp.sum(jnp.where(mine, pg, 0.0), axis=1, keepdims=True)
            stats = jnp.where(lane == i, m, stats)
            stats = jnp.where(lane == pack + i, total, stats)
            stats = jnp.where(lane == 2 * pack + i, inner, stats)
    turned = stats.T[:16]
    per = groups // nk
    for shift, pay in enumerate((own_ref, pay1_ref, pay2_ref, pay3_ref)):
        dest = lax.rem(col + shift, nk)
        pay[0] = turned[:8]
        pay[1] = turned[8:]
        for g in range(per):
            piece = logits_ref[dest * per + g]
            for part in range(pack // 2):
                pay[2 + g * (pack // 2) + part] = piece[:, part * 2 * tile : (part + 1) * 2 * tile]


def values_kernel(ready, ev_ref, wv_ref, norm_ref, wg_ref, v_ref, gate_ref):
    owners, half, tokens, wide = ev_ref.shape
    chans = wv_ref.shape[1]
    gate = jax.nn.sigmoid(nn_dot(norm_ref[...], twice(wg_ref[...])))
    gate_ref[: half * tokens] = gate[:, :chans]
    gate_ref[half * tokens :] = gate[:, chans:]
    wv = twice(wv_ref[...])
    ready()
    for s in range(half):
        x = jnp.concatenate([ev_ref[k, s] for k in range(owners)], axis=0)
        v_ref[s] = nn_dot(x, wv).astype(bf16)


def gradient_kernel(
    ready,
    own_ref, r1_ref, r2_ref, r3_ref, logits_ref, gw_ref, pout_t_ref, score_ref, out_hbm, stat_ref, out_ref, out_sem
):
    groups, heads, lanes = logits_ref.shape
    rows = groups * heads
    score = score_ref[...]
    z = score.shape[1]
    s1 = score.astype(bf16).astype(f32)
    s2 = (score - s1).astype(bf16).astype(f32)
    s3 = score - s1 - s2
    parts = [s1, s1, s1, s2, s2, s3, jnp.zeros((z - 6 * heads, z), f32)]
    sk = jnp.concatenate(parts, axis=0).T[:, : 6 * heads].astype(bf16)
    pays = (own_ref, r1_ref, r2_ref, r3_ref)
    ms = [p[0][:pack] for p in pays]
    ls = [p[0][pack : 2 * pack] for p in pays]
    ns = [p[1][:pack] for p in pays]
    top = functools.reduce(jnp.maximum, ms)
    scales = [jnp.exp(m - top) for m in ms]
    total = sum(a * b for a, b in zip(ls, scales))
    inner = sum(a * b for a, b in zip(ns, scales)) / total
    stacked = jnp.concatenate([top, total, inner, jnp.zeros((rows - 3 * pack, rows), f32)], axis=0)
    stat_ref[...] = stacked.T

    tile = lanes // pack
    low = lax.broadcasted_iota(jnp.int32, (heads, 2 * tile), 1) < tile

    def one(g):
        st = stat_ref[pl.ds(pl.multiple_of(g * heads, heads), heads), :]

        def spread(base):
            halves = [
                jnp.where(
                    low,
                    st[:, base + 2 * half : base + 2 * half + 1],
                    st[:, base + 2 * half + 1 : base + 2 * half + 2],
                )
                for half in range(pack // 2)
            ]
            return jnp.concatenate(halves, axis=1)

        prob = jnp.exp(logits_ref[g] - spread(0)) / spread(pack)
        gl = prob * (gw_ref[g] - spread(2 * pack))
        g1 = gl.astype(bf16).astype(f32)
        g2 = (gl - g1).astype(bf16).astype(f32)
        g3 = gl - g1 - g2
        stack = jnp.concatenate([g1, g2, g3, g1, g2, g1], axis=0).astype(bf16)
        grad = nn_dot(sk, stack)
        x = pout_t_ref[g].astype(f32)
        center = x - jnp.mean(x, axis=0, keepdims=True)
        inverse = lax.rsqrt(jnp.mean(center * center, axis=0, keepdims=True) + epsilon)
        normal = center * inverse
        centered = grad - jnp.mean(grad, axis=0, keepdims=True)
        along = jnp.mean(grad * normal, axis=0, keepdims=True)
        result = inverse * (centered - normal * along)
        out_ref[pl.ds(pl.multiple_of(g * lanes, lanes), lanes), :] = result.T.astype(bf16)

    many = 4

    def some(n, carry):
        for e in range(many):
            one(n * many + e)
        at = pl.ds(pl.multiple_of(n * many * lanes, many * lanes), many * lanes)
        pltpu.make_async_copy(out_ref.at[at], out_hbm.at[at], out_sem.at[n]).start()
        return carry

    lax.fori_loop(0, groups // many, some, 0)
    for n in range(groups // many):
        at = pl.ds(n * many * lanes, many * lanes)
        pltpu.make_async_copy(out_ref.at[at], out_hbm.at[at], out_sem.at[n]).wait()


def alignment_kernel(
    ready,
    col_ref,
    own_ref,
    r1_ref,
    r2_ref,
    r3_ref,
    v_ref,
    gate_ref,
    x_ref,
    wf_ref,
    out_ref,
    w_ref,
    gated_ref,
):
    pays = (own_ref, r1_ref, r2_ref, r3_ref)
    nk = len(pays)
    heads = own_ref.shape[1]
    wide = own_ref.shape[2]
    tile = wide // 2
    pieces = own_ref.shape[0] - 2
    rows = pieces * heads
    half, all_tokens, chans = v_ref.shape
    chans = chans // 2
    tokens = pieces * 2
    head_width = chans // heads
    col = col_ref[0]

    low = lax.broadcasted_iota(jnp.int32, (rows, wide), 1) < tile
    lgs = [p[2:].reshape(rows, wide) for p in pays]
    peak = functools.reduce(jnp.maximum, lgs)
    m0 = jnp.max(jnp.where(low, peak, far_below), axis=1, keepdims=True)
    m1 = jnp.max(jnp.where(low, far_below, peak), axis=1, keepdims=True)
    top = jnp.where(low, m0, m1)
    ps = [jnp.exp(lg - top) for lg in lgs]
    every = sum(ps)
    t0 = jnp.sum(jnp.where(low, every, 0.0), axis=1, keepdims=True)
    t1 = jnp.sum(jnp.where(low, 0.0, every), axis=1, keepdims=True)
    total = jnp.where(low, t0, t1)
    for shift, p in enumerate(ps):
        source = lax.rem(col + nk - shift, nk)
        weight = p / total
        rolled = pltpu.roll(weight, tile, 1)
        for n in range(pieces):
            w_ref[source, :, 2 * n, :] = weight[n * heads : (n + 1) * heads]
            w_ref[source, :, 2 * n + 1, :] = rolled[n * heads : (n + 1) * heads]
    w = jnp.concatenate(
        [w_ref[k].reshape(heads * tokens, wide)[:, :tile] for k in range(nk)], axis=1
    ).astype(bf16)

    owner = lax.broadcasted_iota(jnp.int32, (tokens, chans), 1) // head_width

    def one(s, carry):
        full = nn_dot(w, v_ref[s])
        for e in range(2):
            cut = slice(e * chans, (e + 1) * chans)
            mean = jnp.zeros((tokens, chans), f32)
            for h in range(heads):
                mean = jnp.where(owner == h, full[h * tokens : (h + 1) * tokens, cut], mean)
            at = pl.ds(pl.multiple_of((e * half + s) * tokens, tokens), tokens)
            gated_ref[at, :] = (gate_ref[at, :] * mean).astype(bf16)
        return carry

    lax.fori_loop(0, half, one, 0, unroll=4)
    out_ref[...] = (x_ref[...].astype(f32) + nt_dot(gated_ref[...], wf_ref[...])).astype(bf16)


def on_device(
    counts,
    alignment_input,
    pair_input,
    token_valid_mask,
    first_factor_weights,
    second_factor_weights,
    content_weights_grid,
    sigmoid_weights_grid,
    outer_matrix,
    score_matrix,
    final_mixing_weights,
    adjoint_of_rowset,
):
    nq, nr, nk = counts
    row_index = lax.axis_index("row")
    col_index = lax.axis_index("col")
    seqs, tokens, width = alignment_input.shape
    tile_i, tile_j, z = pair_input.shape
    fc = first_factor_weights.shape[1]
    fd = second_factor_weights.shape[1]
    heads = score_matrix.shape[1]
    chans = content_weights_grid.shape[1]
    groups = tile_i // pack
    lanes = pack * tile_j
    sds = jax.ShapeDtypeStruct

    mask = token_valid_mask.reshape(1, -1)
    own_start = ((row_index * nk + col_index) * tokens).astype(jnp.int32).reshape(1)
    seq_index = lax.axis_index("seq")
    place = jnp.stack([row_index, col_index, seq_index]).astype(jnp.int32)
    col_scalar = col_index.astype(jnp.int32).reshape(1)
    half = seqs // 2

    l_rows = tokens // pack * fc
    r_rows = fd * tokens // 128 * seqs
    n_rows = half * tokens
    rows, cols, normed = call(
        prepare_kernel,
        (
            sds((l_rows + 2 * n_rows, 128), bf16),
            sds((r_rows + n_rows, 128), bf16),
            sds((n_rows, 128), bf16),
        ),
        scratch=(
            pltpu.VMEM((tokens, seqs, width), f32),
            pltpu.VMEM((fd * tokens // 128, seqs, 128), f32),
        ),
        smem=1,
        vmem=60 * 1024 * 1024,
    )(
        own_start,
        alignment_input,
        adjoint_of_rowset,
        first_factor_weights.T,
        second_factor_weights.T,
        mask,
    )

    every = lax.all_gather(normed, ("row", "col"), axis=0).reshape(
        nr * nk, half, tokens, 2 * width
    )
    all_cols = [
        lax.ppermute(
            cols,
            ("row", "col"),
            [(r * nk + c, (c + t) % nr * nk + r) for r in range(nr) for c in range(nk)],
        )
        for t in range(nr)
    ]

    def exchange(x, bit):
        return lax.ppermute(x, "col", [(c, c ^ bit) for c in range(nk)])

    across = exchange(rows, 2)
    all_rows = [rows, exchange(rows, 1), across, exchange(across, 1)]

    (sides,) = call(
        join_kernel,
        (sds((nk * (r_rows + l_rows), 128), bf16),),
        smem=1,
    )(place, *all_rows, *all_cols)
    if nq == 2:
        far_sides = lax.ppermute(sides, "seq", [(0, 1), (1, 0)])
    else:
        far_sides = lax.all_gather(sides, "seq", axis=0, tiled=True)

    head_lanes = seqs * chans // heads
    (gw_own,) = call(
        weights_kernel,
        (sds((groups, heads, lanes), f32),),
        scratch=(
            pltpu.VMEM((heads * tile_i, 2 * tile_j), f32),
            pltpu.VMEM((4 * width, 4 * chans), bf16),
            pltpu.VMEM((4 * width, 4 * chans), bf16),
            pltpu.VMEM((4 * width, 4 * chans), bf16),
            pltpu.VMEM((nk, 2, half, tokens, 2 * width), bf16),
            pltpu.VMEM((nk, half, tokens, 2 * width), bf16),
            pltpu.VMEM((heads, tile_i, head_lanes), bf16),
            pltpu.VMEM((heads, 2 * tile_j, head_lanes), bf16),
        ),
        smem=1,
        flops=3_000_000_000,
        nbytes=3_000_000,
        far=(9, 10, 11),
    )(
        place,
        *all_rows,
        *all_cols,
        content_weights_grid,
        sigmoid_weights_grid,
        final_mixing_weights.T,
    )
    if nq == 2:
        gw_other = lax.ppermute(gw_own, "seq", [(0, 1), (1, 0)])
    else:
        gw_own, gw_other = lax.psum(gw_own, "seq"), jnp.zeros_like(gw_own)

    pair_out, pair_t, logits = call(
        update_kernel,
        (
            sds((tile_i * tile_j, z), bf16),
            sds((groups, z, lanes), bf16),
            sds((groups, heads, lanes), f32),
        ),
        scratch=(
            pltpu.VMEM((tile_i * tile_j, z), bf16),
            pltpu.SemaphoreType.DMA((groups // 4,)),
            pltpu.VMEM((nk, nq * r_rows, 128), bf16),
            pltpu.VMEM((fd, nq * seqs, 4 * tile_j), bf16),
            pltpu.VMEM((groups * fc, nq * pack * seqs), bf16),
            pltpu.VMEM((2 * z, fd * fc), bf16),
            pltpu.VMEM((groups // 4, fd * fc, 4 * lanes), bf16),
            pltpu.VMEM((groups // 4, fd * fc, 4 * lanes), bf16),
            pltpu.VMEM((z, 4 * lanes), f32),
        ),
        smem=1,
        flops=14_000_000_000,
        nbytes=5_000_000,
        vmem=44 * 1024 * 1024,
        far=(3, 4, 5, 6),
        far_out=(0,),
    )(
        place,
        sides,
        far_sides,
        mask,
        outer_matrix,
        score_matrix.T,
        pair_input.reshape(tile_i * tile_j, z),
    )

    values, gating = call(
        values_kernel,
        (sds((half, nr * nk * tokens, 2 * chans), bf16), sds((seqs * tokens, chans), f32)),
        flops=4_000_000_000,
        nbytes=6_000_000,
        far=(0,),
    )(every, content_weights_grid, normed, sigmoid_weights_grid)

    payload = sds((2 + groups // nk * (pack // 2), heads, 2 * tile_j), f32)
    gw, pay0, pay1, pay2, pay3 = call(
        softmax_kernel,
        (sds((groups, heads, lanes), f32), payload, payload, payload, payload),
        smem=1,
    )(col_scalar, logits, gw_own, gw_other, mask)

    got = [
        lax.ppermute(pay, "col", [(c, (c + shift) % nk) for c in range(nk)])
        for shift, pay in ((1, pay1), (2, pay2), (3, pay3))
    ]

    got, values, gating = lax.optimization_barrier((got, values, gating))

    (gradient,) = call(
        gradient_kernel,
        (sds((tile_i * tile_j, z), bf16),),
        scratch=(
            pltpu.VMEM((groups * heads, groups * heads), f32),
            pltpu.VMEM((tile_i * tile_j, z), bf16),
            pltpu.SemaphoreType.DMA((groups // 4,)),
        ),
        far_out=(0,),
        flops=4_000_000_000,
        nbytes=3_000_000,
    )(pay0, *got, logits, gw, pair_t, score_matrix.T)

    (aligned,) = call(
        alignment_kernel,
        (sds((seqs * tokens, width), bf16),),
        scratch=(
            pltpu.VMEM((nk, heads, tokens, 2 * tile_j), f32),
            pltpu.VMEM((seqs * tokens, chans), bf16),
        ),
        smem=1,
        flops=3_000_000_000,
        nbytes=5_000_000,
    )(
        col_scalar,
        pay0,
        *got,
        values,
        gating,
        alignment_input.reshape(seqs * tokens, width),
        final_mixing_weights.T,
    )
    return (
        aligned.reshape(seqs, tokens, width),
        pair_out.reshape(tile_i, tile_j, z),
        gradient.reshape(tile_i, tile_j, z),
    )


def solution(mesh):
    counts = (mesh.shape["seq"], mesh.shape["row"], mesh.shape["col"])
    in_specs = (
        P("seq", ("row", "col"), None),
        P("row", "col", None),
        P(),
        P(),
        P(),
        P(),
        P(),
        P(),
        P(),
        P(),
        P("seq", ("row", "col"), None),
    )
    out_specs = (P("seq", ("row", "col"), None), P("row", "col", None), P("row", "col", None))
    return jax.shard_map(
        functools.partial(on_device, counts),
        mesh=mesh,
        in_specs=in_specs,
        out_specs=out_specs,
        check_vma=False,
    )
```

```python
import functools

import jax
import jax.numpy as jnp
from jax import lax
from jax.experimental import pallas as pl
from jax.experimental.pallas import tpu as pltpu
from jax.sharding import PartitionSpec as P

epsilon = 1e-05
far_below = -1e30
vmem_bytes = 32 * 1024 * 1024
pack = 4

f32 = jnp.float32
bf16 = jnp.bfloat16


def nt_dot(a, b):
    return lax.dot_general(a, b, (((1,), (1,)), ((), ())), preferred_element_type=f32)


def nn_dot(a, b):
    return jnp.dot(a, b, preferred_element_type=f32)


def high_low(x):
    high = x.astype(bf16)
    return high, (x - high.astype(f32)).astype(bf16)


def call(
    kernel, out_shape, scratch=(), smem=0, flops=0, nbytes=0, vmem=vmem_bytes, far=(), far_out=()
):
    def run(*args):
        count = len(args)
        in_specs = [
            pl.BlockSpec(memory_space=pltpu.SMEM if n < smem else pltpu.VMEM) for n in range(count)
        ]
        for n in far:
            in_specs[n] = pl.BlockSpec(memory_space=pltpu.HBM)
        landing = [pltpu.VMEM(args[n].shape, args[n].dtype) for n in far]
        if far:
            landing.append(pltpu.SemaphoreType.DMA((len(far),)))

        def body(*refs):
            inputs = list(refs[:count])
            extra = refs[len(refs) - len(landing) :]
            rest = refs[count : len(refs) - len(landing)]
            copies = []
            for i, n in enumerate(far):
                copies.append(pltpu.make_async_copy(inputs[n], extra[i], extra[-1].at[i]))
                copies[-1].start()
                inputs[n] = extra[i]

            def ready():
                for copy in copies:
                    copy.wait()

            kernel(ready, *inputs, *rest)

        return pl.pallas_call(
            body,
            out_shape=out_shape,
            in_specs=in_specs,
            out_specs=[
                pl.BlockSpec(memory_space=pltpu.HBM if n in far_out else pltpu.VMEM)
                for n in range(len(out_shape))
            ],
            scratch_shapes=list(scratch) + landing,
            compiler_params=pltpu.CompilerParams(vmem_limit_bytes=vmem),
            cost_estimate=pl.CostEstimate(flops=flops, bytes_accessed=nbytes, transcendentals=0),
        )(*args)

    return run


def valid_count(mask_ref):
    return jnp.sum(mask_ref[...].astype(f32), axis=1, keepdims=True)


def column_mask(mask_ref, col, tile, copies):
    lane = lax.broadcasted_iota(jnp.int32, (1, copies * tile), 1)
    token = (lax.rem(lane, tile) + col * tile).astype(f32)
    return (token < valid_count(mask_ref)).astype(f32)


def twice(w):
    none = jnp.zeros_like(w)
    return jnp.concatenate(
        [jnp.concatenate([w, none], axis=1), jnp.concatenate([none, w], axis=1)], axis=0
    )


def prepare_kernel(
    ready,
    own_ref,
    x_ref,
    adj_ref,
    w1_ref,
    w2_ref,
    mask_ref,
    rows_ref,
    cols_ref,
    norm_ref,
    turn_ref,
    place_ref,
):
    seqs, tokens, width = x_ref.shape
    half = seqs // 2
    fd = w2_ref.shape[0]
    x = x_ref[...].astype(f32)
    center = x - jnp.mean(x, axis=-1, keepdims=True)
    inverse = lax.rsqrt(jnp.mean(center * center, axis=-1, keepdims=True) + epsilon)
    normed = center * inverse
    rows = half * tokens
    adj = adj_ref[...].astype(f32)

    def two(x):
        x = jnp.concatenate([x[:half], x[half:]], axis=-1)
        return x.reshape(rows, 2 * width).astype(bf16)

    packed = two(normed)
    norm_ref[...] = packed
    rows_ref[-2 * rows : -rows, :] = packed
    rows_ref[-rows:, :] = two(adj)
    cols_ref[-rows:, :] = packed
    token = lax.broadcasted_iota(jnp.int32, (seqs, tokens, width), 1) + own_ref[0]
    count = valid_count(mask_ref).reshape(1, 1, 1)
    real = jnp.where(token.astype(f32) < count, normed, 0.0)
    for s in range(seqs):
        turn_ref[:, s, :] = real[s]
    turned = turn_ref[...].astype(bf16).reshape(tokens * seqs, width)
    left = nt_dot(w1_ref[...], turned).astype(bf16)
    fc = w1_ref.shape[0]
    wk = pack * seqs
    for g in range(tokens // pack):
        rows_ref[g * fc : (g + 1) * fc, :] = left[:, g * wk : (g + 1) * wk]
    size = 128 // tokens
    real = real.astype(bf16)
    w2 = w2_ref[...]
    d = lax.broadcasted_iota(jnp.int32, (fd, 128), 0)
    lane = lax.broadcasted_iota(jnp.int32, (fd, 128), 1)
    mine = lax.rem(d, size) == lane // tokens
    for s in range(seqs):
        res = nt_dot(w2, jnp.concatenate([real[s]] * size, axis=0))
        res = jnp.where(mine, res, 0.0).reshape(fd // size, size, 128)
        place_ref[:, s, :] = jnp.sum(res, axis=1)
    cols_ref[:-rows, :] = place_ref[...].reshape(fd // size * seqs, 128).astype(bf16)


def join_kernel(
    ready,
    place_ref,
    rows0_ref,
    rows1_ref,
    rows2_ref,
    rows3_ref,
    cols0_ref,
    cols1_ref,
    cols2_ref,
    cols3_ref,
    out_ref,
    norm_ref,
):
    nk = 4
    row, col = place_ref[0], place_ref[1]
    r_rows = l_rows = out_ref.shape[0] // (2 * nk)
    for t, ref in enumerate((cols0_ref, cols1_ref, cols2_ref, cols3_ref)):
        at = pl.ds(pl.multiple_of(lax.rem(row + nk - t, nk) * r_rows, r_rows), r_rows)
        out_ref[at, :] = ref[:r_rows, :]
    for t, ref in enumerate((rows0_ref, rows1_ref, rows2_ref, rows3_ref)):
        start = nk * r_rows + jnp.bitwise_xor(col, t) * l_rows
        at = pl.ds(pl.multiple_of(start, l_rows), l_rows)
        out_ref[at, :] = ref[:l_rows, :]
        half, tokens, _ = norm_ref.shape[1:]
        count = half * tokens
        start = ref.shape[0] - 2 * count
        norm_ref[jnp.bitwise_xor(col, t)] = ref[start : start + count, :].reshape(norm_ref.shape[1:])


def update_kernel(
    ready,
    place_ref,
    sides_ref,
    far_sides_ref,
    mask_ref,
    m_ref,
    score_ref,
    pair_ref,
    pout_hbm,
    pout_t_ref,
    logits_ref,
    pout_ref,
    out_sem,
    rk_ref,
    rab_ref,
    lm_ref,
    mt_ref,
    oh_ref,
    ol_ref,
    update_ref,
):
    nk = rk_ref.shape[0]
    width_d, pair_rows, _ = rab_ref.shape
    col, seq = place_ref[1], place_ref[2]
    z = pair_ref.shape[1]
    groups, heads, lanes = logits_ref.shape
    tile_j = lanes // pack
    tokens = tile_j // nk
    fc = lm_ref.shape[0] // groups
    seqs = 128 // pack
    nq = pair_rows // seqs
    wk = pack * seqs

    r_rows = rk_ref.shape[1] // nq
    l_rows = groups * fc
    if nq == 2:
        sources = ((seq, 0, sides_ref), (1 - seq, 0, far_sides_ref))
    else:
        sources = tuple((q, q, far_sides_ref) for q in range(nq))
    for q, slot, ref in sources:
        base = slot * (nk * r_rows + l_rows)
        at = pl.ds(pl.multiple_of(q * r_rows, r_rows), r_rows)
        for k in range(nk):
            rk_ref[k, at, :] = ref[base + k * r_rows : base + (k + 1) * r_rows, :]
        base = base + nk * r_rows
        to = pl.ds(pl.multiple_of(q * wk, wk), wk)
        lm_ref[:, to] = ref[base : base + l_rows, :]
    size = 128 // tokens
    right = jnp.concatenate([rk_ref[k] for k in range(nk)], axis=1)
    source = lax.broadcasted_iota(jnp.int32, (nk * 128, 4 * tile_j), 0)
    target = lax.broadcasted_iota(jnp.int32, (nk * 128, 4 * tile_j), 1)
    used = jnp.logical_or(target < tile_j, target >= 3 * tile_j)
    j = lax.rem(target, tile_j)
    offset = jnp.where(used, source - (j // tokens * 128 + lax.rem(j, tokens)), -1)
    blocks = width_d // size
    for e in range(size):
        pick = jnp.where(offset == e * tokens, 1.0, 0.0).astype(bf16)
        res = nn_dot(right, pick).astype(bf16)
        for q in range(nq):
            for n in range(blocks):
                at = (q * blocks + n) * seqs
                rab_ref[n * size + e, q * seqs : (q + 1) * seqs, :] = res[at : at + seqs]

    chunk = 8
    many = 4
    wide = oh_ref.shape[2] // lanes
    empty = jnp.zeros((seqs, 2 * tile_j), bf16)

    def block_of(d):
        rows = []
        for q in range(nq):
            both = rab_ref[d, q * seqs : (q + 1) * seqs, :]
            part = both[:, : 2 * tile_j], both[:, 2 * tile_j :]
            for i in range(pack):
                pieces = [empty] * (pack // 2)
                pieces[i // 2] = part[i % 2]
                rows.append(jnp.concatenate(pieces, axis=1))
        return jnp.concatenate(rows, axis=0)

    def outer_of(n, carry):
        block = jnp.concatenate([block_of(many * n + e) for e in range(many)], axis=1)
        for m in range(groups // chunk):
            out = nn_dot(lm_ref[m * chunk * fc : (m + 1) * chunk * fc, :], block)
            high, low = high_low(out)
            for e in range(many):
                at = pl.ds(pl.multiple_of((many * n + e) * fc, fc), fc)
                for g in range(chunk):
                    group = m * chunk + g
                    to = slice(group % wide * lanes, (group % wide + 1) * lanes)
                    cut = slice(g * fc, (g + 1) * fc), slice(e * lanes, (e + 1) * lanes)
                    oh_ref[group // wide, at, to] = high[cut]
                    ol_ref[group // wide, at, to] = low[cut]
        return carry

    lax.fori_loop(0, width_d // many, outer_of, 0)

    ready()
    some = z // fc
    for n in range(width_d // some):
        block = jnp.concatenate(
            [m_ref[pl.ds(n * some + e, fc, stride=width_d), :] for e in range(some)], axis=0
        ).T
        high, low = high_low(block)
        mt_ref[:z, n * z : (n + 1) * z] = high
        mt_ref[z:, n * z : (n + 1) * z] = low
    maskj = column_mask(mask_ref, col, tile_j, 2)

    maskl = jnp.concatenate([maskj] * (pack // 2), axis=1) > 0
    score = score_ref[...]
    s1 = score.astype(bf16).astype(f32)
    s2 = (score - s1).astype(bf16).astype(f32)
    s3 = score - s1 - s2
    none = jnp.zeros_like(s1)
    st = jnp.concatenate(
        [
            jnp.concatenate([s1, s2, s3, none], axis=0),
            jnp.concatenate([s1, s2, none, none], axis=0),
        ],
        axis=1,
    ).astype(bf16)

    def finish(n, carry):
        two = nn_dot(mt_ref[...], oh_ref[n])
        update_ref[...] = two[:z] + two[z:] + nn_dot(mt_ref[:z, :], ol_ref[n])
        for e in range(wide):
            g = n * wide + e
            at = pl.ds(pl.multiple_of(g * lanes, lanes), lanes)
            before = pair_ref[at, :].astype(f32).T
            result = (before + update_ref[:, e * lanes : (e + 1) * lanes]).astype(bf16)
            pout_t_ref[g] = result
            x = result.astype(f32)
            pout_ref[at, :] = x.T.astype(bf16)
            center = x - jnp.mean(x, axis=0, keepdims=True)
            inverse = lax.rsqrt(jnp.mean(center * center, axis=0, keepdims=True) + epsilon)
            high, low = high_low(center * inverse)
            scores = nn_dot(st, jnp.concatenate([high, low], axis=0))
            logits = scores[:heads] + scores[heads : 2 * heads] + scores[2 * heads : 3 * heads]
            logits_ref[g] = jnp.where(maskl, logits, far_below)
        at = pl.ds(pl.multiple_of(n * wide * lanes, wide * lanes), wide * lanes)
        pltpu.make_async_copy(pout_ref.at[at], pout_hbm.at[at], out_sem.at[n]).start()
        return carry

    lax.fori_loop(0, groups // wide, finish, 0)
    for n in range(groups // wide):
        at = pl.ds(n * wide * lanes, wide * lanes)
        pltpu.make_async_copy(pout_ref.at[at], pout_hbm.at[at], out_sem.at[n]).wait()


def by_heads(w, heads, out_ref):
    width, chans = w.shape
    hw = chans // heads
    block = 4 * hw
    slot = lax.broadcasted_iota(jnp.int32, (width, block), 1) // hw
    w = w.astype(f32)
    for t in range(chans // block):
        part = w[:, t * block : (t + 1) * block]
        turns = [part] + [pltpu.roll(part, n * hw, 1) for n in range(1, 4)]
        for e in range(4):
            h = t * 4 + e
            for s in range(4):
                out_ref[s * width : (s + 1) * width, h * block : (h + 1) * block] = jnp.where(
                    slot == s, turns[(s - e) % 4], 0.0
                ).astype(bf16)


def weights_kernel(
    ready,
    place_ref,
    side0_ref,
    side1_ref,
    side2_ref,
    side3_ref,
    cols0_ref,
    cols1_ref,
    cols2_ref,
    cols3_ref,
    wv_ref,
    wg_ref,
    wf_ref,
    gw_ref,
    acc_ref,
    bv_ref,
    bg_ref,
    bf_ref,
    rows_ref,
    cols_ref,
    gs_ref,
    vs_ref,
):
    nk, half, tokens, _ = cols_ref.shape
    tile = nk * tokens
    groups, heads, lanes = gw_ref.shape
    row, col = place_ref[0], place_ref[1]
    count = half * tokens
    for t, ref in enumerate((side0_ref, side1_ref, side2_ref, side3_ref)):
        start = ref.shape[0] - 2 * count
        rows_ref[jnp.bitwise_xor(col, t)] = ref[start:, :].reshape(rows_ref.shape[1:])
    for t, ref in enumerate((cols0_ref, cols1_ref, cols2_ref, cols3_ref)):
        start = ref.shape[0] - count
        cols_ref[lax.rem(row + nk - t, nk)] = ref[start:, :].reshape(cols_ref.shape[1:])
    ready()
    by_heads(wv_ref[...], heads, bv_ref)
    by_heads(wg_ref[...], heads, bg_ref)
    by_heads(wf_ref[...], heads, bf_ref)
    block = bv_ref.shape[1] // heads

    def four(read, n):
        return jnp.concatenate(
            [
                jnp.concatenate(
                    [
                        jnp.concatenate([read(k, 2 * (2 * n + e) + p) for k in range(nk)], axis=0)
                        for p in range(2)
                    ],
                    axis=1,
                )
                for e in range(2)
            ],
            axis=0,
        )

    for hp in range(heads // 2):
        cut = slice(hp * 2 * block, (hp + 1) * 2 * block)
        for n in range(half // 4):
            v = nn_dot(four(lambda k, s: cols_ref[k, s], n), bv_ref[:, cut]).astype(bf16)
            gate = nn_dot(four(lambda k, s: rows_ref[k, 0, s], n), bg_ref[:, cut])
            grad = nn_dot(four(lambda k, s: rows_ref[k, 1, s], n), bf_ref[:, cut])
            g = (grad * jax.nn.sigmoid(gate)).astype(bf16)
            for e in range(2):
                to = slice((2 * n + e) * block, (2 * n + e + 1) * block)
                for o in range(2):
                    mine = slice(o * block, (o + 1) * block)
                    ve = v[e * tile : (e + 1) * tile, mine]
                    vs_ref[2 * hp + o, :tile, to] = ve
                    vs_ref[2 * hp + o, tile:, to] = ve
                    gs_ref[2 * hp + o, :, to] = g[e * tile : (e + 1) * tile, mine]
    for h in range(heads):
        acc_ref[h * tile : (h + 1) * tile, :] = nt_dot(gs_ref[h], vs_ref[h])

    first = lax.broadcasted_iota(jnp.int32, (groups, 2 * tile), 1) < tile
    for h in range(heads):
        for part in range(pack // 2):
            a = acc_ref[pl.ds(h * tile + 2 * part, groups, stride=pack), :]
            b = acc_ref[pl.ds(h * tile + 2 * part + 1, groups, stride=pack), :]
            gw_ref[:, h, part * 2 * tile : (part + 1) * 2 * tile] = jnp.where(first, a, b)


def softmax_kernel(
    ready,
    col_ref,
    logits_ref,
    gwa_ref,
    gwb_ref,
    mask_ref,
    gw_ref,
    own_ref,
    pay1_ref,
    pay2_ref,
    pay3_ref,
):
    groups, heads, lanes = logits_ref.shape
    tile = lanes // pack
    nk = 4
    rows = groups * heads
    col = col_ref[0]
    gw_ref[...] = gwa_ref[...] + gwb_ref[...]
    lane = lax.broadcasted_iota(jnp.int32, (rows, 2 * tile), 1)
    low = lane < tile
    maskj = column_mask(mask_ref, col, tile, 2)
    stats = jnp.zeros((rows, 2 * tile), f32)
    for part in range(pack // 2):
        cut = slice(part * 2 * tile, (part + 1) * 2 * tile)
        lg = logits_ref[:, :, cut].reshape(rows, 2 * tile)
        gw = gw_ref[:, :, cut].reshape(rows, 2 * tile)
        m0 = jnp.max(jnp.where(low, lg, far_below), axis=1, keepdims=True)
        m1 = jnp.max(jnp.where(low, far_below, lg), axis=1, keepdims=True)
        p = jnp.exp(lg - jnp.where(low, m0, m1)) * maskj
        pg = p * gw
        for e, m in ((0, m0), (1, m1)):
            mine = low if e == 0 else jnp.logical_not(low)
            i = 2 * part + e
            total = jnp.sum(jnp.where(mine, p, 0.0), axis=1, keepdims=True)
            inner = jnp.sum(jnp.where(mine, pg, 0.0), axis=1, keepdims=True)
            stats = jnp.where(lane == i, m, stats)
            stats = jnp.where(lane == pack + i, total, stats)
            stats = jnp.where(lane == 2 * pack + i, inner, stats)
    turned = stats.T[:16]
    per = groups // nk
    for shift, pay in enumerate((own_ref, pay1_ref, pay2_ref, pay3_ref)):
        dest = lax.rem(col + shift, nk)
        pay[0] = turned[:8]
        pay[1] = turned[8:]
        for g in range(per):
            piece = logits_ref[dest * per + g]
            for part in range(pack // 2):
                pay[2 + g * (pack // 2) + part] = piece[:, part * 2 * tile : (part + 1) * 2 * tile]


def values_kernel(
    ready, ev0_ref, ev1_ref, ev2_ref, ev3_ref, wv_ref, norm_ref, wg_ref, v_ref, gate_ref
):
    evs = (ev0_ref, ev1_ref, ev2_ref, ev3_ref)
    nk, half, tokens, wide = ev0_ref.shape
    chans = wv_ref.shape[1]
    gate = jax.nn.sigmoid(nn_dot(norm_ref[...], twice(wg_ref[...])))
    gate_ref[: half * tokens] = gate[:, :chans]
    gate_ref[half * tokens :] = gate[:, chans:]
    wv = twice(wv_ref[...])
    for s in range(half):
        x = jnp.concatenate([ev[k, s] for ev in evs for k in range(nk)], axis=0)
        v_ref[s] = nn_dot(x, wv).astype(bf16)


def gradient_kernel(
    ready,
    own_ref, r1_ref, r2_ref, r3_ref, logits_ref, gw_ref, pout_t_ref, score_ref, out_hbm, stat_ref, out_ref, out_sem
):
    groups, heads, lanes = logits_ref.shape
    rows = groups * heads
    score = score_ref[...]
    z = score.shape[1]
    s1 = score.astype(bf16).astype(f32)
    s2 = (score - s1).astype(bf16).astype(f32)
    s3 = score - s1 - s2
    parts = [s1, s1, s1, s2, s2, s3, jnp.zeros((z - 6 * heads, z), f32)]
    sk = jnp.concatenate(parts, axis=0).T[:, : 6 * heads].astype(bf16)
    pays = (own_ref, r1_ref, r2_ref, r3_ref)
    ms = [p[0][:pack] for p in pays]
    ls = [p[0][pack : 2 * pack] for p in pays]
    ns = [p[1][:pack] for p in pays]
    top = functools.reduce(jnp.maximum, ms)
    scales = [jnp.exp(m - top) for m in ms]
    total = sum(a * b for a, b in zip(ls, scales))
    inner = sum(a * b for a, b in zip(ns, scales)) / total
    stacked = jnp.concatenate([top, total, inner, jnp.zeros((rows - 3 * pack, rows), f32)], axis=0)
    stat_ref[...] = stacked.T

    tile = lanes // pack
    low = lax.broadcasted_iota(jnp.int32, (heads, 2 * tile), 1) < tile

    def one(g):
        st = stat_ref[pl.ds(pl.multiple_of(g * heads, heads), heads), :]

        def spread(base):
            halves = [
                jnp.where(
                    low,
                    st[:, base + 2 * half : base + 2 * half + 1],
                    st[:, base + 2 * half + 1 : base + 2 * half + 2],
                )
                for half in range(pack // 2)
            ]
            return jnp.concatenate(halves, axis=1)

        prob = jnp.exp(logits_ref[g] - spread(0)) / spread(pack)
        gl = prob * (gw_ref[g] - spread(2 * pack))
        g1 = gl.astype(bf16).astype(f32)
        g2 = (gl - g1).astype(bf16).astype(f32)
        g3 = gl - g1 - g2
        stack = jnp.concatenate([g1, g2, g3, g1, g2, g1], axis=0).astype(bf16)
        grad = nn_dot(sk, stack)
        x = pout_t_ref[g].astype(f32)
        center = x - jnp.mean(x, axis=0, keepdims=True)
        inverse = lax.rsqrt(jnp.mean(center * center, axis=0, keepdims=True) + epsilon)
        normal = center * inverse
        centered = grad - jnp.mean(grad, axis=0, keepdims=True)
        along = jnp.mean(grad * normal, axis=0, keepdims=True)
        result = inverse * (centered - normal * along)
        out_ref[pl.ds(pl.multiple_of(g * lanes, lanes), lanes), :] = result.T.astype(bf16)

    many = 4

    def some(n, carry):
        for e in range(many):
            one(n * many + e)
        at = pl.ds(pl.multiple_of(n * many * lanes, many * lanes), many * lanes)
        pltpu.make_async_copy(out_ref.at[at], out_hbm.at[at], out_sem.at[n]).start()
        return carry

    lax.fori_loop(0, groups // many, some, 0)
    for n in range(groups // many):
        at = pl.ds(n * many * lanes, many * lanes)
        pltpu.make_async_copy(out_ref.at[at], out_hbm.at[at], out_sem.at[n]).wait()


def alignment_kernel(
    ready,
    place_ref,
    own_ref,
    r1_ref,
    r2_ref,
    r3_ref,
    v_ref,
    gate_ref,
    x_ref,
    wf_ref,
    out_ref,
    w_ref,
    gated_ref,
):
    pays = (own_ref, r1_ref, r2_ref, r3_ref)
    nk = len(pays)
    heads = own_ref.shape[1]
    wide = own_ref.shape[2]
    tile = wide // 2
    pieces = own_ref.shape[0] - 2
    rows = pieces * heads
    half, all_tokens, chans = v_ref.shape
    chans = chans // 2
    tokens = pieces * 2
    head_width = chans // heads
    row, col = place_ref[0], place_ref[1]

    low = lax.broadcasted_iota(jnp.int32, (rows, wide), 1) < tile
    lgs = [p[2:].reshape(rows, wide) for p in pays]
    peak = functools.reduce(jnp.maximum, lgs)
    m0 = jnp.max(jnp.where(low, peak, far_below), axis=1, keepdims=True)
    m1 = jnp.max(jnp.where(low, far_below, peak), axis=1, keepdims=True)
    top = jnp.where(low, m0, m1)
    ps = [jnp.exp(lg - top) for lg in lgs]
    every = sum(ps)
    t0 = jnp.sum(jnp.where(low, every, 0.0), axis=1, keepdims=True)
    t1 = jnp.sum(jnp.where(low, 0.0, every), axis=1, keepdims=True)
    total = jnp.where(low, t0, t1)
    for shift, p in enumerate(ps):
        source = lax.rem(col + nk - shift, nk)
        weight = p / total
        rolled = pltpu.roll(weight, tile, 1)
        for n in range(pieces):
            w_ref[source, :, 2 * n, :] = weight[n * heads : (n + 1) * heads]
            w_ref[source, :, 2 * n + 1, :] = rolled[n * heads : (n + 1) * heads]
    w = jnp.concatenate(
        [
            w_ref[jnp.bitwise_xor(row, t)].reshape(heads * tokens, wide)[:, :tile]
            for t in range(nk)
        ],
        axis=1,
    ).astype(bf16)

    owner = lax.broadcasted_iota(jnp.int32, (tokens, chans), 1) // head_width

    def one(s, carry):
        full = nn_dot(w, v_ref[s])
        for e in range(2):
            cut = slice(e * chans, (e + 1) * chans)
            mean = jnp.zeros((tokens, chans), f32)
            for h in range(heads):
                mean = jnp.where(owner == h, full[h * tokens : (h + 1) * tokens, cut], mean)
            at = pl.ds(pl.multiple_of((e * half + s) * tokens, tokens), tokens)
            gated_ref[at, :] = (gate_ref[at, :] * mean).astype(bf16)
        return carry

    lax.fori_loop(0, half, one, 0, unroll=4)
    out_ref[...] = (x_ref[...].astype(f32) + nt_dot(gated_ref[...], wf_ref[...])).astype(bf16)


def on_device(
    counts,
    alignment_input,
    pair_input,
    token_valid_mask,
    first_factor_weights,
    second_factor_weights,
    content_weights_grid,
    sigmoid_weights_grid,
    outer_matrix,
    score_matrix,
    final_mixing_weights,
    adjoint_of_rowset,
):
    nq, nr, nk = counts
    row_index = lax.axis_index("row")
    col_index = lax.axis_index("col")
    seqs, tokens, width = alignment_input.shape
    tile_i, tile_j, z = pair_input.shape
    fc = first_factor_weights.shape[1]
    fd = second_factor_weights.shape[1]
    heads = score_matrix.shape[1]
    chans = content_weights_grid.shape[1]
    groups = tile_i // pack
    lanes = pack * tile_j
    sds = jax.ShapeDtypeStruct

    mask = token_valid_mask.reshape(1, -1)
    own_start = ((row_index * nk + col_index) * tokens).astype(jnp.int32).reshape(1)
    seq_index = lax.axis_index("seq")
    place = jnp.stack([row_index, col_index, seq_index]).astype(jnp.int32)
    col_scalar = col_index.astype(jnp.int32).reshape(1)
    half = seqs // 2

    l_rows = tokens // pack * fc
    r_rows = fd * tokens // 128 * seqs
    n_rows = half * tokens
    rows, cols, normed = call(
        prepare_kernel,
        (
            sds((l_rows + 2 * n_rows, 128), bf16),
            sds((r_rows + n_rows, 128), bf16),
            sds((n_rows, 128), bf16),
        ),
        scratch=(
            pltpu.VMEM((tokens, seqs, width), f32),
            pltpu.VMEM((fd * tokens // 128, seqs, 128), f32),
        ),
        smem=1,
        vmem=60 * 1024 * 1024,
    )(
        own_start,
        alignment_input,
        adjoint_of_rowset,
        first_factor_weights.T,
        second_factor_weights.T,
        mask,
    )

    all_cols = [
        lax.ppermute(
            cols,
            ("row", "col"),
            [(r * nk + c, (c + t) % nr * nk + r) for r in range(nr) for c in range(nk)],
        )
        for t in range(nr)
    ]

    def exchange(x, bit):
        return lax.ppermute(x, "col", [(c, c ^ bit) for c in range(nk)])

    across = exchange(rows, 2)
    all_rows = [rows, exchange(rows, 1), across, exchange(across, 1)]

    sides, block = call(
        join_kernel,
        (
            sds((nk * (r_rows + l_rows), 128), bf16),
            sds((nk, half, tokens, 2 * width), bf16),
        ),
        smem=1,
    )(place, *all_rows, *all_cols)
    if nq == 2:
        far_sides = lax.ppermute(sides, "seq", [(0, 1), (1, 0)])
    else:
        far_sides = lax.all_gather(sides, "seq", axis=0, tiled=True)

    def exchange_rows(x, bit):
        return lax.ppermute(x, "row", [(r, r ^ bit) for r in range(nr)])

    beyond = exchange_rows(block, 2)
    every = [block, exchange_rows(block, 1), beyond, exchange_rows(beyond, 1)]

    head_lanes = seqs * chans // heads
    (gw_own,) = call(
        weights_kernel,
        (sds((groups, heads, lanes), f32),),
        scratch=(
            pltpu.VMEM((heads * tile_i, 2 * tile_j), f32),
            pltpu.VMEM((4 * width, 4 * chans), bf16),
            pltpu.VMEM((4 * width, 4 * chans), bf16),
            pltpu.VMEM((4 * width, 4 * chans), bf16),
            pltpu.VMEM((nk, 2, half, tokens, 2 * width), bf16),
            pltpu.VMEM((nk, half, tokens, 2 * width), bf16),
            pltpu.VMEM((heads, tile_i, head_lanes), bf16),
            pltpu.VMEM((heads, 2 * tile_j, head_lanes), bf16),
        ),
        smem=1,
        flops=3_000_000_000,
        nbytes=3_000_000,
        far=(9, 10, 11),
    )(
        place,
        *all_rows,
        *all_cols,
        content_weights_grid,
        sigmoid_weights_grid,
        final_mixing_weights.T,
    )
    if nq == 2:
        gw_other = lax.ppermute(gw_own, "seq", [(0, 1), (1, 0)])
    else:
        gw_own, gw_other = lax.psum(gw_own, "seq"), jnp.zeros_like(gw_own)

    pair_out, pair_t, logits = call(
        update_kernel,
        (
            sds((tile_i * tile_j, z), bf16),
            sds((groups, z, lanes), bf16),
            sds((groups, heads, lanes), f32),
        ),
        scratch=(
            pltpu.VMEM((tile_i * tile_j, z), bf16),
            pltpu.SemaphoreType.DMA((groups // 4,)),
            pltpu.VMEM((nk, nq * r_rows, 128), bf16),
            pltpu.VMEM((fd, nq * seqs, 4 * tile_j), bf16),
            pltpu.VMEM((groups * fc, nq * pack * seqs), bf16),
            pltpu.VMEM((2 * z, fd * fc), bf16),
            pltpu.VMEM((groups // 4, fd * fc, 4 * lanes), bf16),
            pltpu.VMEM((groups // 4, fd * fc, 4 * lanes), bf16),
            pltpu.VMEM((z, 4 * lanes), f32),
        ),
        smem=1,
        flops=14_000_000_000,
        nbytes=5_000_000,
        vmem=44 * 1024 * 1024,
        far=(3, 4, 5, 6),
        far_out=(0,),
    )(
        place,
        sides,
        far_sides,
        mask,
        outer_matrix,
        score_matrix.T,
        pair_input.reshape(tile_i * tile_j, z),
    )

    values, gating = call(
        values_kernel,
        (sds((half, nr * nk * tokens, 2 * chans), bf16), sds((seqs * tokens, chans), f32)),
        flops=4_000_000_000,
        nbytes=6_000_000,
    )(*every, content_weights_grid, normed, sigmoid_weights_grid)

    payload = sds((2 + groups // nk * (pack // 2), heads, 2 * tile_j), f32)
    gw, pay0, pay1, pay2, pay3 = call(
        softmax_kernel,
        (sds((groups, heads, lanes), f32), payload, payload, payload, payload),
        smem=1,
    )(col_scalar, logits, gw_own, gw_other, mask)

    got = [
        lax.ppermute(pay, "col", [(c, (c + shift) % nk) for c in range(nk)])
        for shift, pay in ((1, pay1), (2, pay2), (3, pay3))
    ]

    got, values, gating = lax.optimization_barrier((got, values, gating))

    (gradient,) = call(
        gradient_kernel,
        (sds((tile_i * tile_j, z), bf16),),
        scratch=(
            pltpu.VMEM((groups * heads, groups * heads), f32),
            pltpu.VMEM((tile_i * tile_j, z), bf16),
            pltpu.SemaphoreType.DMA((groups // 4,)),
        ),
        far_out=(0,),
        flops=4_000_000_000,
        nbytes=3_000_000,
    )(pay0, *got, logits, gw, pair_t, score_matrix.T)

    (aligned,) = call(
        alignment_kernel,
        (sds((seqs * tokens, width), bf16),),
        scratch=(
            pltpu.VMEM((nk, heads, tokens, 2 * tile_j), f32),
            pltpu.VMEM((seqs * tokens, chans), bf16),
        ),
        smem=1,
        flops=3_000_000_000,
        nbytes=5_000_000,
    )(
        place,
        pay0,
        *got,
        values,
        gating,
        alignment_input.reshape(seqs * tokens, width),
        final_mixing_weights.T,
    )
    return (
        aligned.reshape(seqs, tokens, width),
        pair_out.reshape(tile_i, tile_j, z),
        gradient.reshape(tile_i, tile_j, z),
    )


def solution(mesh):
    counts = (mesh.shape["seq"], mesh.shape["row"], mesh.shape["col"])
    in_specs = (
        P("seq", ("row", "col"), None),
        P("row", "col", None),
        P(),
        P(),
        P(),
        P(),
        P(),
        P(),
        P(),
        P(),
        P("seq", ("row", "col"), None),
    )
    out_specs = (P("seq", ("row", "col"), None), P("row", "col", None), P("row", "col", None))
    return jax.shard_map(
        functools.partial(on_device, counts),
        mesh=mesh,
        in_specs=in_specs,
        out_specs=out_specs,
        check_vma=False,
    )
```

```python
import functools

import jax
import jax.numpy as jnp
from jax import lax
from jax.experimental import pallas as pl
from jax.experimental.pallas import tpu as pltpu
from jax.sharding import PartitionSpec as P

epsilon = 1e-05
far_below = -1e30
vmem_bytes = 32 * 1024 * 1024
pack = 4

f32 = jnp.float32
bf16 = jnp.bfloat16


def nt_dot(a, b):
    return lax.dot_general(a, b, (((1,), (1,)), ((), ())), preferred_element_type=f32)


def nn_dot(a, b):
    return jnp.dot(a, b, preferred_element_type=f32)


def high_low(x):
    high = x.astype(bf16)
    return high, (x - high.astype(f32)).astype(bf16)


def call(
    kernel, out_shape, scratch=(), smem=0, flops=0, nbytes=0, vmem=vmem_bytes, far=(), far_out=()
):
    def run(*args):
        count = len(args)
        in_specs = [
            pl.BlockSpec(memory_space=pltpu.SMEM if n < smem else pltpu.VMEM) for n in range(count)
        ]
        for n in far:
            in_specs[n] = pl.BlockSpec(memory_space=pltpu.HBM)
        landing = [pltpu.VMEM(args[n].shape, args[n].dtype) for n in far]
        if far:
            landing.append(pltpu.SemaphoreType.DMA((len(far),)))

        def body(*refs):
            inputs = list(refs[:count])
            extra = refs[len(refs) - len(landing) :]
            rest = refs[count : len(refs) - len(landing)]
            copies = []
            for i, n in enumerate(far):
                copies.append(pltpu.make_async_copy(inputs[n], extra[i], extra[-1].at[i]))
                copies[-1].start()
                inputs[n] = extra[i]

            def ready():
                for copy in copies:
                    copy.wait()

            kernel(ready, *inputs, *rest)

        return pl.pallas_call(
            body,
            out_shape=out_shape,
            in_specs=in_specs,
            out_specs=[
                pl.BlockSpec(memory_space=pltpu.HBM if n in far_out else pltpu.VMEM)
                for n in range(len(out_shape))
            ],
            scratch_shapes=list(scratch) + landing,
            compiler_params=pltpu.CompilerParams(vmem_limit_bytes=vmem),
            cost_estimate=pl.CostEstimate(flops=flops, bytes_accessed=nbytes, transcendentals=0),
        )(*args)

    return run


def valid_count(mask_ref):
    return jnp.sum(mask_ref[...].astype(f32), axis=1, keepdims=True)


def column_mask(mask_ref, col, tile, copies):
    lane = lax.broadcasted_iota(jnp.int32, (1, copies * tile), 1)
    token = (lax.rem(lane, tile) + col * tile).astype(f32)
    return (token < valid_count(mask_ref)).astype(f32)


def twice(w):
    none = jnp.zeros_like(w)
    return jnp.concatenate(
        [jnp.concatenate([w, none], axis=1), jnp.concatenate([none, w], axis=1)], axis=0
    )


def prepare_kernel(
    ready,
    own_ref,
    x_ref,
    adj_ref,
    w1_ref,
    w2_ref,
    mask_ref,
    wv_ref,
    wg_ref,
    wf_ref,
    rows_ref,
    cols_ref,
    norm_ref,
    weights_ref,
    turn_ref,
    place_ref,
):
    chans = wv_ref.shape[1]
    weights_ref[:, :chans] = wv_ref[...]
    weights_ref[:, chans : 2 * chans] = wg_ref[...]
    weights_ref[:, 2 * chans :] = wf_ref[...]
    seqs, tokens, width = x_ref.shape
    half = seqs // 2
    fd = w2_ref.shape[0]
    x = x_ref[...].astype(f32)
    center = x - jnp.mean(x, axis=-1, keepdims=True)
    inverse = lax.rsqrt(jnp.mean(center * center, axis=-1, keepdims=True) + epsilon)
    normed = center * inverse
    rows = half * tokens
    adj = adj_ref[...].astype(f32)

    def two(x):
        x = jnp.concatenate([x[:half], x[half:]], axis=-1)
        return x.reshape(rows, 2 * width).astype(bf16)

    packed = two(normed)
    norm_ref[...] = packed
    rows_ref[-2 * rows : -rows, :] = packed
    rows_ref[-rows:, :] = two(adj)
    cols_ref[-rows:, :] = packed
    token = lax.broadcasted_iota(jnp.int32, (seqs, tokens, width), 1) + own_ref[0]
    count = valid_count(mask_ref).reshape(1, 1, 1)
    real = jnp.where(token.astype(f32) < count, normed, 0.0)
    for s in range(seqs):
        turn_ref[:, s, :] = real[s]
    turned = turn_ref[...].astype(bf16).reshape(tokens * seqs, width)
    left = nt_dot(w1_ref[...], turned).astype(bf16)
    fc = w1_ref.shape[0]
    wk = pack * seqs
    for g in range(tokens // pack):
        rows_ref[g * fc : (g + 1) * fc, :] = left[:, g * wk : (g + 1) * wk]
    size = 128 // tokens
    real = real.astype(bf16)
    w2 = w2_ref[...]
    d = lax.broadcasted_iota(jnp.int32, (fd, 128), 0)
    lane = lax.broadcasted_iota(jnp.int32, (fd, 128), 1)
    mine = lax.rem(d, size) == lane // tokens
    for s in range(seqs):
        res = nt_dot(w2, jnp.concatenate([real[s]] * size, axis=0))
        res = jnp.where(mine, res, 0.0).reshape(fd // size, size, 128)
        place_ref[:, s, :] = jnp.sum(res, axis=1)
    cols_ref[:-rows, :] = place_ref[...].reshape(fd // size * seqs, 128).astype(bf16)


def join_kernel(
    ready,
    row_ref,
    col_ref,
    rows0_ref,
    rows1_ref,
    rows2_ref,
    rows3_ref,
    cols0_ref,
    cols1_ref,
    cols2_ref,
    cols3_ref,
    out_ref,
    norm_ref,
):
    nk = 4
    row, col = row_ref[0], col_ref[0]
    r_rows = l_rows = out_ref.shape[0] // (2 * nk)
    for t, ref in enumerate((cols0_ref, cols1_ref, cols2_ref, cols3_ref)):
        at = pl.ds(pl.multiple_of(lax.rem(row + nk - t, nk) * r_rows, r_rows), r_rows)
        out_ref[at, :] = ref[:r_rows, :]
    for t, ref in enumerate((rows0_ref, rows1_ref, rows2_ref, rows3_ref)):
        start = nk * r_rows + jnp.bitwise_xor(col, t) * l_rows
        at = pl.ds(pl.multiple_of(start, l_rows), l_rows)
        out_ref[at, :] = ref[:l_rows, :]
        half, tokens, _ = norm_ref.shape[1:]
        count = half * tokens
        start = ref.shape[0] - 2 * count
        norm_ref[jnp.bitwise_xor(col, t)] = ref[start : start + count, :].reshape(norm_ref.shape[1:])


def update_kernel(
    ready,
    col_ref,
    seq_ref,
    sides_ref,
    far_sides_ref,
    mask_ref,
    m_ref,
    score_ref,
    pair_ref,
    pout_hbm,
    pout_t_ref,
    logits_ref,
    pout_ref,
    out_sem,
    rk_ref,
    rab_ref,
    lm_ref,
    mt_ref,
    oh_ref,
    ol_ref,
    update_ref,
):
    nk = rk_ref.shape[0]
    width_d, pair_rows, _ = rab_ref.shape
    col, seq = col_ref[0], seq_ref[0]
    z = pair_ref.shape[1]
    groups, heads, lanes = logits_ref.shape
    tile_j = lanes // pack
    tokens = tile_j // nk
    fc = lm_ref.shape[0] // groups
    seqs = 128 // pack
    nq = pair_rows // seqs
    wk = pack * seqs

    r_rows = rk_ref.shape[1] // nq
    l_rows = groups * fc
    if nq == 2:
        sources = ((seq, 0, sides_ref), (1 - seq, 0, far_sides_ref))
    else:
        sources = tuple((q, q, far_sides_ref) for q in range(nq))
    for q, slot, ref in sources:
        base = slot * (nk * r_rows + l_rows)
        at = pl.ds(pl.multiple_of(q * r_rows, r_rows), r_rows)
        for k in range(nk):
            rk_ref[k, at, :] = ref[base + k * r_rows : base + (k + 1) * r_rows, :]
        base = base + nk * r_rows
        to = pl.ds(pl.multiple_of(q * wk, wk), wk)
        lm_ref[:, to] = ref[base : base + l_rows, :]
    size = 128 // tokens
    right = jnp.concatenate([rk_ref[k] for k in range(nk)], axis=1)
    source = lax.broadcasted_iota(jnp.int32, (nk * 128, 4 * tile_j), 0)
    target = lax.broadcasted_iota(jnp.int32, (nk * 128, 4 * tile_j), 1)
    used = jnp.logical_or(target < tile_j, target >= 3 * tile_j)
    j = lax.rem(target, tile_j)
    offset = jnp.where(used, source - (j // tokens * 128 + lax.rem(j, tokens)), -1)
    blocks = width_d // size
    for e in range(size):
        pick = jnp.where(offset == e * tokens, 1.0, 0.0).astype(bf16)
        res = nn_dot(right, pick).astype(bf16)
        for q in range(nq):
            for n in range(blocks):
                at = (q * blocks + n) * seqs
                rab_ref[n * size + e, q * seqs : (q + 1) * seqs, :] = res[at : at + seqs]

    chunk = 8
    many = 4
    wide = oh_ref.shape[2] // lanes
    empty = jnp.zeros((seqs, 2 * tile_j), bf16)

    def block_of(d):
        rows = []
        for q in range(nq):
            both = rab_ref[d, q * seqs : (q + 1) * seqs, :]
            part = both[:, : 2 * tile_j], both[:, 2 * tile_j :]
            for i in range(pack):
                pieces = [empty] * (pack // 2)
                pieces[i // 2] = part[i % 2]
                rows.append(jnp.concatenate(pieces, axis=1))
        return jnp.concatenate(rows, axis=0)

    def outer_of(n, carry):
        block = jnp.concatenate([block_of(many * n + e) for e in range(many)], axis=1)
        for m in range(groups // chunk):
            out = nn_dot(lm_ref[m * chunk * fc : (m + 1) * chunk * fc, :], block)
            high, low = high_low(out)
            for e in range(many):
                at = pl.ds(pl.multiple_of((many * n + e) * fc, fc), fc)
                for g in range(chunk):
                    group = m * chunk + g
                    to = slice(group % wide * lanes, (group % wide + 1) * lanes)
                    cut = slice(g * fc, (g + 1) * fc), slice(e * lanes, (e + 1) * lanes)
                    oh_ref[group // wide, at, to] = high[cut]
                    ol_ref[group // wide, at, to] = low[cut]
        return carry

    lax.fori_loop(0, width_d // many, outer_of, 0)

    ready()
    some = z // fc
    for n in range(width_d // some):
        block = jnp.concatenate(
            [m_ref[pl.ds(n * some + e, fc, stride=width_d), :] for e in range(some)], axis=0
        ).T
        high, low = high_low(block)
        mt_ref[:z, n * z : (n + 1) * z] = high
        mt_ref[z:, n * z : (n + 1) * z] = low
    maskj = column_mask(mask_ref, col, tile_j, 2)

    maskl = jnp.concatenate([maskj] * (pack // 2), axis=1) > 0
    score = score_ref[...]
    s1 = score.astype(bf16).astype(f32)
    s2 = (score - s1).astype(bf16).astype(f32)
    s3 = score - s1 - s2
    none = jnp.zeros_like(s1)
    st = jnp.concatenate(
        [
            jnp.concatenate([s1, s2, s3, none], axis=0),
            jnp.concatenate([s1, s2, none, none], axis=0),
        ],
        axis=1,
    ).astype(bf16)

    def finish(n, carry):
        two = nn_dot(mt_ref[...], oh_ref[n])
        update_ref[...] = two[:z] + two[z:] + nn_dot(mt_ref[:z, :], ol_ref[n])
        for e in range(wide):
            g = n * wide + e
            at = pl.ds(pl.multiple_of(g * lanes, lanes), lanes)
            before = pair_ref[at, :].T.astype(f32)
            result = (before + update_ref[:, e * lanes : (e + 1) * lanes]).astype(bf16)
            pout_t_ref[g] = result
            x = result.astype(f32)
            pout_ref[at, :] = result.T
            center = x - jnp.mean(x, axis=0, keepdims=True)
            inverse = lax.rsqrt(jnp.mean(center * center, axis=0, keepdims=True) + epsilon)
            high, low = high_low(center * inverse)
            scores = nn_dot(st, jnp.concatenate([high, low], axis=0))
            logits = scores[:heads] + scores[heads : 2 * heads] + scores[2 * heads : 3 * heads]
            logits_ref[g] = jnp.where(maskl, logits, far_below)
        at = pl.ds(pl.multiple_of(n * wide * lanes, wide * lanes), wide * lanes)
        pltpu.make_async_copy(pout_ref.at[at], pout_hbm.at[at], out_sem.at[n]).start()
        return carry

    lax.fori_loop(0, groups // wide, finish, 0)
    for n in range(groups // wide):
        at = pl.ds(n * wide * lanes, wide * lanes)
        pltpu.make_async_copy(pout_ref.at[at], pout_hbm.at[at], out_sem.at[n]).wait()


def by_heads(w, heads, out_ref):
    width, chans = w.shape
    hw = chans // heads
    block = 4 * hw
    slot = lax.broadcasted_iota(jnp.int32, (width, block), 1) // hw
    w = w.astype(f32)
    for t in range(chans // block):
        part = w[:, t * block : (t + 1) * block]
        turns = [part] + [pltpu.roll(part, n * hw, 1) for n in range(1, 4)]
        for e in range(4):
            h = t * 4 + e
            for s in range(4):
                out_ref[s * width : (s + 1) * width, h * block : (h + 1) * block] = jnp.where(
                    slot == s, turns[(s - e) % 4], 0.0
                ).astype(bf16)


def weights_kernel(
    ready,
    row_ref,
    col_ref,
    side0_ref,
    side1_ref,
    side2_ref,
    side3_ref,
    cols0_ref,
    cols1_ref,
    cols2_ref,
    cols3_ref,
    weights_ref,
    gw_ref,
    acc_ref,
    bv_ref,
    bg_ref,
    bf_ref,
    rows_ref,
    cols_ref,
    gs_ref,
    vs_ref,
):
    nk, half, tokens, _ = cols_ref.shape
    tile = nk * tokens
    groups, heads, lanes = gw_ref.shape
    row, col = row_ref[0], col_ref[0]
    count = half * tokens
    for t, ref in enumerate((side0_ref, side1_ref, side2_ref, side3_ref)):
        start = ref.shape[0] - 2 * count
        rows_ref[jnp.bitwise_xor(col, t)] = ref[start:, :].reshape(rows_ref.shape[1:])
    for t, ref in enumerate((cols0_ref, cols1_ref, cols2_ref, cols3_ref)):
        start = ref.shape[0] - count
        cols_ref[lax.rem(row + nk - t, nk)] = ref[start:, :].reshape(cols_ref.shape[1:])
    chans = weights_ref.shape[1] // 3
    by_heads(weights_ref[:, :chans], heads, bv_ref)
    by_heads(weights_ref[:, chans : 2 * chans], heads, bg_ref)
    by_heads(weights_ref[:, 2 * chans :], heads, bf_ref)
    block = bv_ref.shape[1] // heads

    def four(read, n):
        return jnp.concatenate(
            [
                jnp.concatenate(
                    [
                        jnp.concatenate([read(k, 2 * (2 * n + e) + p) for k in range(nk)], axis=0)
                        for p in range(2)
                    ],
                    axis=1,
                )
                for e in range(2)
            ],
            axis=0,
        )

    for hp in range(heads // 2):
        cut = slice(hp * 2 * block, (hp + 1) * 2 * block)
        for n in range(half // 4):
            v = nn_dot(four(lambda k, s: cols_ref[k, s], n), bv_ref[:, cut]).astype(bf16)
            gate = nn_dot(four(lambda k, s: rows_ref[k, 0, s], n), bg_ref[:, cut])
            grad = nn_dot(four(lambda k, s: rows_ref[k, 1, s], n), bf_ref[:, cut])
            g = (grad * jax.nn.sigmoid(gate)).astype(bf16)
            for e in range(2):
                to = slice((2 * n + e) * block, (2 * n + e + 1) * block)
                for o in range(2):
                    mine = slice(o * block, (o + 1) * block)
                    ve = v[e * tile : (e + 1) * tile, mine]
                    vs_ref[2 * hp + o, :tile, to] = ve
                    vs_ref[2 * hp + o, tile:, to] = ve
                    gs_ref[2 * hp + o, :, to] = g[e * tile : (e + 1) * tile, mine]
    for h in range(heads):
        acc_ref[h * tile : (h + 1) * tile, :] = nt_dot(gs_ref[h], vs_ref[h])

    first = lax.broadcasted_iota(jnp.int32, (groups, 2 * tile), 1) < tile
    for h in range(heads):
        for part in range(pack // 2):
            a = acc_ref[pl.ds(h * tile + 2 * part, groups, stride=pack), :]
            b = acc_ref[pl.ds(h * tile + 2 * part + 1, groups, stride=pack), :]
            gw_ref[:, h, part * 2 * tile : (part + 1) * 2 * tile] = jnp.where(first, a, b)


def softmax_kernel(
    ready,
    col_ref,
    logits_ref,
    gwa_ref,
    gwb_ref,
    mask_ref,
    gw_ref,
    own_ref,
    pay1_ref,
    pay2_ref,
    pay3_ref,
):
    groups, heads, lanes = logits_ref.shape
    tile = lanes // pack
    nk = 4
    rows = groups * heads
    col = col_ref[0]
    gw_ref[...] = gwa_ref[...] + gwb_ref[...]
    lane = lax.broadcasted_iota(jnp.int32, (rows, 2 * tile), 1)
    low = lane < tile
    maskj = column_mask(mask_ref, col, tile, 2)
    stats = jnp.zeros((rows, 2 * tile), f32)
    for part in range(pack // 2):
        cut = slice(part * 2 * tile, (part + 1) * 2 * tile)
        lg = logits_ref[:, :, cut].reshape(rows, 2 * tile)
        gw = gw_ref[:, :, cut].reshape(rows, 2 * tile)
        m0 = jnp.max(jnp.where(low, lg, far_below), axis=1, keepdims=True)
        m1 = jnp.max(jnp.where(low, far_below, lg), axis=1, keepdims=True)
        p = jnp.exp(lg - jnp.where(low, m0, m1)) * maskj
        pg = p * gw
        for e, m in ((0, m0), (1, m1)):
            mine = low if e == 0 else jnp.logical_not(low)
            i = 2 * part + e
            total = jnp.sum(jnp.where(mine, p, 0.0), axis=1, keepdims=True)
            inner = jnp.sum(jnp.where(mine, pg, 0.0), axis=1, keepdims=True)
            stats = jnp.where(lane == i, m, stats)
            stats = jnp.where(lane == pack + i, total, stats)
            stats = jnp.where(lane == 2 * pack + i, inner, stats)
    turned = stats.T[:16]
    per = groups // nk
    for shift, pay in enumerate((own_ref, pay1_ref, pay2_ref, pay3_ref)):
        dest = lax.rem(col + shift, nk)
        pay[0] = turned[:8]
        pay[1] = turned[8:]
        for g in range(per):
            piece = logits_ref[dest * per + g]
            for part in range(pack // 2):
                pay[2 + g * (pack // 2) + part] = piece[:, part * 2 * tile : (part + 1) * 2 * tile]


def values_kernel(
    ready, ev0_ref, ev1_ref, ev2_ref, ev3_ref, wv_ref, norm_ref, wg_ref, v_ref, gate_ref
):
    evs = (ev0_ref, ev1_ref, ev2_ref, ev3_ref)
    nk, half, tokens, wide = ev0_ref.shape
    chans = wv_ref.shape[1]
    gate = jax.nn.sigmoid(nn_dot(norm_ref[...], twice(wg_ref[...])))
    gate_ref[: half * tokens] = gate[:, :chans]
    gate_ref[half * tokens :] = gate[:, chans:]
    wv = twice(wv_ref[...])
    for s in range(half):
        x = jnp.concatenate([ev[k, s] for ev in evs for k in range(nk)], axis=0)
        v_ref[s] = nn_dot(x, wv).astype(bf16)


def gradient_kernel(
    ready,
    own_ref, r1_ref, r2_ref, r3_ref, logits_ref, gw_ref, pout_t_ref, score_ref, out_hbm, stat_ref, out_ref, out_sem
):
    groups, heads, lanes = logits_ref.shape
    rows = groups * heads
    score = score_ref[...]
    z = score.shape[1]
    s1 = score.astype(bf16).astype(f32)
    s2 = (score - s1).astype(bf16).astype(f32)
    s3 = score - s1 - s2
    parts = [s1, s1, s1, s2, s2, s3, jnp.zeros((z - 6 * heads, z), f32)]
    sk = jnp.concatenate(parts, axis=0).T[:, : 6 * heads].astype(bf16)
    pays = (own_ref, r1_ref, r2_ref, r3_ref)
    ms = [p[0][:pack] for p in pays]
    ls = [p[0][pack : 2 * pack] for p in pays]
    ns = [p[1][:pack] for p in pays]
    top = functools.reduce(jnp.maximum, ms)
    scales = [jnp.exp(m - top) for m in ms]
    total = sum(a * b for a, b in zip(ls, scales))
    inner = sum(a * b for a, b in zip(ns, scales)) / total
    stacked = jnp.concatenate([top, total, inner, jnp.zeros((rows - 3 * pack, rows), f32)], axis=0)
    stat_ref[...] = stacked.T

    tile = lanes // pack
    low = lax.broadcasted_iota(jnp.int32, (heads, 2 * tile), 1) < tile

    def one(g):
        st = stat_ref[pl.ds(pl.multiple_of(g * heads, heads), heads), :]

        def spread(base):
            halves = [
                jnp.where(
                    low,
                    st[:, base + 2 * half : base + 2 * half + 1],
                    st[:, base + 2 * half + 1 : base + 2 * half + 2],
                )
                for half in range(pack // 2)
            ]
            return jnp.concatenate(halves, axis=1)

        prob = jnp.exp(logits_ref[g] - spread(0)) / spread(pack)
        gl = prob * (gw_ref[g] - spread(2 * pack))
        g1 = gl.astype(bf16).astype(f32)
        g2 = (gl - g1).astype(bf16).astype(f32)
        g3 = gl - g1 - g2
        stack = jnp.concatenate([g1, g2, g3, g1, g2, g1], axis=0).astype(bf16)
        grad = nn_dot(sk, stack)
        x = pout_t_ref[g].astype(f32)
        center = x - jnp.mean(x, axis=0, keepdims=True)
        inverse = lax.rsqrt(jnp.mean(center * center, axis=0, keepdims=True) + epsilon)
        normal = center * inverse
        centered = grad - jnp.mean(grad, axis=0, keepdims=True)
        along = jnp.mean(grad * normal, axis=0, keepdims=True)
        result = inverse * (centered - normal * along)
        out_ref[pl.ds(pl.multiple_of(g * lanes, lanes), lanes), :] = result.astype(bf16).T

    many = 4

    def some(n, carry):
        for e in range(many):
            one(n * many + e)
        at = pl.ds(pl.multiple_of(n * many * lanes, many * lanes), many * lanes)
        pltpu.make_async_copy(out_ref.at[at], out_hbm.at[at], out_sem.at[n]).start()
        return carry

    lax.fori_loop(0, groups // many, some, 0)
    for n in range(groups // many):
        at = pl.ds(n * many * lanes, many * lanes)
        pltpu.make_async_copy(out_ref.at[at], out_hbm.at[at], out_sem.at[n]).wait()


def alignment_kernel(
    ready,
    row_ref,
    col_ref,
    own_ref,
    r1_ref,
    r2_ref,
    r3_ref,
    v_ref,
    gate_ref,
    x_ref,
    wf_ref,
    out_ref,
    w_ref,
    gated_ref,
):
    pays = (own_ref, r1_ref, r2_ref, r3_ref)
    nk = len(pays)
    heads = own_ref.shape[1]
    wide = own_ref.shape[2]
    tile = wide // 2
    pieces = own_ref.shape[0] - 2
    rows = pieces * heads
    half, all_tokens, chans = v_ref.shape
    chans = chans // 2
    tokens = pieces * 2
    head_width = chans // heads
    row, col = row_ref[0], col_ref[0]

    low = lax.broadcasted_iota(jnp.int32, (rows, wide), 1) < tile
    lgs = [p[2:].reshape(rows, wide) for p in pays]
    peak = functools.reduce(jnp.maximum, lgs)
    m0 = jnp.max(jnp.where(low, peak, far_below), axis=1, keepdims=True)
    m1 = jnp.max(jnp.where(low, far_below, peak), axis=1, keepdims=True)
    top = jnp.where(low, m0, m1)
    ps = [jnp.exp(lg - top) for lg in lgs]
    every = sum(ps)
    t0 = jnp.sum(jnp.where(low, every, 0.0), axis=1, keepdims=True)
    t1 = jnp.sum(jnp.where(low, 0.0, every), axis=1, keepdims=True)
    total = jnp.where(low, t0, t1)
    for shift, p in enumerate(ps):
        source = lax.rem(col + nk - shift, nk)
        weight = p / total
        rolled = pltpu.roll(weight, tile, 1)
        for n in range(pieces):
            w_ref[source, :, 2 * n, :] = weight[n * heads : (n + 1) * heads]
            w_ref[source, :, 2 * n + 1, :] = rolled[n * heads : (n + 1) * heads]
    w = jnp.concatenate(
        [
            w_ref[jnp.bitwise_xor(row, t)].reshape(heads * tokens, wide)[:, :tile]
            for t in range(nk)
        ],
        axis=1,
    ).astype(bf16)

    owner = lax.broadcasted_iota(jnp.int32, (tokens, chans), 1) // head_width

    def one(s, carry):
        full = nn_dot(w, v_ref[s])
        for e in range(2):
            cut = slice(e * chans, (e + 1) * chans)
            mean = jnp.zeros((tokens, chans), f32)
            for h in range(heads):
                mean = jnp.where(owner == h, full[h * tokens : (h + 1) * tokens, cut], mean)
            at = pl.ds(pl.multiple_of((e * half + s) * tokens, tokens), tokens)
            gated_ref[at, :] = (gate_ref[at, :] * mean).astype(bf16)
        return carry

    lax.fori_loop(0, half, one, 0, unroll=4)
    out_ref[...] = (x_ref[...].astype(f32) + nt_dot(gated_ref[...], wf_ref[...])).astype(bf16)


def on_device(
    counts,
    alignment_input,
    pair_input,
    token_valid_mask,
    first_factor_weights,
    second_factor_weights,
    content_weights_grid,
    sigmoid_weights_grid,
    outer_matrix,
    score_matrix,
    final_mixing_weights,
    adjoint_of_rowset,
):
    nq, nr, nk = counts
    row_index = lax.axis_index("row")
    col_index = lax.axis_index("col")
    seqs, tokens, width = alignment_input.shape
    tile_i, tile_j, z = pair_input.shape
    fc = first_factor_weights.shape[1]
    fd = second_factor_weights.shape[1]
    heads = score_matrix.shape[1]
    chans = content_weights_grid.shape[1]
    groups = tile_i // pack
    lanes = pack * tile_j
    sds = jax.ShapeDtypeStruct

    mask = token_valid_mask.reshape(1, -1)
    own_start = ((row_index * nk + col_index) * tokens).astype(jnp.int32).reshape(1)
    seq_index = lax.axis_index("seq")
    place = tuple(x.astype(jnp.int32).reshape(1) for x in (row_index, col_index, seq_index))
    col_scalar = col_index.astype(jnp.int32).reshape(1)
    half = seqs // 2

    l_rows = tokens // pack * fc
    r_rows = fd * tokens // 128 * seqs
    n_rows = half * tokens
    rows, cols, normed, weights = call(
        prepare_kernel,
        (
            sds((l_rows + 2 * n_rows, 128), bf16),
            sds((r_rows + n_rows, 128), bf16),
            sds((n_rows, 128), bf16),
            sds((width, 3 * chans), bf16),
        ),
        scratch=(
            pltpu.VMEM((tokens, seqs, width), f32),
            pltpu.VMEM((fd * tokens // 128, seqs, 128), f32),
        ),
        smem=1,
        vmem=60 * 1024 * 1024,
    )(
        own_start,
        alignment_input,
        adjoint_of_rowset,
        first_factor_weights.T,
        second_factor_weights.T,
        mask,
        content_weights_grid,
        sigmoid_weights_grid,
        final_mixing_weights.T,
    )

    all_cols = [
        lax.ppermute(
            cols,
            ("row", "col"),
            [(r * nk + c, (c + t) % nr * nk + r) for r in range(nr) for c in range(nk)],
        )
        for t in range(nr)
    ]

    def exchange(x, bit):
        return lax.ppermute(x, "col", [(c, c ^ bit) for c in range(nk)])

    across = exchange(rows, 2)
    all_rows = [rows, exchange(rows, 1), across, exchange(across, 1)]

    sides, block = call(
        join_kernel,
        (
            sds((nk * (r_rows + l_rows), 128), bf16),
            sds((nk, half, tokens, 2 * width), bf16),
        ),
        smem=2,
    )(*place[:2], *all_rows, *all_cols)
    if nq == 2:
        far_sides = lax.ppermute(sides, "seq", [(0, 1), (1, 0)])
    else:
        far_sides = lax.all_gather(sides, "seq", axis=0, tiled=True)

    head_lanes = seqs * chans // heads
    (gw_own,) = call(
        weights_kernel,
        (sds((groups, heads, lanes), f32),),
        scratch=(
            pltpu.VMEM((heads * tile_i, 2 * tile_j), f32),
            pltpu.VMEM((4 * width, 4 * chans), bf16),
            pltpu.VMEM((4 * width, 4 * chans), bf16),
            pltpu.VMEM((4 * width, 4 * chans), bf16),
            pltpu.VMEM((nk, 2, half, tokens, 2 * width), bf16),
            pltpu.VMEM((nk, half, tokens, 2 * width), bf16),
            pltpu.VMEM((heads, tile_i, head_lanes), bf16),
            pltpu.VMEM((heads, 2 * tile_j, head_lanes), bf16),
        ),
        smem=2,
        flops=3_000_000_000,
        nbytes=3_000_000,
    )(*place[:2], *all_rows, *all_cols, weights)
    if nq == 2:
        gw_other = lax.ppermute(gw_own, "seq", [(0, 1), (1, 0)])
    else:
        gw_own, gw_other = lax.psum(gw_own, "seq"), jnp.zeros_like(gw_own)

    def exchange_rows(x, bit):
        return lax.ppermute(x, "row", [(r, r ^ bit) for r in range(nr)])

    block, gw_own = lax.optimization_barrier((block, gw_own))
    near, beyond = exchange_rows(block, 1), exchange_rows(block, 2)

    pair_out, pair_t, logits = call(
        update_kernel,
        (
            sds((tile_i * tile_j, z), bf16),
            sds((groups, z, lanes), bf16),
            sds((groups, heads, lanes), f32),
        ),
        scratch=(
            pltpu.VMEM((tile_i * tile_j, z), bf16),
            pltpu.SemaphoreType.DMA((groups // 4,)),
            pltpu.VMEM((nk, nq * r_rows, 128), bf16),
            pltpu.VMEM((fd, nq * seqs, 4 * tile_j), bf16),
            pltpu.VMEM((groups * fc, nq * pack * seqs), bf16),
            pltpu.VMEM((2 * z, fd * fc), bf16),
            pltpu.VMEM((groups // 4, fd * fc, 4 * lanes), bf16),
            pltpu.VMEM((groups // 4, fd * fc, 4 * lanes), bf16),
            pltpu.VMEM((z, 4 * lanes), f32),
        ),
        smem=2,
        flops=14_000_000_000,
        nbytes=5_000_000,
        vmem=44 * 1024 * 1024,
        far=(4, 5, 6, 7),
        far_out=(0,),
    )(
        *place[1:],
        sides,
        far_sides,
        mask,
        outer_matrix,
        score_matrix.T,
        pair_input.reshape(tile_i * tile_j, z),
    )

    beyond, logits = lax.optimization_barrier((beyond, logits))
    every = [block, near, beyond, exchange_rows(beyond, 1)]
    values, gating = call(
        values_kernel,
        (sds((half, nr * nk * tokens, 2 * chans), bf16), sds((seqs * tokens, chans), f32)),
        flops=4_000_000_000,
        nbytes=6_000_000,
    )(*every, content_weights_grid, normed, sigmoid_weights_grid)

    payload = sds((2 + groups // nk * (pack // 2), heads, 2 * tile_j), f32)
    gw, pay0, pay1, pay2, pay3 = call(
        softmax_kernel,
        (sds((groups, heads, lanes), f32), payload, payload, payload, payload),
        smem=1,
    )(col_scalar, logits, gw_own, gw_other, mask)

    got = [
        lax.ppermute(pay, "col", [(c, (c + shift) % nk) for c in range(nk)])
        for shift, pay in ((1, pay1), (2, pay2), (3, pay3))
    ]

    got, values, gating = lax.optimization_barrier((got, values, gating))

    (gradient,) = call(
        gradient_kernel,
        (sds((tile_i * tile_j, z), bf16),),
        scratch=(
            pltpu.VMEM((groups * heads, groups * heads), f32),
            pltpu.VMEM((tile_i * tile_j, z), bf16),
            pltpu.SemaphoreType.DMA((groups // 4,)),
        ),
        far_out=(0,),
        flops=4_000_000_000,
        nbytes=3_000_000,
    )(pay0, *got, logits, gw, pair_t, score_matrix.T)

    (aligned,) = call(
        alignment_kernel,
        (sds((seqs * tokens, width), bf16),),
        scratch=(
            pltpu.VMEM((nk, heads, tokens, 2 * tile_j), f32),
            pltpu.VMEM((seqs * tokens, chans), bf16),
        ),
        smem=2,
        flops=3_000_000_000,
        nbytes=5_000_000,
    )(
        *place[:2],
        pay0,
        *got,
        values,
        gating,
        alignment_input.reshape(seqs * tokens, width),
        final_mixing_weights.T,
    )
    return (
        aligned.reshape(seqs, tokens, width),
        pair_out.reshape(tile_i, tile_j, z),
        gradient.reshape(tile_i, tile_j, z),
    )


def solution(mesh):
    counts = (mesh.shape["seq"], mesh.shape["row"], mesh.shape["col"])
    in_specs = (
        P("seq", ("row", "col"), None),
        P("row", "col", None),
        P(),
        P(),
        P(),
        P(),
        P(),
        P(),
        P(),
        P(),
        P("seq", ("row", "col"), None),
    )
    out_specs = (P("seq", ("row", "col"), None), P("row", "col", None), P("row", "col", None))
    return jax.shard_map(
        functools.partial(on_device, counts),
        mesh=mesh,
        in_specs=in_specs,
        out_specs=out_specs,
        check_vma=False,
    )
```

```python
import functools

import jax
import jax.numpy as jnp
from jax import lax
from jax.experimental import pallas as pl
from jax.experimental.pallas import tpu as pltpu
from jax.sharding import PartitionSpec as P

epsilon = 1e-05
far_below = -1e30
vmem_bytes = 32 * 1024 * 1024
pack = 4

f32 = jnp.float32
bf16 = jnp.bfloat16


def nt_dot(a, b):
    return lax.dot_general(a, b, (((1,), (1,)), ((), ())), preferred_element_type=f32)


def nn_dot(a, b):
    return jnp.dot(a, b, preferred_element_type=f32)


def high_low(x):
    high = x.astype(bf16)
    return high, (x - high.astype(f32)).astype(bf16)


def call(
    kernel, out_shape, scratch=(), smem=0, flops=0, nbytes=0, vmem=vmem_bytes, far=(), far_out=()
):
    def run(*args):
        count = len(args)
        in_specs = [
            pl.BlockSpec(memory_space=pltpu.SMEM if n < smem else pltpu.VMEM) for n in range(count)
        ]
        for n in far:
            in_specs[n] = pl.BlockSpec(memory_space=pltpu.HBM)
        landing = [pltpu.VMEM(args[n].shape, args[n].dtype) for n in far]
        if far:
            landing.append(pltpu.SemaphoreType.DMA((len(far),)))

        def body(*refs):
            inputs = list(refs[:count])
            extra = refs[len(refs) - len(landing) :]
            rest = refs[count : len(refs) - len(landing)]
            copies = []
            for i, n in enumerate(far):
                copies.append(pltpu.make_async_copy(inputs[n], extra[i], extra[-1].at[i]))
                copies[-1].start()
                inputs[n] = extra[i]

            def ready():
                for copy in copies:
                    copy.wait()

            kernel(ready, *inputs, *rest)

        return pl.pallas_call(
            body,
            out_shape=out_shape,
            in_specs=in_specs,
            out_specs=[
                pl.BlockSpec(memory_space=pltpu.HBM if n in far_out else pltpu.VMEM)
                for n in range(len(out_shape))
            ],
            scratch_shapes=list(scratch) + landing,
            compiler_params=pltpu.CompilerParams(vmem_limit_bytes=vmem),
            cost_estimate=pl.CostEstimate(flops=flops, bytes_accessed=nbytes, transcendentals=0),
        )(*args)

    return run


def valid_count(mask_ref):
    return jnp.sum(mask_ref[...].astype(f32), axis=1, keepdims=True)


def column_mask(mask_ref, col, tile, copies):
    lane = lax.broadcasted_iota(jnp.int32, (1, copies * tile), 1)
    token = (lax.rem(lane, tile) + col * tile).astype(f32)
    return (token < valid_count(mask_ref)).astype(f32)


def twice(w):
    none = jnp.zeros_like(w)
    return jnp.concatenate(
        [jnp.concatenate([w, none], axis=1), jnp.concatenate([none, w], axis=1)], axis=0
    )


def prepare_kernel(
    ready,
    own_ref,
    x_ref,
    adj_ref,
    w1_ref,
    w2_ref,
    mask_ref,
    wv_ref,
    wg_ref,
    wf_ref,
    rows_ref,
    cols_ref,
    norm_ref,
    weights_ref,
    turn_ref,
    place_ref,
):
    chans = wv_ref.shape[1]
    weights_ref[:, :chans] = wv_ref[...]
    weights_ref[:, chans : 2 * chans] = wg_ref[...]
    weights_ref[:, 2 * chans :] = wf_ref[...]
    seqs, tokens, width = x_ref.shape
    half = seqs // 2
    fd = w2_ref.shape[0]
    x = x_ref[...].astype(f32)
    center = x - jnp.mean(x, axis=-1, keepdims=True)
    inverse = lax.rsqrt(jnp.mean(center * center, axis=-1, keepdims=True) + epsilon)
    normed = center * inverse
    rows = half * tokens
    adj = adj_ref[...].astype(f32)

    def two(x):
        x = jnp.concatenate([x[:half], x[half:]], axis=-1)
        return x.reshape(rows, 2 * width).astype(bf16)

    packed = two(normed)
    norm_ref[...] = packed
    adj = two(adj)
    copies = rows_ref.shape[0]
    for n in range(copies):
        rows_ref[n, -2 * rows : -rows, :] = packed
        rows_ref[n, -rows:, :] = adj
        cols_ref[n, -rows:, :] = packed
    token = lax.broadcasted_iota(jnp.int32, (seqs, tokens, width), 1) + own_ref[0]
    count = valid_count(mask_ref).reshape(1, 1, 1)
    real = jnp.where(token.astype(f32) < count, normed, 0.0)
    for s in range(seqs):
        turn_ref[:, s, :] = real[s]
    turned = turn_ref[...].astype(bf16).reshape(tokens * seqs, width)
    left = nt_dot(w1_ref[...], turned).astype(bf16)
    fc = w1_ref.shape[0]
    wk = pack * seqs
    for g in range(tokens // pack):
        for n in range(copies):
            rows_ref[n, g * fc : (g + 1) * fc, :] = left[:, g * wk : (g + 1) * wk]
    size = 128 // tokens
    real = real.astype(bf16)
    w2 = w2_ref[...]
    d = lax.broadcasted_iota(jnp.int32, (fd, 128), 0)
    lane = lax.broadcasted_iota(jnp.int32, (fd, 128), 1)
    mine = lax.rem(d, size) == lane // tokens
    for s in range(seqs):
        res = nt_dot(w2, jnp.concatenate([real[s]] * size, axis=0))
        res = jnp.where(mine, res, 0.0).reshape(fd // size, size, 128)
        place_ref[:, s, :] = jnp.sum(res, axis=1)
    right = place_ref[...].reshape(fd // size * seqs, 128).astype(bf16)
    for n in range(copies):
        cols_ref[n, :-rows, :] = right


def join_kernel(ready, rows_ref, cols_ref, parts_ref, out_ref, norm_ref):
    nk = rows_ref.shape[0]
    size = out_ref.shape[0] // (2 * nk)
    count = norm_ref.shape[1]
    for k in range(nk):
        out_ref[k * size : (k + 1) * size, :] = cols_ref[k, :size, :]
        out_ref[(nk + k) * size : (nk + k + 1) * size, :] = rows_ref[k, :size, :]
    for r in range(parts_ref.shape[0]):
        norm_ref[r] = parts_ref[r, parts_ref.shape[1] - count :, :]


def update_kernel(
    ready,
    col_ref,
    seq_ref,
    sides_ref,
    far_sides_ref,
    mask_ref,
    m_ref,
    score_ref,
    pair_ref,
    pout_hbm,
    pout_t_ref,
    logits_ref,
    pout_ref,
    out_sem,
    rk_ref,
    rab_ref,
    lm_ref,
    mt_ref,
    oh_ref,
    ol_ref,
    update_ref,
):
    nk = rk_ref.shape[0]
    width_d, pair_rows, _ = rab_ref.shape
    col, seq = col_ref[0], seq_ref[0]
    z = pair_ref.shape[1]
    groups, heads, lanes = logits_ref.shape
    tile_j = lanes // pack
    tokens = tile_j // nk
    fc = lm_ref.shape[0] // groups
    seqs = 128 // pack
    nq = pair_rows // seqs
    wk = pack * seqs

    r_rows = rk_ref.shape[1] // nq
    l_rows = groups * fc
    if nq == 2:
        sources = ((seq, 0, sides_ref), (1 - seq, 0, far_sides_ref))
    else:
        sources = tuple((q, q, far_sides_ref) for q in range(nq))
    for q, slot, ref in sources:
        base = slot * (nk * r_rows + l_rows)
        at = pl.ds(pl.multiple_of(q * r_rows, r_rows), r_rows)
        for k in range(nk):
            rk_ref[k, at, :] = ref[base + k * r_rows : base + (k + 1) * r_rows, :]
        base = base + nk * r_rows
        to = pl.ds(pl.multiple_of(q * wk, wk), wk)
        lm_ref[:, to] = ref[base : base + l_rows, :]
    size = 128 // tokens
    right = jnp.concatenate([rk_ref[k] for k in range(nk)], axis=1)
    source = lax.broadcasted_iota(jnp.int32, (nk * 128, 4 * tile_j), 0)
    target = lax.broadcasted_iota(jnp.int32, (nk * 128, 4 * tile_j), 1)
    used = jnp.logical_or(target < tile_j, target >= 3 * tile_j)
    j = lax.rem(target, tile_j)
    offset = jnp.where(used, source - (j // tokens * 128 + lax.rem(j, tokens)), -1)
    blocks = width_d // size
    for e in range(size):
        pick = jnp.where(offset == e * tokens, 1.0, 0.0).astype(bf16)
        res = nn_dot(right, pick).astype(bf16)
        for q in range(nq):
            for n in range(blocks):
                at = (q * blocks + n) * seqs
                rab_ref[n * size + e, q * seqs : (q + 1) * seqs, :] = res[at : at + seqs]

    chunk = 8
    many = 4
    wide = oh_ref.shape[2] // lanes
    empty = jnp.zeros((seqs, 2 * tile_j), bf16)

    def block_of(d):
        rows = []
        for q in range(nq):
            both = rab_ref[d, q * seqs : (q + 1) * seqs, :]
            part = both[:, : 2 * tile_j], both[:, 2 * tile_j :]
            for i in range(pack):
                pieces = [empty] * (pack // 2)
                pieces[i // 2] = part[i % 2]
                rows.append(jnp.concatenate(pieces, axis=1))
        return jnp.concatenate(rows, axis=0)

    def outer_of(n, carry):
        block = jnp.concatenate([block_of(many * n + e) for e in range(many)], axis=1)
        for m in range(groups // chunk):
            out = nn_dot(lm_ref[m * chunk * fc : (m + 1) * chunk * fc, :], block)
            high, low = high_low(out)
            for e in range(many):
                at = pl.ds(pl.multiple_of((many * n + e) * fc, fc), fc)
                for g in range(chunk):
                    group = m * chunk + g
                    to = slice(group % wide * lanes, (group % wide + 1) * lanes)
                    cut = slice(g * fc, (g + 1) * fc), slice(e * lanes, (e + 1) * lanes)
                    oh_ref[group // wide, at, to] = high[cut]
                    ol_ref[group // wide, at, to] = low[cut]
        return carry

    lax.fori_loop(0, width_d // many, outer_of, 0)

    ready()
    some = z // fc
    for n in range(width_d // some):
        block = jnp.concatenate(
            [m_ref[pl.ds(n * some + e, fc, stride=width_d), :] for e in range(some)], axis=0
        ).T
        high, low = high_low(block)
        mt_ref[:z, n * z : (n + 1) * z] = high
        mt_ref[z:, n * z : (n + 1) * z] = low
    maskj = column_mask(mask_ref, col, tile_j, 2)

    maskl = jnp.concatenate([maskj] * (pack // 2), axis=1) > 0
    score = score_ref[...]
    s1 = score.astype(bf16).astype(f32)
    s2 = (score - s1).astype(bf16).astype(f32)
    s3 = score - s1 - s2
    none = jnp.zeros_like(s1)
    st = jnp.concatenate(
        [
            jnp.concatenate([s1, s2, s3, none], axis=0),
            jnp.concatenate([s1, s2, none, none], axis=0),
        ],
        axis=1,
    ).astype(bf16)

    def finish(n, carry):
        two = nn_dot(mt_ref[...], oh_ref[n])
        update_ref[...] = two[:z] + two[z:] + nn_dot(mt_ref[:z, :], ol_ref[n])
        for e in range(wide):
            g = n * wide + e
            at = pl.ds(pl.multiple_of(g * lanes, lanes), lanes)
            before = pair_ref[at, :].T.astype(f32)
            result = (before + update_ref[:, e * lanes : (e + 1) * lanes]).astype(bf16)
            pout_t_ref[g] = result
            x = result.astype(f32)
            pout_ref[at, :] = result.T
            center = x - jnp.mean(x, axis=0, keepdims=True)
            inverse = lax.rsqrt(jnp.mean(center * center, axis=0, keepdims=True) + epsilon)
            high, low = high_low(center * inverse)
            scores = nn_dot(st, jnp.concatenate([high, low], axis=0))
            logits = scores[:heads] + scores[heads : 2 * heads] + scores[2 * heads : 3 * heads]
            logits_ref[g] = jnp.where(maskl, logits, far_below)
        at = pl.ds(pl.multiple_of(n * wide * lanes, wide * lanes), wide * lanes)
        pltpu.make_async_copy(pout_ref.at[at], pout_hbm.at[at], out_sem.at[n]).start()
        return carry

    lax.fori_loop(0, groups // wide, finish, 0)
    for n in range(groups // wide):
        at = pl.ds(n * wide * lanes, wide * lanes)
        pltpu.make_async_copy(pout_ref.at[at], pout_hbm.at[at], out_sem.at[n]).wait()


def by_heads(w, heads, out_ref):
    width, chans = w.shape
    hw = chans // heads
    block = 4 * hw
    slot = lax.broadcasted_iota(jnp.int32, (width, block), 1) // hw
    w = w.astype(f32)
    for t in range(chans // block):
        part = w[:, t * block : (t + 1) * block]
        turns = [part] + [pltpu.roll(part, n * hw, 1) for n in range(1, 4)]
        for e in range(4):
            h = t * 4 + e
            for s in range(4):
                out_ref[s * width : (s + 1) * width, h * block : (h + 1) * block] = jnp.where(
                    slot == s, turns[(s - e) % 4], 0.0
                ).astype(bf16)


def weights_kernel(
    ready,
    rows_ref,
    cols_ref,
    weights_ref,
    gw_ref,
    acc_ref,
    bv_ref,
    bg_ref,
    bf_ref,
    gs_ref,
    vs_ref,
):
    groups, heads, lanes = gw_ref.shape
    tile = lanes // pack
    nk = rows_ref.shape[0]
    tokens = tile // nk
    half = gs_ref.shape[2] // bv_ref.shape[1] * heads * 2
    count = half * tokens

    def part(ref, k, which, s):
        start = ref.shape[1] - which * count + s * tokens
        return ref[k, start : start + tokens, :]

    chans = weights_ref.shape[1] // 3
    by_heads(weights_ref[:, :chans], heads, bv_ref)
    by_heads(weights_ref[:, chans : 2 * chans], heads, bg_ref)
    by_heads(weights_ref[:, 2 * chans :], heads, bf_ref)
    block = bv_ref.shape[1] // heads

    def four(read, n):
        return jnp.concatenate(
            [
                jnp.concatenate(
                    [
                        jnp.concatenate([read(k, 2 * (2 * n + e) + p) for k in range(nk)], axis=0)
                        for p in range(2)
                    ],
                    axis=1,
                )
                for e in range(2)
            ],
            axis=0,
        )

    for hp in range(heads // 2):
        cut = slice(hp * 2 * block, (hp + 1) * 2 * block)
        for n in range(half // 4):
            v = nn_dot(four(lambda k, s: part(cols_ref, k, 1, s), n), bv_ref[:, cut]).astype(bf16)
            gate = nn_dot(four(lambda k, s: part(rows_ref, k, 2, s), n), bg_ref[:, cut])
            grad = nn_dot(four(lambda k, s: part(rows_ref, k, 1, s), n), bf_ref[:, cut])
            g = (grad * jax.nn.sigmoid(gate)).astype(bf16)
            for e in range(2):
                to = slice((2 * n + e) * block, (2 * n + e + 1) * block)
                for o in range(2):
                    mine = slice(o * block, (o + 1) * block)
                    ve = v[e * tile : (e + 1) * tile, mine]
                    vs_ref[2 * hp + o, :tile, to] = ve
                    vs_ref[2 * hp + o, tile:, to] = ve
                    gs_ref[2 * hp + o, :, to] = g[e * tile : (e + 1) * tile, mine]
    for h in range(heads):
        acc_ref[h * tile : (h + 1) * tile, :] = nt_dot(gs_ref[h], vs_ref[h])

    first = lax.broadcasted_iota(jnp.int32, (groups, 2 * tile), 1) < tile
    for h in range(heads):
        for part in range(pack // 2):
            a = acc_ref[pl.ds(h * tile + 2 * part, groups, stride=pack), :]
            b = acc_ref[pl.ds(h * tile + 2 * part + 1, groups, stride=pack), :]
            gw_ref[:, h, part * 2 * tile : (part + 1) * 2 * tile] = jnp.where(first, a, b)


def softmax_kernel(
    ready,
    col_ref,
    logits_ref,
    gwa_ref,
    gwb_ref,
    mask_ref,
    gw_ref,
    pay_ref,
):
    groups, heads, lanes = logits_ref.shape
    tile = lanes // pack
    nk = pay_ref.shape[0]
    rows = groups * heads
    col = col_ref[0]
    gw_ref[...] = gwa_ref[...] + gwb_ref[...]
    lane = lax.broadcasted_iota(jnp.int32, (rows, 2 * tile), 1)
    low = lane < tile
    maskj = column_mask(mask_ref, col, tile, 2)
    stats = jnp.zeros((rows, 2 * tile), f32)
    for part in range(pack // 2):
        cut = slice(part * 2 * tile, (part + 1) * 2 * tile)
        lg = logits_ref[:, :, cut].reshape(rows, 2 * tile)
        gw = gw_ref[:, :, cut].reshape(rows, 2 * tile)
        m0 = jnp.max(jnp.where(low, lg, far_below), axis=1, keepdims=True)
        m1 = jnp.max(jnp.where(low, far_below, lg), axis=1, keepdims=True)
        p = jnp.exp(lg - jnp.where(low, m0, m1)) * maskj
        pg = p * gw
        for e, m in ((0, m0), (1, m1)):
            mine = low if e == 0 else jnp.logical_not(low)
            i = 2 * part + e
            total = jnp.sum(jnp.where(mine, p, 0.0), axis=1, keepdims=True)
            inner = jnp.sum(jnp.where(mine, pg, 0.0), axis=1, keepdims=True)
            stats = jnp.where(lane == i, m, stats)
            stats = jnp.where(lane == pack + i, total, stats)
            stats = jnp.where(lane == 2 * pack + i, inner, stats)
    turned = stats.T[:16]
    per = groups // nk
    for dest in range(nk):
        pay_ref[dest, 0] = turned[:8]
        pay_ref[dest, 1] = turned[8:]
        for g in range(per):
            piece = logits_ref[dest * per + g]
            for part in range(pack // 2):
                cut = slice(part * 2 * tile, (part + 1) * 2 * tile)
                pay_ref[dest, 2 + g * (pack // 2) + part] = piece[:, cut]


def values_kernel(
    ready, col_ref, ev0_ref, ev1_ref, ev2_ref, ev3_ref, wv_ref, norm_ref, wg_ref, v_ref, gate_ref, ev_ref
):
    nk, nr, count, wide = ev_ref.shape
    half = v_ref.shape[0]
    tokens = count // half
    chans = wv_ref.shape[1]
    for t, ref in enumerate((ev0_ref, ev1_ref, ev2_ref, ev3_ref)):
        ev_ref[jnp.bitwise_xor(col_ref[0], t)] = ref[...]
    gate = jax.nn.sigmoid(nn_dot(norm_ref[...], twice(wg_ref[...])))
    gate_ref[: half * tokens] = gate[:, :chans]
    gate_ref[half * tokens :] = gate[:, chans:]
    wv = twice(wv_ref[...])
    for s in range(half):
        at = slice(s * tokens, (s + 1) * tokens)
        x = jnp.concatenate([ev_ref[k, r, at, :] for r in range(nr) for k in range(nk)], axis=0)
        v_ref[s] = nn_dot(x, wv).astype(bf16)


def gradient_kernel(
    ready,
    pay_ref, logits_ref, gw_ref, pout_t_ref, score_ref, out_hbm, stat_ref, out_ref, out_sem
):
    groups, heads, lanes = logits_ref.shape
    rows = groups * heads
    score = score_ref[...]
    z = score.shape[1]
    s1 = score.astype(bf16).astype(f32)
    s2 = (score - s1).astype(bf16).astype(f32)
    s3 = score - s1 - s2
    parts = [s1, s1, s1, s2, s2, s3, jnp.zeros((z - 6 * heads, z), f32)]
    sk = jnp.concatenate(parts, axis=0).T[:, : 6 * heads].astype(bf16)
    pays = [pay_ref.at[k] for k in range(pay_ref.shape[0])]
    ms = [p[0][:pack] for p in pays]
    ls = [p[0][pack : 2 * pack] for p in pays]
    ns = [p[1][:pack] for p in pays]
    top = functools.reduce(jnp.maximum, ms)
    scales = [jnp.exp(m - top) for m in ms]
    total = sum(a * b for a, b in zip(ls, scales))
    inner = sum(a * b for a, b in zip(ns, scales)) / total
    stacked = jnp.concatenate([top, total, inner, jnp.zeros((rows - 3 * pack, rows), f32)], axis=0)
    stat_ref[...] = stacked.T

    tile = lanes // pack
    low = lax.broadcasted_iota(jnp.int32, (heads, 2 * tile), 1) < tile

    def one(g):
        st = stat_ref[pl.ds(pl.multiple_of(g * heads, heads), heads), :]

        def spread(base):
            halves = [
                jnp.where(
                    low,
                    st[:, base + 2 * half : base + 2 * half + 1],
                    st[:, base + 2 * half + 1 : base + 2 * half + 2],
                )
                for half in range(pack // 2)
            ]
            return jnp.concatenate(halves, axis=1)

        prob = jnp.exp(logits_ref[g] - spread(0)) / spread(pack)
        gl = prob * (gw_ref[g] - spread(2 * pack))
        g1 = gl.astype(bf16).astype(f32)
        g2 = (gl - g1).astype(bf16).astype(f32)
        g3 = gl - g1 - g2
        stack = jnp.concatenate([g1, g2, g3, g1, g2, g1], axis=0).astype(bf16)
        grad = nn_dot(sk, stack)
        x = pout_t_ref[g].astype(f32)
        center = x - jnp.mean(x, axis=0, keepdims=True)
        inverse = lax.rsqrt(jnp.mean(center * center, axis=0, keepdims=True) + epsilon)
        normal = center * inverse
        centered = grad - jnp.mean(grad, axis=0, keepdims=True)
        along = jnp.mean(grad * normal, axis=0, keepdims=True)
        result = inverse * (centered - normal * along)
        out_ref[pl.ds(pl.multiple_of(g * lanes, lanes), lanes), :] = result.astype(bf16).T

    many = 4

    def some(n, carry):
        for e in range(many):
            one(n * many + e)
        at = pl.ds(pl.multiple_of(n * many * lanes, many * lanes), many * lanes)
        pltpu.make_async_copy(out_ref.at[at], out_hbm.at[at], out_sem.at[n]).start()
        return carry

    lax.fori_loop(0, groups // many, some, 0)
    for n in range(groups // many):
        at = pl.ds(n * many * lanes, many * lanes)
        pltpu.make_async_copy(out_ref.at[at], out_hbm.at[at], out_sem.at[n]).wait()


def alignment_kernel(ready, pay_ref, v_ref, gate_ref, x_ref, wf_ref, out_ref, w_ref, gated_ref):
    nk, count, heads, wide = pay_ref.shape
    tile = wide // 2
    pieces = count - 2
    rows = pieces * heads
    half, all_tokens, chans = v_ref.shape
    chans = chans // 2
    tokens = pieces * 2
    head_width = chans // heads
    low = lax.broadcasted_iota(jnp.int32, (rows, wide), 1) < tile
    lgs = [pay_ref[k, 2:].reshape(rows, wide) for k in range(nk)]
    peak = functools.reduce(jnp.maximum, lgs)
    m0 = jnp.max(jnp.where(low, peak, far_below), axis=1, keepdims=True)
    m1 = jnp.max(jnp.where(low, far_below, peak), axis=1, keepdims=True)
    top = jnp.where(low, m0, m1)
    ps = [jnp.exp(lg - top) for lg in lgs]
    every = sum(ps)
    t0 = jnp.sum(jnp.where(low, every, 0.0), axis=1, keepdims=True)
    t1 = jnp.sum(jnp.where(low, 0.0, every), axis=1, keepdims=True)
    total = jnp.where(low, t0, t1)
    for source, p in enumerate(ps):
        weight = p / total
        rolled = pltpu.roll(weight, tile, 1)
        for n in range(pieces):
            w_ref[source, :, 2 * n, :] = weight[n * heads : (n + 1) * heads]
            w_ref[source, :, 2 * n + 1, :] = rolled[n * heads : (n + 1) * heads]
    w = jnp.concatenate(
        [
            w_ref[k].reshape(heads * tokens, wide)[:, :tile]
            for k in range(nk)
        ],
        axis=1,
    ).astype(bf16)

    owner = lax.broadcasted_iota(jnp.int32, (tokens, chans), 1) // head_width

    def one(s, carry):
        full = nn_dot(w, v_ref[s])
        for e in range(2):
            cut = slice(e * chans, (e + 1) * chans)
            mean = jnp.zeros((tokens, chans), f32)
            for h in range(heads):
                mean = jnp.where(owner == h, full[h * tokens : (h + 1) * tokens, cut], mean)
            at = pl.ds(pl.multiple_of((e * half + s) * tokens, tokens), tokens)
            gated_ref[at, :] = (gate_ref[at, :] * mean).astype(bf16)
        return carry

    lax.fori_loop(0, half, one, 0, unroll=4)
    out_ref[...] = (x_ref[...].astype(f32) + nt_dot(gated_ref[...], wf_ref[...])).astype(bf16)


def on_device(
    counts,
    alignment_input,
    pair_input,
    token_valid_mask,
    first_factor_weights,
    second_factor_weights,
    content_weights_grid,
    sigmoid_weights_grid,
    outer_matrix,
    score_matrix,
    final_mixing_weights,
    adjoint_of_rowset,
):
    nq, nr, nk = counts
    row_index = lax.axis_index("row")
    col_index = lax.axis_index("col")
    seqs, tokens, width = alignment_input.shape
    tile_i, tile_j, z = pair_input.shape
    fc = first_factor_weights.shape[1]
    fd = second_factor_weights.shape[1]
    heads = score_matrix.shape[1]
    chans = content_weights_grid.shape[1]
    groups = tile_i // pack
    lanes = pack * tile_j
    sds = jax.ShapeDtypeStruct

    mask = token_valid_mask.reshape(1, -1)
    own_start = ((row_index * nk + col_index) * tokens).astype(jnp.int32).reshape(1)
    seq_index = lax.axis_index("seq")
    place = tuple(x.astype(jnp.int32).reshape(1) for x in (row_index, col_index, seq_index))
    col_scalar = col_index.astype(jnp.int32).reshape(1)
    half = seqs // 2

    l_rows = tokens // pack * fc
    r_rows = fd * tokens // 128 * seqs
    n_rows = half * tokens
    rows, cols, normed, weights = call(
        prepare_kernel,
        (
            sds((nk, l_rows + 2 * n_rows, 128), bf16),
            sds((nr, r_rows + n_rows, 128), bf16),
            sds((n_rows, 128), bf16),
            sds((width, 3 * chans), bf16),
        ),
        scratch=(
            pltpu.VMEM((tokens, seqs, width), f32),
            pltpu.VMEM((fd * tokens // 128, seqs, 128), f32),
        ),
        smem=1,
        vmem=60 * 1024 * 1024,
    )(
        own_start,
        alignment_input,
        adjoint_of_rowset,
        first_factor_weights.T,
        second_factor_weights.T,
        mask,
        content_weights_grid,
        sigmoid_weights_grid,
        final_mixing_weights.T,
    )

    parts = lax.all_to_all(cols, "row", 0, 0)
    all_rows = lax.all_to_all(rows, "col", 0, 0)
    all_cols = lax.all_to_all(parts, "col", 0, 0)

    sides, block = call(
        join_kernel,
        (
            sds((nk * (r_rows + l_rows), 128), bf16),
            sds((nr, n_rows, 2 * width), bf16),
        ),
    )(all_rows, all_cols, parts)
    if nq == 2:
        far_sides = lax.ppermute(sides, "seq", [(0, 1), (1, 0)])
    else:
        far_sides = lax.all_gather(sides, "seq", axis=0, tiled=True)

    head_lanes = seqs * chans // heads
    (gw_own,) = call(
        weights_kernel,
        (sds((groups, heads, lanes), f32),),
        scratch=(
            pltpu.VMEM((heads * tile_i, 2 * tile_j), f32),
            pltpu.VMEM((4 * width, 4 * chans), bf16),
            pltpu.VMEM((4 * width, 4 * chans), bf16),
            pltpu.VMEM((4 * width, 4 * chans), bf16),
            pltpu.VMEM((heads, tile_i, head_lanes), bf16),
            pltpu.VMEM((heads, 2 * tile_j, head_lanes), bf16),
        ),
        flops=3_000_000_000,
        nbytes=3_000_000,
    )(all_rows, all_cols, weights)
    if nq == 2:
        gw_other = lax.ppermute(gw_own, "seq", [(0, 1), (1, 0)])
    else:
        gw_own, gw_other = lax.psum(gw_own, "seq"), jnp.zeros_like(gw_own)

    block, gw_own = lax.optimization_barrier((block, gw_own))
    every = [block] + [
        lax.ppermute(block, "col", [(c, c ^ t) for c in range(nk)]) for t in range(1, nk)
    ]
    sides, far_sides, gw_other = lax.optimization_barrier((sides, far_sides, gw_other))

    pair_out, pair_t, logits = call(
        update_kernel,
        (
            sds((tile_i * tile_j, z), bf16),
            sds((groups, z, lanes), bf16),
            sds((groups, heads, lanes), f32),
        ),
        scratch=(
            pltpu.VMEM((tile_i * tile_j, z), bf16),
            pltpu.SemaphoreType.DMA((groups // 4,)),
            pltpu.VMEM((nk, nq * r_rows, 128), bf16),
            pltpu.VMEM((fd, nq * seqs, 4 * tile_j), bf16),
            pltpu.VMEM((groups * fc, nq * pack * seqs), bf16),
            pltpu.VMEM((2 * z, fd * fc), bf16),
            pltpu.VMEM((groups // 4, fd * fc, 4 * lanes), bf16),
            pltpu.VMEM((groups // 4, fd * fc, 4 * lanes), bf16),
            pltpu.VMEM((z, 4 * lanes), f32),
        ),
        smem=2,
        flops=14_000_000_000,
        nbytes=5_000_000,
        vmem=44 * 1024 * 1024,
        far=(4, 5, 6, 7),
        far_out=(0,),
    )(
        *place[1:],
        sides,
        far_sides,
        mask,
        outer_matrix,
        score_matrix.T,
        pair_input.reshape(tile_i * tile_j, z),
    )

    values, gating = call(
        values_kernel,
        (sds((half, nr * nk * tokens, 2 * chans), bf16), sds((seqs * tokens, chans), f32)),
        scratch=(pltpu.VMEM((nk, nr, n_rows, 2 * width), bf16),),
        smem=1,
        flops=4_000_000_000,
        nbytes=6_000_000,
    )(col_scalar, *every, content_weights_grid, normed, sigmoid_weights_grid)

    payload = sds((nk, 2 + groups // nk * (pack // 2), heads, 2 * tile_j), f32)
    gw, pay = call(
        softmax_kernel,
        (sds((groups, heads, lanes), f32), payload),
        smem=1,
    )(col_scalar, logits, gw_own, gw_other, mask)

    got = lax.all_to_all(pay, "col", 0, 0)
    got, values, gating = lax.optimization_barrier((got, values, gating))

    (gradient,) = call(
        gradient_kernel,
        (sds((tile_i * tile_j, z), bf16),),
        scratch=(
            pltpu.VMEM((groups * heads, groups * heads), f32),
            pltpu.VMEM((tile_i * tile_j, z), bf16),
            pltpu.SemaphoreType.DMA((groups // 4,)),
        ),
        far_out=(0,),
        flops=4_000_000_000,
        nbytes=3_000_000,
    )(got, logits, gw, pair_t, score_matrix.T)

    (aligned,) = call(
        alignment_kernel,
        (sds((seqs * tokens, width), bf16),),
        scratch=(
            pltpu.VMEM((nk, heads, tokens, 2 * tile_j), f32),
            pltpu.VMEM((seqs * tokens, chans), bf16),
        ),
        flops=3_000_000_000,
        nbytes=5_000_000,
    )(
        got,
        values,
        gating,
        alignment_input.reshape(seqs * tokens, width),
        final_mixing_weights.T,
    )
    return (
        aligned.reshape(seqs, tokens, width),
        pair_out.reshape(tile_i, tile_j, z),
        gradient.reshape(tile_i, tile_j, z),
    )


def solution(mesh):
    counts = (mesh.shape["seq"], mesh.shape["row"], mesh.shape["col"])
    in_specs = (
        P("seq", ("row", "col"), None),
        P("row", "col", None),
        P(),
        P(),
        P(),
        P(),
        P(),
        P(),
        P(),
        P(),
        P("seq", ("row", "col"), None),
    )
    out_specs = (P("seq", ("row", "col"), None), P("row", "col", None), P("row", "col", None))
    return jax.shard_map(
        functools.partial(on_device, counts),
        mesh=mesh,
        in_specs=in_specs,
        out_specs=out_specs,
        check_vma=False,
    )
```

```python
import functools

import jax
import jax.numpy as jnp
from jax import lax
from jax.experimental import pallas as pl
from jax.experimental.pallas import tpu as pltpu
from jax.sharding import PartitionSpec as P

epsilon = 1e-05
far_below = -1e30
vmem_bytes = 32 * 1024 * 1024
pack = 4

f32 = jnp.float32
bf16 = jnp.bfloat16


def nt_dot(a, b):
    return lax.dot_general(a, b, (((1,), (1,)), ((), ())), preferred_element_type=f32)


def nn_dot(a, b):
    return jnp.dot(a, b, preferred_element_type=f32)


def high_low(x):
    high = x.astype(bf16)
    return high, (x - high.astype(f32)).astype(bf16)


def call(
    kernel, out_shape, scratch=(), smem=0, flops=0, nbytes=0, vmem=vmem_bytes, far=(), far_out=()
):
    def run(*args):
        count = len(args)
        in_specs = [
            pl.BlockSpec(memory_space=pltpu.SMEM if n < smem else pltpu.VMEM) for n in range(count)
        ]
        for n in far:
            in_specs[n] = pl.BlockSpec(memory_space=pltpu.HBM)
        landing = [pltpu.VMEM(args[n].shape, args[n].dtype) for n in far]
        if far:
            landing.append(pltpu.SemaphoreType.DMA((len(far),)))

        def body(*refs):
            inputs = list(refs[:count])
            extra = refs[len(refs) - len(landing) :]
            rest = refs[count : len(refs) - len(landing)]
            copies = []
            for i, n in enumerate(far):
                copies.append(pltpu.make_async_copy(inputs[n], extra[i], extra[-1].at[i]))
                copies[-1].start()
                inputs[n] = extra[i]

            def ready():
                for copy in copies:
                    copy.wait()

            kernel(ready, *inputs, *rest)

        return pl.pallas_call(
            body,
            out_shape=out_shape,
            in_specs=in_specs,
            out_specs=[
                pl.BlockSpec(memory_space=pltpu.HBM if n in far_out else pltpu.VMEM)
                for n in range(len(out_shape))
            ],
            scratch_shapes=list(scratch) + landing,
            compiler_params=pltpu.CompilerParams(vmem_limit_bytes=vmem),
            cost_estimate=pl.CostEstimate(flops=flops, bytes_accessed=nbytes, transcendentals=0),
        )(*args)

    return run


def valid_count(mask_ref):
    return jnp.sum(mask_ref[...].astype(f32), axis=1, keepdims=True)


def column_mask(mask_ref, col, tile, copies):
    lane = lax.broadcasted_iota(jnp.int32, (1, copies * tile), 1)
    token = (lax.rem(lane, tile) + col * tile).astype(f32)
    return (token < valid_count(mask_ref)).astype(f32)


def twice(w):
    none = jnp.zeros_like(w)
    return jnp.concatenate(
        [jnp.concatenate([w, none], axis=1), jnp.concatenate([none, w], axis=1)], axis=0
    )


def prepare_kernel(
    ready,
    own_ref,
    x_ref,
    adj_ref,
    w1_ref,
    w2_ref,
    mask_ref,
    wv_ref,
    wg_ref,
    wf_ref,
    shard_ref,
    norm_ref,
    weights_ref,
    turn_ref,
    place_ref,
):
    chans = wv_ref.shape[1]
    weights_ref[:, :chans] = wv_ref[...]
    weights_ref[:, chans : 2 * chans] = wg_ref[...]
    weights_ref[:, 2 * chans :] = wf_ref[...]
    seqs, tokens, width = x_ref.shape
    half = seqs // 2
    fd = w2_ref.shape[0]
    x = x_ref[...].astype(f32)
    center = x - jnp.mean(x, axis=-1, keepdims=True)
    inverse = lax.rsqrt(jnp.mean(center * center, axis=-1, keepdims=True) + epsilon)
    normed = center * inverse
    rows = half * tokens
    adj = adj_ref[...].astype(f32)

    def two(x):
        x = jnp.concatenate([x[:half], x[half:]], axis=-1)
        return x.reshape(rows, 2 * width).astype(bf16)

    packed = two(normed)
    norm_ref[...] = packed
    base = tokens // pack * w1_ref.shape[0]
    shard_ref[base : base + rows, :] = two(adj)
    shard_ref[base + rows : base + 2 * rows, :] = packed
    token = lax.broadcasted_iota(jnp.int32, (seqs, tokens, width), 1) + own_ref[0]
    count = valid_count(mask_ref).reshape(1, 1, 1)
    real = jnp.where(token.astype(f32) < count, normed, 0.0)
    for s in range(seqs):
        turn_ref[:, s, :] = real[s]
    turned = turn_ref[...].astype(bf16).reshape(tokens * seqs, width)
    left = nt_dot(w1_ref[...], turned).astype(bf16)
    fc = w1_ref.shape[0]
    wk = pack * seqs
    for g in range(tokens // pack):
        shard_ref[g * fc : (g + 1) * fc, :] = left[:, g * wk : (g + 1) * wk]
    size = 128 // tokens
    real = real.astype(bf16)
    w2 = w2_ref[...]
    d = lax.broadcasted_iota(jnp.int32, (fd, 128), 0)
    lane = lax.broadcasted_iota(jnp.int32, (fd, 128), 1)
    mine = lax.rem(d, size) == lane // tokens
    for s in range(seqs):
        res = nt_dot(w2, jnp.concatenate([real[s]] * size, axis=0))
        res = jnp.where(mine, res, 0.0).reshape(fd // size, size, 128)
        place_ref[:, s, :] = jnp.sum(res, axis=1)
    right = place_ref[...].reshape(fd // size * seqs, 128).astype(bf16)
    shard_ref[base + 2 * rows :, :] = right


def join_kernel(
    ready,
    row_ref,
    col_ref,
    shard0_ref,
    shard1_ref,
    shard2_ref,
    shard3_ref,
    cols0_ref,
    cols1_ref,
    out_ref,
    norm_ref,
):
    nk = 4
    row, col = row_ref[0], col_ref[0]
    size = out_ref.shape[0] // (2 * nk)
    half, tokens, _ = norm_ref.shape[1:]
    count = half * tokens
    for t in range(nk):
        ref = (cols0_ref, cols1_ref)[t // 2]
        at = pl.ds(pl.multiple_of(jnp.bitwise_xor(row, t) * size, size), size)
        end = ref.shape[0] // 2 * (t % 2 + 1)
        out_ref[at, :] = ref[end - size : end, :]
    for t, ref in enumerate((shard0_ref, shard1_ref, shard2_ref, shard3_ref)):
        k = jnp.bitwise_xor(col, t)
        at = pl.ds(pl.multiple_of((nk + k) * size, size), size)
        out_ref[at, :] = ref[:size, :]
        norm_ref[k] = ref[size + count : size + 2 * count, :].reshape(norm_ref.shape[1:])


def update_kernel(
    ready,
    col_ref,
    seq_ref,
    sides_ref,
    far_sides_ref,
    mask_ref,
    m_ref,
    score_ref,
    pair_ref,
    pout_hbm,
    normal_ref,
    inverse_ref,
    logits_ref,
    pout_ref,
    out_sem,
    rk_ref,
    rab_ref,
    lm_ref,
    mt_ref,
    oh_ref,
    ol_ref,
    update_ref,
):
    nk = rk_ref.shape[0]
    width_d, pair_rows, _ = rab_ref.shape
    col, seq = col_ref[0], seq_ref[0]
    z = pair_ref.shape[1]
    groups, heads, lanes = logits_ref.shape
    tile_j = lanes // pack
    tokens = tile_j // nk
    fc = lm_ref.shape[0] // groups
    seqs = 128 // pack
    nq = pair_rows // seqs
    wk = pack * seqs

    r_rows = rk_ref.shape[1] // nq
    l_rows = groups * fc
    if nq == 2:
        sources = ((seq, 0, sides_ref), (1 - seq, 0, far_sides_ref))
    else:
        sources = tuple((q, q, far_sides_ref) for q in range(nq))
    for q, slot, ref in sources:
        base = slot * (nk * r_rows + l_rows)
        at = pl.ds(pl.multiple_of(q * r_rows, r_rows), r_rows)
        for k in range(nk):
            rk_ref[k, at, :] = ref[base + k * r_rows : base + (k + 1) * r_rows, :]
        base = base + nk * r_rows
        to = pl.ds(pl.multiple_of(q * wk, wk), wk)
        lm_ref[:, to] = ref[base : base + l_rows, :]
    size = 128 // tokens
    right = jnp.concatenate([rk_ref[k] for k in range(nk)], axis=1)
    source = lax.broadcasted_iota(jnp.int32, (nk * 128, 4 * tile_j), 0)
    target = lax.broadcasted_iota(jnp.int32, (nk * 128, 4 * tile_j), 1)
    used = jnp.logical_or(target < tile_j, target >= 3 * tile_j)
    j = lax.rem(target, tile_j)
    offset = jnp.where(used, source - (j // tokens * 128 + lax.rem(j, tokens)), -1)
    blocks = width_d // size
    for e in range(size):
        pick = jnp.where(offset == e * tokens, 1.0, 0.0).astype(bf16)
        res = nn_dot(right, pick).astype(bf16)
        for q in range(nq):
            for n in range(blocks):
                at = (q * blocks + n) * seqs
                rab_ref[n * size + e, q * seqs : (q + 1) * seqs, :] = res[at : at + seqs]

    chunk = 8
    many = 4
    wide = oh_ref.shape[2] // lanes
    empty = jnp.zeros((seqs, 2 * tile_j), bf16)

    def block_of(d):
        rows = []
        for q in range(nq):
            both = rab_ref[d, q * seqs : (q + 1) * seqs, :]
            part = both[:, : 2 * tile_j], both[:, 2 * tile_j :]
            for i in range(pack):
                pieces = [empty] * (pack // 2)
                pieces[i // 2] = part[i % 2]
                rows.append(jnp.concatenate(pieces, axis=1))
        return jnp.concatenate(rows, axis=0)

    def outer_of(n, carry):
        block = jnp.concatenate([block_of(many * n + e) for e in range(many)], axis=1)
        for m in range(groups // chunk):
            out = nn_dot(lm_ref[m * chunk * fc : (m + 1) * chunk * fc, :], block)
            high, low = high_low(out)
            for e in range(many):
                at = pl.ds(pl.multiple_of((many * n + e) * fc, fc), fc)
                for g in range(chunk):
                    group = m * chunk + g
                    to = slice(group % wide * lanes, (group % wide + 1) * lanes)
                    cut = slice(g * fc, (g + 1) * fc), slice(e * lanes, (e + 1) * lanes)
                    oh_ref[group // wide, at, to] = high[cut]
                    ol_ref[group // wide, at, to] = low[cut]
        return carry

    lax.fori_loop(0, width_d // many, outer_of, 0)

    ready()
    some = z // fc
    for n in range(width_d // some):
        block = jnp.concatenate(
            [m_ref[pl.ds(n * some + e, fc, stride=width_d), :] for e in range(some)], axis=0
        ).T
        high, low = high_low(block)
        mt_ref[:z, n * z : (n + 1) * z] = high
        mt_ref[z:, n * z : (n + 1) * z] = low
    maskj = column_mask(mask_ref, col, tile_j, 2)

    maskl = jnp.concatenate([maskj] * (pack // 2), axis=1) > 0
    score = score_ref[...]
    s1 = score.astype(bf16).astype(f32)
    s2 = (score - s1).astype(bf16).astype(f32)
    s3 = score - s1 - s2
    none = jnp.zeros_like(s1)
    st = jnp.concatenate(
        [
            jnp.concatenate([s1, s2, s3, none], axis=0),
            jnp.concatenate([s1, s2, none, none], axis=0),
        ],
        axis=1,
    ).astype(bf16)

    def finish(n, carry):
        two = nn_dot(mt_ref[...], oh_ref[n])
        update_ref[...] = two[:z] + two[z:] + nn_dot(mt_ref[:z, :], ol_ref[n])
        for e in range(wide):
            g = n * wide + e
            at = pl.ds(pl.multiple_of(g * lanes, lanes), lanes)
            before = pair_ref[at, :].T.astype(f32)
            result = (before + update_ref[:, e * lanes : (e + 1) * lanes]).astype(bf16)
            x = result.astype(f32)
            pout_ref[at, :] = result.T
            center = x - jnp.mean(x, axis=0, keepdims=True)
            inverse = lax.rsqrt(jnp.mean(center * center, axis=0, keepdims=True) + epsilon)
            normal = center * inverse
            normal_ref[g] = normal
            inverse_ref[g] = jnp.broadcast_to(inverse, inverse_ref.shape[1:])
            high, low = high_low(normal)
            scores = nn_dot(st, jnp.concatenate([high, low], axis=0))
            logits = scores[:heads] + scores[heads : 2 * heads] + scores[2 * heads : 3 * heads]
            logits_ref[g] = jnp.where(maskl, logits, far_below)
        at = pl.ds(pl.multiple_of(n * wide * lanes, wide * lanes), wide * lanes)
        pltpu.make_async_copy(pout_ref.at[at], pout_hbm.at[at], out_sem.at[n]).start()
        return carry

    lax.fori_loop(0, groups // wide, finish, 0)
    for n in range(groups // wide):
        at = pl.ds(n * wide * lanes, wide * lanes)
        pltpu.make_async_copy(pout_ref.at[at], pout_hbm.at[at], out_sem.at[n]).wait()


def by_heads(w, heads, out_ref):
    width, chans = w.shape
    hw = chans // heads
    block = 4 * hw
    slot = lax.broadcasted_iota(jnp.int32, (width, block), 1) // hw
    w = w.astype(f32)
    for t in range(chans // block):
        part = w[:, t * block : (t + 1) * block]
        turns = [part] + [pltpu.roll(part, n * hw, 1) for n in range(1, 4)]
        for e in range(4):
            h = t * 4 + e
            for s in range(4):
                out_ref[s * width : (s + 1) * width, h * block : (h + 1) * block] = jnp.where(
                    slot == s, turns[(s - e) % 4], 0.0
                ).astype(bf16)


def weights_kernel(
    ready,
    row_ref,
    col_ref,
    side0_ref,
    side1_ref,
    side2_ref,
    side3_ref,
    cols0_ref,
    cols1_ref,
    weights_ref,
    gw_ref,
    acc_ref,
    bv_ref,
    bg_ref,
    bf_ref,
    rows_ref,
    cols_ref,
    gs_ref,
    vs_ref,
):
    nk, half, tokens, _ = cols_ref.shape
    tile = nk * tokens
    groups, heads, lanes = gw_ref.shape
    row, col = row_ref[0], col_ref[0]
    count = half * tokens
    size = side0_ref.shape[0] - 2 * count - cols0_ref.shape[0] // 2 + count
    for t, ref in enumerate((side0_ref, side1_ref, side2_ref, side3_ref)):
        k = jnp.bitwise_xor(col, t)
        rows_ref[k] = ref[size : size + 2 * count, :].reshape(rows_ref.shape[1:])
    for t in range(nk):
        ref = (cols0_ref, cols1_ref)[t // 2]
        start = ref.shape[0] // 2 * (t % 2)
        part = ref[start : start + count, :]
        cols_ref[jnp.bitwise_xor(row, t)] = part.reshape(cols_ref.shape[1:])
    chans = weights_ref.shape[1] // 3
    by_heads(weights_ref[:, :chans], heads, bv_ref)
    by_heads(weights_ref[:, chans : 2 * chans], heads, bg_ref)
    by_heads(weights_ref[:, 2 * chans :], heads, bf_ref)
    block = bv_ref.shape[1] // heads

    def four(read, n):
        return jnp.concatenate(
            [
                jnp.concatenate(
                    [
                        jnp.concatenate([read(k, 2 * (2 * n + e) + p) for k in range(nk)], axis=0)
                        for p in range(2)
                    ],
                    axis=1,
                )
                for e in range(2)
            ],
            axis=0,
        )

    for hp in range(heads // 2):
        cut = slice(hp * 2 * block, (hp + 1) * 2 * block)
        for n in range(half // 4):
            v = nn_dot(four(lambda k, s: cols_ref[k, s], n), bv_ref[:, cut]).astype(bf16)
            gate = nn_dot(four(lambda k, s: rows_ref[k, 1, s], n), bg_ref[:, cut])
            grad = nn_dot(four(lambda k, s: rows_ref[k, 0, s], n), bf_ref[:, cut])
            g = (grad * jax.nn.sigmoid(gate)).astype(bf16)
            for e in range(2):
                to = slice((2 * n + e) * block, (2 * n + e + 1) * block)
                for o in range(2):
                    mine = slice(o * block, (o + 1) * block)
                    ve = v[e * tile : (e + 1) * tile, mine]
                    vs_ref[2 * hp + o, :tile, to] = ve
                    vs_ref[2 * hp + o, tile:, to] = ve
                    gs_ref[2 * hp + o, :, to] = g[e * tile : (e + 1) * tile, mine]
    for h in range(heads):
        acc_ref[h * tile : (h + 1) * tile, :] = nt_dot(gs_ref[h], vs_ref[h])

    first = lax.broadcasted_iota(jnp.int32, (groups, 2 * tile), 1) < tile
    for h in range(heads):
        for part in range(pack // 2):
            a = acc_ref[pl.ds(h * tile + 2 * part, groups, stride=pack), :]
            b = acc_ref[pl.ds(h * tile + 2 * part + 1, groups, stride=pack), :]
            gw_ref[:, h, part * 2 * tile : (part + 1) * 2 * tile] = jnp.where(first, a, b)


def softmax_kernel(
    ready,
    col_ref,
    logits_ref,
    gwa_ref,
    gwb_ref,
    mask_ref,
    gw_ref,
    own_ref,
    pay1_ref,
    pay2_ref,
    pay3_ref,
):
    groups, heads, lanes = logits_ref.shape
    tile = lanes // pack
    nk = 4
    rows = groups * heads
    col = col_ref[0]
    gw_ref[...] = gwa_ref[...] + gwb_ref[...]
    lane = lax.broadcasted_iota(jnp.int32, (rows, 2 * tile), 1)
    low = lane < tile
    maskj = column_mask(mask_ref, col, tile, 2)
    stats = jnp.zeros((rows, 2 * tile), f32)
    for part in range(pack // 2):
        cut = slice(part * 2 * tile, (part + 1) * 2 * tile)
        lg = logits_ref[:, :, cut].reshape(rows, 2 * tile)
        gw = gw_ref[:, :, cut].reshape(rows, 2 * tile)
        m0 = jnp.max(jnp.where(low, lg, far_below), axis=1, keepdims=True)
        m1 = jnp.max(jnp.where(low, far_below, lg), axis=1, keepdims=True)
        p = jnp.exp(lg - jnp.where(low, m0, m1)) * maskj
        pg = p * gw
        for e, m in ((0, m0), (1, m1)):
            mine = low if e == 0 else jnp.logical_not(low)
            i = 2 * part + e
            total = jnp.sum(jnp.where(mine, p, 0.0), axis=1, keepdims=True)
            inner = jnp.sum(jnp.where(mine, pg, 0.0), axis=1, keepdims=True)
            stats = jnp.where(lane == i, m, stats)
            stats = jnp.where(lane == pack + i, total, stats)
            stats = jnp.where(lane == 2 * pack + i, inner, stats)
    turned = stats.T[:16]
    per = groups // nk
    for shift, pay in enumerate((own_ref, pay1_ref, pay2_ref, pay3_ref)):
        dest = lax.rem(col + shift, nk)
        pay[0] = turned[:8]
        pay[1] = turned[8:]
        for g in range(per):
            piece = logits_ref[dest * per + g]
            for part in range(pack // 2):
                pay[2 + g * (pack // 2) + part] = piece[:, part * 2 * tile : (part + 1) * 2 * tile]


def values_kernel(
    ready, ev0_ref, ev1_ref, ev2_ref, ev3_ref, wv_ref, norm_ref, wg_ref, v_ref, gate_ref
):
    evs = (ev0_ref, ev1_ref, ev2_ref, ev3_ref)
    nk, half, tokens, wide = ev0_ref.shape
    chans = wv_ref.shape[1]
    gate = jax.nn.sigmoid(nn_dot(norm_ref[...], twice(wg_ref[...])))
    gate_ref[: half * tokens] = gate[:, :chans]
    gate_ref[half * tokens :] = gate[:, chans:]
    wv = twice(wv_ref[...])
    for s in range(half):
        x = jnp.concatenate([ev[k, s] for ev in evs for k in range(nk)], axis=0)
        v_ref[s] = nn_dot(x, wv).astype(bf16)


def gradient_kernel(
    ready,
    own_ref, r1_ref, r2_ref, r3_ref, logits_ref, gw_ref, normal_ref, inverse_ref, score_ref, out_hbm, stat_ref, out_ref, out_sem
):
    groups, heads, lanes = logits_ref.shape
    rows = groups * heads
    score = score_ref[...]
    z = score.shape[1]
    s1 = score.astype(bf16).astype(f32)
    s2 = (score - s1).astype(bf16).astype(f32)
    s3 = score - s1 - s2
    parts = [s1, s1, s1, s2, s2, s3, jnp.zeros((z - 6 * heads, z), f32)]
    sk = jnp.concatenate(parts, axis=0).T[:, : 6 * heads].astype(bf16)
    pays = (own_ref, r1_ref, r2_ref, r3_ref)
    ms = [p[0][:pack] for p in pays]
    ls = [p[0][pack : 2 * pack] for p in pays]
    ns = [p[1][:pack] for p in pays]
    top = functools.reduce(jnp.maximum, ms)
    scales = [jnp.exp(m - top) for m in ms]
    total = sum(a * b for a, b in zip(ls, scales))
    inner = sum(a * b for a, b in zip(ns, scales)) / total
    stacked = jnp.concatenate([top, total, inner, jnp.zeros((rows - 3 * pack, rows), f32)], axis=0)
    stat_ref[...] = stacked.T

    tile = lanes // pack
    low = lax.broadcasted_iota(jnp.int32, (heads, 2 * tile), 1) < tile

    def one(g):
        st = stat_ref[pl.ds(pl.multiple_of(g * heads, heads), heads), :]

        def spread(base):
            halves = [
                jnp.where(
                    low,
                    st[:, base + 2 * half : base + 2 * half + 1],
                    st[:, base + 2 * half + 1 : base + 2 * half + 2],
                )
                for half in range(pack // 2)
            ]
            return jnp.concatenate(halves, axis=1)

        prob = jnp.exp(logits_ref[g] - spread(0)) / spread(pack)
        gl = prob * (gw_ref[g] - spread(2 * pack))
        g1 = gl.astype(bf16).astype(f32)
        g2 = (gl - g1).astype(bf16).astype(f32)
        g3 = gl - g1 - g2
        stack = jnp.concatenate([g1, g2, g3, g1, g2, g1], axis=0).astype(bf16)
        grad = nn_dot(sk, stack)
        normal = normal_ref[g]
        inverse = inverse_ref[g][:1]
        centered = grad - jnp.mean(grad, axis=0, keepdims=True)
        along = jnp.mean(grad * normal, axis=0, keepdims=True)
        result = inverse * (centered - normal * along)
        out_ref[pl.ds(pl.multiple_of(g * lanes, lanes), lanes), :] = result.astype(bf16).T

    many = 4

    def some(n, carry):
        for e in range(many):
            one(n * many + e)
        at = pl.ds(pl.multiple_of(n * many * lanes, many * lanes), many * lanes)
        pltpu.make_async_copy(out_ref.at[at], out_hbm.at[at], out_sem.at[n]).start()
        return carry

    lax.fori_loop(0, groups // many, some, 0)
    for n in range(groups // many):
        at = pl.ds(n * many * lanes, many * lanes)
        pltpu.make_async_copy(out_ref.at[at], out_hbm.at[at], out_sem.at[n]).wait()


def alignment_kernel(
    ready,
    row_ref,
    col_ref,
    own_ref,
    r1_ref,
    r2_ref,
    r3_ref,
    v_ref,
    gate_ref,
    x_ref,
    wf_ref,
    out_ref,
    w_ref,
    gated_ref,
):
    pays = (own_ref, r1_ref, r2_ref, r3_ref)
    nk = len(pays)
    heads = own_ref.shape[1]
    wide = own_ref.shape[2]
    tile = wide // 2
    pieces = own_ref.shape[0] - 2
    rows = pieces * heads
    half, all_tokens, chans = v_ref.shape
    chans = chans // 2
    tokens = pieces * 2
    head_width = chans // heads
    row, col = row_ref[0], col_ref[0]

    low = lax.broadcasted_iota(jnp.int32, (rows, wide), 1) < tile
    lgs = [p[2:].reshape(rows, wide) for p in pays]
    peak = functools.reduce(jnp.maximum, lgs)
    m0 = jnp.max(jnp.where(low, peak, far_below), axis=1, keepdims=True)
    m1 = jnp.max(jnp.where(low, far_below, peak), axis=1, keepdims=True)
    top = jnp.where(low, m0, m1)
    ps = [jnp.exp(lg - top) for lg in lgs]
    every = sum(ps)
    t0 = jnp.sum(jnp.where(low, every, 0.0), axis=1, keepdims=True)
    t1 = jnp.sum(jnp.where(low, 0.0, every), axis=1, keepdims=True)
    total = jnp.where(low, t0, t1)
    for shift, p in enumerate(ps):
        source = lax.rem(col + nk - shift, nk)
        weight = p / total
        rolled = pltpu.roll(weight, tile, 1)
        for n in range(pieces):
            w_ref[source, :, 2 * n, :] = weight[n * heads : (n + 1) * heads]
            w_ref[source, :, 2 * n + 1, :] = rolled[n * heads : (n + 1) * heads]
    w = jnp.concatenate(
        [
            w_ref[jnp.bitwise_xor(row, t)].reshape(heads * tokens, wide)[:, :tile]
            for t in range(nk)
        ],
        axis=1,
    ).astype(bf16)

    owner = lax.broadcasted_iota(jnp.int32, (tokens, chans), 1) // head_width

    def one(s, carry):
        full = nn_dot(w, v_ref[s])
        for e in range(2):
            cut = slice(e * chans, (e + 1) * chans)
            mean = jnp.zeros((tokens, chans), f32)
            for h in range(heads):
                mean = jnp.where(owner == h, full[h * tokens : (h + 1) * tokens, cut], mean)
            at = pl.ds(pl.multiple_of((e * half + s) * tokens, tokens), tokens)
            gated_ref[at, :] = (gate_ref[at, :] * mean).astype(bf16)
        return carry

    lax.fori_loop(0, half, one, 0, unroll=4)
    out_ref[...] = (x_ref[...].astype(f32) + nt_dot(gated_ref[...], wf_ref[...])).astype(bf16)


def on_device(
    counts,
    alignment_input,
    pair_input,
    token_valid_mask,
    first_factor_weights,
    second_factor_weights,
    content_weights_grid,
    sigmoid_weights_grid,
    outer_matrix,
    score_matrix,
    final_mixing_weights,
    adjoint_of_rowset,
):
    nq, nr, nk = counts
    row_index = lax.axis_index("row")
    col_index = lax.axis_index("col")
    seqs, tokens, width = alignment_input.shape
    tile_i, tile_j, z = pair_input.shape
    fc = first_factor_weights.shape[1]
    fd = second_factor_weights.shape[1]
    heads = score_matrix.shape[1]
    chans = content_weights_grid.shape[1]
    groups = tile_i // pack
    lanes = pack * tile_j
    sds = jax.ShapeDtypeStruct

    mask = token_valid_mask.reshape(1, -1)
    own_start = ((row_index * nk + col_index) * tokens).astype(jnp.int32).reshape(1)
    seq_index = lax.axis_index("seq")
    place = tuple(x.astype(jnp.int32).reshape(1) for x in (row_index, col_index, seq_index))
    col_scalar = col_index.astype(jnp.int32).reshape(1)
    half = seqs // 2

    l_rows = tokens // pack * fc
    r_rows = fd * tokens // 128 * seqs
    n_rows = half * tokens
    shard, normed, weights = call(
        prepare_kernel,
        (
            sds((l_rows + 2 * n_rows + r_rows, 128), bf16),
            sds((n_rows, 128), bf16),
            sds((width, 3 * chans), bf16),
        ),
        scratch=(
            pltpu.VMEM((tokens, seqs, width), f32),
            pltpu.VMEM((fd * tokens // 128, seqs, 128), f32),
        ),
        smem=1,
        vmem=60 * 1024 * 1024,
    )(
        own_start,
        alignment_input,
        adjoint_of_rowset,
        first_factor_weights.T,
        second_factor_weights.T,
        mask,
        content_weights_grid,
        sigmoid_weights_grid,
        final_mixing_weights.T,
    )

    def exchange(x, bit):
        return lax.ppermute(x, "col", [(c, c ^ bit) for c in range(nk)])

    other = exchange(shard, 1)
    across = exchange(shard, 2)
    all_rows = [shard, other, across, exchange(across, 1)]
    pair = jnp.concatenate([x[l_rows + n_rows :] for x in (shard, other)], axis=0)
    all_cols = [
        lax.ppermute(
            pair,
            ("row", "col"),
            [(r * nk + c, (c ^ flip) * nk + r) for r in range(nr) for c in range(nk)],
        )
        for flip in (0, 2)
    ]

    sides, block = call(
        join_kernel,
        (
            sds((nk * (r_rows + l_rows), 128), bf16),
            sds((nk, half, tokens, 2 * width), bf16),
        ),
        smem=2,
    )(*place[:2], *all_rows, *all_cols)
    if nq == 2:
        far_sides = lax.ppermute(sides, "seq", [(0, 1), (1, 0)])
    else:
        far_sides = lax.all_gather(sides, "seq", axis=0, tiled=True)

    head_lanes = seqs * chans // heads
    (gw_own,) = call(
        weights_kernel,
        (sds((groups, heads, lanes), f32),),
        scratch=(
            pltpu.VMEM((heads * tile_i, 2 * tile_j), f32),
            pltpu.VMEM((4 * width, 4 * chans), bf16),
            pltpu.VMEM((4 * width, 4 * chans), bf16),
            pltpu.VMEM((4 * width, 4 * chans), bf16),
            pltpu.VMEM((nk, 2, half, tokens, 2 * width), bf16),
            pltpu.VMEM((nk, half, tokens, 2 * width), bf16),
            pltpu.VMEM((heads, tile_i, head_lanes), bf16),
            pltpu.VMEM((heads, 2 * tile_j, head_lanes), bf16),
        ),
        smem=2,
        flops=3_000_000_000,
        nbytes=3_000_000,
    )(*place[:2], *all_rows, *all_cols, weights)
    if nq == 2:
        gw_other = lax.ppermute(gw_own, "seq", [(0, 1), (1, 0)])
    else:
        gw_own, gw_other = lax.psum(gw_own, "seq"), jnp.zeros_like(gw_own)

    def exchange_rows(x, bit):
        return lax.ppermute(x, "row", [(r, r ^ bit) for r in range(nr)])

    block, _ = lax.optimization_barrier((block, gw_own))
    near, beyond = exchange_rows(block, 1), exchange_rows(block, 2)

    pair_out, normal, inverse, logits = call(
        update_kernel,
        (
            sds((tile_i * tile_j, z), bf16),
            sds((groups, z, lanes), f32),
            sds((groups, 8, lanes), f32),
            sds((groups, heads, lanes), f32),
        ),
        scratch=(
            pltpu.VMEM((tile_i * tile_j, z), bf16),
            pltpu.SemaphoreType.DMA((groups // 4,)),
            pltpu.VMEM((nk, nq * r_rows, 128), bf16),
            pltpu.VMEM((fd, nq * seqs, 4 * tile_j), bf16),
            pltpu.VMEM((groups * fc, nq * pack * seqs), bf16),
            pltpu.VMEM((2 * z, fd * fc), bf16),
            pltpu.VMEM((groups // 4, fd * fc, 4 * lanes), bf16),
            pltpu.VMEM((groups // 4, fd * fc, 4 * lanes), bf16),
            pltpu.VMEM((z, 4 * lanes), f32),
        ),
        smem=2,
        flops=14_000_000_000,
        nbytes=5_000_000,
        vmem=44 * 1024 * 1024,
        far=(4, 5, 6, 7),
        far_out=(0,),
    )(
        *place[1:],
        sides,
        far_sides,
        mask,
        outer_matrix,
        score_matrix.T,
        pair_input.reshape(tile_i * tile_j, z),
    )

    payload = sds((2 + groups // nk * (pack // 2), heads, 2 * tile_j), f32)
    gw, pay0, pay1, pay2, pay3 = call(
        softmax_kernel,
        (sds((groups, heads, lanes), f32), payload, payload, payload, payload),
        smem=1,
    )(col_scalar, logits, gw_own, gw_other, mask)

    got = [
        lax.ppermute(pay, "col", [(c, (c + shift) % nk) for c in range(nk)])
        for shift, pay in ((1, pay1), (2, pay2), (3, pay3))
    ]

    near, beyond, pay0 = lax.optimization_barrier((near, beyond, pay0))
    every = [block, near, beyond, exchange_rows(beyond, 1)]

    (gradient,) = call(
        gradient_kernel,
        (sds((tile_i * tile_j, z), bf16),),
        scratch=(
            pltpu.VMEM((groups * heads, groups * heads), f32),
            pltpu.VMEM((tile_i * tile_j, z), bf16),
            pltpu.SemaphoreType.DMA((groups // 4,)),
        ),
        far_out=(0,),
        flops=4_000_000_000,
        nbytes=3_000_000,
    )(pay0, *got, logits, gw, normal, inverse, score_matrix.T)

    values, gating = call(
        values_kernel,
        (sds((half, nr * nk * tokens, 2 * chans), bf16), sds((seqs * tokens, chans), f32)),
        flops=4_000_000_000,
        nbytes=6_000_000,
    )(*every, content_weights_grid, normed, sigmoid_weights_grid)

    (aligned,) = call(
        alignment_kernel,
        (sds((seqs * tokens, width), bf16),),
        scratch=(
            pltpu.VMEM((nk, heads, tokens, 2 * tile_j), f32),
            pltpu.VMEM((seqs * tokens, chans), bf16),
        ),
        smem=2,
        flops=3_000_000_000,
        nbytes=5_000_000,
    )(
        *place[:2],
        pay0,
        *got,
        values,
        gating,
        alignment_input.reshape(seqs * tokens, width),
        final_mixing_weights.T,
    )
    return (
        aligned.reshape(seqs, tokens, width),
        pair_out.reshape(tile_i, tile_j, z),
        gradient.reshape(tile_i, tile_j, z),
    )


def solution(mesh):
    counts = (mesh.shape["seq"], mesh.shape["row"], mesh.shape["col"])
    in_specs = (
        P("seq", ("row", "col"), None),
        P("row", "col", None),
        P(),
        P(),
        P(),
        P(),
        P(),
        P(),
        P(),
        P(),
        P("seq", ("row", "col"), None),
    )
    out_specs = (P("seq", ("row", "col"), None), P("row", "col", None), P("row", "col", None))
    return jax.shard_map(
        functools.partial(on_device, counts),
        mesh=mesh,
        in_specs=in_specs,
        out_specs=out_specs,
        check_vma=False,
    )
```

```python
import functools

import jax
import jax.numpy as jnp
from jax import lax
from jax.experimental import pallas as pl
from jax.experimental.pallas import tpu as pltpu
from jax.sharding import PartitionSpec as P

epsilon = 1e-05
far_below = -1e30
vmem_bytes = 32 * 1024 * 1024
pack = 4

f32 = jnp.float32
bf16 = jnp.bfloat16


def nt_dot(a, b):
    return lax.dot_general(a, b, (((1,), (1,)), ((), ())), preferred_element_type=f32)


def nn_dot(a, b):
    return jnp.dot(a, b, preferred_element_type=f32)


def high_low(x):
    high = x.astype(bf16)
    return high, (x - high.astype(f32)).astype(bf16)


def call(
    kernel, out_shape, scratch=(), smem=0, flops=0, nbytes=0, vmem=vmem_bytes, far=(), far_out=()
):
    def run(*args):
        count = len(args)
        in_specs = [
            pl.BlockSpec(memory_space=pltpu.SMEM if n < smem else pltpu.VMEM) for n in range(count)
        ]
        for n in far:
            in_specs[n] = pl.BlockSpec(memory_space=pltpu.HBM)
        landing = [pltpu.VMEM(args[n].shape, args[n].dtype) for n in far]
        if far:
            landing.append(pltpu.SemaphoreType.DMA((len(far),)))

        def body(*refs):
            inputs = list(refs[:count])
            extra = refs[len(refs) - len(landing) :]
            rest = refs[count : len(refs) - len(landing)]
            copies = []
            for i, n in enumerate(far):
                copies.append(pltpu.make_async_copy(inputs[n], extra[i], extra[-1].at[i]))
                copies[-1].start()
                inputs[n] = extra[i]

            def ready():
                for copy in copies:
                    copy.wait()

            kernel(ready, *inputs, *rest)

        return pl.pallas_call(
            body,
            out_shape=out_shape,
            in_specs=in_specs,
            out_specs=[
                pl.BlockSpec(memory_space=pltpu.HBM if n in far_out else pltpu.VMEM)
                for n in range(len(out_shape))
            ],
            scratch_shapes=list(scratch) + landing,
            compiler_params=pltpu.CompilerParams(vmem_limit_bytes=vmem),
            cost_estimate=pl.CostEstimate(flops=flops, bytes_accessed=nbytes, transcendentals=0),
        )(*args)

    return run


def valid_count(mask_ref):
    return jnp.sum(mask_ref[...].astype(f32), axis=1, keepdims=True)


def column_mask(mask_ref, col, tile, copies):
    lane = lax.broadcasted_iota(jnp.int32, (1, copies * tile), 1)
    token = (lax.rem(lane, tile) + col * tile).astype(f32)
    return (token < valid_count(mask_ref)).astype(f32)


def twice(w):
    none = jnp.zeros_like(w)
    return jnp.concatenate(
        [jnp.concatenate([w, none], axis=1), jnp.concatenate([none, w], axis=1)], axis=0
    )


def prepare_kernel(
    ready,
    own_ref,
    x_ref,
    adj_ref,
    w1_ref,
    w2_ref,
    mask_ref,
    wv_ref,
    wg_ref,
    wf_ref,
    shard_ref,
    right_ref,
    norm_ref,
    weights_ref,
    turn_ref,
    place_ref,
):
    chans = wv_ref.shape[1]
    weights_ref[:, :chans] = wv_ref[...]
    weights_ref[:, chans : 2 * chans] = wg_ref[...]
    weights_ref[:, 2 * chans :] = wf_ref[...]
    seqs, tokens, width = x_ref.shape
    half = seqs // 2
    fd = w2_ref.shape[0]
    x = x_ref[...].astype(f32)
    center = x - jnp.mean(x, axis=-1, keepdims=True)
    inverse = lax.rsqrt(jnp.mean(center * center, axis=-1, keepdims=True) + epsilon)
    normed = center * inverse
    rows = half * tokens
    adj = adj_ref[...].astype(f32)

    def two(x):
        x = jnp.concatenate([x[:half], x[half:]], axis=-1)
        return x.reshape(rows, 2 * width).astype(bf16)

    packed = two(normed)
    norm_ref[...] = packed
    base = tokens // pack * w1_ref.shape[0]
    shard_ref[base : base + rows, :] = two(adj)
    shard_ref[base + rows : base + 2 * rows, :] = packed
    token = lax.broadcasted_iota(jnp.int32, (seqs, tokens, width), 1) + own_ref[0]
    count = valid_count(mask_ref).reshape(1, 1, 1)
    real = jnp.where(token.astype(f32) < count, normed, 0.0)
    for s in range(seqs):
        turn_ref[:, s, :] = real[s]
    turned = turn_ref[...].astype(bf16).reshape(tokens * seqs, width)
    left = nt_dot(w1_ref[...], turned).astype(bf16)
    fc = w1_ref.shape[0]
    wk = pack * seqs
    for g in range(tokens // pack):
        shard_ref[g * fc : (g + 1) * fc, :] = left[:, g * wk : (g + 1) * wk]
    size = 128 // tokens
    real = real.astype(bf16)
    w2 = w2_ref[...]
    d = lax.broadcasted_iota(jnp.int32, (fd, 128), 0)
    lane = lax.broadcasted_iota(jnp.int32, (fd, 128), 1)
    mine = lax.rem(d, size) == lane // tokens
    for s in range(seqs):
        res = nt_dot(w2, jnp.concatenate([real[s]] * size, axis=0))
        res = jnp.where(mine, res, 0.0).reshape(fd // size, size, 128)
        place_ref[:, s, :] = jnp.sum(res, axis=1)
    right_ref[...] = place_ref[...].reshape(fd // size * seqs, 128).astype(bf16)


def join_kernel(
    ready,
    row_ref,
    col_ref,
    shard0_ref,
    shard1_ref,
    shard2_ref,
    shard3_ref,
    right0_ref,
    right1_ref,
    right2_ref,
    right3_ref,
    norm0_ref,
    norm1_ref,
    norm2_ref,
    norm3_ref,
    sides_ref,
    parts_ref,
    cols0_ref,
    cols1_ref,
    cols2_ref,
    cols3_ref,
):
    nk = 4
    row, col = row_ref[0], col_ref[0]
    size = right0_ref.shape[0]
    for t, ref in enumerate((right0_ref, right1_ref, right2_ref, right3_ref)):
        at = pl.ds(pl.multiple_of(lax.rem(row + nk - t, nk) * size, size), size)
        sides_ref[at, :] = ref[...]
    for t, ref in enumerate((shard0_ref, shard1_ref, shard2_ref, shard3_ref)):
        at = pl.ds(pl.multiple_of((nk + jnp.bitwise_xor(col, t)) * size, size), size)
        sides_ref[at, :] = ref[:size, :]
    for t, ref in enumerate((norm0_ref, norm1_ref, norm2_ref, norm3_ref)):
        parts_ref[jnp.bitwise_xor(row, t)] = ref[...]
    for t, ref in enumerate((cols0_ref, cols1_ref, cols2_ref, cols3_ref)):
        ref[...] = parts_ref[jnp.bitwise_xor(col, t)]


def update_kernel(
    ready,
    col_ref,
    seq_ref,
    sides_ref,
    far_sides_ref,
    mask_ref,
    m_ref,
    score_ref,
    pair_ref,
    pout_hbm,
    normal_ref,
    inverse_ref,
    logits_ref,
    pout_ref,
    out_sem,
    rk_ref,
    rab_ref,
    lm_ref,
    mt_ref,
    oh_ref,
    ol_ref,
    update_ref,
):
    nk = rk_ref.shape[0]
    width_d, pair_rows, _ = rab_ref.shape
    col, seq = col_ref[0], seq_ref[0]
    z = pair_ref.shape[1]
    groups, heads, lanes = logits_ref.shape
    tile_j = lanes // pack
    tokens = tile_j // nk
    fc = lm_ref.shape[0] // groups
    seqs = 128 // pack
    nq = pair_rows // seqs
    wk = pack * seqs

    r_rows = rk_ref.shape[1] // nq
    l_rows = groups * fc
    if nq == 2:
        sources = ((seq, 0, sides_ref), (1 - seq, 0, far_sides_ref))
    else:
        sources = tuple((q, q, far_sides_ref) for q in range(nq))
    for q, slot, ref in sources:
        base = slot * (nk * r_rows + l_rows)
        at = pl.ds(pl.multiple_of(q * r_rows, r_rows), r_rows)
        for k in range(nk):
            rk_ref[k, at, :] = ref[base + k * r_rows : base + (k + 1) * r_rows, :]
        base = base + nk * r_rows
        to = pl.ds(pl.multiple_of(q * wk, wk), wk)
        lm_ref[:, to] = ref[base : base + l_rows, :]
    size = 128 // tokens
    right = jnp.concatenate([rk_ref[k] for k in range(nk)], axis=1)
    source = lax.broadcasted_iota(jnp.int32, (nk * 128, 4 * tile_j), 0)
    target = lax.broadcasted_iota(jnp.int32, (nk * 128, 4 * tile_j), 1)
    used = jnp.logical_or(target < tile_j, target >= 3 * tile_j)
    j = lax.rem(target, tile_j)
    offset = jnp.where(used, source - (j // tokens * 128 + lax.rem(j, tokens)), -1)
    blocks = width_d // size
    for e in range(size):
        pick = jnp.where(offset == e * tokens, 1.0, 0.0).astype(bf16)
        res = nn_dot(right, pick).astype(bf16)
        for q in range(nq):
            for n in range(blocks):
                at = (q * blocks + n) * seqs
                rab_ref[n * size + e, q * seqs : (q + 1) * seqs, :] = res[at : at + seqs]

    chunk = 8
    many = 4
    wide = oh_ref.shape[2] // lanes
    empty = jnp.zeros((seqs, 2 * tile_j), bf16)

    def block_of(d):
        rows = []
        for q in range(nq):
            both = rab_ref[d, q * seqs : (q + 1) * seqs, :]
            part = both[:, : 2 * tile_j], both[:, 2 * tile_j :]
            for i in range(pack):
                pieces = [empty] * (pack // 2)
                pieces[i // 2] = part[i % 2]
                rows.append(jnp.concatenate(pieces, axis=1))
        return jnp.concatenate(rows, axis=0)

    def outer_of(n, carry):
        block = jnp.concatenate([block_of(many * n + e) for e in range(many)], axis=1)
        for m in range(groups // chunk):
            out = nn_dot(lm_ref[m * chunk * fc : (m + 1) * chunk * fc, :], block)
            high, low = high_low(out)
            for e in range(many):
                at = pl.ds(pl.multiple_of((many * n + e) * fc, fc), fc)
                for g in range(chunk):
                    group = m * chunk + g
                    to = slice(group % wide * lanes, (group % wide + 1) * lanes)
                    cut = slice(g * fc, (g + 1) * fc), slice(e * lanes, (e + 1) * lanes)
                    oh_ref[group // wide, at, to] = high[cut]
                    ol_ref[group // wide, at, to] = low[cut]
        return carry

    lax.fori_loop(0, width_d // many, outer_of, 0)

    ready()
    some = z // fc
    for n in range(width_d // some):
        block = jnp.concatenate(
            [m_ref[pl.ds(n * some + e, fc, stride=width_d), :] for e in range(some)], axis=0
        ).T
        high, low = high_low(block)
        mt_ref[:z, n * z : (n + 1) * z] = high
        mt_ref[z:, n * z : (n + 1) * z] = low
    maskj = column_mask(mask_ref, col, tile_j, 2)

    maskl = jnp.concatenate([maskj] * (pack // 2), axis=1) > 0
    score = score_ref[...]
    s1 = score.astype(bf16).astype(f32)
    s2 = (score - s1).astype(bf16).astype(f32)
    s3 = score - s1 - s2
    none = jnp.zeros_like(s1)
    st = jnp.concatenate(
        [
            jnp.concatenate([s1, s2, s3, none], axis=0),
            jnp.concatenate([s1, s2, none, none], axis=0),
        ],
        axis=1,
    ).astype(bf16)

    def finish(n, carry):
        two = nn_dot(mt_ref[...], oh_ref[n])
        update_ref[...] = two[:z] + two[z:] + nn_dot(mt_ref[:z, :], ol_ref[n])
        for e in range(wide):
            g = n * wide + e
            at = pl.ds(pl.multiple_of(g * lanes, lanes), lanes)
            before = pair_ref[at, :].T.astype(f32)
            result = (before + update_ref[:, e * lanes : (e + 1) * lanes]).astype(bf16)
            x = result.astype(f32)
            pout_ref[at, :] = result.T
            center = x - jnp.mean(x, axis=0, keepdims=True)
            inverse = lax.rsqrt(jnp.mean(center * center, axis=0, keepdims=True) + epsilon)
            normal = center * inverse
            normal_ref[g] = normal
            inverse_ref[g] = jnp.broadcast_to(inverse, inverse_ref.shape[1:])
            high, low = high_low(normal)
            scores = nn_dot(st, jnp.concatenate([high, low], axis=0))
            logits = scores[:heads] + scores[heads : 2 * heads] + scores[2 * heads : 3 * heads]
            logits_ref[g] = jnp.where(maskl, logits, far_below)
        at = pl.ds(pl.multiple_of(n * wide * lanes, wide * lanes), wide * lanes)
        pltpu.make_async_copy(pout_ref.at[at], pout_hbm.at[at], out_sem.at[n]).start()
        return carry

    lax.fori_loop(0, groups // wide, finish, 0)
    for n in range(groups // wide):
        at = pl.ds(n * wide * lanes, wide * lanes)
        pltpu.make_async_copy(pout_ref.at[at], pout_hbm.at[at], out_sem.at[n]).wait()


def by_heads(w, heads, out_ref):
    width, chans = w.shape
    hw = chans // heads
    block = 4 * hw
    slot = lax.broadcasted_iota(jnp.int32, (width, block), 1) // hw
    w = w.astype(f32)
    for t in range(chans // block):
        part = w[:, t * block : (t + 1) * block]
        turns = [part] + [pltpu.roll(part, n * hw, 1) for n in range(1, 4)]
        for e in range(4):
            h = t * 4 + e
            for s in range(4):
                out_ref[s * width : (s + 1) * width, h * block : (h + 1) * block] = jnp.where(
                    slot == s, turns[(s - e) % 4], 0.0
                ).astype(bf16)


def weights_kernel(
    ready,
    col_ref,
    side0_ref,
    side1_ref,
    side2_ref,
    side3_ref,
    cols0_ref,
    cols1_ref,
    cols2_ref,
    cols3_ref,
    weights_ref,
    gw_ref,
    acc_ref,
    bv_ref,
    bg_ref,
    bf_ref,
    rows_ref,
    cols_ref,
    gs_ref,
    vs_ref,
):
    nk, half, tokens, _ = cols_ref.shape
    tile = nk * tokens
    groups, heads, lanes = gw_ref.shape
    col = col_ref[0]
    count = half * tokens
    start = side0_ref.shape[0] - 2 * count
    for t, ref in enumerate((side0_ref, side1_ref, side2_ref, side3_ref)):
        rows_ref[jnp.bitwise_xor(col, t)] = ref[start:, :].reshape(rows_ref.shape[1:])
    for t, ref in enumerate((cols0_ref, cols1_ref, cols2_ref, cols3_ref)):
        cols_ref[jnp.bitwise_xor(col, t)] = ref[...].reshape(cols_ref.shape[1:])
    chans = weights_ref.shape[1] // 3
    by_heads(weights_ref[:, :chans], heads, bv_ref)
    by_heads(weights_ref[:, chans : 2 * chans], heads, bg_ref)
    by_heads(weights_ref[:, 2 * chans :], heads, bf_ref)
    block = bv_ref.shape[1] // heads

    def four(read, n):
        return jnp.concatenate(
            [
                jnp.concatenate(
                    [
                        jnp.concatenate([read(k, 2 * (2 * n + e) + p) for k in range(nk)], axis=0)
                        for p in range(2)
                    ],
                    axis=1,
                )
                for e in range(2)
            ],
            axis=0,
        )

    for hp in range(heads // 2):
        cut = slice(hp * 2 * block, (hp + 1) * 2 * block)
        for n in range(half // 4):
            v = nn_dot(four(lambda k, s: cols_ref[k, s], n), bv_ref[:, cut]).astype(bf16)
            gate = nn_dot(four(lambda k, s: rows_ref[k, 1, s], n), bg_ref[:, cut])
            grad = nn_dot(four(lambda k, s: rows_ref[k, 0, s], n), bf_ref[:, cut])
            g = (grad * jax.nn.sigmoid(gate)).astype(bf16)
            for e in range(2):
                to = slice((2 * n + e) * block, (2 * n + e + 1) * block)
                for o in range(2):
                    mine = slice(o * block, (o + 1) * block)
                    ve = v[e * tile : (e + 1) * tile, mine]
                    vs_ref[2 * hp + o, :tile, to] = ve
                    vs_ref[2 * hp + o, tile:, to] = ve
                    gs_ref[2 * hp + o, :, to] = g[e * tile : (e + 1) * tile, mine]
    for h in range(heads):
        acc_ref[h * tile : (h + 1) * tile, :] = nt_dot(gs_ref[h], vs_ref[h])

    first = lax.broadcasted_iota(jnp.int32, (groups, 2 * tile), 1) < tile
    for h in range(heads):
        for part in range(pack // 2):
            a = acc_ref[pl.ds(h * tile + 2 * part, groups, stride=pack), :]
            b = acc_ref[pl.ds(h * tile + 2 * part + 1, groups, stride=pack), :]
            gw_ref[:, h, part * 2 * tile : (part + 1) * 2 * tile] = jnp.where(first, a, b)


def softmax_kernel(
    ready,
    col_ref,
    logits_ref,
    gwa_ref,
    gwb_ref,
    mask_ref,
    gw_ref,
    own_ref,
    pay1_ref,
    pay2_ref,
    pay3_ref,
):
    groups, heads, lanes = logits_ref.shape
    tile = lanes // pack
    nk = 4
    rows = groups * heads
    col = col_ref[0]
    gw_ref[...] = gwa_ref[...] + gwb_ref[...]
    lane = lax.broadcasted_iota(jnp.int32, (rows, 2 * tile), 1)
    low = lane < tile
    maskj = column_mask(mask_ref, col, tile, 2)
    stats = jnp.zeros((rows, 2 * tile), f32)
    for part in range(pack // 2):
        cut = slice(part * 2 * tile, (part + 1) * 2 * tile)
        lg = logits_ref[:, :, cut].reshape(rows, 2 * tile)
        gw = gw_ref[:, :, cut].reshape(rows, 2 * tile)
        m0 = jnp.max(jnp.where(low, lg, far_below), axis=1, keepdims=True)
        m1 = jnp.max(jnp.where(low, far_below, lg), axis=1, keepdims=True)
        p = jnp.exp(lg - jnp.where(low, m0, m1)) * maskj
        pg = p * gw
        for e, m in ((0, m0), (1, m1)):
            mine = low if e == 0 else jnp.logical_not(low)
            i = 2 * part + e
            total = jnp.sum(jnp.where(mine, p, 0.0), axis=1, keepdims=True)
            inner = jnp.sum(jnp.where(mine, pg, 0.0), axis=1, keepdims=True)
            stats = jnp.where(lane == i, m, stats)
            stats = jnp.where(lane == pack + i, total, stats)
            stats = jnp.where(lane == 2 * pack + i, inner, stats)
    turned = stats.T[:16]
    per = groups // nk
    for shift, pay in enumerate((own_ref, pay1_ref, pay2_ref, pay3_ref)):
        dest = lax.rem(col + shift, nk)
        pay[0] = turned[:8]
        pay[1] = turned[8:]
        for g in range(per):
            piece = logits_ref[dest * per + g]
            for part in range(pack // 2):
                pay[2 + g * (pack // 2) + part] = piece[:, part * 2 * tile : (part + 1) * 2 * tile]


def values_kernel(
    ready, col_ref, ev0_ref, ev1_ref, ev2_ref, ev3_ref, wv_ref, norm_ref, wg_ref, v_ref, gate_ref, ev_ref
):
    nk, nr, count, wide = ev_ref.shape
    half = v_ref.shape[0]
    tokens = count // half
    chans = wv_ref.shape[1]
    for t, ref in enumerate((ev0_ref, ev1_ref, ev2_ref, ev3_ref)):
        ev_ref[jnp.bitwise_xor(col_ref[0], t)] = ref[...]
    gate = jax.nn.sigmoid(nn_dot(norm_ref[...], twice(wg_ref[...])))
    gate_ref[: half * tokens] = gate[:, :chans]
    gate_ref[half * tokens :] = gate[:, chans:]
    wv = twice(wv_ref[...])
    for s in range(half):
        at = slice(s * tokens, (s + 1) * tokens)
        x = jnp.concatenate([ev_ref[k, r, at, :] for r in range(nr) for k in range(nk)], axis=0)
        v_ref[s] = nn_dot(x, wv).astype(bf16)


def gradient_kernel(
    ready,
    own_ref, r1_ref, r2_ref, r3_ref, logits_ref, gw_ref, normal_ref, inverse_ref, score_ref, out_hbm, stat_ref, out_ref, out_sem
):
    groups, heads, lanes = logits_ref.shape
    rows = groups * heads
    score = score_ref[...]
    z = score.shape[1]
    s1 = score.astype(bf16).astype(f32)
    s2 = (score - s1).astype(bf16).astype(f32)
    s3 = score - s1 - s2
    parts = [s1, s1, s1, s2, s2, s3, jnp.zeros((z - 6 * heads, z), f32)]
    sk = jnp.concatenate(parts, axis=0).T[:, : 6 * heads].astype(bf16)
    pays = (own_ref, r1_ref, r2_ref, r3_ref)
    ms = [p[0][:pack] for p in pays]
    ls = [p[0][pack : 2 * pack] for p in pays]
    ns = [p[1][:pack] for p in pays]
    top = functools.reduce(jnp.maximum, ms)
    scales = [jnp.exp(m - top) for m in ms]
    total = sum(a * b for a, b in zip(ls, scales))
    inner = sum(a * b for a, b in zip(ns, scales)) / total
    stacked = jnp.concatenate([top, total, inner, jnp.zeros((rows - 3 * pack, rows), f32)], axis=0)
    stat_ref[...] = stacked.T

    tile = lanes // pack
    low = lax.broadcasted_iota(jnp.int32, (heads, 2 * tile), 1) < tile

    def one(g):
        st = stat_ref[pl.ds(pl.multiple_of(g * heads, heads), heads), :]

        def spread(base):
            halves = [
                jnp.where(
                    low,
                    st[:, base + 2 * half : base + 2 * half + 1],
                    st[:, base + 2 * half + 1 : base + 2 * half + 2],
                )
                for half in range(pack // 2)
            ]
            return jnp.concatenate(halves, axis=1)

        prob = jnp.exp(logits_ref[g] - spread(0)) / spread(pack)
        gl = prob * (gw_ref[g] - spread(2 * pack))
        g1 = gl.astype(bf16).astype(f32)
        g2 = (gl - g1).astype(bf16).astype(f32)
        g3 = gl - g1 - g2
        stack = jnp.concatenate([g1, g2, g3, g1, g2, g1], axis=0).astype(bf16)
        grad = nn_dot(sk, stack)
        normal = normal_ref[g]
        inverse = inverse_ref[g][:1]
        centered = grad - jnp.mean(grad, axis=0, keepdims=True)
        along = jnp.mean(grad * normal, axis=0, keepdims=True)
        result = inverse * (centered - normal * along)
        out_ref[pl.ds(pl.multiple_of(g * lanes, lanes), lanes), :] = result.astype(bf16).T

    many = 4

    def some(n, carry):
        for e in range(many):
            one(n * many + e)
        at = pl.ds(pl.multiple_of(n * many * lanes, many * lanes), many * lanes)
        pltpu.make_async_copy(out_ref.at[at], out_hbm.at[at], out_sem.at[n]).start()
        return carry

    lax.fori_loop(0, groups // many, some, 0)
    for n in range(groups // many):
        at = pl.ds(n * many * lanes, many * lanes)
        pltpu.make_async_copy(out_ref.at[at], out_hbm.at[at], out_sem.at[n]).wait()


def alignment_kernel(
    ready,
    col_ref,
    own_ref,
    r1_ref,
    r2_ref,
    r3_ref,
    v_ref,
    gate_ref,
    x_ref,
    wf_ref,
    out_ref,
    w_ref,
    gated_ref,
):
    pays = (own_ref, r1_ref, r2_ref, r3_ref)
    nk = len(pays)
    heads = own_ref.shape[1]
    wide = own_ref.shape[2]
    tile = wide // 2
    pieces = own_ref.shape[0] - 2
    rows = pieces * heads
    half, all_tokens, chans = v_ref.shape
    chans = chans // 2
    tokens = pieces * 2
    head_width = chans // heads
    col = col_ref[0]

    low = lax.broadcasted_iota(jnp.int32, (rows, wide), 1) < tile
    lgs = [p[2:].reshape(rows, wide) for p in pays]
    peak = functools.reduce(jnp.maximum, lgs)
    m0 = jnp.max(jnp.where(low, peak, far_below), axis=1, keepdims=True)
    m1 = jnp.max(jnp.where(low, far_below, peak), axis=1, keepdims=True)
    top = jnp.where(low, m0, m1)
    ps = [jnp.exp(lg - top) for lg in lgs]
    every = sum(ps)
    t0 = jnp.sum(jnp.where(low, every, 0.0), axis=1, keepdims=True)
    t1 = jnp.sum(jnp.where(low, 0.0, every), axis=1, keepdims=True)
    total = jnp.where(low, t0, t1)
    for shift, p in enumerate(ps):
        source = lax.rem(col + nk - shift, nk)
        weight = p / total
        rolled = pltpu.roll(weight, tile, 1)
        for n in range(pieces):
            w_ref[source, :, 2 * n, :] = weight[n * heads : (n + 1) * heads]
            w_ref[source, :, 2 * n + 1, :] = rolled[n * heads : (n + 1) * heads]
    w = jnp.concatenate(
        [
            w_ref[k].reshape(heads * tokens, wide)[:, :tile]
            for k in range(nk)
        ],
        axis=1,
    ).astype(bf16)

    owner = lax.broadcasted_iota(jnp.int32, (tokens, chans), 1) // head_width

    def one(s, carry):
        full = nn_dot(w, v_ref[s])
        for e in range(2):
            cut = slice(e * chans, (e + 1) * chans)
            mean = jnp.zeros((tokens, chans), f32)
            for h in range(heads):
                mean = jnp.where(owner == h, full[h * tokens : (h + 1) * tokens, cut], mean)
            at = pl.ds(pl.multiple_of((e * half + s) * tokens, tokens), tokens)
            gated_ref[at, :] = (gate_ref[at, :] * mean).astype(bf16)
        return carry

    lax.fori_loop(0, half, one, 0, unroll=4)
    out_ref[...] = (x_ref[...].astype(f32) + nt_dot(gated_ref[...], wf_ref[...])).astype(bf16)


def on_device(
    counts,
    alignment_input,
    pair_input,
    token_valid_mask,
    first_factor_weights,
    second_factor_weights,
    content_weights_grid,
    sigmoid_weights_grid,
    outer_matrix,
    score_matrix,
    final_mixing_weights,
    adjoint_of_rowset,
):
    nq, nr, nk = counts
    row_index = lax.axis_index("row")
    col_index = lax.axis_index("col")
    seqs, tokens, width = alignment_input.shape
    tile_i, tile_j, z = pair_input.shape
    fc = first_factor_weights.shape[1]
    fd = second_factor_weights.shape[1]
    heads = score_matrix.shape[1]
    chans = content_weights_grid.shape[1]
    groups = tile_i // pack
    lanes = pack * tile_j
    sds = jax.ShapeDtypeStruct

    mask = token_valid_mask.reshape(1, -1)
    own_start = ((row_index * nk + col_index) * tokens).astype(jnp.int32).reshape(1)
    seq_index = lax.axis_index("seq")
    place = tuple(x.astype(jnp.int32).reshape(1) for x in (row_index, col_index, seq_index))
    col_scalar = col_index.astype(jnp.int32).reshape(1)
    half = seqs // 2

    l_rows = tokens // pack * fc
    r_rows = fd * tokens // 128 * seqs
    n_rows = half * tokens
    shard, right, normed, weights = call(
        prepare_kernel,
        (
            sds((l_rows + 2 * n_rows, 128), bf16),
            sds((r_rows, 128), bf16),
            sds((n_rows, 128), bf16),
            sds((width, 3 * chans), bf16),
        ),
        scratch=(
            pltpu.VMEM((tokens, seqs, width), f32),
            pltpu.VMEM((fd * tokens // 128, seqs, 128), f32),
        ),
        smem=1,
        vmem=60 * 1024 * 1024,
    )(
        own_start,
        alignment_input,
        adjoint_of_rowset,
        first_factor_weights.T,
        second_factor_weights.T,
        mask,
        content_weights_grid,
        sigmoid_weights_grid,
        final_mixing_weights.T,
    )

    def exchange(x, bit):
        return lax.ppermute(x, "col", [(c, c ^ bit) for c in range(nk)])

    def exchange_rows(x, bit):
        return lax.ppermute(x, "row", [(r, r ^ bit) for r in range(nr)])

    rights = [
        lax.ppermute(
            right,
            ("row", "col"),
            [(r * nk + c, (c + t) % nr * nk + r) for r in range(nr) for c in range(nk)],
        )
        for t in range(nr)
    ]
    across, beyond = exchange(shard, 2), exchange_rows(normed, 2)
    across, beyond, *rights = lax.optimization_barrier((across, beyond, *rights))
    all_rows = [shard, exchange(shard, 1), across, exchange(across, 1)]
    norms = [normed, exchange_rows(normed, 1), beyond, exchange_rows(beyond, 1)]

    sides, block, *all_cols = call(
        join_kernel,
        (
            sds((nk * (r_rows + l_rows), 128), bf16),
            sds((nr, n_rows, 2 * width), bf16),
        )
        + (sds((n_rows, 2 * width), bf16),) * nk,
        smem=2,
    )(*place[:2], *all_rows, *rights, *norms)
    all_cols = all_cols[:1] + [exchange(all_cols[t], t) for t in range(1, nk)]
    if nq == 2:
        far_sides = lax.ppermute(sides, "seq", [(0, 1), (1, 0)])
    else:
        far_sides = lax.all_gather(sides, "seq", axis=0, tiled=True)

    head_lanes = seqs * chans // heads
    (gw_own,) = call(
        weights_kernel,
        (sds((groups, heads, lanes), f32),),
        scratch=(
            pltpu.VMEM((heads * tile_i, 2 * tile_j), f32),
            pltpu.VMEM((4 * width, 4 * chans), bf16),
            pltpu.VMEM((4 * width, 4 * chans), bf16),
            pltpu.VMEM((4 * width, 4 * chans), bf16),
            pltpu.VMEM((nk, 2, half, tokens, 2 * width), bf16),
            pltpu.VMEM((nk, half, tokens, 2 * width), bf16),
            pltpu.VMEM((heads, tile_i, head_lanes), bf16),
            pltpu.VMEM((heads, 2 * tile_j, head_lanes), bf16),
        ),
        smem=1,
        flops=3_000_000_000,
        nbytes=3_000_000,
    )(col_scalar, *all_rows, *all_cols, weights)
    if nq == 2:
        gw_other = lax.ppermute(gw_own, "seq", [(0, 1), (1, 0)])
    else:
        gw_own, gw_other = lax.psum(gw_own, "seq"), jnp.zeros_like(gw_own)

    block, _ = lax.optimization_barrier((block, gw_own))
    close, remote = exchange(block, 1), exchange(block, 2)

    pair_out, normal, inverse, logits = call(
        update_kernel,
        (
            sds((tile_i * tile_j, z), bf16),
            sds((groups, z, lanes), f32),
            sds((groups, 8, lanes), f32),
            sds((groups, heads, lanes), f32),
        ),
        scratch=(
            pltpu.VMEM((tile_i * tile_j, z), bf16),
            pltpu.SemaphoreType.DMA((groups // 4,)),
            pltpu.VMEM((nk, nq * r_rows, 128), bf16),
            pltpu.VMEM((fd, nq * seqs, 4 * tile_j), bf16),
            pltpu.VMEM((groups * fc, nq * pack * seqs), bf16),
            pltpu.VMEM((2 * z, fd * fc), bf16),
            pltpu.VMEM((groups // 4, fd * fc, 4 * lanes), bf16),
            pltpu.VMEM((groups // 4, fd * fc, 4 * lanes), bf16),
            pltpu.VMEM((z, 4 * lanes), f32),
        ),
        smem=2,
        flops=14_000_000_000,
        nbytes=5_000_000,
        vmem=44 * 1024 * 1024,
        far=(4, 5, 6, 7),
        far_out=(0,),
    )(
        *place[1:],
        sides,
        far_sides,
        mask,
        outer_matrix,
        score_matrix.T,
        pair_input.reshape(tile_i * tile_j, z),
    )

    payload = sds((2 + groups // nk * (pack // 2), heads, 2 * tile_j), f32)
    gw, pay0, pay1, pay2, pay3 = call(
        softmax_kernel,
        (sds((groups, heads, lanes), f32), payload, payload, payload, payload),
        smem=1,
    )(col_scalar, logits, gw_own, gw_other, mask)

    got = [
        lax.ppermute(pay, "col", [(c, (c + shift) % nk) for c in range(nk)])
        for shift, pay in ((1, pay1), (2, pay2), (3, pay3))
    ]


    close, remote, pay0 = lax.optimization_barrier((close, remote, pay0))
    every = [block, close, remote, exchange(remote, 1)]
    values, gating = call(
        values_kernel,
        (sds((half, nr * nk * tokens, 2 * chans), bf16), sds((seqs * tokens, chans), f32)),
        scratch=(pltpu.VMEM((nk, nr, n_rows, 2 * width), bf16),),
        smem=1,
        flops=4_000_000_000,
        nbytes=6_000_000,
    )(col_scalar, *every, content_weights_grid, normed, sigmoid_weights_grid)

    got, values, gating = lax.optimization_barrier((got, values, gating))

    (gradient,) = call(
        gradient_kernel,
        (sds((tile_i * tile_j, z), bf16),),
        scratch=(
            pltpu.VMEM((groups * heads, groups * heads), f32),
            pltpu.VMEM((tile_i * tile_j, z), bf16),
            pltpu.SemaphoreType.DMA((groups // 4,)),
        ),
        far_out=(0,),
        flops=4_000_000_000,
        nbytes=3_000_000,
    )(pay0, *got, logits, gw, normal, inverse, score_matrix.T)

    (aligned,) = call(
        alignment_kernel,
        (sds((seqs * tokens, width), bf16),),
        scratch=(
            pltpu.VMEM((nk, heads, tokens, 2 * tile_j), f32),
            pltpu.VMEM((seqs * tokens, chans), bf16),
        ),
        smem=1,
        flops=3_000_000_000,
        nbytes=5_000_000,
    )(
        col_scalar,
        pay0,
        *got,
        values,
        gating,
        alignment_input.reshape(seqs * tokens, width),
        final_mixing_weights.T,
    )
    return (
        aligned.reshape(seqs, tokens, width),
        pair_out.reshape(tile_i, tile_j, z),
        gradient.reshape(tile_i, tile_j, z),
    )


def solution(mesh):
    counts = (mesh.shape["seq"], mesh.shape["row"], mesh.shape["col"])
    in_specs = (
        P("seq", ("row", "col"), None),
        P("row", "col", None),
        P(),
        P(),
        P(),
        P(),
        P(),
        P(),
        P(),
        P(),
        P("seq", ("row", "col"), None),
    )
    out_specs = (P("seq", ("row", "col"), None), P("row", "col", None), P("row", "col", None))
    return jax.shard_map(
        functools.partial(on_device, counts),
        mesh=mesh,
        in_specs=in_specs,
        out_specs=out_specs,
        check_vma=False,
    )
```

```python
import functools

import jax
import jax.numpy as jnp
from jax import lax
from jax.experimental import pallas as pl
from jax.experimental.pallas import tpu as pltpu
from jax.sharding import PartitionSpec as P

epsilon = 1e-05
far_below = -1e30
vmem_bytes = 32 * 1024 * 1024
pack = 4

f32 = jnp.float32
bf16 = jnp.bfloat16


def nt_dot(a, b):
    return lax.dot_general(a, b, (((1,), (1,)), ((), ())), preferred_element_type=f32)


def nn_dot(a, b):
    return jnp.dot(a, b, preferred_element_type=f32)


def high_low(x):
    high = x.astype(bf16)
    return high, (x - high.astype(f32)).astype(bf16)


def call(
    kernel, out_shape, scratch=(), smem=0, flops=0, nbytes=0, vmem=vmem_bytes, far=(), far_out=()
):
    def run(*args):
        count = len(args)
        in_specs = [
            pl.BlockSpec(memory_space=pltpu.SMEM if n < smem else pltpu.VMEM) for n in range(count)
        ]
        for n in far:
            in_specs[n] = pl.BlockSpec(memory_space=pltpu.HBM)
        landing = [pltpu.VMEM(args[n].shape, args[n].dtype) for n in far]
        if far:
            landing.append(pltpu.SemaphoreType.DMA((len(far),)))

        def body(*refs):
            inputs = list(refs[:count])
            extra = refs[len(refs) - len(landing) :]
            rest = refs[count : len(refs) - len(landing)]
            copies = []
            for i, n in enumerate(far):
                copies.append(pltpu.make_async_copy(inputs[n], extra[i], extra[-1].at[i]))
                copies[-1].start()
                inputs[n] = extra[i]

            def ready():
                for copy in copies:
                    copy.wait()

            kernel(ready, *inputs, *rest)

        return pl.pallas_call(
            body,
            out_shape=out_shape,
            in_specs=in_specs,
            out_specs=[
                pl.BlockSpec(memory_space=pltpu.HBM if n in far_out else pltpu.VMEM)
                for n in range(len(out_shape))
            ],
            scratch_shapes=list(scratch) + landing,
            compiler_params=pltpu.CompilerParams(vmem_limit_bytes=vmem),
            cost_estimate=pl.CostEstimate(flops=flops, bytes_accessed=nbytes, transcendentals=0),
        )(*args)

    return run


def valid_count(mask_ref):
    return jnp.sum(mask_ref[...].astype(f32), axis=1, keepdims=True)


def column_mask(mask_ref, col, tile, copies):
    lane = lax.broadcasted_iota(jnp.int32, (1, copies * tile), 1)
    token = (lax.rem(lane, tile) + col * tile).astype(f32)
    return (token < valid_count(mask_ref)).astype(f32)


def twice(w):
    none = jnp.zeros_like(w)
    return jnp.concatenate(
        [jnp.concatenate([w, none], axis=1), jnp.concatenate([none, w], axis=1)], axis=0
    )


def prepare_kernel(
    ready,
    own_ref,
    x_ref,
    adj_ref,
    w1_ref,
    w2_ref,
    mask_ref,
    wv_ref,
    wg_ref,
    wf_ref,
    shard_ref,
    norm_ref,
    weights_ref,
    turn_ref,
    place_ref,
):
    chans = wv_ref.shape[1]
    weights_ref[:, :chans] = wv_ref[...]
    weights_ref[:, chans : 2 * chans] = wg_ref[...]
    weights_ref[:, 2 * chans :] = wf_ref[...]
    seqs, tokens, width = x_ref.shape
    half = seqs // 2
    fd = w2_ref.shape[0]
    x = x_ref[...].astype(f32)
    center = x - jnp.mean(x, axis=-1, keepdims=True)
    inverse = lax.rsqrt(jnp.mean(center * center, axis=-1, keepdims=True) + epsilon)
    normed = center * inverse
    rows = half * tokens
    adj = adj_ref[...].astype(f32)

    def two(x):
        x = jnp.concatenate([x[:half], x[half:]], axis=-1)
        return x.reshape(rows, 2 * width).astype(bf16)

    packed = two(normed)
    norm_ref[...] = packed
    base = tokens // pack * w1_ref.shape[0]
    shard_ref[base : base + rows, :] = two(adj)
    shard_ref[base + rows : base + 2 * rows, :] = packed
    token = lax.broadcasted_iota(jnp.int32, (seqs, tokens, width), 1) + own_ref[0]
    count = valid_count(mask_ref).reshape(1, 1, 1)
    real = jnp.where(token.astype(f32) < count, normed, 0.0)
    for s in range(seqs):
        turn_ref[:, s, :] = real[s]
    turned = turn_ref[...].astype(bf16).reshape(tokens * seqs, width)
    left = nt_dot(w1_ref[...], turned).astype(bf16)
    fc = w1_ref.shape[0]
    wk = pack * seqs
    for g in range(tokens // pack):
        shard_ref[g * fc : (g + 1) * fc, :] = left[:, g * wk : (g + 1) * wk]
    size = 128 // tokens
    real = real.astype(bf16)
    w2 = w2_ref[...]
    d = lax.broadcasted_iota(jnp.int32, (fd, 128), 0)
    lane = lax.broadcasted_iota(jnp.int32, (fd, 128), 1)
    mine = lax.rem(d, size) == lane // tokens
    for s in range(seqs):
        res = nt_dot(w2, jnp.concatenate([real[s]] * size, axis=0))
        res = jnp.where(mine, res, 0.0).reshape(fd // size, size, 128)
        place_ref[:, s, :] = jnp.sum(res, axis=1)
    right = place_ref[...].reshape(fd // size * seqs, 128).astype(bf16)
    shard_ref[base + 2 * rows :, :] = right


def join_kernel(
    ready,
    row_ref,
    col_ref,
    shard0_ref,
    shard1_ref,
    shard2_ref,
    shard3_ref,
    right0_ref,
    right1_ref,
    out_ref,
):
    nk = 4
    row, col = row_ref[0], col_ref[0]
    size = out_ref.shape[0] // (2 * nk)
    for t in range(nk):
        ref = (right0_ref, right1_ref)[t // 2]
        at = pl.ds(pl.multiple_of(jnp.bitwise_xor(row, t) * size, size), size)
        out_ref[at, :] = ref[t % 2 * size : (t % 2 + 1) * size, :]
    for t, ref in enumerate((shard0_ref, shard1_ref, shard2_ref, shard3_ref)):
        at = pl.ds(pl.multiple_of((nk + jnp.bitwise_xor(col, t)) * size, size), size)
        out_ref[at, :] = ref[:size, :]


def update_kernel(
    ready,
    col_ref,
    seq_ref,
    sides_ref,
    far_sides_ref,
    mask_ref,
    m_ref,
    score_ref,
    pair_ref,
    pout_hbm,
    normal_ref,
    inverse_ref,
    logits_ref,
    pout_ref,
    out_sem,
    rk_ref,
    rab_ref,
    lm_ref,
    mt_ref,
    oh_ref,
    ol_ref,
    update_ref,
):
    nk = rk_ref.shape[0]
    width_d, pair_rows, _ = rab_ref.shape
    col, seq = col_ref[0], seq_ref[0]
    z = pair_ref.shape[1]
    groups, heads, lanes = logits_ref.shape
    tile_j = lanes // pack
    tokens = tile_j // nk
    fc = lm_ref.shape[0] // groups
    seqs = 128 // pack
    nq = pair_rows // seqs
    wk = pack * seqs

    r_rows = rk_ref.shape[1] // nq
    l_rows = groups * fc
    if nq == 2:
        sources = ((seq, 0, sides_ref), (1 - seq, 0, far_sides_ref))
    else:
        sources = tuple((q, q, far_sides_ref) for q in range(nq))
    for q, slot, ref in sources:
        base = slot * (nk * r_rows + l_rows)
        at = pl.ds(pl.multiple_of(q * r_rows, r_rows), r_rows)
        for k in range(nk):
            rk_ref[k, at, :] = ref[base + k * r_rows : base + (k + 1) * r_rows, :]
        base = base + nk * r_rows
        to = pl.ds(pl.multiple_of(q * wk, wk), wk)
        lm_ref[:, to] = ref[base : base + l_rows, :]
    size = 128 // tokens
    right = jnp.concatenate([rk_ref[k] for k in range(nk)], axis=1)
    source = lax.broadcasted_iota(jnp.int32, (nk * 128, 4 * tile_j), 0)
    target = lax.broadcasted_iota(jnp.int32, (nk * 128, 4 * tile_j), 1)
    used = jnp.logical_or(target < tile_j, target >= 3 * tile_j)
    j = lax.rem(target, tile_j)
    offset = jnp.where(used, source - (j // tokens * 128 + lax.rem(j, tokens)), -1)
    blocks = width_d // size
    for e in range(size):
        pick = jnp.where(offset == e * tokens, 1.0, 0.0).astype(bf16)
        res = nn_dot(right, pick).astype(bf16)
        for q in range(nq):
            for n in range(blocks):
                at = (q * blocks + n) * seqs
                rab_ref[n * size + e, q * seqs : (q + 1) * seqs, :] = res[at : at + seqs]

    chunk = 8
    many = 4
    wide = oh_ref.shape[2] // lanes
    empty = jnp.zeros((seqs, 2 * tile_j), bf16)

    def block_of(d):
        rows = []
        for q in range(nq):
            both = rab_ref[d, q * seqs : (q + 1) * seqs, :]
            part = both[:, : 2 * tile_j], both[:, 2 * tile_j :]
            for i in range(pack):
                pieces = [empty] * (pack // 2)
                pieces[i // 2] = part[i % 2]
                rows.append(jnp.concatenate(pieces, axis=1))
        return jnp.concatenate(rows, axis=0)

    def outer_of(n, carry):
        block = jnp.concatenate([block_of(many * n + e) for e in range(many)], axis=1)
        for m in range(groups // chunk):
            out = nn_dot(lm_ref[m * chunk * fc : (m + 1) * chunk * fc, :], block)
            high, low = high_low(out)
            for e in range(many):
                at = pl.ds(pl.multiple_of((many * n + e) * fc, fc), fc)
                for g in range(chunk):
                    group = m * chunk + g
                    to = slice(group % wide * lanes, (group % wide + 1) * lanes)
                    cut = slice(g * fc, (g + 1) * fc), slice(e * lanes, (e + 1) * lanes)
                    oh_ref[group // wide, at, to] = high[cut]
                    ol_ref[group // wide, at, to] = low[cut]
        return carry

    lax.fori_loop(0, width_d // many, outer_of, 0)

    ready()
    some = z // fc
    for n in range(width_d // some):
        block = jnp.concatenate(
            [m_ref[pl.ds(n * some + e, fc, stride=width_d), :] for e in range(some)], axis=0
        ).T
        high, low = high_low(block)
        mt_ref[:z, n * z : (n + 1) * z] = high
        mt_ref[z:, n * z : (n + 1) * z] = low
    maskj = column_mask(mask_ref, col, tile_j, 2)

    maskl = jnp.concatenate([maskj] * (pack // 2), axis=1) > 0
    score = score_ref[...]
    s1 = score.astype(bf16).astype(f32)
    s2 = (score - s1).astype(bf16).astype(f32)
    s3 = score - s1 - s2
    none = jnp.zeros_like(s1)
    st = jnp.concatenate(
        [
            jnp.concatenate([s1, s2, s3, none], axis=0),
            jnp.concatenate([s1, s2, none, none], axis=0),
        ],
        axis=1,
    ).astype(bf16)

    def finish(n, carry):
        two = nn_dot(mt_ref[...], oh_ref[n])
        update_ref[...] = two[:z] + two[z:] + nn_dot(mt_ref[:z, :], ol_ref[n])
        for e in range(wide):
            g = n * wide + e
            at = pl.ds(pl.multiple_of(g * lanes, lanes), lanes)
            before = pair_ref[at, :].T.astype(f32)
            result = (before + update_ref[:, e * lanes : (e + 1) * lanes]).astype(bf16)
            x = result.astype(f32)
            pout_ref[at, :] = result.T
            center = x - jnp.mean(x, axis=0, keepdims=True)
            inverse = lax.rsqrt(jnp.mean(center * center, axis=0, keepdims=True) + epsilon)
            normal = center * inverse
            normal_ref[g] = normal
            inverse_ref[g] = jnp.broadcast_to(inverse, inverse_ref.shape[1:])
            high, low = high_low(normal)
            scores = nn_dot(st, jnp.concatenate([high, low], axis=0))
            logits = scores[:heads] + scores[heads : 2 * heads] + scores[2 * heads : 3 * heads]
            logits_ref[g] = jnp.where(maskl, logits, far_below)
        at = pl.ds(pl.multiple_of(n * wide * lanes, wide * lanes), wide * lanes)
        pltpu.make_async_copy(pout_ref.at[at], pout_hbm.at[at], out_sem.at[n]).start()
        return carry

    lax.fori_loop(0, groups // wide, finish, 0)
    for n in range(groups // wide):
        at = pl.ds(n * wide * lanes, wide * lanes)
        pltpu.make_async_copy(pout_ref.at[at], pout_hbm.at[at], out_sem.at[n]).wait()


def by_heads(w, heads, out_ref):
    width, chans = w.shape
    hw = chans // heads
    block = 4 * hw
    slot = lax.broadcasted_iota(jnp.int32, (width, block), 1) // hw
    w = w.astype(f32)
    for t in range(chans // block):
        part = w[:, t * block : (t + 1) * block]
        turns = [part] + [pltpu.roll(part, n * hw, 1) for n in range(1, 4)]
        for e in range(4):
            h = t * 4 + e
            for s in range(4):
                out_ref[s * width : (s + 1) * width, h * block : (h + 1) * block] = jnp.where(
                    slot == s, turns[(s - e) % 4], 0.0
                ).astype(bf16)


def weights_kernel(
    ready,
    row_ref,
    col_ref,
    side0_ref,
    side1_ref,
    side2_ref,
    side3_ref,
    cols0_ref,
    cols1_ref,
    weights_ref,
    gw_ref,
    cols_ref,
    acc_ref,
    bv_ref,
    bg_ref,
    bf_ref,
    rows_ref,
    gs_ref,
    vs_ref,
):
    nk, half, tokens, _ = cols_ref.shape
    tile = nk * tokens
    groups, heads, lanes = gw_ref.shape
    row, col = row_ref[0], col_ref[0]
    count = half * tokens
    size = (side0_ref.shape[0] - 2 * count) // 2
    for t, ref in enumerate((side0_ref, side1_ref, side2_ref, side3_ref)):
        k = jnp.bitwise_xor(col, t)
        rows_ref[k] = ref[size : size + 2 * count, :].reshape(rows_ref.shape[1:])
    for t in range(nk):
        ref = (cols0_ref, cols1_ref)[t // 2]
        part = ref[t % 2 * count : (t % 2 + 1) * count, :]
        cols_ref[jnp.bitwise_xor(row, t)] = part.reshape(cols_ref.shape[1:])
    chans = weights_ref.shape[1] // 3
    by_heads(weights_ref[:, :chans], heads, bv_ref)
    by_heads(weights_ref[:, chans : 2 * chans], heads, bg_ref)
    by_heads(weights_ref[:, 2 * chans :], heads, bf_ref)
    block = bv_ref.shape[1] // heads

    def four(read, n):
        return jnp.concatenate(
            [
                jnp.concatenate(
                    [
                        jnp.concatenate([read(k, 2 * (2 * n + e) + p) for k in range(nk)], axis=0)
                        for p in range(2)
                    ],
                    axis=1,
                )
                for e in range(2)
            ],
            axis=0,
        )

    for hp in range(heads // 2):
        cut = slice(hp * 2 * block, (hp + 1) * 2 * block)
        for n in range(half // 4):
            v = nn_dot(four(lambda k, s: cols_ref[k, s], n), bv_ref[:, cut]).astype(bf16)
            gate = nn_dot(four(lambda k, s: rows_ref[k, 1, s], n), bg_ref[:, cut])
            grad = nn_dot(four(lambda k, s: rows_ref[k, 0, s], n), bf_ref[:, cut])
            g = (grad * jax.nn.sigmoid(gate)).astype(bf16)
            for e in range(2):
                to = slice((2 * n + e) * block, (2 * n + e + 1) * block)
                for o in range(2):
                    mine = slice(o * block, (o + 1) * block)
                    ve = v[e * tile : (e + 1) * tile, mine]
                    vs_ref[2 * hp + o, :tile, to] = ve
                    vs_ref[2 * hp + o, tile:, to] = ve
                    gs_ref[2 * hp + o, :, to] = g[e * tile : (e + 1) * tile, mine]
    for h in range(heads):
        acc_ref[h * tile : (h + 1) * tile, :] = nt_dot(gs_ref[h], vs_ref[h])

    first = lax.broadcasted_iota(jnp.int32, (groups, 2 * tile), 1) < tile
    for h in range(heads):
        for part in range(pack // 2):
            a = acc_ref[pl.ds(h * tile + 2 * part, groups, stride=pack), :]
            b = acc_ref[pl.ds(h * tile + 2 * part + 1, groups, stride=pack), :]
            gw_ref[:, h, part * 2 * tile : (part + 1) * 2 * tile] = jnp.where(first, a, b)


def softmax_kernel(
    ready,
    col_ref,
    logits_ref,
    gwa_ref,
    gwb_ref,
    mask_ref,
    gw_ref,
    own_ref,
    pay1_ref,
    pay2_ref,
    pay3_ref,
):
    groups, heads, lanes = logits_ref.shape
    tile = lanes // pack
    nk = 4
    rows = groups * heads
    col = col_ref[0]
    gw_ref[...] = gwa_ref[...] + gwb_ref[...]
    lane = lax.broadcasted_iota(jnp.int32, (rows, 2 * tile), 1)
    low = lane < tile
    maskj = column_mask(mask_ref, col, tile, 2)
    stats = jnp.zeros((rows, 2 * tile), f32)
    for part in range(pack // 2):
        cut = slice(part * 2 * tile, (part + 1) * 2 * tile)
        lg = logits_ref[:, :, cut].reshape(rows, 2 * tile)
        gw = gw_ref[:, :, cut].reshape(rows, 2 * tile)
        m0 = jnp.max(jnp.where(low, lg, far_below), axis=1, keepdims=True)
        m1 = jnp.max(jnp.where(low, far_below, lg), axis=1, keepdims=True)
        p = jnp.exp(lg - jnp.where(low, m0, m1)) * maskj
        pg = p * gw
        for e, m in ((0, m0), (1, m1)):
            mine = low if e == 0 else jnp.logical_not(low)
            i = 2 * part + e
            total = jnp.sum(jnp.where(mine, p, 0.0), axis=1, keepdims=True)
            inner = jnp.sum(jnp.where(mine, pg, 0.0), axis=1, keepdims=True)
            stats = jnp.where(lane == i, m, stats)
            stats = jnp.where(lane == pack + i, total, stats)
            stats = jnp.where(lane == 2 * pack + i, inner, stats)
    turned = stats.T[:16]
    per = groups // nk
    for shift, pay in enumerate((own_ref, pay1_ref, pay2_ref, pay3_ref)):
        dest = lax.rem(col + shift, nk)
        pay[0] = turned[:8]
        pay[1] = turned[8:]
        for g in range(per):
            piece = logits_ref[dest * per + g]
            for part in range(pack // 2):
                pay[2 + g * (pack // 2) + part] = piece[:, part * 2 * tile : (part + 1) * 2 * tile]


def values_kernel(
    ready, col_ref, ev0_ref, ev1_ref, ev2_ref, ev3_ref, wv_ref, norm_ref, wg_ref, v_ref, gate_ref, ev_ref
):
    nr, nk, half, tokens, wide = ev_ref.shape
    chans = wv_ref.shape[1]
    for t, ref in enumerate((ev0_ref, ev1_ref, ev2_ref, ev3_ref)):
        ev_ref[jnp.bitwise_xor(col_ref[0], t)] = ref[...]
    gate = jax.nn.sigmoid(nn_dot(norm_ref[...], twice(wg_ref[...])))
    gate_ref[: half * tokens] = gate[:, :chans]
    gate_ref[half * tokens :] = gate[:, chans:]
    wv = twice(wv_ref[...])
    for s in range(half):
        x = jnp.concatenate([ev_ref[r, k, s] for r in range(nr) for k in range(nk)], axis=0)
        v_ref[s] = nn_dot(x, wv).astype(bf16)


def gradient_kernel(
    ready,
    own_ref, r1_ref, r2_ref, r3_ref, logits_ref, gw_ref, normal_ref, inverse_ref, score_ref, out_hbm, stat_ref, out_ref, out_sem
):
    groups, heads, lanes = logits_ref.shape
    rows = groups * heads
    score = score_ref[...]
    z = score.shape[1]
    s1 = score.astype(bf16).astype(f32)
    s2 = (score - s1).astype(bf16).astype(f32)
    s3 = score - s1 - s2
    parts = [s1, s1, s1, s2, s2, s3, jnp.zeros((z - 6 * heads, z), f32)]
    sk = jnp.concatenate(parts, axis=0).T[:, : 6 * heads].astype(bf16)
    pays = (own_ref, r1_ref, r2_ref, r3_ref)
    ms = [p[0][:pack] for p in pays]
    ls = [p[0][pack : 2 * pack] for p in pays]
    ns = [p[1][:pack] for p in pays]
    top = functools.reduce(jnp.maximum, ms)
    scales = [jnp.exp(m - top) for m in ms]
    total = sum(a * b for a, b in zip(ls, scales))
    inner = sum(a * b for a, b in zip(ns, scales)) / total
    stacked = jnp.concatenate([top, total, inner, jnp.zeros((rows - 3 * pack, rows), f32)], axis=0)
    stat_ref[...] = stacked.T

    tile = lanes // pack
    low = lax.broadcasted_iota(jnp.int32, (heads, 2 * tile), 1) < tile

    def one(g):
        st = stat_ref[pl.ds(pl.multiple_of(g * heads, heads), heads), :]

        def spread(base):
            halves = [
                jnp.where(
                    low,
                    st[:, base + 2 * half : base + 2 * half + 1],
                    st[:, base + 2 * half + 1 : base + 2 * half + 2],
                )
                for half in range(pack // 2)
            ]
            return jnp.concatenate(halves, axis=1)

        prob = jnp.exp(logits_ref[g] - spread(0)) / spread(pack)
        gl = prob * (gw_ref[g] - spread(2 * pack))
        g1 = gl.astype(bf16).astype(f32)
        g2 = (gl - g1).astype(bf16).astype(f32)
        g3 = gl - g1 - g2
        stack = jnp.concatenate([g1, g2, g3, g1, g2, g1], axis=0).astype(bf16)
        grad = nn_dot(sk, stack)
        normal = normal_ref[g]
        inverse = inverse_ref[g][:1]
        centered = grad - jnp.mean(grad, axis=0, keepdims=True)
        along = jnp.mean(grad * normal, axis=0, keepdims=True)
        result = inverse * (centered - normal * along)
        out_ref[pl.ds(pl.multiple_of(g * lanes, lanes), lanes), :] = result.astype(bf16).T

    many = 4

    def some(n, carry):
        for e in range(many):
            one(n * many + e)
        at = pl.ds(pl.multiple_of(n * many * lanes, many * lanes), many * lanes)
        pltpu.make_async_copy(out_ref.at[at], out_hbm.at[at], out_sem.at[n]).start()
        return carry

    lax.fori_loop(0, groups // many, some, 0)
    for n in range(groups // many):
        at = pl.ds(n * many * lanes, many * lanes)
        pltpu.make_async_copy(out_ref.at[at], out_hbm.at[at], out_sem.at[n]).wait()


def alignment_kernel(
    ready,
    col_ref,
    own_ref,
    r1_ref,
    r2_ref,
    r3_ref,
    v_ref,
    gate_ref,
    x_ref,
    wf_ref,
    out_ref,
    w_ref,
    gated_ref,
):
    pays = (own_ref, r1_ref, r2_ref, r3_ref)
    nk = len(pays)
    heads = own_ref.shape[1]
    wide = own_ref.shape[2]
    tile = wide // 2
    pieces = own_ref.shape[0] - 2
    rows = pieces * heads
    half, all_tokens, chans = v_ref.shape
    chans = chans // 2
    tokens = pieces * 2
    head_width = chans // heads
    col = col_ref[0]

    low = lax.broadcasted_iota(jnp.int32, (rows, wide), 1) < tile
    lgs = [p[2:].reshape(rows, wide) for p in pays]
    peak = functools.reduce(jnp.maximum, lgs)
    m0 = jnp.max(jnp.where(low, peak, far_below), axis=1, keepdims=True)
    m1 = jnp.max(jnp.where(low, far_below, peak), axis=1, keepdims=True)
    top = jnp.where(low, m0, m1)
    ps = [jnp.exp(lg - top) for lg in lgs]
    every = sum(ps)
    t0 = jnp.sum(jnp.where(low, every, 0.0), axis=1, keepdims=True)
    t1 = jnp.sum(jnp.where(low, 0.0, every), axis=1, keepdims=True)
    total = jnp.where(low, t0, t1)
    for shift, p in enumerate(ps):
        source = lax.rem(col + nk - shift, nk)
        weight = p / total
        rolled = pltpu.roll(weight, tile, 1)
        for n in range(pieces):
            w_ref[source, :, 2 * n, :] = weight[n * heads : (n + 1) * heads]
            w_ref[source, :, 2 * n + 1, :] = rolled[n * heads : (n + 1) * heads]
    w = jnp.concatenate(
        [
            w_ref[k].reshape(heads * tokens, wide)[:, :tile]
            for k in range(nk)
        ],
        axis=1,
    ).astype(bf16)

    owner = lax.broadcasted_iota(jnp.int32, (tokens, chans), 1) // head_width

    def one(s, carry):
        full = nn_dot(w, v_ref[s])
        for e in range(2):
            cut = slice(e * chans, (e + 1) * chans)
            mean = jnp.zeros((tokens, chans), f32)
            for h in range(heads):
                mean = jnp.where(owner == h, full[h * tokens : (h + 1) * tokens, cut], mean)
            at = pl.ds(pl.multiple_of((e * half + s) * tokens, tokens), tokens)
            gated_ref[at, :] = (gate_ref[at, :] * mean).astype(bf16)
        return carry

    lax.fori_loop(0, half, one, 0, unroll=4)
    out_ref[...] = (x_ref[...].astype(f32) + nt_dot(gated_ref[...], wf_ref[...])).astype(bf16)


def on_device(
    counts,
    alignment_input,
    pair_input,
    token_valid_mask,
    first_factor_weights,
    second_factor_weights,
    content_weights_grid,
    sigmoid_weights_grid,
    outer_matrix,
    score_matrix,
    final_mixing_weights,
    adjoint_of_rowset,
):
    nq, nr, nk = counts
    row_index = lax.axis_index("row")
    col_index = lax.axis_index("col")
    seqs, tokens, width = alignment_input.shape
    tile_i, tile_j, z = pair_input.shape
    fc = first_factor_weights.shape[1]
    fd = second_factor_weights.shape[1]
    heads = score_matrix.shape[1]
    chans = content_weights_grid.shape[1]
    groups = tile_i // pack
    lanes = pack * tile_j
    sds = jax.ShapeDtypeStruct

    mask = token_valid_mask.reshape(1, -1)
    own_start = ((row_index * nk + col_index) * tokens).astype(jnp.int32).reshape(1)
    seq_index = lax.axis_index("seq")
    place = tuple(x.astype(jnp.int32).reshape(1) for x in (row_index, col_index, seq_index))
    col_scalar = col_index.astype(jnp.int32).reshape(1)
    half = seqs // 2

    l_rows = tokens // pack * fc
    r_rows = fd * tokens // 128 * seqs
    n_rows = half * tokens
    shard, normed, weights = call(
        prepare_kernel,
        (
            sds((l_rows + 2 * n_rows + r_rows, 128), bf16),
            sds((n_rows, 128), bf16),
            sds((width, 3 * chans), bf16),
        ),
        scratch=(
            pltpu.VMEM((tokens, seqs, width), f32),
            pltpu.VMEM((fd * tokens // 128, seqs, 128), f32),
        ),
        smem=1,
        vmem=60 * 1024 * 1024,
    )(
        own_start,
        alignment_input,
        adjoint_of_rowset,
        first_factor_weights.T,
        second_factor_weights.T,
        mask,
        content_weights_grid,
        sigmoid_weights_grid,
        final_mixing_weights.T,
    )

    def exchange(x, bit):
        return lax.ppermute(x, "col", [(c, c ^ bit) for c in range(nk)])

    def to_columns(start, size):
        pair = jnp.concatenate([x[start : start + size] for x in (shard, other)], axis=0)
        return [
            lax.ppermute(
                pair,
                ("row", "col"),
                [(r * nk + c, (c ^ flip) * nk + r) for r in range(nr) for c in range(nk)],
            )
            for flip in (0, 2)
        ]

    other, across = exchange(shard, 1), exchange(shard, 2)
    rights = to_columns(l_rows + 2 * n_rows, r_rows)
    across, *rights = lax.optimization_barrier((across, *rights))
    all_rows = [shard, other, across, exchange(across, 1)]
    all_cols = to_columns(l_rows + n_rows, n_rows)

    (sides,) = call(
        join_kernel,
        (sds((nk * (r_rows + l_rows), 128), bf16),),
        smem=2,
    )(*place[:2], *all_rows, *rights)
    if nq == 2:
        far_sides = lax.ppermute(sides, "seq", [(0, 1), (1, 0)])
    else:
        far_sides = lax.all_gather(sides, "seq", axis=0, tiled=True)

    head_lanes = seqs * chans // heads
    gw_own, block = call(
        weights_kernel,
        (
            sds((groups, heads, lanes), f32),
            sds((nk, half, tokens, 2 * width), bf16),
        ),
        scratch=(
            pltpu.VMEM((heads * tile_i, 2 * tile_j), f32),
            pltpu.VMEM((4 * width, 4 * chans), bf16),
            pltpu.VMEM((4 * width, 4 * chans), bf16),
            pltpu.VMEM((4 * width, 4 * chans), bf16),
            pltpu.VMEM((nk, 2, half, tokens, 2 * width), bf16),
            pltpu.VMEM((heads, tile_i, head_lanes), bf16),
            pltpu.VMEM((heads, 2 * tile_j, head_lanes), bf16),
        ),
        smem=2,
        flops=3_000_000_000,
        nbytes=3_000_000,
    )(*place[:2], *all_rows, *all_cols, weights)
    if nq == 2:
        gw_other = lax.ppermute(gw_own, "seq", [(0, 1), (1, 0)])
    else:
        gw_own, gw_other = lax.psum(gw_own, "seq"), jnp.zeros_like(gw_own)

    close, remote = exchange(block, 1), exchange(block, 2)

    pair_out, normal, inverse, logits = call(
        update_kernel,
        (
            sds((tile_i * tile_j, z), bf16),
            sds((groups, z, lanes), f32),
            sds((groups, 8, lanes), f32),
            sds((groups, heads, lanes), f32),
        ),
        scratch=(
            pltpu.VMEM((tile_i * tile_j, z), bf16),
            pltpu.SemaphoreType.DMA((groups // 4,)),
            pltpu.VMEM((nk, nq * r_rows, 128), bf16),
            pltpu.VMEM((fd, nq * seqs, 4 * tile_j), bf16),
            pltpu.VMEM((groups * fc, nq * pack * seqs), bf16),
            pltpu.VMEM((2 * z, fd * fc), bf16),
            pltpu.VMEM((groups // 4, fd * fc, 4 * lanes), bf16),
            pltpu.VMEM((groups // 4, fd * fc, 4 * lanes), bf16),
            pltpu.VMEM((z, 4 * lanes), f32),
        ),
        smem=2,
        flops=14_000_000_000,
        nbytes=5_000_000,
        vmem=44 * 1024 * 1024,
        far=(4, 5, 6, 7),
        far_out=(0,),
    )(
        *place[1:],
        sides,
        far_sides,
        mask,
        outer_matrix,
        score_matrix.T,
        pair_input.reshape(tile_i * tile_j, z),
    )

    payload = sds((2 + groups // nk * (pack // 2), heads, 2 * tile_j), f32)
    gw, pay0, pay1, pay2, pay3 = call(
        softmax_kernel,
        (sds((groups, heads, lanes), f32), payload, payload, payload, payload),
        smem=1,
    )(col_scalar, logits, gw_own, gw_other, mask)

    got = [
        lax.ppermute(pay, "col", [(c, (c + shift) % nk) for c in range(nk)])
        for shift, pay in ((1, pay1), (2, pay2), (3, pay3))
    ]


    close, remote, pay0 = lax.optimization_barrier((close, remote, pay0))
    every = [block, close, remote, exchange(remote, 1)]
    values, gating = call(
        values_kernel,
        (sds((half, nr * nk * tokens, 2 * chans), bf16), sds((seqs * tokens, chans), f32)),
        scratch=(pltpu.VMEM((nr, nk, half, tokens, 2 * width), bf16),),
        smem=1,
        flops=4_000_000_000,
        nbytes=6_000_000,
    )(col_scalar, *every, content_weights_grid, normed, sigmoid_weights_grid)

    got, values, gating = lax.optimization_barrier((got, values, gating))

    (gradient,) = call(
        gradient_kernel,
        (sds((tile_i * tile_j, z), bf16),),
        scratch=(
            pltpu.VMEM((groups * heads, groups * heads), f32),
            pltpu.VMEM((tile_i * tile_j, z), bf16),
            pltpu.SemaphoreType.DMA((groups // 4,)),
        ),
        far_out=(0,),
        flops=4_000_000_000,
        nbytes=3_000_000,
    )(pay0, *got, logits, gw, normal, inverse, score_matrix.T)

    (aligned,) = call(
        alignment_kernel,
        (sds((seqs * tokens, width), bf16),),
        scratch=(
            pltpu.VMEM((nk, heads, tokens, 2 * tile_j), f32),
            pltpu.VMEM((seqs * tokens, chans), bf16),
        ),
        smem=1,
        flops=3_000_000_000,
        nbytes=5_000_000,
    )(
        col_scalar,
        pay0,
        *got,
        values,
        gating,
        alignment_input.reshape(seqs * tokens, width),
        final_mixing_weights.T,
    )
    return (
        aligned.reshape(seqs, tokens, width),
        pair_out.reshape(tile_i, tile_j, z),
        gradient.reshape(tile_i, tile_j, z),
    )


def solution(mesh):
    counts = (mesh.shape["seq"], mesh.shape["row"], mesh.shape["col"])
    in_specs = (
        P("seq", ("row", "col"), None),
        P("row", "col", None),
        P(),
        P(),
        P(),
        P(),
        P(),
        P(),
        P(),
        P(),
        P("seq", ("row", "col"), None),
    )
    out_specs = (P("seq", ("row", "col"), None), P("row", "col", None), P("row", "col", None))
    return jax.shard_map(
        functools.partial(on_device, counts),
        mesh=mesh,
        in_specs=in_specs,
        out_specs=out_specs,
        check_vma=False,
    )
```

```python
import functools

import jax
import jax.numpy as jnp
from jax import lax
from jax.experimental import pallas as pl
from jax.experimental.pallas import tpu as pltpu
from jax.sharding import PartitionSpec as P

epsilon = 1e-05
far_below = -1e30
vmem_bytes = 32 * 1024 * 1024
pack = 4

f32 = jnp.float32
bf16 = jnp.bfloat16


def nt_dot(a, b):
    return lax.dot_general(a, b, (((1,), (1,)), ((), ())), preferred_element_type=f32)


def nn_dot(a, b):
    return jnp.dot(a, b, preferred_element_type=f32)


def high_low(x):
    high = x.astype(bf16)
    return high, (x - high.astype(f32)).astype(bf16)


def call(
    kernel, out_shape, scratch=(), smem=0, flops=0, nbytes=0, vmem=vmem_bytes, far=(), far_out=()
):
    def run(*args):
        count = len(args)
        in_specs = [
            pl.BlockSpec(memory_space=pltpu.SMEM if n < smem else pltpu.VMEM) for n in range(count)
        ]
        for n in far:
            in_specs[n] = pl.BlockSpec(memory_space=pltpu.HBM)
        landing = [pltpu.VMEM(args[n].shape, args[n].dtype) for n in far]
        if far:
            landing.append(pltpu.SemaphoreType.DMA((len(far),)))

        def body(*refs):
            inputs = list(refs[:count])
            extra = refs[len(refs) - len(landing) :]
            rest = refs[count : len(refs) - len(landing)]
            copies = []
            for i, n in enumerate(far):
                copies.append(pltpu.make_async_copy(inputs[n], extra[i], extra[-1].at[i]))
                copies[-1].start()
                inputs[n] = extra[i]

            def ready():
                for copy in copies:
                    copy.wait()

            kernel(ready, *inputs, *rest)

        return pl.pallas_call(
            body,
            out_shape=out_shape,
            in_specs=in_specs,
            out_specs=[
                pl.BlockSpec(memory_space=pltpu.HBM if n in far_out else pltpu.VMEM)
                for n in range(len(out_shape))
            ],
            scratch_shapes=list(scratch) + landing,
            compiler_params=pltpu.CompilerParams(vmem_limit_bytes=vmem),
            cost_estimate=pl.CostEstimate(flops=flops, bytes_accessed=nbytes, transcendentals=0),
        )(*args)

    return run


def valid_count(mask_ref):
    return jnp.sum(mask_ref[...].astype(f32), axis=1, keepdims=True)


def column_mask(mask_ref, col, tile, copies):
    lane = lax.broadcasted_iota(jnp.int32, (1, copies * tile), 1)
    token = (lax.rem(lane, tile) + col * tile).astype(f32)
    return (token < valid_count(mask_ref)).astype(f32)


def twice(w):
    none = jnp.zeros_like(w)
    return jnp.concatenate(
        [jnp.concatenate([w, none], axis=1), jnp.concatenate([none, w], axis=1)], axis=0
    )


def prepare_kernel(
    ready,
    own_ref,
    x_ref,
    adj_ref,
    w1_ref,
    w2_ref,
    mask_ref,
    wv_ref,
    wg_ref,
    wf_ref,
    shard_ref,
    rows_ref,
    norm_ref,
    weights_ref,
    turn_ref,
    place_ref,
):
    chans = wv_ref.shape[1]
    weights_ref[:, :chans] = wv_ref[...]
    weights_ref[:, chans : 2 * chans] = wg_ref[...]
    weights_ref[:, 2 * chans :] = wf_ref[...]
    seqs, tokens, width = x_ref.shape
    half = seqs // 2
    fd = w2_ref.shape[0]
    x = x_ref[...].astype(f32)
    center = x - jnp.mean(x, axis=-1, keepdims=True)
    inverse = lax.rsqrt(jnp.mean(center * center, axis=-1, keepdims=True) + epsilon)
    normed = center * inverse
    rows = half * tokens
    adj = adj_ref[...].astype(f32)

    def two(x):
        x = jnp.concatenate([x[:half], x[half:]], axis=-1)
        return x.reshape(rows, 2 * width).astype(bf16)

    packed = two(normed)
    norm_ref[...] = packed
    base = tokens // pack * w1_ref.shape[0]
    shard_ref[base : base + rows, :] = two(adj)
    shard_ref[base + rows : base + 2 * rows, :] = packed
    token = lax.broadcasted_iota(jnp.int32, (seqs, tokens, width), 1) + own_ref[0]
    count = valid_count(mask_ref).reshape(1, 1, 1)
    real = jnp.where(token.astype(f32) < count, normed, 0.0)
    for s in range(seqs):
        turn_ref[:, s, :] = real[s]
    turned = turn_ref[...].astype(bf16).reshape(tokens * seqs, width)
    left = nt_dot(w1_ref[...], turned).astype(bf16)
    fc = w1_ref.shape[0]
    wk = pack * seqs
    for g in range(tokens // pack):
        shard_ref[g * fc : (g + 1) * fc, :] = left[:, g * wk : (g + 1) * wk]
    size = 128 // tokens
    real = real.astype(bf16)
    w2 = w2_ref[...]
    d = lax.broadcasted_iota(jnp.int32, (fd, 128), 0)
    lane = lax.broadcasted_iota(jnp.int32, (fd, 128), 1)
    mine = lax.rem(d, size) == lane // tokens
    for s in range(seqs):
        res = nt_dot(w2, jnp.concatenate([real[s]] * size, axis=0))
        res = jnp.where(mine, res, 0.0).reshape(fd // size, size, 128)
        place_ref[:, s, :] = jnp.sum(res, axis=1)
    right = place_ref[...].reshape(fd // size * seqs, 128).astype(bf16)
    rows_ref[...] = shard_ref[: base + 2 * rows, :]
    shard_ref[base + 2 * rows :, :] = right


def join_left_kernel(ready, col_ref, rows0_ref, rows1_ref, rows2_ref, rows3_ref, out_ref):
    size = out_ref.shape[0] // 4
    for t, ref in enumerate((rows0_ref, rows1_ref, rows2_ref, rows3_ref)):
        at = pl.ds(pl.multiple_of(jnp.bitwise_xor(col_ref[0], t) * size, size), size)
        out_ref[at, :] = ref[:size, :]


def join_right_kernel(ready, row_ref, pair0_ref, pair1_ref, out_ref):
    size = out_ref.shape[0] // 4
    for t in range(4):
        ref = (pair0_ref, pair1_ref)[t // 2]
        at = pl.ds(pl.multiple_of(jnp.bitwise_xor(row_ref[0], t) * size, size), size)
        end = ref.shape[0] // 2 * (t % 2 + 1)
        out_ref[at, :] = ref[end - size : end, :]


def update_kernel(
    ready,
    col_ref,
    seq_ref,
    left_ref,
    right_ref,
    far_left_ref,
    far_right_ref,
    mask_ref,
    m_ref,
    score_ref,
    pair_ref,
    pout_hbm,
    normal_ref,
    inverse_ref,
    logits_ref,
    pout_ref,
    out_sem,
    rk_ref,
    rab_ref,
    lm_ref,
    mt_ref,
    oh_ref,
    ol_ref,
    update_ref,
):
    nk = rk_ref.shape[0]
    width_d, pair_rows, _ = rab_ref.shape
    col, seq = col_ref[0], seq_ref[0]
    z = pair_ref.shape[1]
    groups, heads, lanes = logits_ref.shape
    tile_j = lanes // pack
    tokens = tile_j // nk
    fc = lm_ref.shape[0] // groups
    seqs = 128 // pack
    nq = pair_rows // seqs
    wk = pack * seqs

    r_rows = rk_ref.shape[1] // nq
    l_rows = groups * fc
    if nq == 2:
        sources = ((seq, 0, left_ref, right_ref), (1 - seq, 0, far_left_ref, far_right_ref))
    else:
        sources = tuple((q, q, far_left_ref, far_right_ref) for q in range(nq))
    for q, slot, from_left, from_right in sources:
        at = pl.ds(pl.multiple_of(q * r_rows, r_rows), r_rows)
        for k in range(nk):
            first = (slot * nk + k) * r_rows
            rk_ref[k, at, :] = from_right[first : first + r_rows, :]
        to = pl.ds(pl.multiple_of(q * wk, wk), wk)
        lm_ref[:, to] = from_left[slot * l_rows : (slot + 1) * l_rows, :]
    size = 128 // tokens
    right = jnp.concatenate([rk_ref[k] for k in range(nk)], axis=1)
    source = lax.broadcasted_iota(jnp.int32, (nk * 128, 4 * tile_j), 0)
    target = lax.broadcasted_iota(jnp.int32, (nk * 128, 4 * tile_j), 1)
    used = jnp.logical_or(target < tile_j, target >= 3 * tile_j)
    j = lax.rem(target, tile_j)
    offset = jnp.where(used, source - (j // tokens * 128 + lax.rem(j, tokens)), -1)
    blocks = width_d // size
    for e in range(size):
        pick = jnp.where(offset == e * tokens, 1.0, 0.0).astype(bf16)
        res = nn_dot(right, pick).astype(bf16)
        for q in range(nq):
            for n in range(blocks):
                at = (q * blocks + n) * seqs
                rab_ref[n * size + e, q * seqs : (q + 1) * seqs, :] = res[at : at + seqs]

    chunk = 8
    many = 4
    wide = oh_ref.shape[2] // lanes
    empty = jnp.zeros((seqs, 2 * tile_j), bf16)

    def block_of(d):
        rows = []
        for q in range(nq):
            both = rab_ref[d, q * seqs : (q + 1) * seqs, :]
            part = both[:, : 2 * tile_j], both[:, 2 * tile_j :]
            for i in range(pack):
                pieces = [empty] * (pack // 2)
                pieces[i // 2] = part[i % 2]
                rows.append(jnp.concatenate(pieces, axis=1))
        return jnp.concatenate(rows, axis=0)

    def outer_of(n, carry):
        block = jnp.concatenate([block_of(many * n + e) for e in range(many)], axis=1)
        for m in range(groups // chunk):
            out = nn_dot(lm_ref[m * chunk * fc : (m + 1) * chunk * fc, :], block)
            high, low = high_low(out)
            for e in range(many):
                at = pl.ds(pl.multiple_of((many * n + e) * fc, fc), fc)
                for g in range(chunk):
                    group = m * chunk + g
                    to = slice(group % wide * lanes, (group % wide + 1) * lanes)
                    cut = slice(g * fc, (g + 1) * fc), slice(e * lanes, (e + 1) * lanes)
                    oh_ref[group // wide, at, to] = high[cut]
                    ol_ref[group // wide, at, to] = low[cut]
        return carry

    lax.fori_loop(0, width_d // many, outer_of, 0)

    ready()
    some = z // fc
    for n in range(width_d // some):
        block = jnp.concatenate(
            [m_ref[pl.ds(n * some + e, fc, stride=width_d), :] for e in range(some)], axis=0
        ).T
        high, low = high_low(block)
        mt_ref[:z, n * z : (n + 1) * z] = high
        mt_ref[z:, n * z : (n + 1) * z] = low
    maskj = column_mask(mask_ref, col, tile_j, 2)

    maskl = jnp.concatenate([maskj] * (pack // 2), axis=1) > 0
    score = score_ref[...]
    s1 = score.astype(bf16).astype(f32)
    s2 = (score - s1).astype(bf16).astype(f32)
    s3 = score - s1 - s2
    none = jnp.zeros_like(s1)
    st = jnp.concatenate(
        [
            jnp.concatenate([s1, s2, s3, none], axis=0),
            jnp.concatenate([s1, s2, none, none], axis=0),
        ],
        axis=1,
    ).astype(bf16)

    def finish(n, carry):
        two = nn_dot(mt_ref[...], oh_ref[n])
        update_ref[...] = two[:z] + two[z:] + nn_dot(mt_ref[:z, :], ol_ref[n])
        for e in range(wide):
            g = n * wide + e
            at = pl.ds(pl.multiple_of(g * lanes, lanes), lanes)
            before = pair_ref[at, :].T.astype(f32)
            result = (before + update_ref[:, e * lanes : (e + 1) * lanes]).astype(bf16)
            x = result.astype(f32)
            pout_ref[at, :] = result.T
            center = x - jnp.mean(x, axis=0, keepdims=True)
            inverse = lax.rsqrt(jnp.mean(center * center, axis=0, keepdims=True) + epsilon)
            normal = center * inverse
            normal_ref[g] = normal
            inverse_ref[g] = jnp.broadcast_to(inverse, inverse_ref.shape[1:])
            high, low = high_low(normal)
            scores = nn_dot(st, jnp.concatenate([high, low], axis=0))
            logits = scores[:heads] + scores[heads : 2 * heads] + scores[2 * heads : 3 * heads]
            logits_ref[g] = jnp.where(maskl, logits, far_below)
        at = pl.ds(pl.multiple_of(n * wide * lanes, wide * lanes), wide * lanes)
        pltpu.make_async_copy(pout_ref.at[at], pout_hbm.at[at], out_sem.at[n]).start()
        return carry

    lax.fori_loop(0, groups // wide, finish, 0)
    for n in range(groups // wide):
        at = pl.ds(n * wide * lanes, wide * lanes)
        pltpu.make_async_copy(pout_ref.at[at], pout_hbm.at[at], out_sem.at[n]).wait()


def by_heads(w, heads, out_ref):
    width, chans = w.shape
    hw = chans // heads
    block = 4 * hw
    slot = lax.broadcasted_iota(jnp.int32, (width, block), 1) // hw
    w = w.astype(f32)
    for t in range(chans // block):
        part = w[:, t * block : (t + 1) * block]
        turns = [part] + [pltpu.roll(part, n * hw, 1) for n in range(1, 4)]
        for e in range(4):
            h = t * 4 + e
            for s in range(4):
                out_ref[s * width : (s + 1) * width, h * block : (h + 1) * block] = jnp.where(
                    slot == s, turns[(s - e) % 4], 0.0
                ).astype(bf16)


def weights_kernel(
    ready,
    row_ref,
    col_ref,
    side0_ref,
    side1_ref,
    side2_ref,
    side3_ref,
    cols0_ref,
    cols1_ref,
    weights_ref,
    gw_ref,
    cols_ref,
    acc_ref,
    bv_ref,
    bg_ref,
    bf_ref,
    rows_ref,
    gs_ref,
    vs_ref,
):
    nk, half, tokens, _ = cols_ref.shape
    tile = nk * tokens
    groups, heads, lanes = gw_ref.shape
    row, col = row_ref[0], col_ref[0]
    count = half * tokens
    size = side0_ref.shape[0] - 2 * count
    for t, ref in enumerate((side0_ref, side1_ref, side2_ref, side3_ref)):
        k = jnp.bitwise_xor(col, t)
        rows_ref[k] = ref[size : size + 2 * count, :].reshape(rows_ref.shape[1:])
    for t in range(nk):
        ref = (cols0_ref, cols1_ref)[t // 2]
        start = ref.shape[0] // 2 * (t % 2)
        part = ref[start : start + count, :]
        cols_ref[jnp.bitwise_xor(row, t)] = part.reshape(cols_ref.shape[1:])
    chans = weights_ref.shape[1] // 3
    by_heads(weights_ref[:, :chans], heads, bv_ref)
    by_heads(weights_ref[:, chans : 2 * chans], heads, bg_ref)
    by_heads(weights_ref[:, 2 * chans :], heads, bf_ref)
    block = bv_ref.shape[1] // heads

    def four(read, n):
        return jnp.concatenate(
            [
                jnp.concatenate(
                    [
                        jnp.concatenate([read(k, 2 * (2 * n + e) + p) for k in range(nk)], axis=0)
                        for p in range(2)
                    ],
                    axis=1,
                )
                for e in range(2)
            ],
            axis=0,
        )

    for hp in range(heads // 2):
        cut = slice(hp * 2 * block, (hp + 1) * 2 * block)
        for n in range(half // 4):
            v = nn_dot(four(lambda k, s: cols_ref[k, s], n), bv_ref[:, cut]).astype(bf16)
            gate = nn_dot(four(lambda k, s: rows_ref[k, 1, s], n), bg_ref[:, cut])
            grad = nn_dot(four(lambda k, s: rows_ref[k, 0, s], n), bf_ref[:, cut])
            g = (grad * jax.nn.sigmoid(gate)).astype(bf16)
            for e in range(2):
                to = slice((2 * n + e) * block, (2 * n + e + 1) * block)
                for o in range(2):
                    mine = slice(o * block, (o + 1) * block)
                    ve = v[e * tile : (e + 1) * tile, mine]
                    vs_ref[2 * hp + o, :tile, to] = ve
                    vs_ref[2 * hp + o, tile:, to] = ve
                    gs_ref[2 * hp + o, :, to] = g[e * tile : (e + 1) * tile, mine]
    for h in range(heads):
        acc_ref[h * tile : (h + 1) * tile, :] = nt_dot(gs_ref[h], vs_ref[h])

    first = lax.broadcasted_iota(jnp.int32, (groups, 2 * tile), 1) < tile
    for h in range(heads):
        for part in range(pack // 2):
            a = acc_ref[pl.ds(h * tile + 2 * part, groups, stride=pack), :]
            b = acc_ref[pl.ds(h * tile + 2 * part + 1, groups, stride=pack), :]
            gw_ref[:, h, part * 2 * tile : (part + 1) * 2 * tile] = jnp.where(first, a, b)


def softmax_kernel(
    ready,
    col_ref,
    logits_ref,
    gwa_ref,
    gwb_ref,
    mask_ref,
    gw_ref,
    own_ref,
    pay1_ref,
    pay2_ref,
    pay3_ref,
):
    groups, heads, lanes = logits_ref.shape
    tile = lanes // pack
    nk = 4
    rows = groups * heads
    col = col_ref[0]
    gw_ref[...] = gwa_ref[...] + gwb_ref[...]
    lane = lax.broadcasted_iota(jnp.int32, (rows, 2 * tile), 1)
    low = lane < tile
    maskj = column_mask(mask_ref, col, tile, 2)
    stats = jnp.zeros((rows, 2 * tile), f32)
    for part in range(pack // 2):
        cut = slice(part * 2 * tile, (part + 1) * 2 * tile)
        lg = logits_ref[:, :, cut].reshape(rows, 2 * tile)
        gw = gw_ref[:, :, cut].reshape(rows, 2 * tile)
        m0 = jnp.max(jnp.where(low, lg, far_below), axis=1, keepdims=True)
        m1 = jnp.max(jnp.where(low, far_below, lg), axis=1, keepdims=True)
        p = jnp.exp(lg - jnp.where(low, m0, m1)) * maskj
        pg = p * gw
        for e, m in ((0, m0), (1, m1)):
            mine = low if e == 0 else jnp.logical_not(low)
            i = 2 * part + e
            total = jnp.sum(jnp.where(mine, p, 0.0), axis=1, keepdims=True)
            inner = jnp.sum(jnp.where(mine, pg, 0.0), axis=1, keepdims=True)
            stats = jnp.where(lane == i, m, stats)
            stats = jnp.where(lane == pack + i, total, stats)
            stats = jnp.where(lane == 2 * pack + i, inner, stats)
    turned = stats.T[:16]
    per = groups // nk
    for shift, pay in enumerate((own_ref, pay1_ref, pay2_ref, pay3_ref)):
        dest = lax.rem(col + shift, nk)
        pay[0] = turned[:8]
        pay[1] = turned[8:]
        for g in range(per):
            piece = logits_ref[dest * per + g]
            for part in range(pack // 2):
                pay[2 + g * (pack // 2) + part] = piece[:, part * 2 * tile : (part + 1) * 2 * tile]


def values_kernel(
    ready, col_ref, ev0_ref, ev1_ref, ev2_ref, ev3_ref, wv_ref, norm_ref, wg_ref, v_ref, gate_ref, ev_ref
):
    nr, nk, half, tokens, wide = ev_ref.shape
    chans = wv_ref.shape[1]
    for t, ref in enumerate((ev0_ref, ev1_ref, ev2_ref, ev3_ref)):
        ev_ref[jnp.bitwise_xor(col_ref[0], t)] = ref[...]
    gate = jax.nn.sigmoid(nn_dot(norm_ref[...], twice(wg_ref[...])))
    gate_ref[: half * tokens] = gate[:, :chans]
    gate_ref[half * tokens :] = gate[:, chans:]
    wv = twice(wv_ref[...])
    for s in range(half):
        x = jnp.concatenate([ev_ref[r, k, s] for r in range(nr) for k in range(nk)], axis=0)
        v_ref[s] = nn_dot(x, wv).astype(bf16)


def gradient_kernel(
    ready,
    own_ref, r1_ref, r2_ref, r3_ref, logits_ref, gw_ref, normal_ref, inverse_ref, score_ref, out_hbm, stat_ref, out_ref, out_sem
):
    groups, heads, lanes = logits_ref.shape
    rows = groups * heads
    score = score_ref[...]
    z = score.shape[1]
    s1 = score.astype(bf16).astype(f32)
    s2 = (score - s1).astype(bf16).astype(f32)
    s3 = score - s1 - s2
    parts = [s1, s1, s1, s2, s2, s3, jnp.zeros((z - 6 * heads, z), f32)]
    sk = jnp.concatenate(parts, axis=0).T[:, : 6 * heads].astype(bf16)
    pays = (own_ref, r1_ref, r2_ref, r3_ref)
    ms = [p[0][:pack] for p in pays]
    ls = [p[0][pack : 2 * pack] for p in pays]
    ns = [p[1][:pack] for p in pays]
    top = functools.reduce(jnp.maximum, ms)
    scales = [jnp.exp(m - top) for m in ms]
    total = sum(a * b for a, b in zip(ls, scales))
    inner = sum(a * b for a, b in zip(ns, scales)) / total
    stacked = jnp.concatenate([top, total, inner, jnp.zeros((rows - 3 * pack, rows), f32)], axis=0)
    stat_ref[...] = stacked.T

    tile = lanes // pack
    low = lax.broadcasted_iota(jnp.int32, (heads, 2 * tile), 1) < tile

    def one(g):
        st = stat_ref[pl.ds(pl.multiple_of(g * heads, heads), heads), :]

        def spread(base):
            halves = [
                jnp.where(
                    low,
                    st[:, base + 2 * half : base + 2 * half + 1],
                    st[:, base + 2 * half + 1 : base + 2 * half + 2],
                )
                for half in range(pack // 2)
            ]
            return jnp.concatenate(halves, axis=1)

        prob = jnp.exp(logits_ref[g] - spread(0)) / spread(pack)
        gl = prob * (gw_ref[g] - spread(2 * pack))
        g1 = gl.astype(bf16).astype(f32)
        g2 = (gl - g1).astype(bf16).astype(f32)
        g3 = gl - g1 - g2
        stack = jnp.concatenate([g1, g2, g3, g1, g2, g1], axis=0).astype(bf16)
        grad = nn_dot(sk, stack)
        normal = normal_ref[g]
        inverse = inverse_ref[g][:1]
        centered = grad - jnp.mean(grad, axis=0, keepdims=True)
        along = jnp.mean(grad * normal, axis=0, keepdims=True)
        result = inverse * (centered - normal * along)
        out_ref[pl.ds(pl.multiple_of(g * lanes, lanes), lanes), :] = result.astype(bf16).T

    many = 4

    def some(n, carry):
        for e in range(many):
            one(n * many + e)
        at = pl.ds(pl.multiple_of(n * many * lanes, many * lanes), many * lanes)
        pltpu.make_async_copy(out_ref.at[at], out_hbm.at[at], out_sem.at[n]).start()
        return carry

    lax.fori_loop(0, groups // many, some, 0)
    for n in range(groups // many):
        at = pl.ds(n * many * lanes, many * lanes)
        pltpu.make_async_copy(out_ref.at[at], out_hbm.at[at], out_sem.at[n]).wait()


def alignment_kernel(
    ready,
    col_ref,
    own_ref,
    r1_ref,
    r2_ref,
    r3_ref,
    v_ref,
    gate_ref,
    x_ref,
    wf_ref,
    out_ref,
    w_ref,
    gated_ref,
):
    pays = (own_ref, r1_ref, r2_ref, r3_ref)
    nk = len(pays)
    heads = own_ref.shape[1]
    wide = own_ref.shape[2]
    tile = wide // 2
    pieces = own_ref.shape[0] - 2
    rows = pieces * heads
    half, all_tokens, chans = v_ref.shape
    chans = chans // 2
    tokens = pieces * 2
    head_width = chans // heads
    col = col_ref[0]

    low = lax.broadcasted_iota(jnp.int32, (rows, wide), 1) < tile
    lgs = [p[2:].reshape(rows, wide) for p in pays]
    peak = functools.reduce(jnp.maximum, lgs)
    m0 = jnp.max(jnp.where(low, peak, far_below), axis=1, keepdims=True)
    m1 = jnp.max(jnp.where(low, far_below, peak), axis=1, keepdims=True)
    top = jnp.where(low, m0, m1)
    ps = [jnp.exp(lg - top) for lg in lgs]
    every = sum(ps)
    t0 = jnp.sum(jnp.where(low, every, 0.0), axis=1, keepdims=True)
    t1 = jnp.sum(jnp.where(low, 0.0, every), axis=1, keepdims=True)
    total = jnp.where(low, t0, t1)
    for shift, p in enumerate(ps):
        source = lax.rem(col + nk - shift, nk)
        weight = p / total
        rolled = pltpu.roll(weight, tile, 1)
        for n in range(pieces):
            w_ref[source, :, 2 * n, :] = weight[n * heads : (n + 1) * heads]
            w_ref[source, :, 2 * n + 1, :] = rolled[n * heads : (n + 1) * heads]
    w = jnp.concatenate(
        [
            w_ref[k].reshape(heads * tokens, wide)[:, :tile]
            for k in range(nk)
        ],
        axis=1,
    ).astype(bf16)

    owner = lax.broadcasted_iota(jnp.int32, (tokens, chans), 1) // head_width

    def one(s, carry):
        full = nn_dot(w, v_ref[s])
        for e in range(2):
            cut = slice(e * chans, (e + 1) * chans)
            mean = jnp.zeros((tokens, chans), f32)
            for h in range(heads):
                mean = jnp.where(owner == h, full[h * tokens : (h + 1) * tokens, cut], mean)
            at = pl.ds(pl.multiple_of((e * half + s) * tokens, tokens), tokens)
            gated_ref[at, :] = (gate_ref[at, :] * mean).astype(bf16)
        return carry

    lax.fori_loop(0, half, one, 0, unroll=4)
    out_ref[...] = (x_ref[...].astype(f32) + nt_dot(gated_ref[...], wf_ref[...])).astype(bf16)


def on_device(
    counts,
    alignment_input,
    pair_input,
    token_valid_mask,
    first_factor_weights,
    second_factor_weights,
    content_weights_grid,
    sigmoid_weights_grid,
    outer_matrix,
    score_matrix,
    final_mixing_weights,
    adjoint_of_rowset,
):
    nq, nr, nk = counts
    row_index = lax.axis_index("row")
    col_index = lax.axis_index("col")
    seqs, tokens, width = alignment_input.shape
    tile_i, tile_j, z = pair_input.shape
    fc = first_factor_weights.shape[1]
    fd = second_factor_weights.shape[1]
    heads = score_matrix.shape[1]
    chans = content_weights_grid.shape[1]
    groups = tile_i // pack
    lanes = pack * tile_j
    sds = jax.ShapeDtypeStruct

    mask = token_valid_mask.reshape(1, -1)
    own_start = ((row_index * nk + col_index) * tokens).astype(jnp.int32).reshape(1)
    seq_index = lax.axis_index("seq")
    place = tuple(x.astype(jnp.int32).reshape(1) for x in (row_index, col_index, seq_index))
    col_scalar = col_index.astype(jnp.int32).reshape(1)
    half = seqs // 2

    l_rows = tokens // pack * fc
    r_rows = fd * tokens // 128 * seqs
    n_rows = half * tokens
    shard, rows, normed, weights = call(
        prepare_kernel,
        (
            sds((l_rows + 2 * n_rows + r_rows, 128), bf16),
            sds((l_rows + 2 * n_rows, 128), bf16),
            sds((n_rows, 128), bf16),
            sds((width, 3 * chans), bf16),
        ),
        scratch=(
            pltpu.VMEM((tokens, seqs, width), f32),
            pltpu.VMEM((fd * tokens // 128, seqs, 128), f32),
        ),
        smem=1,
        vmem=60 * 1024 * 1024,
    )(
        own_start,
        alignment_input,
        adjoint_of_rowset,
        first_factor_weights.T,
        second_factor_weights.T,
        mask,
        content_weights_grid,
        sigmoid_weights_grid,
        final_mixing_weights.T,
    )

    def exchange(x, bit):
        return lax.ppermute(x, "col", [(c, c ^ bit) for c in range(nk)])

    other = exchange(shard, 1)
    all_rows = [rows, other, exchange(rows, 2), exchange(rows, 3)]
    pair = jnp.concatenate([x[l_rows + n_rows :] for x in (shard, other)], axis=0)
    all_cols = [
        lax.ppermute(
            pair,
            ("row", "col"),
            [(r * nk + c, (c ^ flip) * nk + r) for r in range(nr) for c in range(nk)],
        )
        for flip in (0, 2)
    ]

    def over_seq(x):
        if nq == 2:
            return lax.ppermute(x, "seq", [(0, 1), (1, 0)])
        return lax.all_gather(x, "seq", axis=0, tiled=True)

    (left,) = call(join_left_kernel, (sds((nk * l_rows, 128), bf16),), smem=1)(place[1], *all_rows)
    (right,) = call(join_right_kernel, (sds((nk * r_rows, 128), bf16),), smem=1)(
        place[0], *all_cols
    )
    far_left, far_right = over_seq(left), over_seq(right)

    head_lanes = seqs * chans // heads
    gw_own, block = call(
        weights_kernel,
        (
            sds((groups, heads, lanes), f32),
            sds((nk, half, tokens, 2 * width), bf16),
        ),
        scratch=(
            pltpu.VMEM((heads * tile_i, 2 * tile_j), f32),
            pltpu.VMEM((4 * width, 4 * chans), bf16),
            pltpu.VMEM((4 * width, 4 * chans), bf16),
            pltpu.VMEM((4 * width, 4 * chans), bf16),
            pltpu.VMEM((nk, 2, half, tokens, 2 * width), bf16),
            pltpu.VMEM((heads, tile_i, head_lanes), bf16),
            pltpu.VMEM((heads, 2 * tile_j, head_lanes), bf16),
        ),
        smem=2,
        flops=3_000_000_000,
        nbytes=3_000_000,
    )(*place[:2], *all_rows, *all_cols, weights)
    if nq == 2:
        gw_other = lax.ppermute(gw_own, "seq", [(0, 1), (1, 0)])
    else:
        gw_own, gw_other = lax.psum(gw_own, "seq"), jnp.zeros_like(gw_own)

    close, remote = exchange(block, 1), exchange(block, 2)

    pair_out, normal, inverse, logits = call(
        update_kernel,
        (
            sds((tile_i * tile_j, z), bf16),
            sds((groups, z, lanes), f32),
            sds((groups, 8, lanes), f32),
            sds((groups, heads, lanes), f32),
        ),
        scratch=(
            pltpu.VMEM((tile_i * tile_j, z), bf16),
            pltpu.SemaphoreType.DMA((groups // 4,)),
            pltpu.VMEM((nk, nq * r_rows, 128), bf16),
            pltpu.VMEM((fd, nq * seqs, 4 * tile_j), bf16),
            pltpu.VMEM((groups * fc, nq * pack * seqs), bf16),
            pltpu.VMEM((2 * z, fd * fc), bf16),
            pltpu.VMEM((groups // 4, fd * fc, 4 * lanes), bf16),
            pltpu.VMEM((groups // 4, fd * fc, 4 * lanes), bf16),
            pltpu.VMEM((z, 4 * lanes), f32),
        ),
        smem=2,
        flops=14_000_000_000,
        nbytes=5_000_000,
        vmem=44 * 1024 * 1024,
        far=(6, 7, 8, 9),
        far_out=(0,),
    )(
        *place[1:],
        left,
        right,
        far_left,
        far_right,
        mask,
        outer_matrix,
        score_matrix.T,
        pair_input.reshape(tile_i * tile_j, z),
    )

    payload = sds((2 + groups // nk * (pack // 2), heads, 2 * tile_j), f32)
    gw, pay0, pay1, pay2, pay3 = call(
        softmax_kernel,
        (sds((groups, heads, lanes), f32), payload, payload, payload, payload),
        smem=1,
    )(col_scalar, logits, gw_own, gw_other, mask)

    got = [
        lax.ppermute(pay, "col", [(c, (c + shift) % nk) for c in range(nk)])
        for shift, pay in ((1, pay1), (2, pay2), (3, pay3))
    ]


    close, remote, pay0 = lax.optimization_barrier((close, remote, pay0))
    every = [block, close, remote, exchange(remote, 1)]
    values, gating = call(
        values_kernel,
        (sds((half, nr * nk * tokens, 2 * chans), bf16), sds((seqs * tokens, chans), f32)),
        scratch=(pltpu.VMEM((nr, nk, half, tokens, 2 * width), bf16),),
        smem=1,
        flops=4_000_000_000,
        nbytes=6_000_000,
    )(col_scalar, *every, content_weights_grid, normed, sigmoid_weights_grid)

    got, values, gating = lax.optimization_barrier((got, values, gating))

    (gradient,) = call(
        gradient_kernel,
        (sds((tile_i * tile_j, z), bf16),),
        scratch=(
            pltpu.VMEM((groups * heads, groups * heads), f32),
            pltpu.VMEM((tile_i * tile_j, z), bf16),
            pltpu.SemaphoreType.DMA((groups // 4,)),
        ),
        far_out=(0,),
        flops=4_000_000_000,
        nbytes=3_000_000,
    )(pay0, *got, logits, gw, normal, inverse, score_matrix.T)

    (aligned,) = call(
        alignment_kernel,
        (sds((seqs * tokens, width), bf16),),
        scratch=(
            pltpu.VMEM((nk, heads, tokens, 2 * tile_j), f32),
            pltpu.VMEM((seqs * tokens, chans), bf16),
        ),
        smem=1,
        flops=3_000_000_000,
        nbytes=5_000_000,
    )(
        col_scalar,
        pay0,
        *got,
        values,
        gating,
        alignment_input.reshape(seqs * tokens, width),
        final_mixing_weights.T,
    )
    return (
        aligned.reshape(seqs, tokens, width),
        pair_out.reshape(tile_i, tile_j, z),
        gradient.reshape(tile_i, tile_j, z),
    )


def solution(mesh):
    counts = (mesh.shape["seq"], mesh.shape["row"], mesh.shape["col"])
    in_specs = (
        P("seq", ("row", "col"), None),
        P("row", "col", None),
        P(),
        P(),
        P(),
        P(),
        P(),
        P(),
        P(),
        P(),
        P("seq", ("row", "col"), None),
    )
    out_specs = (P("seq", ("row", "col"), None), P("row", "col", None), P("row", "col", None))
    return jax.shard_map(
        functools.partial(on_device, counts),
        mesh=mesh,
        in_specs=in_specs,
        out_specs=out_specs,
        check_vma=False,
    )
```

```python
import functools

import jax
import jax.numpy as jnp
from jax import lax
from jax.experimental import pallas as pl
from jax.experimental.pallas import tpu as pltpu
from jax.sharding import PartitionSpec as P

epsilon = 1e-05
far_below = -1e30
vmem_bytes = 32 * 1024 * 1024
pack = 4

f32 = jnp.float32
bf16 = jnp.bfloat16


def nt_dot(a, b):
    return lax.dot_general(a, b, (((1,), (1,)), ((), ())), preferred_element_type=f32)


def nn_dot(a, b):
    return jnp.dot(a, b, preferred_element_type=f32)


def high_low(x):
    high = x.astype(bf16)
    return high, (x - high.astype(f32)).astype(bf16)


def call(
    kernel, out_shape, scratch=(), smem=0, flops=0, nbytes=0, vmem=vmem_bytes, far=(), far_out=()
):
    def run(*args):
        count = len(args)
        in_specs = [
            pl.BlockSpec(memory_space=pltpu.SMEM if n < smem else pltpu.VMEM) for n in range(count)
        ]
        for n in far:
            in_specs[n] = pl.BlockSpec(memory_space=pltpu.HBM)
        landing = [pltpu.VMEM(args[n].shape, args[n].dtype) for n in far]
        if far:
            landing.append(pltpu.SemaphoreType.DMA((len(far),)))

        def body(*refs):
            inputs = list(refs[:count])
            extra = refs[len(refs) - len(landing) :]
            rest = refs[count : len(refs) - len(landing)]
            copies = []
            for i, n in enumerate(far):
                copies.append(pltpu.make_async_copy(inputs[n], extra[i], extra[-1].at[i]))
                copies[-1].start()
                inputs[n] = extra[i]

            def ready():
                for copy in copies:
                    copy.wait()

            kernel(ready, *inputs, *rest)

        return pl.pallas_call(
            body,
            out_shape=out_shape,
            in_specs=in_specs,
            out_specs=[
                pl.BlockSpec(memory_space=pltpu.HBM if n in far_out else pltpu.VMEM)
                for n in range(len(out_shape))
            ],
            scratch_shapes=list(scratch) + landing,
            compiler_params=pltpu.CompilerParams(vmem_limit_bytes=vmem),
            cost_estimate=pl.CostEstimate(flops=flops, bytes_accessed=nbytes, transcendentals=0),
        )(*args)

    return run


def valid_count(mask_ref):
    return jnp.sum(mask_ref[...].astype(f32), axis=1, keepdims=True)


def column_mask(mask_ref, col, tile, copies):
    lane = lax.broadcasted_iota(jnp.int32, (1, copies * tile), 1)
    token = (lax.rem(lane, tile) + col * tile).astype(f32)
    return (token < valid_count(mask_ref)).astype(f32)


def twice(w):
    none = jnp.zeros_like(w)
    return jnp.concatenate(
        [jnp.concatenate([w, none], axis=1), jnp.concatenate([none, w], axis=1)], axis=0
    )


def prepare_kernel(
    ready,
    own_ref,
    x_ref,
    adj_ref,
    w1_ref,
    w2_ref,
    mask_ref,
    wv_ref,
    wg_ref,
    wf_ref,
    shard_ref,
    rows_ref,
    norm_ref,
    weights_ref,
    turn_ref,
    place_ref,
):
    chans = wv_ref.shape[1]
    weights_ref[:, :chans] = wv_ref[...]
    weights_ref[:, chans : 2 * chans] = wg_ref[...]
    weights_ref[:, 2 * chans :] = wf_ref[...]
    seqs, tokens, width = x_ref.shape
    half = seqs // 2
    fd = w2_ref.shape[0]
    x = x_ref[...].astype(f32)
    center = x - jnp.mean(x, axis=-1, keepdims=True)
    inverse = lax.rsqrt(jnp.mean(center * center, axis=-1, keepdims=True) + epsilon)
    normed = center * inverse
    rows = half * tokens
    adj = adj_ref[...].astype(f32)

    def two(x):
        x = jnp.concatenate([x[:half], x[half:]], axis=-1)
        return x.reshape(rows, 2 * width).astype(bf16)

    packed = two(normed)
    norm_ref[...] = packed
    base = tokens // pack * w1_ref.shape[0]
    shard_ref[base : base + rows, :] = two(adj)
    shard_ref[base + rows : base + 2 * rows, :] = packed
    token = lax.broadcasted_iota(jnp.int32, (seqs, tokens, width), 1) + own_ref[0]
    count = valid_count(mask_ref).reshape(1, 1, 1)
    real = jnp.where(token.astype(f32) < count, normed, 0.0)
    for s in range(seqs):
        turn_ref[:, s, :] = real[s]
    turned = turn_ref[...].astype(bf16).reshape(tokens * seqs, width)
    left = nt_dot(w1_ref[...], turned).astype(bf16)
    fc = w1_ref.shape[0]
    wk = pack * seqs
    for g in range(tokens // pack):
        shard_ref[g * fc : (g + 1) * fc, :] = left[:, g * wk : (g + 1) * wk]
    size = 128 // tokens
    real = real.astype(bf16)
    w2 = w2_ref[...]
    d = lax.broadcasted_iota(jnp.int32, (fd, 128), 0)
    lane = lax.broadcasted_iota(jnp.int32, (fd, 128), 1)
    mine = lax.rem(d, size) == lane // tokens
    for s in range(seqs):
        res = nt_dot(w2, jnp.concatenate([real[s]] * size, axis=0))
        res = jnp.where(mine, res, 0.0).reshape(fd // size, size, 128)
        place_ref[:, s, :] = jnp.sum(res, axis=1)
    right = place_ref[...].reshape(fd // size * seqs, 128).astype(bf16)
    rows_ref[...] = shard_ref[: base + 2 * rows, :]
    shard_ref[base + 2 * rows :, :] = right


def join_left_kernel(ready, col_ref, rows0_ref, rows1_ref, rows2_ref, rows3_ref, out_ref):
    size = out_ref.shape[0] // 4
    for t, ref in enumerate((rows0_ref, rows1_ref, rows2_ref, rows3_ref)):
        at = pl.ds(pl.multiple_of(jnp.bitwise_xor(col_ref[0], t) * size, size), size)
        out_ref[at, :] = ref[:size, :]


def join_right_kernel(ready, row_ref, pair0_ref, pair1_ref, out_ref):
    size = out_ref.shape[0] // 4
    for t in range(4):
        ref = (pair0_ref, pair1_ref)[t // 2]
        at = pl.ds(pl.multiple_of(jnp.bitwise_xor(row_ref[0], t) * size, size), size)
        end = ref.shape[0] // 2 * (t % 2 + 1)
        out_ref[at, :] = ref[end - size : end, :]


def update_kernel(
    ready,
    col_ref,
    seq_ref,
    left_ref,
    right_ref,
    far_left_ref,
    far_right_ref,
    mask_ref,
    m_ref,
    score_ref,
    pair_ref,
    pout_hbm,
    normal_ref,
    inverse_ref,
    logits_ref,
    pout_ref,
    out_sem,
    rk_ref,
    rab_ref,
    lm_ref,
    mt_ref,
    oh_ref,
    ol_ref,
    update_ref,
):
    nk = rk_ref.shape[0]
    width_d, pair_rows, _ = rab_ref.shape
    col, seq = col_ref[0], seq_ref[0]
    z = pair_ref.shape[1]
    groups, heads, lanes = logits_ref.shape
    tile_j = lanes // pack
    tokens = tile_j // nk
    fc = lm_ref.shape[0] // groups
    seqs = 128 // pack
    nq = pair_rows // seqs
    wk = pack * seqs

    r_rows = rk_ref.shape[1] // nq
    l_rows = groups * fc
    if nq == 2:
        sources = ((seq, 0, left_ref, right_ref), (1 - seq, 0, far_left_ref, far_right_ref))
    else:
        sources = tuple((q, q, far_left_ref, far_right_ref) for q in range(nq))
    for q, slot, from_left, from_right in sources:
        at = pl.ds(pl.multiple_of(q * r_rows, r_rows), r_rows)
        for k in range(nk):
            first = (slot * nk + k) * r_rows
            rk_ref[k, at, :] = from_right[first : first + r_rows, :]
        to = pl.ds(pl.multiple_of(q * wk, wk), wk)
        lm_ref[:, to] = from_left[slot * l_rows : (slot + 1) * l_rows, :]
    size = 128 // tokens
    right = jnp.concatenate([rk_ref[k] for k in range(nk)], axis=1)
    source = lax.broadcasted_iota(jnp.int32, (nk * 128, 4 * tile_j), 0)
    target = lax.broadcasted_iota(jnp.int32, (nk * 128, 4 * tile_j), 1)
    used = jnp.logical_or(target < tile_j, target >= 3 * tile_j)
    j = lax.rem(target, tile_j)
    offset = jnp.where(used, source - (j // tokens * 128 + lax.rem(j, tokens)), -1)
    blocks = width_d // size
    for e in range(size):
        pick = jnp.where(offset == e * tokens, 1.0, 0.0).astype(bf16)
        res = nn_dot(right, pick).astype(bf16)
        for q in range(nq):
            for n in range(blocks):
                at = (q * blocks + n) * seqs
                rab_ref[n * size + e, q * seqs : (q + 1) * seqs, :] = res[at : at + seqs]

    chunk = 8
    many = 4
    wide = oh_ref.shape[2] // lanes
    empty = jnp.zeros((seqs, 2 * tile_j), bf16)

    def block_of(d):
        rows = []
        for q in range(nq):
            both = rab_ref[d, q * seqs : (q + 1) * seqs, :]
            part = both[:, : 2 * tile_j], both[:, 2 * tile_j :]
            for i in range(pack):
                pieces = [empty] * (pack // 2)
                pieces[i // 2] = part[i % 2]
                rows.append(jnp.concatenate(pieces, axis=1))
        return jnp.concatenate(rows, axis=0)

    def outer_of(n, carry):
        block = jnp.concatenate([block_of(many * n + e) for e in range(many)], axis=1)
        for m in range(groups // chunk):
            out = nn_dot(lm_ref[m * chunk * fc : (m + 1) * chunk * fc, :], block)
            high, low = high_low(out)
            for e in range(many):
                at = pl.ds(pl.multiple_of((many * n + e) * fc, fc), fc)
                for g in range(chunk):
                    group = m * chunk + g
                    to = slice(group % wide * lanes, (group % wide + 1) * lanes)
                    cut = slice(g * fc, (g + 1) * fc), slice(e * lanes, (e + 1) * lanes)
                    oh_ref[group // wide, at, to] = high[cut]
                    ol_ref[group // wide, at, to] = low[cut]
        return carry

    lax.fori_loop(0, width_d // many, outer_of, 0)

    ready()
    some = z // fc
    for n in range(width_d // some):
        block = jnp.concatenate(
            [m_ref[pl.ds(n * some + e, fc, stride=width_d), :] for e in range(some)], axis=0
        ).T
        high, low = high_low(block)
        mt_ref[:z, n * z : (n + 1) * z] = high
        mt_ref[z:, n * z : (n + 1) * z] = low
    maskj = column_mask(mask_ref, col, tile_j, 2)

    maskl = jnp.concatenate([maskj] * (pack // 2), axis=1) > 0
    score = score_ref[...]
    s1 = score.astype(bf16).astype(f32)
    s2 = (score - s1).astype(bf16).astype(f32)
    s3 = score - s1 - s2
    none = jnp.zeros_like(s1)
    st = jnp.concatenate(
        [
            jnp.concatenate([s1, s2, s3, none], axis=0),
            jnp.concatenate([s1, s2, none, none], axis=0),
        ],
        axis=1,
    ).astype(bf16)

    def finish(n, carry):
        two = nn_dot(mt_ref[...], oh_ref[n])
        update_ref[...] = two[:z] + two[z:] + nn_dot(mt_ref[:z, :], ol_ref[n])
        for e in range(wide):
            g = n * wide + e
            at = pl.ds(pl.multiple_of(g * lanes, lanes), lanes)
            before = pair_ref[at, :].T.astype(f32)
            result = (before + update_ref[:, e * lanes : (e + 1) * lanes]).astype(bf16)
            x = result.astype(f32)
            pout_ref[at, :] = result.T
            center = x - jnp.mean(x, axis=0, keepdims=True)
            inverse = lax.rsqrt(jnp.mean(center * center, axis=0, keepdims=True) + epsilon)
            normal = center * inverse
            normal_ref[g] = normal
            inverse_ref[g] = jnp.broadcast_to(inverse, inverse_ref.shape[1:])
            high, low = high_low(normal)
            scores = nn_dot(st, jnp.concatenate([high, low], axis=0))
            logits = scores[:heads] + scores[heads : 2 * heads] + scores[2 * heads : 3 * heads]
            logits_ref[g] = jnp.where(maskl, logits, far_below)
        at = pl.ds(pl.multiple_of(n * wide * lanes, wide * lanes), wide * lanes)
        pltpu.make_async_copy(pout_ref.at[at], pout_hbm.at[at], out_sem.at[n]).start()
        return carry

    lax.fori_loop(0, groups // wide, finish, 0)
    for n in range(groups // wide):
        at = pl.ds(n * wide * lanes, wide * lanes)
        pltpu.make_async_copy(pout_ref.at[at], pout_hbm.at[at], out_sem.at[n]).wait()


def by_heads(w, heads, out_ref):
    width, chans = w.shape
    hw = chans // heads
    block = 4 * hw
    slot = lax.broadcasted_iota(jnp.int32, (width, block), 1) // hw
    w = w.astype(f32)
    for t in range(chans // block):
        part = w[:, t * block : (t + 1) * block]
        turns = [part] + [pltpu.roll(part, n * hw, 1) for n in range(1, 4)]
        for e in range(4):
            h = t * 4 + e
            for s in range(4):
                out_ref[s * width : (s + 1) * width, h * block : (h + 1) * block] = jnp.where(
                    slot == s, turns[(s - e) % 4], 0.0
                ).astype(bf16)


def weights_kernel(
    ready,
    row_ref,
    col_ref,
    side0_ref,
    side1_ref,
    side2_ref,
    side3_ref,
    cols0_ref,
    cols1_ref,
    weights_ref,
    gw_ref,
    cols_ref,
    acc_ref,
    bv_ref,
    bg_ref,
    bf_ref,
    rows_ref,
    gs_ref,
    vs_ref,
):
    nk, half, tokens, _ = cols_ref.shape
    tile = nk * tokens
    groups, heads, lanes = gw_ref.shape
    row, col = row_ref[0], col_ref[0]
    count = half * tokens
    size = side0_ref.shape[0] - 2 * count
    for t, ref in enumerate((side0_ref, side1_ref, side2_ref, side3_ref)):
        k = jnp.bitwise_xor(col, t)
        rows_ref[k] = ref[size : size + 2 * count, :].reshape(rows_ref.shape[1:])
    for t in range(nk):
        ref = (cols0_ref, cols1_ref)[t // 2]
        start = ref.shape[0] // 2 * (t % 2)
        part = ref[start : start + count, :]
        cols_ref[jnp.bitwise_xor(row, t)] = part.reshape(cols_ref.shape[1:])
    chans = weights_ref.shape[1] // 3
    by_heads(weights_ref[:, :chans], heads, bv_ref)
    by_heads(weights_ref[:, chans : 2 * chans], heads, bg_ref)
    by_heads(weights_ref[:, 2 * chans :], heads, bf_ref)
    block = bv_ref.shape[1] // heads

    def four(read, n):
        return jnp.concatenate(
            [
                jnp.concatenate(
                    [
                        jnp.concatenate([read(k, 2 * (2 * n + e) + p) for k in range(nk)], axis=0)
                        for p in range(2)
                    ],
                    axis=1,
                )
                for e in range(2)
            ],
            axis=0,
        )

    for hp in range(heads // 2):
        cut = slice(hp * 2 * block, (hp + 1) * 2 * block)
        for n in range(half // 4):
            v = nn_dot(four(lambda k, s: cols_ref[k, s], n), bv_ref[:, cut]).astype(bf16)
            gate = nn_dot(four(lambda k, s: rows_ref[k, 1, s], n), bg_ref[:, cut])
            grad = nn_dot(four(lambda k, s: rows_ref[k, 0, s], n), bf_ref[:, cut])
            g = (grad * jax.nn.sigmoid(gate)).astype(bf16)
            for e in range(2):
                to = slice((2 * n + e) * block, (2 * n + e + 1) * block)
                for o in range(2):
                    mine = slice(o * block, (o + 1) * block)
                    ve = v[e * tile : (e + 1) * tile, mine]
                    vs_ref[2 * hp + o, :tile, to] = ve
                    vs_ref[2 * hp + o, tile:, to] = ve
                    gs_ref[2 * hp + o, :, to] = g[e * tile : (e + 1) * tile, mine]
    for h in range(heads):
        acc_ref[h * tile : (h + 1) * tile, :] = nt_dot(gs_ref[h], vs_ref[h])

    first = lax.broadcasted_iota(jnp.int32, (groups, 2 * tile), 1) < tile
    for h in range(heads):
        for part in range(pack // 2):
            a = acc_ref[pl.ds(h * tile + 2 * part, groups, stride=pack), :]
            b = acc_ref[pl.ds(h * tile + 2 * part + 1, groups, stride=pack), :]
            gw_ref[:, h, part * 2 * tile : (part + 1) * 2 * tile] = jnp.where(first, a, b)


def softmax_kernel(
    ready,
    col_ref,
    logits_ref,
    gwa_ref,
    gwb_ref,
    mask_ref,
    gw_ref,
    own_ref,
    pay1_ref,
    pay2_ref,
    pay3_ref,
):
    groups, heads, lanes = logits_ref.shape
    tile = lanes // pack
    nk = 4
    rows = groups * heads
    col = col_ref[0]
    gw_ref[...] = gwa_ref[...] + gwb_ref[...]
    lane = lax.broadcasted_iota(jnp.int32, (rows, 2 * tile), 1)
    low = lane < tile
    maskj = column_mask(mask_ref, col, tile, 2)
    stats = jnp.zeros((rows, 2 * tile), f32)
    for part in range(pack // 2):
        cut = slice(part * 2 * tile, (part + 1) * 2 * tile)
        lg = logits_ref[:, :, cut].reshape(rows, 2 * tile)
        gw = gw_ref[:, :, cut].reshape(rows, 2 * tile)
        m0 = jnp.max(jnp.where(low, lg, far_below), axis=1, keepdims=True)
        m1 = jnp.max(jnp.where(low, far_below, lg), axis=1, keepdims=True)
        p = jnp.exp(lg - jnp.where(low, m0, m1)) * maskj
        pg = p * gw
        for e, m in ((0, m0), (1, m1)):
            mine = low if e == 0 else jnp.logical_not(low)
            i = 2 * part + e
            total = jnp.sum(jnp.where(mine, p, 0.0), axis=1, keepdims=True)
            inner = jnp.sum(jnp.where(mine, pg, 0.0), axis=1, keepdims=True)
            stats = jnp.where(lane == i, m, stats)
            stats = jnp.where(lane == pack + i, total, stats)
            stats = jnp.where(lane == 2 * pack + i, inner, stats)
    turned = stats.T[:16]
    per = groups // nk
    for shift, pay in enumerate((own_ref, pay1_ref, pay2_ref, pay3_ref)):
        dest = lax.rem(col + shift, nk)
        pay[0] = turned[:8]
        pay[1] = turned[8:]
        for g in range(per):
            piece = logits_ref[dest * per + g]
            for part in range(pack // 2):
                pay[2 + g * (pack // 2) + part] = piece[:, part * 2 * tile : (part + 1) * 2 * tile]


def values_kernel(
    ready, col_ref, ev0_ref, ev1_ref, ev2_ref, ev3_ref, wv_ref, norm_ref, wg_ref, v_ref, gate_ref, ev_ref
):
    nr, nk, half, tokens, wide = ev_ref.shape
    chans = wv_ref.shape[1]
    for t, ref in enumerate((ev0_ref, ev1_ref, ev2_ref, ev3_ref)):
        ev_ref[jnp.bitwise_xor(col_ref[0], t)] = ref[...]
    gate = jax.nn.sigmoid(nn_dot(norm_ref[...], twice(wg_ref[...])))
    gate_ref[: half * tokens] = gate[:, :chans]
    gate_ref[half * tokens :] = gate[:, chans:]
    wv = twice(wv_ref[...])
    for s in range(half):
        x = jnp.concatenate([ev_ref[r, k, s] for r in range(nr) for k in range(nk)], axis=0)
        v_ref[s] = nn_dot(x, wv).astype(bf16)


def gradient_kernel(
    ready,
    own_ref, r1_ref, r2_ref, r3_ref, logits_ref, gw_ref, normal_ref, inverse_ref, score_ref, out_hbm, stat_ref, out_ref, out_sem
):
    groups, heads, lanes = logits_ref.shape
    rows = groups * heads
    score = score_ref[...]
    z = score.shape[1]
    s1 = score.astype(bf16).astype(f32)
    s2 = (score - s1).astype(bf16).astype(f32)
    s3 = score - s1 - s2
    parts = [s1, s1, s1, s2, s2, s3, jnp.zeros((z - 6 * heads, z), f32)]
    sk = jnp.concatenate(parts, axis=0).T[:, : 6 * heads].astype(bf16)
    pays = (own_ref, r1_ref, r2_ref, r3_ref)
    ms = [p[0][:pack] for p in pays]
    ls = [p[0][pack : 2 * pack] for p in pays]
    ns = [p[1][:pack] for p in pays]
    top = functools.reduce(jnp.maximum, ms)
    scales = [jnp.exp(m - top) for m in ms]
    total = sum(a * b for a, b in zip(ls, scales))
    inner = sum(a * b for a, b in zip(ns, scales)) / total
    stacked = jnp.concatenate([top, total, inner, jnp.zeros((rows - 3 * pack, rows), f32)], axis=0)
    stat_ref[...] = stacked.T

    tile = lanes // pack
    low = lax.broadcasted_iota(jnp.int32, (heads, 2 * tile), 1) < tile

    def one(g):
        st = stat_ref[pl.ds(pl.multiple_of(g * heads, heads), heads), :]

        def spread(base):
            halves = [
                jnp.where(
                    low,
                    st[:, base + 2 * half : base + 2 * half + 1],
                    st[:, base + 2 * half + 1 : base + 2 * half + 2],
                )
                for half in range(pack // 2)
            ]
            return jnp.concatenate(halves, axis=1)

        prob = jnp.exp(logits_ref[g] - spread(0)) / spread(pack)
        gl = prob * (gw_ref[g] - spread(2 * pack))
        g1 = gl.astype(bf16).astype(f32)
        g2 = (gl - g1).astype(bf16).astype(f32)
        g3 = gl - g1 - g2
        stack = jnp.concatenate([g1, g2, g3, g1, g2, g1], axis=0).astype(bf16)
        grad = nn_dot(sk, stack)
        normal = normal_ref[g]
        inverse = inverse_ref[g][:1]
        centered = grad - jnp.mean(grad, axis=0, keepdims=True)
        along = jnp.mean(grad * normal, axis=0, keepdims=True)
        result = inverse * (centered - normal * along)
        out_ref[pl.ds(pl.multiple_of(g * lanes, lanes), lanes), :] = result.astype(bf16).T

    many = 4

    def some(n, carry):
        for e in range(many):
            one(n * many + e)
        at = pl.ds(pl.multiple_of(n * many * lanes, many * lanes), many * lanes)
        pltpu.make_async_copy(out_ref.at[at], out_hbm.at[at], out_sem.at[n]).start()
        return carry

    lax.fori_loop(0, groups // many, some, 0)
    for n in range(groups // many):
        at = pl.ds(n * many * lanes, many * lanes)
        pltpu.make_async_copy(out_ref.at[at], out_hbm.at[at], out_sem.at[n]).wait()


def alignment_kernel(
    ready,
    col_ref,
    own_ref,
    r1_ref,
    r2_ref,
    r3_ref,
    v_ref,
    gate_ref,
    x_ref,
    wf_ref,
    out_ref,
    w_ref,
    gated_ref,
):
    pays = (own_ref, r1_ref, r2_ref, r3_ref)
    nk = len(pays)
    heads = own_ref.shape[1]
    wide = own_ref.shape[2]
    tile = wide // 2
    pieces = own_ref.shape[0] - 2
    rows = pieces * heads
    half, all_tokens, chans = v_ref.shape
    chans = chans // 2
    tokens = pieces * 2
    head_width = chans // heads
    col = col_ref[0]

    low = lax.broadcasted_iota(jnp.int32, (rows, wide), 1) < tile
    lgs = [p[2:].reshape(rows, wide) for p in pays]
    peak = functools.reduce(jnp.maximum, lgs)
    m0 = jnp.max(jnp.where(low, peak, far_below), axis=1, keepdims=True)
    m1 = jnp.max(jnp.where(low, far_below, peak), axis=1, keepdims=True)
    top = jnp.where(low, m0, m1)
    ps = [jnp.exp(lg - top) for lg in lgs]
    every = sum(ps)
    t0 = jnp.sum(jnp.where(low, every, 0.0), axis=1, keepdims=True)
    t1 = jnp.sum(jnp.where(low, 0.0, every), axis=1, keepdims=True)
    total = jnp.where(low, t0, t1)
    for shift, p in enumerate(ps):
        source = lax.rem(col + nk - shift, nk)
        weight = p / total
        rolled = pltpu.roll(weight, tile, 1)
        for n in range(pieces):
            w_ref[source, :, 2 * n, :] = weight[n * heads : (n + 1) * heads]
            w_ref[source, :, 2 * n + 1, :] = rolled[n * heads : (n + 1) * heads]
    w = jnp.concatenate(
        [
            w_ref[k].reshape(heads * tokens, wide)[:, :tile]
            for k in range(nk)
        ],
        axis=1,
    ).astype(bf16)

    owner = lax.broadcasted_iota(jnp.int32, (tokens, chans), 1) // head_width

    def one(s, carry):
        full = nn_dot(w, v_ref[s])
        for e in range(2):
            cut = slice(e * chans, (e + 1) * chans)
            mean = jnp.zeros((tokens, chans), f32)
            for h in range(heads):
                mean = jnp.where(owner == h, full[h * tokens : (h + 1) * tokens, cut], mean)
            at = pl.ds(pl.multiple_of((e * half + s) * tokens, tokens), tokens)
            gated_ref[at, :] = (gate_ref[at, :] * mean).astype(bf16)
        return carry

    lax.fori_loop(0, half, one, 0, unroll=4)
    out_ref[...] = (x_ref[...].astype(f32) + nt_dot(gated_ref[...], wf_ref[...])).astype(bf16)


def on_device(
    counts,
    alignment_input,
    pair_input,
    token_valid_mask,
    first_factor_weights,
    second_factor_weights,
    content_weights_grid,
    sigmoid_weights_grid,
    outer_matrix,
    score_matrix,
    final_mixing_weights,
    adjoint_of_rowset,
):
    nq, nr, nk = counts
    row_index = lax.axis_index("row")
    col_index = lax.axis_index("col")
    seqs, tokens, width = alignment_input.shape
    tile_i, tile_j, z = pair_input.shape
    fc = first_factor_weights.shape[1]
    fd = second_factor_weights.shape[1]
    heads = score_matrix.shape[1]
    chans = content_weights_grid.shape[1]
    groups = tile_i // pack
    lanes = pack * tile_j
    sds = jax.ShapeDtypeStruct

    mask = token_valid_mask.reshape(1, -1)
    own_start = ((row_index * nk + col_index) * tokens).astype(jnp.int32).reshape(1)
    seq_index = lax.axis_index("seq")
    place = tuple(x.astype(jnp.int32).reshape(1) for x in (row_index, col_index, seq_index))
    col_scalar = col_index.astype(jnp.int32).reshape(1)
    half = seqs // 2

    l_rows = tokens // pack * fc
    r_rows = fd * tokens // 128 * seqs
    n_rows = half * tokens
    shard, rows, normed, weights = call(
        prepare_kernel,
        (
            sds((l_rows + 2 * n_rows + r_rows, 128), bf16),
            sds((l_rows + 2 * n_rows, 128), bf16),
            sds((n_rows, 128), bf16),
            sds((width, 3 * chans), bf16),
        ),
        scratch=(
            pltpu.VMEM((tokens, seqs, width), f32),
            pltpu.VMEM((fd * tokens // 128, seqs, 128), f32),
        ),
        smem=1,
        vmem=60 * 1024 * 1024,
    )(
        own_start,
        alignment_input,
        adjoint_of_rowset,
        first_factor_weights.T,
        second_factor_weights.T,
        mask,
        content_weights_grid,
        sigmoid_weights_grid,
        final_mixing_weights.T,
    )

    def exchange(x, bit):
        return lax.ppermute(x, "col", [(c, c ^ bit) for c in range(nk)])

    other = exchange(shard, 1)
    across = exchange(rows, 2)
    pair = jnp.concatenate([x[l_rows + n_rows :] for x in (shard, other)], axis=0)
    all_cols = [
        lax.ppermute(
            pair,
            ("row", "col"),
            [(r * nk + c, (c ^ flip) * nk + r) for r in range(nr) for c in range(nk)],
        )
        for flip in (0, 2)
    ]

    across, *all_cols = lax.optimization_barrier((across, *all_cols))
    all_rows = [rows, other, across, exchange(across, 1)]

    def over_seq(x):
        if nq == 2:
            return lax.ppermute(x, "seq", [(0, 1), (1, 0)])
        return lax.all_gather(x, "seq", axis=0, tiled=True)

    (left,) = call(join_left_kernel, (sds((nk * l_rows, 128), bf16),), smem=1)(place[1], *all_rows)
    (right,) = call(join_right_kernel, (sds((nk * r_rows, 128), bf16),), smem=1)(
        place[0], *all_cols
    )
    far_left, far_right = over_seq(left), over_seq(right)

    head_lanes = seqs * chans // heads
    gw_own, block = call(
        weights_kernel,
        (
            sds((groups, heads, lanes), f32),
            sds((nk, half, tokens, 2 * width), bf16),
        ),
        scratch=(
            pltpu.VMEM((heads * tile_i, 2 * tile_j), f32),
            pltpu.VMEM((4 * width, 4 * chans), bf16),
            pltpu.VMEM((4 * width, 4 * chans), bf16),
            pltpu.VMEM((4 * width, 4 * chans), bf16),
            pltpu.VMEM((nk, 2, half, tokens, 2 * width), bf16),
            pltpu.VMEM((heads, tile_i, head_lanes), bf16),
            pltpu.VMEM((heads, 2 * tile_j, head_lanes), bf16),
        ),
        smem=2,
        flops=3_000_000_000,
        nbytes=3_000_000,
    )(*place[:2], *all_rows, *all_cols, weights)
    if nq == 2:
        gw_other = lax.ppermute(gw_own, "seq", [(0, 1), (1, 0)])
    else:
        gw_own, gw_other = lax.psum(gw_own, "seq"), jnp.zeros_like(gw_own)

    close, remote = exchange(block, 1), exchange(block, 2)

    pair_out, normal, inverse, logits = call(
        update_kernel,
        (
            sds((tile_i * tile_j, z), bf16),
            sds((groups, z, lanes), f32),
            sds((groups, 8, lanes), f32),
            sds((groups, heads, lanes), f32),
        ),
        scratch=(
            pltpu.VMEM((tile_i * tile_j, z), bf16),
            pltpu.SemaphoreType.DMA((groups // 4,)),
            pltpu.VMEM((nk, nq * r_rows, 128), bf16),
            pltpu.VMEM((fd, nq * seqs, 4 * tile_j), bf16),
            pltpu.VMEM((groups * fc, nq * pack * seqs), bf16),
            pltpu.VMEM((2 * z, fd * fc), bf16),
            pltpu.VMEM((groups // 4, fd * fc, 4 * lanes), bf16),
            pltpu.VMEM((groups // 4, fd * fc, 4 * lanes), bf16),
            pltpu.VMEM((z, 4 * lanes), f32),
        ),
        smem=2,
        flops=14_000_000_000,
        nbytes=5_000_000,
        vmem=44 * 1024 * 1024,
        far=(6, 7, 8, 9),
        far_out=(0,),
    )(
        *place[1:],
        left,
        right,
        far_left,
        far_right,
        mask,
        outer_matrix,
        score_matrix.T,
        pair_input.reshape(tile_i * tile_j, z),
    )

    payload = sds((2 + groups // nk * (pack // 2), heads, 2 * tile_j), f32)
    gw, pay0, pay1, pay2, pay3 = call(
        softmax_kernel,
        (sds((groups, heads, lanes), f32), payload, payload, payload, payload),
        smem=1,
    )(col_scalar, logits, gw_own, gw_other, mask)

    got = [
        lax.ppermute(pay, "col", [(c, (c + shift) % nk) for c in range(nk)])
        for shift, pay in ((1, pay1), (2, pay2), (3, pay3))
    ]


    close, remote, pay0 = lax.optimization_barrier((close, remote, pay0))
    every = [block, close, remote, exchange(remote, 1)]
    values, gating = call(
        values_kernel,
        (sds((half, nr * nk * tokens, 2 * chans), bf16), sds((seqs * tokens, chans), f32)),
        scratch=(pltpu.VMEM((nr, nk, half, tokens, 2 * width), bf16),),
        smem=1,
        flops=4_000_000_000,
        nbytes=6_000_000,
    )(col_scalar, *every, content_weights_grid, normed, sigmoid_weights_grid)

    got, values, gating = lax.optimization_barrier((got, values, gating))

    (gradient,) = call(
        gradient_kernel,
        (sds((tile_i * tile_j, z), bf16),),
        scratch=(
            pltpu.VMEM((groups * heads, groups * heads), f32),
            pltpu.VMEM((tile_i * tile_j, z), bf16),
            pltpu.SemaphoreType.DMA((groups // 4,)),
        ),
        far_out=(0,),
        flops=4_000_000_000,
        nbytes=3_000_000,
    )(pay0, *got, logits, gw, normal, inverse, score_matrix.T)

    (aligned,) = call(
        alignment_kernel,
        (sds((seqs * tokens, width), bf16),),
        scratch=(
            pltpu.VMEM((nk, heads, tokens, 2 * tile_j), f32),
            pltpu.VMEM((seqs * tokens, chans), bf16),
        ),
        smem=1,
        flops=3_000_000_000,
        nbytes=5_000_000,
    )(
        col_scalar,
        pay0,
        *got,
        values,
        gating,
        alignment_input.reshape(seqs * tokens, width),
        final_mixing_weights.T,
    )
    return (
        aligned.reshape(seqs, tokens, width),
        pair_out.reshape(tile_i, tile_j, z),
        gradient.reshape(tile_i, tile_j, z),
    )


def solution(mesh):
    counts = (mesh.shape["seq"], mesh.shape["row"], mesh.shape["col"])
    in_specs = (
        P("seq", ("row", "col"), None),
        P("row", "col", None),
        P(),
        P(),
        P(),
        P(),
        P(),
        P(),
        P(),
        P(),
        P("seq", ("row", "col"), None),
    )
    out_specs = (P("seq", ("row", "col"), None), P("row", "col", None), P("row", "col", None))
    return jax.shard_map(
        functools.partial(on_device, counts),
        mesh=mesh,
        in_specs=in_specs,
        out_specs=out_specs,
        check_vma=False,
    )
```

```python
import functools

import jax
import jax.numpy as jnp
from jax import lax
from jax.experimental import pallas as pl
from jax.experimental.pallas import tpu as pltpu
from jax.sharding import PartitionSpec as P

epsilon = 1e-05
far_below = -1e30
vmem_bytes = 32 * 1024 * 1024
pack = 4

f32 = jnp.float32
bf16 = jnp.bfloat16


def nt_dot(a, b):
    return lax.dot_general(a, b, (((1,), (1,)), ((), ())), preferred_element_type=f32)


def nn_dot(a, b):
    return jnp.dot(a, b, preferred_element_type=f32)


def high_low(x):
    high = x.astype(bf16)
    return high, (x - high.astype(f32)).astype(bf16)


def call(
    kernel, out_shape, scratch=(), smem=0, flops=0, nbytes=0, vmem=vmem_bytes, far=(), far_out=()
):
    def run(*args):
        count = len(args)
        in_specs = [
            pl.BlockSpec(memory_space=pltpu.SMEM if n < smem else pltpu.VMEM) for n in range(count)
        ]
        for n in far:
            in_specs[n] = pl.BlockSpec(memory_space=pltpu.HBM)
        landing = [pltpu.VMEM(args[n].shape, args[n].dtype) for n in far]
        if far:
            landing.append(pltpu.SemaphoreType.DMA((len(far),)))

        def body(*refs):
            inputs = list(refs[:count])
            extra = refs[len(refs) - len(landing) :]
            rest = refs[count : len(refs) - len(landing)]
            copies = []
            for i, n in enumerate(far):
                copies.append(pltpu.make_async_copy(inputs[n], extra[i], extra[-1].at[i]))
                copies[-1].start()
                inputs[n] = extra[i]

            def ready():
                for copy in copies:
                    copy.wait()

            kernel(ready, *inputs, *rest)

        return pl.pallas_call(
            body,
            out_shape=out_shape,
            in_specs=in_specs,
            out_specs=[
                pl.BlockSpec(memory_space=pltpu.HBM if n in far_out else pltpu.VMEM)
                for n in range(len(out_shape))
            ],
            scratch_shapes=list(scratch) + landing,
            compiler_params=pltpu.CompilerParams(vmem_limit_bytes=vmem),
            cost_estimate=pl.CostEstimate(flops=flops, bytes_accessed=nbytes, transcendentals=0),
        )(*args)

    return run


def valid_count(mask_ref):
    return jnp.sum(mask_ref[...].astype(f32), axis=1, keepdims=True)


def column_mask(mask_ref, col, tile, copies):
    lane = lax.broadcasted_iota(jnp.int32, (1, copies * tile), 1)
    token = (lax.rem(lane, tile) + col * tile).astype(f32)
    return (token < valid_count(mask_ref)).astype(f32)


def twice(w):
    none = jnp.zeros_like(w)
    return jnp.concatenate(
        [jnp.concatenate([w, none], axis=1), jnp.concatenate([none, w], axis=1)], axis=0
    )


def prepare_kernel(
    ready,
    own_ref,
    x_ref,
    adj_ref,
    w1_ref,
    w2_ref,
    mask_ref,
    wv_ref,
    wg_ref,
    wf_ref,
    shard_ref,
    rows_ref,
    left_ref,
    norm_ref,
    weights_ref,
    turn_ref,
    place_ref,
):
    chans = wv_ref.shape[1]
    weights_ref[:, :chans] = wv_ref[...]
    weights_ref[:, chans : 2 * chans] = wg_ref[...]
    weights_ref[:, 2 * chans :] = wf_ref[...]
    seqs, tokens, width = x_ref.shape
    half = seqs // 2
    fd = w2_ref.shape[0]
    x = x_ref[...].astype(f32)
    center = x - jnp.mean(x, axis=-1, keepdims=True)
    inverse = lax.rsqrt(jnp.mean(center * center, axis=-1, keepdims=True) + epsilon)
    normed = center * inverse
    rows = half * tokens
    adj = adj_ref[...].astype(f32)

    def two(x):
        x = jnp.concatenate([x[:half], x[half:]], axis=-1)
        return x.reshape(rows, 2 * width).astype(bf16)

    packed = two(normed)
    norm_ref[...] = packed
    base = tokens // pack * w1_ref.shape[0]
    shard_ref[base : base + rows, :] = two(adj)
    shard_ref[base + rows : base + 2 * rows, :] = packed
    token = lax.broadcasted_iota(jnp.int32, (seqs, tokens, width), 1) + own_ref[0]
    count = valid_count(mask_ref).reshape(1, 1, 1)
    real = jnp.where(token.astype(f32) < count, normed, 0.0)
    for s in range(seqs):
        turn_ref[:, s, :] = real[s]
    turned = turn_ref[...].astype(bf16).reshape(tokens * seqs, width)
    left = nt_dot(w1_ref[...], turned).astype(bf16)
    fc = w1_ref.shape[0]
    wk = pack * seqs
    for g in range(tokens // pack):
        shard_ref[g * fc : (g + 1) * fc, :] = left[:, g * wk : (g + 1) * wk]
    size = 128 // tokens
    real = real.astype(bf16)
    w2 = w2_ref[...]
    d = lax.broadcasted_iota(jnp.int32, (fd, 128), 0)
    lane = lax.broadcasted_iota(jnp.int32, (fd, 128), 1)
    mine = lax.rem(d, size) == lane // tokens
    for s in range(seqs):
        res = nt_dot(w2, jnp.concatenate([real[s]] * size, axis=0))
        res = jnp.where(mine, res, 0.0).reshape(fd // size, size, 128)
        place_ref[:, s, :] = jnp.sum(res, axis=1)
    right = place_ref[...].reshape(fd // size * seqs, 128).astype(bf16)
    rows_ref[...] = shard_ref[: base + 2 * rows, :]
    left_ref[...] = shard_ref[:base, :]
    shard_ref[base + 2 * rows :, :] = right


def join_left_kernel(ready, col_ref, rows0_ref, rows1_ref, rows2_ref, rows3_ref, out_ref):
    size = out_ref.shape[0] // 4
    for t, ref in enumerate((rows0_ref, rows1_ref, rows2_ref, rows3_ref)):
        at = pl.ds(pl.multiple_of(jnp.bitwise_xor(col_ref[0], t) * size, size), size)
        out_ref[at, :] = ref[:size, :]


def join_right_kernel(ready, row_ref, pair0_ref, pair1_ref, out_ref):
    size = out_ref.shape[0] // 4
    for t in range(4):
        ref = (pair0_ref, pair1_ref)[t // 2]
        at = pl.ds(pl.multiple_of(jnp.bitwise_xor(row_ref[0], t) * size, size), size)
        end = ref.shape[0] // 2 * (t % 2 + 1)
        out_ref[at, :] = ref[end - size : end, :]


def update_kernel(
    ready,
    col_ref,
    seq_ref,
    left_ref,
    right_ref,
    far_left_ref,
    far_right_ref,
    mask_ref,
    m_ref,
    score_ref,
    pair_ref,
    pout_hbm,
    normal_ref,
    inverse_ref,
    logits_ref,
    pout_ref,
    out_sem,
    rk_ref,
    rab_ref,
    lm_ref,
    mt_ref,
    oh_ref,
    ol_ref,
    update0_ref,
    update1_ref,
):
    nk = rk_ref.shape[0]
    width_d, pair_rows, _ = rab_ref.shape
    col, seq = col_ref[0], seq_ref[0]
    z = pair_ref.shape[1]
    groups, heads, lanes = logits_ref.shape
    tile_j = lanes // pack
    tokens = tile_j // nk
    fc = lm_ref.shape[0] // groups
    seqs = 128 // pack
    nq = pair_rows // seqs
    wk = pack * seqs

    r_rows = rk_ref.shape[1] // nq
    l_rows = groups * fc
    if nq == 2:
        sources = ((seq, 0, left_ref, right_ref), (1 - seq, 0, far_left_ref, far_right_ref))
    else:
        sources = tuple((q, q, far_left_ref, far_right_ref) for q in range(nq))
    for q, slot, from_left, from_right in sources:
        at = pl.ds(pl.multiple_of(q * r_rows, r_rows), r_rows)
        for k in range(nk):
            first = (slot * nk + k) * r_rows
            rk_ref[k, at, :] = from_right[first : first + r_rows, :]
        to = pl.ds(pl.multiple_of(q * wk, wk), wk)
        lm_ref[:, to] = from_left[slot * l_rows : (slot + 1) * l_rows, :]
    size = 128 // tokens
    right = jnp.concatenate([rk_ref[k] for k in range(nk)], axis=1)
    source = lax.broadcasted_iota(jnp.int32, (nk * 128, 4 * tile_j), 0)
    target = lax.broadcasted_iota(jnp.int32, (nk * 128, 4 * tile_j), 1)
    used = jnp.logical_or(target < tile_j, target >= 3 * tile_j)
    j = lax.rem(target, tile_j)
    offset = jnp.where(used, source - (j // tokens * 128 + lax.rem(j, tokens)), -1)
    blocks = width_d // size
    for e in range(size):
        pick = jnp.where(offset == e * tokens, 1.0, 0.0).astype(bf16)
        res = nn_dot(right, pick).astype(bf16)
        for q in range(nq):
            for n in range(blocks):
                at = (q * blocks + n) * seqs
                rab_ref[n * size + e, q * seqs : (q + 1) * seqs, :] = res[at : at + seqs]

    chunk = 8
    many = 4
    wide = oh_ref.shape[2] // lanes
    empty = jnp.zeros((seqs, 2 * tile_j), bf16)

    def block_of(d):
        rows = []
        for q in range(nq):
            both = rab_ref[d, q * seqs : (q + 1) * seqs, :]
            part = both[:, : 2 * tile_j], both[:, 2 * tile_j :]
            for i in range(pack):
                pieces = [empty] * (pack // 2)
                pieces[i // 2] = part[i % 2]
                rows.append(jnp.concatenate(pieces, axis=1))
        return jnp.concatenate(rows, axis=0)

    def outer_of(n, carry):
        block = jnp.concatenate([block_of(many * n + e) for e in range(many)], axis=1)
        for m in range(groups // chunk):
            out = nn_dot(lm_ref[m * chunk * fc : (m + 1) * chunk * fc, :], block)
            high, low = high_low(out)
            for e in range(many):
                at = pl.ds(pl.multiple_of((many * n + e) * fc, fc), fc)
                for g in range(chunk):
                    group = m * chunk + g
                    to = slice(group % wide * lanes, (group % wide + 1) * lanes)
                    cut = slice(g * fc, (g + 1) * fc), slice(e * lanes, (e + 1) * lanes)
                    oh_ref[group // wide, at, to] = high[cut]
                    ol_ref[group // wide, at, to] = low[cut]
        return carry

    lax.fori_loop(0, width_d // many, outer_of, 0, unroll=2)

    ready()
    some = z // fc
    for n in range(width_d // some):
        block = jnp.concatenate(
            [m_ref[pl.ds(n * some + e, fc, stride=width_d), :] for e in range(some)], axis=0
        ).T
        high, low = high_low(block)
        mt_ref[:z, n * z : (n + 1) * z] = high
        mt_ref[z:, n * z : (n + 1) * z] = low
    maskj = column_mask(mask_ref, col, tile_j, 2)

    maskl = jnp.concatenate([maskj] * (pack // 2), axis=1) > 0
    score = score_ref[...]
    s1 = score.astype(bf16).astype(f32)
    s2 = (score - s1).astype(bf16).astype(f32)
    s3 = score - s1 - s2
    none = jnp.zeros_like(s1)
    st = jnp.concatenate(
        [
            jnp.concatenate([s1, s2, s3, none], axis=0),
            jnp.concatenate([s1, s2, none, none], axis=0),
        ],
        axis=1,
    ).astype(bf16)

    def product(n):
        two = nn_dot(mt_ref[...], oh_ref[n])
        update_refs[n % 2][...] = two[:z] + two[z:] + nn_dot(mt_ref[:z, :], ol_ref[n])

    def finish(n):
        for e in range(wide):
            g = n * wide + e
            at = slice(g * lanes, (g + 1) * lanes)
            before = pair_ref[at, :].T.astype(f32)
            update = update_refs[n % 2][:, e * lanes : (e + 1) * lanes]
            result = (before + update).astype(bf16)
            x = result.astype(f32)
            pout_ref[at, :] = result.T
            center = x - jnp.mean(x, axis=0, keepdims=True)
            inverse = lax.rsqrt(jnp.mean(center * center, axis=0, keepdims=True) + epsilon)
            normal = center * inverse
            normal_ref[g] = normal
            inverse_ref[g] = jnp.broadcast_to(inverse, inverse_ref.shape[1:])
            high, low = high_low(normal)
            scores = nn_dot(st, jnp.concatenate([high, low], axis=0))
            logits = scores[:heads] + scores[heads : 2 * heads] + scores[2 * heads : 3 * heads]
            logits_ref[g] = jnp.where(maskl, logits, far_below)

    steps = groups // wide
    update_refs = (update0_ref, update1_ref)
    product(0)
    for n in range(1, steps):
        product(n)
        finish(n - 1)
    finish(steps - 1)
    copies = []
    for n in range(steps):
        at = pl.ds(n * wide * lanes, wide * lanes)
        copies.append(pltpu.make_async_copy(pout_ref.at[at], pout_hbm.at[at], out_sem.at[n]))
        copies[-1].start()
    for copy in copies:
        copy.wait()


def by_heads(w, heads, out_ref):
    width, chans = w.shape
    hw = chans // heads
    block = 4 * hw
    slot = lax.broadcasted_iota(jnp.int32, (width, block), 1) // hw
    w = w.astype(f32)
    for t in range(chans // block):
        part = w[:, t * block : (t + 1) * block]
        turns = [part] + [pltpu.roll(part, n * hw, 1) for n in range(1, 4)]
        for e in range(4):
            h = t * 4 + e
            for s in range(4):
                out_ref[s * width : (s + 1) * width, h * block : (h + 1) * block] = jnp.where(
                    slot == s, turns[(s - e) % 4], 0.0
                ).astype(bf16)


def weights_kernel(
    ready,
    row_ref,
    col_ref,
    side0_ref,
    side1_ref,
    side2_ref,
    side3_ref,
    cols0_ref,
    cols1_ref,
    weights_ref,
    gw_ref,
    cols_ref,
    acc_ref,
    bv_ref,
    bg_ref,
    bf_ref,
    rows_ref,
    gs_ref,
    vs_ref,
):
    nk, half, tokens, _ = cols_ref.shape
    tile = nk * tokens
    groups, heads, lanes = gw_ref.shape
    row, col = row_ref[0], col_ref[0]
    count = half * tokens
    size = side0_ref.shape[0] - 2 * count
    for t, ref in enumerate((side0_ref, side1_ref, side2_ref, side3_ref)):
        k = jnp.bitwise_xor(col, t)
        rows_ref[k] = ref[size : size + 2 * count, :].reshape(rows_ref.shape[1:])
    for t in range(nk):
        ref = (cols0_ref, cols1_ref)[t // 2]
        start = ref.shape[0] // 2 * (t % 2)
        part = ref[start : start + count, :]
        cols_ref[jnp.bitwise_xor(row, t)] = part.reshape(cols_ref.shape[1:])
    chans = weights_ref.shape[1] // 3
    by_heads(weights_ref[:, :chans], heads, bv_ref)
    by_heads(weights_ref[:, chans : 2 * chans], heads, bg_ref)
    by_heads(weights_ref[:, 2 * chans :], heads, bf_ref)
    block = bv_ref.shape[1] // heads

    def four(read, n):
        return jnp.concatenate(
            [
                jnp.concatenate(
                    [
                        jnp.concatenate([read(k, 2 * (2 * n + e) + p) for k in range(nk)], axis=0)
                        for p in range(2)
                    ],
                    axis=1,
                )
                for e in range(2)
            ],
            axis=0,
        )

    for hp in range(heads // 2):
        cut = slice(hp * 2 * block, (hp + 1) * 2 * block)
        for n in range(half // 4):
            v = nn_dot(four(lambda k, s: cols_ref[k, s], n), bv_ref[:, cut]).astype(bf16)
            gate = nn_dot(four(lambda k, s: rows_ref[k, 1, s], n), bg_ref[:, cut])
            grad = nn_dot(four(lambda k, s: rows_ref[k, 0, s], n), bf_ref[:, cut])
            g = (grad * jax.nn.sigmoid(gate)).astype(bf16)
            for e in range(2):
                to = slice((2 * n + e) * block, (2 * n + e + 1) * block)
                for o in range(2):
                    mine = slice(o * block, (o + 1) * block)
                    ve = v[e * tile : (e + 1) * tile, mine]
                    vs_ref[2 * hp + o, :tile, to] = ve
                    vs_ref[2 * hp + o, tile:, to] = ve
                    gs_ref[2 * hp + o, :, to] = g[e * tile : (e + 1) * tile, mine]
    for h in range(heads):
        acc_ref[h * tile : (h + 1) * tile, :] = nt_dot(gs_ref[h], vs_ref[h])

    first = lax.broadcasted_iota(jnp.int32, (groups, 2 * tile), 1) < tile
    for h in range(heads):
        for part in range(pack // 2):
            a = acc_ref[pl.ds(h * tile + 2 * part, groups, stride=pack), :]
            b = acc_ref[pl.ds(h * tile + 2 * part + 1, groups, stride=pack), :]
            gw_ref[:, h, part * 2 * tile : (part + 1) * 2 * tile] = jnp.where(first, a, b)


def softmax_kernel(
    ready,
    col_ref,
    logits_ref,
    gwa_ref,
    gwb_ref,
    mask_ref,
    gw_ref,
    own_ref,
    pay1_ref,
    pay2_ref,
    pay3_ref,
):
    groups, heads, lanes = logits_ref.shape
    tile = lanes // pack
    nk = 4
    rows = groups * heads
    col = col_ref[0]
    gw_ref[...] = gwa_ref[...] + gwb_ref[...]
    lane = lax.broadcasted_iota(jnp.int32, (rows, 2 * tile), 1)
    low = lane < tile
    maskj = column_mask(mask_ref, col, tile, 2)
    stats = jnp.zeros((rows, 2 * tile), f32)
    for part in range(pack // 2):
        cut = slice(part * 2 * tile, (part + 1) * 2 * tile)
        lg = logits_ref[:, :, cut].reshape(rows, 2 * tile)
        gw = gw_ref[:, :, cut].reshape(rows, 2 * tile)
        m0 = jnp.max(jnp.where(low, lg, far_below), axis=1, keepdims=True)
        m1 = jnp.max(jnp.where(low, far_below, lg), axis=1, keepdims=True)
        p = jnp.exp(lg - jnp.where(low, m0, m1)) * maskj
        pg = p * gw
        for e, m in ((0, m0), (1, m1)):
            mine = low if e == 0 else jnp.logical_not(low)
            i = 2 * part + e
            total = jnp.sum(jnp.where(mine, p, 0.0), axis=1, keepdims=True)
            inner = jnp.sum(jnp.where(mine, pg, 0.0), axis=1, keepdims=True)
            stats = jnp.where(lane == i, m, stats)
            stats = jnp.where(lane == pack + i, total, stats)
            stats = jnp.where(lane == 2 * pack + i, inner, stats)
    turned = stats.T[:16]
    per = groups // nk
    for shift, pay in enumerate((own_ref, pay1_ref, pay2_ref, pay3_ref)):
        dest = lax.rem(col + shift, nk)
        pay[0] = turned[:8]
        pay[1] = turned[8:]
        for g in range(per):
            piece = logits_ref[dest * per + g]
            for part in range(pack // 2):
                pay[2 + g * (pack // 2) + part] = piece[:, part * 2 * tile : (part + 1) * 2 * tile]


def values_kernel(
    ready, col_ref, ev0_ref, ev1_ref, ev2_ref, ev3_ref, wv_ref, norm_ref, wg_ref, v_ref, gate_ref, ev_ref
):
    nr, nk, half, tokens, wide = ev_ref.shape
    chans = wv_ref.shape[1]
    for t, ref in enumerate((ev0_ref, ev1_ref, ev2_ref, ev3_ref)):
        ev_ref[jnp.bitwise_xor(col_ref[0], t)] = ref[...]
    gate = jax.nn.sigmoid(nn_dot(norm_ref[...], twice(wg_ref[...])))
    gate_ref[: half * tokens] = gate[:, :chans]
    gate_ref[half * tokens :] = gate[:, chans:]
    wv = twice(wv_ref[...])
    for s in range(half):
        x = jnp.concatenate([ev_ref[r, k, s] for r in range(nr) for k in range(nk)], axis=0)
        v_ref[s] = nn_dot(x, wv).astype(bf16)


def gradient_kernel(
    ready,
    own_ref, r1_ref, r2_ref, r3_ref, logits_ref, gw_ref, normal_ref, inverse_ref, score_ref, out_hbm, stat_ref, out_ref, out_sem
):
    groups, heads, lanes = logits_ref.shape
    rows = groups * heads
    score = score_ref[...]
    z = score.shape[1]
    s1 = score.astype(bf16).astype(f32)
    s2 = (score - s1).astype(bf16).astype(f32)
    s3 = score - s1 - s2
    parts = [s1, s1, s1, s2, s2, s3, jnp.zeros((z - 6 * heads, z), f32)]
    sk = jnp.concatenate(parts, axis=0).T[:, : 6 * heads].astype(bf16)
    pays = (own_ref, r1_ref, r2_ref, r3_ref)
    ms = [p[0][:pack] for p in pays]
    ls = [p[0][pack : 2 * pack] for p in pays]
    ns = [p[1][:pack] for p in pays]
    top = functools.reduce(jnp.maximum, ms)
    scales = [jnp.exp(m - top) for m in ms]
    total = sum(a * b for a, b in zip(ls, scales))
    inner = sum(a * b for a, b in zip(ns, scales)) / total
    stacked = jnp.concatenate([top, total, inner, jnp.zeros((rows - 3 * pack, rows), f32)], axis=0)
    stat_ref[...] = stacked.T

    tile = lanes // pack
    low = lax.broadcasted_iota(jnp.int32, (heads, 2 * tile), 1) < tile

    def one(g):
        st = stat_ref[pl.ds(pl.multiple_of(g * heads, heads), heads), :]

        def spread(base):
            halves = [
                jnp.where(
                    low,
                    st[:, base + 2 * half : base + 2 * half + 1],
                    st[:, base + 2 * half + 1 : base + 2 * half + 2],
                )
                for half in range(pack // 2)
            ]
            return jnp.concatenate(halves, axis=1)

        prob = jnp.exp(logits_ref[g] - spread(0)) / spread(pack)
        gl = prob * (gw_ref[g] - spread(2 * pack))
        g1 = gl.astype(bf16).astype(f32)
        g2 = (gl - g1).astype(bf16).astype(f32)
        g3 = gl - g1 - g2
        stack = jnp.concatenate([g1, g2, g3, g1, g2, g1], axis=0).astype(bf16)
        grad = nn_dot(sk, stack)
        normal = normal_ref[g]
        inverse = inverse_ref[g][:1]
        centered = grad - jnp.mean(grad, axis=0, keepdims=True)
        along = jnp.mean(grad * normal, axis=0, keepdims=True)
        result = inverse * (centered - normal * along)
        out_ref[pl.ds(pl.multiple_of(g * lanes, lanes), lanes), :] = result.astype(bf16).T

    many = 4

    def some(n, carry):
        for e in range(many):
            one(n * many + e)
        at = pl.ds(pl.multiple_of(n * many * lanes, many * lanes), many * lanes)
        pltpu.make_async_copy(out_ref.at[at], out_hbm.at[at], out_sem.at[n]).start()
        return carry

    lax.fori_loop(0, groups // many, some, 0)
    for n in range(groups // many):
        at = pl.ds(n * many * lanes, many * lanes)
        pltpu.make_async_copy(out_ref.at[at], out_hbm.at[at], out_sem.at[n]).wait()


def alignment_kernel(
    ready,
    col_ref,
    own_ref,
    r1_ref,
    r2_ref,
    r3_ref,
    v_ref,
    gate_ref,
    x_ref,
    wf_ref,
    out_ref,
    w_ref,
    gated_ref,
):
    pays = (own_ref, r1_ref, r2_ref, r3_ref)
    nk = len(pays)
    heads = own_ref.shape[1]
    wide = own_ref.shape[2]
    tile = wide // 2
    pieces = own_ref.shape[0] - 2
    rows = pieces * heads
    half, all_tokens, chans = v_ref.shape
    chans = chans // 2
    tokens = pieces * 2
    head_width = chans // heads
    col = col_ref[0]

    low = lax.broadcasted_iota(jnp.int32, (rows, wide), 1) < tile
    lgs = [p[2:].reshape(rows, wide) for p in pays]
    peak = functools.reduce(jnp.maximum, lgs)
    m0 = jnp.max(jnp.where(low, peak, far_below), axis=1, keepdims=True)
    m1 = jnp.max(jnp.where(low, far_below, peak), axis=1, keepdims=True)
    top = jnp.where(low, m0, m1)
    ps = [jnp.exp(lg - top) for lg in lgs]
    every = sum(ps)
    t0 = jnp.sum(jnp.where(low, every, 0.0), axis=1, keepdims=True)
    t1 = jnp.sum(jnp.where(low, 0.0, every), axis=1, keepdims=True)
    total = jnp.where(low, t0, t1)
    for shift, p in enumerate(ps):
        source = lax.rem(col + nk - shift, nk)
        weight = p / total
        rolled = pltpu.roll(weight, tile, 1)
        for n in range(pieces):
            w_ref[source, :, 2 * n, :] = weight[n * heads : (n + 1) * heads]
            w_ref[source, :, 2 * n + 1, :] = rolled[n * heads : (n + 1) * heads]
    w = jnp.concatenate(
        [
            w_ref[k].reshape(heads * tokens, wide)[:, :tile]
            for k in range(nk)
        ],
        axis=1,
    ).astype(bf16)

    owner = lax.broadcasted_iota(jnp.int32, (tokens, chans), 1) // head_width

    def one(s, carry):
        full = nn_dot(w, v_ref[s])
        for e in range(2):
            cut = slice(e * chans, (e + 1) * chans)
            mean = jnp.zeros((tokens, chans), f32)
            for h in range(heads):
                mean = jnp.where(owner == h, full[h * tokens : (h + 1) * tokens, cut], mean)
            at = pl.ds(pl.multiple_of((e * half + s) * tokens, tokens), tokens)
            gated_ref[at, :] = (gate_ref[at, :] * mean).astype(bf16)
        return carry

    lax.fori_loop(0, half, one, 0, unroll=4)
    out_ref[...] = (x_ref[...].astype(f32) + nt_dot(gated_ref[...], wf_ref[...])).astype(bf16)


def on_device(
    counts,
    alignment_input,
    pair_input,
    token_valid_mask,
    first_factor_weights,
    second_factor_weights,
    content_weights_grid,
    sigmoid_weights_grid,
    outer_matrix,
    score_matrix,
    final_mixing_weights,
    adjoint_of_rowset,
):
    nq, nr, nk = counts
    row_index = lax.axis_index("row")
    col_index = lax.axis_index("col")
    seqs, tokens, width = alignment_input.shape
    tile_i, tile_j, z = pair_input.shape
    fc = first_factor_weights.shape[1]
    fd = second_factor_weights.shape[1]
    heads = score_matrix.shape[1]
    chans = content_weights_grid.shape[1]
    groups = tile_i // pack
    lanes = pack * tile_j
    sds = jax.ShapeDtypeStruct

    mask = token_valid_mask.reshape(1, -1)
    own_start = ((row_index * nk + col_index) * tokens).astype(jnp.int32).reshape(1)
    seq_index = lax.axis_index("seq")
    place = tuple(x.astype(jnp.int32).reshape(1) for x in (row_index, col_index, seq_index))
    col_scalar = col_index.astype(jnp.int32).reshape(1)
    half = seqs // 2

    l_rows = tokens // pack * fc
    r_rows = fd * tokens // 128 * seqs
    n_rows = half * tokens
    shard, rows, own_left, normed, weights = call(
        prepare_kernel,
        (
            sds((l_rows + 2 * n_rows + r_rows, 128), bf16),
            sds((l_rows + 2 * n_rows, 128), bf16),
            sds((l_rows, 128), bf16),
            sds((n_rows, 128), bf16),
            sds((width, 3 * chans), bf16),
        ),
        scratch=(
            pltpu.VMEM((tokens, seqs, width), f32),
            pltpu.VMEM((fd * tokens // 128, seqs, 128), f32),
        ),
        smem=1,
        vmem=60 * 1024 * 1024,
    )(
        own_start,
        alignment_input,
        adjoint_of_rowset,
        first_factor_weights.T,
        second_factor_weights.T,
        mask,
        content_weights_grid,
        sigmoid_weights_grid,
        final_mixing_weights.T,
    )

    def exchange(x, bit):
        return lax.ppermute(x, "col", [(c, c ^ bit) for c in range(nk)])

    other = exchange(shard, 1)
    across = exchange(rows, 2)
    pair = jnp.concatenate([x[l_rows + n_rows :] for x in (shard, other)], axis=0)
    all_cols = [
        lax.ppermute(
            pair,
            ("row", "col"),
            [(r * nk + c, (c ^ flip) * nk + r) for r in range(nr) for c in range(nk)],
        )
        for flip in (0, 2)
    ]

    def over_seq(x):
        if nq == 2:
            return lax.ppermute(x, "seq", [(0, 1), (1, 0)])
        return lax.all_gather(x, "seq", axis=0, tiled=True)

    lefts = [own_left, other, across, exchange(own_left, 3)]
    (left,) = call(join_left_kernel, (sds((nk * l_rows, 128), bf16),), smem=1)(place[1], *lefts)
    far_left = over_seq(left)
    across, far_left, *all_cols = lax.optimization_barrier((across, far_left, *all_cols))
    all_rows = [rows, other, across, exchange(across, 1)]

    (right,) = call(join_right_kernel, (sds((nk * r_rows, 128), bf16),), smem=1)(
        place[0], *all_cols
    )
    far_right = over_seq(right)

    head_lanes = seqs * chans // heads
    gw_own, block = call(
        weights_kernel,
        (
            sds((groups, heads, lanes), f32),
            sds((nk, half, tokens, 2 * width), bf16),
        ),
        scratch=(
            pltpu.VMEM((heads * tile_i, 2 * tile_j), f32),
            pltpu.VMEM((4 * width, 4 * chans), bf16),
            pltpu.VMEM((4 * width, 4 * chans), bf16),
            pltpu.VMEM((4 * width, 4 * chans), bf16),
            pltpu.VMEM((nk, 2, half, tokens, 2 * width), bf16),
            pltpu.VMEM((heads, tile_i, head_lanes), bf16),
            pltpu.VMEM((heads, 2 * tile_j, head_lanes), bf16),
        ),
        smem=2,
        flops=3_000_000_000,
        nbytes=3_000_000,
    )(*place[:2], *all_rows, *all_cols, weights)
    if nq == 2:
        gw_other = lax.ppermute(gw_own, "seq", [(0, 1), (1, 0)])
    else:
        gw_own, gw_other = lax.psum(gw_own, "seq"), jnp.zeros_like(gw_own)

    close, remote = exchange(block, 1), exchange(block, 2)

    pair_out, normal, inverse, logits = call(
        update_kernel,
        (
            sds((tile_i * tile_j, z), bf16),
            sds((groups, z, lanes), f32),
            sds((groups, 8, lanes), f32),
            sds((groups, heads, lanes), f32),
        ),
        scratch=(
            pltpu.VMEM((tile_i * tile_j, z), bf16),
            pltpu.SemaphoreType.DMA((groups // 4,)),
            pltpu.VMEM((nk, nq * r_rows, 128), bf16),
            pltpu.VMEM((fd, nq * seqs, 4 * tile_j), bf16),
            pltpu.VMEM((groups * fc, nq * pack * seqs), bf16),
            pltpu.VMEM((2 * z, fd * fc), bf16),
            pltpu.VMEM((groups // 4, fd * fc, 4 * lanes), bf16),
            pltpu.VMEM((groups // 4, fd * fc, 4 * lanes), bf16),
            pltpu.VMEM((z, 4 * lanes), f32),
            pltpu.VMEM((z, 4 * lanes), f32),
        ),
        smem=2,
        flops=14_000_000_000,
        nbytes=5_000_000,
        vmem=44 * 1024 * 1024,
        far=(6, 7, 8, 9),
        far_out=(0,),
    )(
        *place[1:],
        left,
        right,
        far_left,
        far_right,
        mask,
        outer_matrix,
        score_matrix.T,
        pair_input.reshape(tile_i * tile_j, z),
    )

    payload = sds((2 + groups // nk * (pack // 2), heads, 2 * tile_j), f32)
    gw, pay0, pay1, pay2, pay3 = call(
        softmax_kernel,
        (sds((groups, heads, lanes), f32), payload, payload, payload, payload),
        smem=1,
    )(col_scalar, logits, gw_own, gw_other, mask)

    got = [
        lax.ppermute(pay, "col", [(c, (c + shift) % nk) for c in range(nk)])
        for shift, pay in ((1, pay1), (2, pay2), (3, pay3))
    ]


    close, remote, pay0 = lax.optimization_barrier((close, remote, pay0))
    every = [block, close, remote, exchange(remote, 1)]
    values, gating = call(
        values_kernel,
        (sds((half, nr * nk * tokens, 2 * chans), bf16), sds((seqs * tokens, chans), f32)),
        scratch=(pltpu.VMEM((nr, nk, half, tokens, 2 * width), bf16),),
        smem=1,
        flops=4_000_000_000,
        nbytes=6_000_000,
    )(col_scalar, *every, content_weights_grid, normed, sigmoid_weights_grid)

    got, values, gating = lax.optimization_barrier((got, values, gating))

    (gradient,) = call(
        gradient_kernel,
        (sds((tile_i * tile_j, z), bf16),),
        scratch=(
            pltpu.VMEM((groups * heads, groups * heads), f32),
            pltpu.VMEM((tile_i * tile_j, z), bf16),
            pltpu.SemaphoreType.DMA((groups // 4,)),
        ),
        far_out=(0,),
        flops=4_000_000_000,
        nbytes=3_000_000,
    )(pay0, *got, logits, gw, normal, inverse, score_matrix.T)

    (aligned,) = call(
        alignment_kernel,
        (sds((seqs * tokens, width), bf16),),
        scratch=(
            pltpu.VMEM((nk, heads, tokens, 2 * tile_j), f32),
            pltpu.VMEM((seqs * tokens, chans), bf16),
        ),
        smem=1,
        flops=3_000_000_000,
        nbytes=5_000_000,
    )(
        col_scalar,
        pay0,
        *got,
        values,
        gating,
        alignment_input.reshape(seqs * tokens, width),
        final_mixing_weights.T,
    )
    return (
        aligned.reshape(seqs, tokens, width),
        pair_out.reshape(tile_i, tile_j, z),
        gradient.reshape(tile_i, tile_j, z),
    )


def solution(mesh):
    counts = (mesh.shape["seq"], mesh.shape["row"], mesh.shape["col"])
    in_specs = (
        P("seq", ("row", "col"), None),
        P("row", "col", None),
        P(),
        P(),
        P(),
        P(),
        P(),
        P(),
        P(),
        P(),
        P("seq", ("row", "col"), None),
    )
    out_specs = (P("seq", ("row", "col"), None), P("row", "col", None), P("row", "col", None))
    return jax.shard_map(
        functools.partial(on_device, counts),
        mesh=mesh,
        in_specs=in_specs,
        out_specs=out_specs,
        check_vma=False,
    )
```

```python
import functools

import jax
import jax.numpy as jnp
from jax import lax
from jax.experimental import pallas as pl
from jax.experimental.pallas import tpu as pltpu
from jax.sharding import PartitionSpec as P

epsilon = 1e-05
far_below = -1e30
vmem_bytes = 32 * 1024 * 1024
pack = 4

f32 = jnp.float32
bf16 = jnp.bfloat16


def nt_dot(a, b):
    return lax.dot_general(a, b, (((1,), (1,)), ((), ())), preferred_element_type=f32)


def nn_dot(a, b):
    return jnp.dot(a, b, preferred_element_type=f32)


def high_low(x):
    high = x.astype(bf16)
    return high, (x - high.astype(f32)).astype(bf16)


def call(
    kernel, out_shape, scratch=(), smem=0, flops=0, nbytes=0, vmem=vmem_bytes, far=(), far_out=()
):
    def run(*args):
        count = len(args)
        in_specs = [
            pl.BlockSpec(memory_space=pltpu.SMEM if n < smem else pltpu.VMEM) for n in range(count)
        ]
        for n in far:
            in_specs[n] = pl.BlockSpec(memory_space=pltpu.HBM)
        landing = [pltpu.VMEM(args[n].shape, args[n].dtype) for n in far]
        if far:
            landing.append(pltpu.SemaphoreType.DMA((len(far),)))

        def body(*refs):
            inputs = list(refs[:count])
            extra = refs[len(refs) - len(landing) :]
            rest = refs[count : len(refs) - len(landing)]
            copies = []
            for i, n in enumerate(far):
                copies.append(pltpu.make_async_copy(inputs[n], extra[i], extra[-1].at[i]))
                copies[-1].start()
                inputs[n] = extra[i]

            def ready():
                for copy in copies:
                    copy.wait()

            kernel(ready, *inputs, *rest)

        return pl.pallas_call(
            body,
            out_shape=out_shape,
            in_specs=in_specs,
            out_specs=[
                pl.BlockSpec(memory_space=pltpu.HBM if n in far_out else pltpu.VMEM)
                for n in range(len(out_shape))
            ],
            scratch_shapes=list(scratch) + landing,
            compiler_params=pltpu.CompilerParams(vmem_limit_bytes=vmem),
            cost_estimate=pl.CostEstimate(flops=flops, bytes_accessed=nbytes, transcendentals=0),
        )(*args)

    return run


def valid_count(mask_ref):
    return jnp.sum(mask_ref[...].astype(f32), axis=1, keepdims=True)


def column_mask(mask_ref, col, tile, copies):
    lane = lax.broadcasted_iota(jnp.int32, (1, copies * tile), 1)
    token = (lax.rem(lane, tile) + col * tile).astype(f32)
    return (token < valid_count(mask_ref)).astype(f32)


def twice(w):
    none = jnp.zeros_like(w)
    return jnp.concatenate(
        [jnp.concatenate([w, none], axis=1), jnp.concatenate([none, w], axis=1)], axis=0
    )


def prepare_kernel(
    ready,
    own_ref,
    x_ref,
    adj_ref,
    w1_ref,
    w2_ref,
    mask_ref,
    wv_ref,
    wg_ref,
    wf_ref,
    shard_ref,
    rows_ref,
    left_ref,
    norm_ref,
    weights_ref,
    turn_ref,
    place_ref,
):
    chans = wv_ref.shape[1]
    weights_ref[:, :chans] = wv_ref[...]
    weights_ref[:, chans : 2 * chans] = wg_ref[...]
    weights_ref[:, 2 * chans :] = wf_ref[...]
    seqs, tokens, width = x_ref.shape
    half = seqs // 2
    fd = w2_ref.shape[0]
    x = x_ref[...].astype(f32)
    center = x - jnp.mean(x, axis=-1, keepdims=True)
    inverse = lax.rsqrt(jnp.mean(center * center, axis=-1, keepdims=True) + epsilon)
    normed = center * inverse
    rows = half * tokens
    adj = adj_ref[...].astype(f32)

    def two(x):
        x = jnp.concatenate([x[:half], x[half:]], axis=-1)
        return x.reshape(rows, 2 * width).astype(bf16)

    packed = two(normed)
    norm_ref[...] = packed
    base = tokens // pack * w1_ref.shape[0]
    shard_ref[base : base + rows, :] = two(adj)
    shard_ref[base + rows : base + 2 * rows, :] = packed
    token = lax.broadcasted_iota(jnp.int32, (seqs, tokens, width), 1) + own_ref[0]
    count = valid_count(mask_ref).reshape(1, 1, 1)
    real = jnp.where(token.astype(f32) < count, normed, 0.0)
    for s in range(seqs):
        turn_ref[:, s, :] = real[s]
    turned = turn_ref[...].astype(bf16).reshape(tokens * seqs, width)
    left = nt_dot(w1_ref[...], turned).astype(bf16)
    fc = w1_ref.shape[0]
    wk = pack * seqs
    for g in range(tokens // pack):
        shard_ref[g * fc : (g + 1) * fc, :] = left[:, g * wk : (g + 1) * wk]
    size = 128 // tokens
    real = real.astype(bf16)
    w2 = w2_ref[...]
    d = lax.broadcasted_iota(jnp.int32, (fd, 128), 0)
    lane = lax.broadcasted_iota(jnp.int32, (fd, 128), 1)
    mine = lax.rem(d, size) == lane // tokens
    for s in range(seqs):
        res = nt_dot(w2, jnp.concatenate([real[s]] * size, axis=0))
        res = jnp.where(mine, res, 0.0).reshape(fd // size, size, 128)
        place_ref[:, s, :] = jnp.sum(res, axis=1)
    right = place_ref[...].reshape(fd // size * seqs, 128).astype(bf16)
    rows_ref[...] = shard_ref[: base + 2 * rows, :]
    left_ref[...] = shard_ref[:base, :]
    shard_ref[base + 2 * rows :, :] = right


def join_left_kernel(ready, col_ref, rows0_ref, rows1_ref, rows2_ref, rows3_ref, out_ref):
    size = out_ref.shape[0] // 4
    for t, ref in enumerate((rows0_ref, rows1_ref, rows2_ref, rows3_ref)):
        at = pl.ds(pl.multiple_of(jnp.bitwise_xor(col_ref[0], t) * size, size), size)
        out_ref[at, :] = ref[:size, :]


def join_right_kernel(ready, row_ref, pair0_ref, pair1_ref, out_ref):
    size = out_ref.shape[0] // 4
    for t in range(4):
        ref = (pair0_ref, pair1_ref)[t // 2]
        at = pl.ds(pl.multiple_of(jnp.bitwise_xor(row_ref[0], t) * size, size), size)
        end = ref.shape[0] // 2 * (t % 2 + 1)
        out_ref[at, :] = ref[end - size : end, :]


def update_kernel(
    ready,
    col_ref,
    seq_ref,
    left_ref,
    right_ref,
    far_left_ref,
    far_right_ref,
    mask_ref,
    m_ref,
    score_ref,
    pair_ref,
    pout_hbm,
    normal_ref,
    inverse_ref,
    logits_ref,
    pout_ref,
    out_sem,
    rk_ref,
    rab_ref,
    lm_ref,
    mt_ref,
    oh_ref,
    ol_ref,
    update0_ref,
    update1_ref,
):
    nk = rk_ref.shape[0]
    width_d, pair_rows, _ = rab_ref.shape
    col, seq = col_ref[0], seq_ref[0]
    z = pair_ref.shape[1]
    groups, heads, lanes = logits_ref.shape
    tile_j = lanes // pack
    tokens = tile_j // nk
    fc = lm_ref.shape[0] // groups
    seqs = 128 // pack
    nq = pair_rows // seqs
    wk = pack * seqs

    r_rows = rk_ref.shape[1] // nq
    l_rows = groups * fc
    if nq == 2:
        sources = ((seq, 0, left_ref, right_ref), (1 - seq, 0, far_left_ref, far_right_ref))
    else:
        sources = tuple((q, q, far_left_ref, far_right_ref) for q in range(nq))
    for q, slot, from_left, from_right in sources:
        at = pl.ds(pl.multiple_of(q * r_rows, r_rows), r_rows)
        for k in range(nk):
            first = (slot * nk + k) * r_rows
            rk_ref[k, at, :] = from_right[first : first + r_rows, :]
        to = pl.ds(pl.multiple_of(q * wk, wk), wk)
        lm_ref[:, to] = from_left[slot * l_rows : (slot + 1) * l_rows, :]
    size = 128 // tokens
    right = jnp.concatenate([rk_ref[k] for k in range(nk)], axis=1)
    source = lax.broadcasted_iota(jnp.int32, (nk * 128, 4 * tile_j), 0)
    target = lax.broadcasted_iota(jnp.int32, (nk * 128, 4 * tile_j), 1)
    used = jnp.logical_or(target < tile_j, target >= 3 * tile_j)
    j = lax.rem(target, tile_j)
    offset = jnp.where(used, source - (j // tokens * 128 + lax.rem(j, tokens)), -1)
    blocks = width_d // size
    for e in range(size):
        pick = jnp.where(offset == e * tokens, 1.0, 0.0).astype(bf16)
        res = nn_dot(right, pick).astype(bf16)
        for q in range(nq):
            for n in range(blocks):
                at = (q * blocks + n) * seqs
                rab_ref[n * size + e, q * seqs : (q + 1) * seqs, :] = res[at : at + seqs]

    chunk = 8
    many = 4
    wide = oh_ref.shape[2] // lanes
    empty = jnp.zeros((seqs, 2 * tile_j), bf16)

    def block_of(d):
        rows = []
        for q in range(nq):
            both = rab_ref[d, q * seqs : (q + 1) * seqs, :]
            part = both[:, : 2 * tile_j], both[:, 2 * tile_j :]
            for i in range(pack):
                pieces = [empty] * (pack // 2)
                pieces[i // 2] = part[i % 2]
                rows.append(jnp.concatenate(pieces, axis=1))
        return jnp.concatenate(rows, axis=0)

    def outer_of(n, carry):
        block = jnp.concatenate([block_of(many * n + e) for e in range(many)], axis=1)
        for m in range(groups // chunk):
            out = nn_dot(lm_ref[m * chunk * fc : (m + 1) * chunk * fc, :], block)
            high, low = high_low(out)
            for e in range(many):
                at = pl.ds(pl.multiple_of((many * n + e) * fc, fc), fc)
                for g in range(chunk):
                    group = m * chunk + g
                    to = slice(group % wide * lanes, (group % wide + 1) * lanes)
                    cut = slice(g * fc, (g + 1) * fc), slice(e * lanes, (e + 1) * lanes)
                    oh_ref[group // wide, at, to] = high[cut]
                    ol_ref[group // wide, at, to] = low[cut]
        return carry

    lax.fori_loop(0, width_d // many, outer_of, 0, unroll=2)

    ready()
    some = z // fc
    for n in range(width_d // some):
        block = jnp.concatenate(
            [m_ref[pl.ds(n * some + e, fc, stride=width_d), :] for e in range(some)], axis=0
        ).T
        high, low = high_low(block)
        mt_ref[:z, n * z : (n + 1) * z] = high
        mt_ref[z:, n * z : (n + 1) * z] = low
    maskj = column_mask(mask_ref, col, tile_j, 2)

    maskl = jnp.concatenate([maskj] * (pack // 2), axis=1) > 0
    score = score_ref[...]
    s1 = score.astype(bf16).astype(f32)
    s2 = (score - s1).astype(bf16).astype(f32)
    s3 = score - s1 - s2
    none = jnp.zeros_like(s1)
    st = jnp.concatenate(
        [
            jnp.concatenate([s1, s2, s3, none], axis=0),
            jnp.concatenate([s1, s2, none, none], axis=0),
        ],
        axis=1,
    ).astype(bf16)

    def product(n):
        two = nn_dot(mt_ref[...], oh_ref[n])
        update_refs[n % 2][...] = two[:z] + two[z:] + nn_dot(mt_ref[:z, :], ol_ref[n])

    def finish(n):
        for e in range(wide):
            g = n * wide + e
            at = slice(g * lanes, (g + 1) * lanes)
            before = pair_ref[at, :].T.astype(f32)
            update = update_refs[n % 2][:, e * lanes : (e + 1) * lanes]
            result = (before + update).astype(bf16)
            x = result.astype(f32)
            pout_ref[at, :] = result.T
            center = x - jnp.mean(x, axis=0, keepdims=True)
            inverse = lax.rsqrt(jnp.mean(center * center, axis=0, keepdims=True) + epsilon)
            normal = center * inverse
            normal_ref[g] = normal
            inverse_ref[g] = jnp.broadcast_to(inverse, inverse_ref.shape[1:])
            high, low = high_low(normal)
            scores = nn_dot(st, jnp.concatenate([high, low], axis=0))
            logits = scores[:heads] + scores[heads : 2 * heads] + scores[2 * heads : 3 * heads]
            logits_ref[g] = jnp.where(maskl, logits, far_below)

    steps = groups // wide
    update_refs = (update0_ref, update1_ref)
    copies = []
    for n in range(steps + 1):
        if n < steps:
            product(n)
        if n > 0:
            finish(n - 1)
            at = pl.ds((n - 1) * wide * lanes, wide * lanes)
            part = pltpu.make_async_copy(pout_ref.at[at], pout_hbm.at[at], out_sem.at[n - 1])
            part.start()
            copies.append(part)
    for copy in copies:
        copy.wait()


def by_heads(w, heads, out_ref):
    width, chans = w.shape
    hw = chans // heads
    block = 4 * hw
    slot = lax.broadcasted_iota(jnp.int32, (width, block), 1) // hw
    w = w.astype(f32)
    for t in range(chans // block):
        part = w[:, t * block : (t + 1) * block]
        turns = [part] + [pltpu.roll(part, n * hw, 1) for n in range(1, 4)]
        for e in range(4):
            h = t * 4 + e
            for s in range(4):
                out_ref[s * width : (s + 1) * width, h * block : (h + 1) * block] = jnp.where(
                    slot == s, turns[(s - e) % 4], 0.0
                ).astype(bf16)


def weights_kernel(
    ready,
    row_ref,
    col_ref,
    side0_ref,
    side1_ref,
    side2_ref,
    side3_ref,
    cols0_ref,
    cols1_ref,
    weights_ref,
    gw_ref,
    cols_ref,
    acc_ref,
    bv_ref,
    bg_ref,
    bf_ref,
    rows_ref,
    gs_ref,
    vs_ref,
):
    nk, half, tokens, _ = cols_ref.shape
    tile = nk * tokens
    groups, heads, lanes = gw_ref.shape
    row, col = row_ref[0], col_ref[0]
    count = half * tokens
    size = side0_ref.shape[0] - 2 * count
    for t, ref in enumerate((side0_ref, side1_ref, side2_ref, side3_ref)):
        k = jnp.bitwise_xor(col, t)
        rows_ref[k] = ref[size : size + 2 * count, :].reshape(rows_ref.shape[1:])
    for t in range(nk):
        ref = (cols0_ref, cols1_ref)[t // 2]
        start = ref.shape[0] // 2 * (t % 2)
        part = ref[start : start + count, :]
        cols_ref[jnp.bitwise_xor(row, t)] = part.reshape(cols_ref.shape[1:])
    chans = weights_ref.shape[1] // 3
    by_heads(weights_ref[:, :chans], heads, bv_ref)
    by_heads(weights_ref[:, chans : 2 * chans], heads, bg_ref)
    by_heads(weights_ref[:, 2 * chans :], heads, bf_ref)
    block = bv_ref.shape[1] // heads

    def four(read, n):
        return jnp.concatenate(
            [
                jnp.concatenate(
                    [
                        jnp.concatenate([read(k, 2 * (2 * n + e) + p) for k in range(nk)], axis=0)
                        for p in range(2)
                    ],
                    axis=1,
                )
                for e in range(2)
            ],
            axis=0,
        )

    for hp in range(heads // 2):
        cut = slice(hp * 2 * block, (hp + 1) * 2 * block)
        for n in range(half // 4):
            v = nn_dot(four(lambda k, s: cols_ref[k, s], n), bv_ref[:, cut]).astype(bf16)
            gate = nn_dot(four(lambda k, s: rows_ref[k, 1, s], n), bg_ref[:, cut])
            grad = nn_dot(four(lambda k, s: rows_ref[k, 0, s], n), bf_ref[:, cut])
            g = (grad * jax.nn.sigmoid(gate)).astype(bf16)
            for e in range(2):
                to = slice((2 * n + e) * block, (2 * n + e + 1) * block)
                for o in range(2):
                    mine = slice(o * block, (o + 1) * block)
                    ve = v[e * tile : (e + 1) * tile, mine]
                    vs_ref[2 * hp + o, :tile, to] = ve
                    vs_ref[2 * hp + o, tile:, to] = ve
                    gs_ref[2 * hp + o, :, to] = g[e * tile : (e + 1) * tile, mine]
    for h in range(heads):
        acc_ref[h * tile : (h + 1) * tile, :] = nt_dot(gs_ref[h], vs_ref[h])

    first = lax.broadcasted_iota(jnp.int32, (groups, 2 * tile), 1) < tile
    for h in range(heads):
        for part in range(pack // 2):
            a = acc_ref[pl.ds(h * tile + 2 * part, groups, stride=pack), :]
            b = acc_ref[pl.ds(h * tile + 2 * part + 1, groups, stride=pack), :]
            gw_ref[:, h, part * 2 * tile : (part + 1) * 2 * tile] = jnp.where(first, a, b)


def softmax_kernel(
    ready,
    col_ref,
    logits_ref,
    gwa_ref,
    gwb_ref,
    mask_ref,
    gw_ref,
    own_ref,
    pay1_ref,
    pay2_ref,
    pay3_ref,
):
    groups, heads, lanes = logits_ref.shape
    tile = lanes // pack
    nk = 4
    rows = groups * heads
    col = col_ref[0]
    gw_ref[...] = gwa_ref[...] + gwb_ref[...]
    lane = lax.broadcasted_iota(jnp.int32, (rows, 2 * tile), 1)
    low = lane < tile
    maskj = column_mask(mask_ref, col, tile, 2)
    stats = jnp.zeros((rows, 2 * tile), f32)
    for part in range(pack // 2):
        cut = slice(part * 2 * tile, (part + 1) * 2 * tile)
        lg = logits_ref[:, :, cut].reshape(rows, 2 * tile)
        gw = gw_ref[:, :, cut].reshape(rows, 2 * tile)
        m0 = jnp.max(jnp.where(low, lg, far_below), axis=1, keepdims=True)
        m1 = jnp.max(jnp.where(low, far_below, lg), axis=1, keepdims=True)
        p = jnp.exp(lg - jnp.where(low, m0, m1)) * maskj
        pg = p * gw
        for e, m in ((0, m0), (1, m1)):
            mine = low if e == 0 else jnp.logical_not(low)
            i = 2 * part + e
            total = jnp.sum(jnp.where(mine, p, 0.0), axis=1, keepdims=True)
            inner = jnp.sum(jnp.where(mine, pg, 0.0), axis=1, keepdims=True)
            stats = jnp.where(lane == i, m, stats)
            stats = jnp.where(lane == pack + i, total, stats)
            stats = jnp.where(lane == 2 * pack + i, inner, stats)
    turned = stats.T[:16]
    per = groups // nk
    for shift, pay in enumerate((own_ref, pay1_ref, pay2_ref, pay3_ref)):
        dest = lax.rem(col + shift, nk)
        pay[0] = turned[:8]
        pay[1] = turned[8:]
        for g in range(per):
            piece = logits_ref[dest * per + g]
            for part in range(pack // 2):
                pay[2 + g * (pack // 2) + part] = piece[:, part * 2 * tile : (part + 1) * 2 * tile]


def values_kernel(
    ready, col_ref, ev0_ref, ev1_ref, ev2_ref, ev3_ref, wv_ref, norm_ref, wg_ref, v_ref, gate_ref, ev_ref
):
    nr, nk, half, tokens, wide = ev_ref.shape
    chans = wv_ref.shape[1]
    for t, ref in enumerate((ev0_ref, ev1_ref, ev2_ref, ev3_ref)):
        ev_ref[jnp.bitwise_xor(col_ref[0], t)] = ref[...]
    gate = jax.nn.sigmoid(nn_dot(norm_ref[...], twice(wg_ref[...])))
    gate_ref[: half * tokens] = gate[:, :chans]
    gate_ref[half * tokens :] = gate[:, chans:]
    wv = twice(wv_ref[...])
    for s in range(half):
        x = jnp.concatenate([ev_ref[r, k, s] for r in range(nr) for k in range(nk)], axis=0)
        v_ref[s] = nn_dot(x, wv).astype(bf16)


def gradient_kernel(
    ready,
    own_ref, r1_ref, r2_ref, r3_ref, logits_ref, gw_ref, normal_ref, inverse_ref, score_ref, out_hbm, stat_ref, out_ref, out_sem
):
    groups, heads, lanes = logits_ref.shape
    rows = groups * heads
    score = score_ref[...]
    z = score.shape[1]
    s1 = score.astype(bf16).astype(f32)
    s2 = (score - s1).astype(bf16).astype(f32)
    s3 = score - s1 - s2
    parts = [s1, s1, s1, s2, s2, s3, jnp.zeros((z - 6 * heads, z), f32)]
    sk = jnp.concatenate(parts, axis=0).T[:, : 6 * heads].astype(bf16)
    pays = (own_ref, r1_ref, r2_ref, r3_ref)
    ms = [p[0][:pack] for p in pays]
    ls = [p[0][pack : 2 * pack] for p in pays]
    ns = [p[1][:pack] for p in pays]
    top = functools.reduce(jnp.maximum, ms)
    scales = [jnp.exp(m - top) for m in ms]
    total = sum(a * b for a, b in zip(ls, scales))
    inner = sum(a * b for a, b in zip(ns, scales)) / total
    stacked = jnp.concatenate([top, total, inner, jnp.zeros((rows - 3 * pack, rows), f32)], axis=0)
    stat_ref[...] = stacked.T

    tile = lanes // pack
    low = lax.broadcasted_iota(jnp.int32, (heads, 2 * tile), 1) < tile

    def one(g):
        st = stat_ref[g * heads : (g + 1) * heads, :]

        def spread(base):
            halves = [
                jnp.where(
                    low,
                    st[:, base + 2 * half : base + 2 * half + 1],
                    st[:, base + 2 * half + 1 : base + 2 * half + 2],
                )
                for half in range(pack // 2)
            ]
            return jnp.concatenate(halves, axis=1)

        prob = jnp.exp(logits_ref[g] - spread(0)) / spread(pack)
        gl = prob * (gw_ref[g] - spread(2 * pack))
        g1 = gl.astype(bf16).astype(f32)
        g2 = (gl - g1).astype(bf16).astype(f32)
        g3 = gl - g1 - g2
        stack = jnp.concatenate([g1, g2, g3, g1, g2, g1], axis=0).astype(bf16)
        grad = nn_dot(sk, stack)
        normal = normal_ref[g]
        inverse = inverse_ref[g][:1]
        centered = grad - jnp.mean(grad, axis=0, keepdims=True)
        along = jnp.mean(grad * normal, axis=0, keepdims=True)
        result = inverse * (centered - normal * along)
        out_ref[g * lanes : (g + 1) * lanes, :] = result.astype(bf16).T

    many = 4

    copies = []
    for n in range(groups // many):
        for e in range(many):
            one(n * many + e)
        at = pl.ds(n * many * lanes, many * lanes)
        part = pltpu.make_async_copy(out_ref.at[at], out_hbm.at[at], out_sem.at[n])
        part.start()
        copies.append(part)
    for copy in copies:
        copy.wait()


def alignment_kernel(
    ready,
    col_ref,
    own_ref,
    r1_ref,
    r2_ref,
    r3_ref,
    v_ref,
    gate_ref,
    x_ref,
    wf_ref,
    out_ref,
    w_ref,
    gated_ref,
):
    pays = (own_ref, r1_ref, r2_ref, r3_ref)
    nk = len(pays)
    heads = own_ref.shape[1]
    wide = own_ref.shape[2]
    tile = wide // 2
    pieces = own_ref.shape[0] - 2
    rows = pieces * heads
    half, all_tokens, chans = v_ref.shape
    chans = chans // 2
    tokens = pieces * 2
    head_width = chans // heads
    col = col_ref[0]

    low = lax.broadcasted_iota(jnp.int32, (rows, wide), 1) < tile
    lgs = [p[2:].reshape(rows, wide) for p in pays]
    peak = functools.reduce(jnp.maximum, lgs)
    m0 = jnp.max(jnp.where(low, peak, far_below), axis=1, keepdims=True)
    m1 = jnp.max(jnp.where(low, far_below, peak), axis=1, keepdims=True)
    top = jnp.where(low, m0, m1)
    ps = [jnp.exp(lg - top) for lg in lgs]
    every = sum(ps)
    t0 = jnp.sum(jnp.where(low, every, 0.0), axis=1, keepdims=True)
    t1 = jnp.sum(jnp.where(low, 0.0, every), axis=1, keepdims=True)
    total = jnp.where(low, t0, t1)
    for shift, p in enumerate(ps):
        source = lax.rem(col + nk - shift, nk)
        weight = p / total
        rolled = pltpu.roll(weight, tile, 1)
        for n in range(pieces):
            w_ref[source, :, 2 * n, :] = weight[n * heads : (n + 1) * heads]
            w_ref[source, :, 2 * n + 1, :] = rolled[n * heads : (n + 1) * heads]
    w = jnp.concatenate(
        [
            w_ref[k].reshape(heads * tokens, wide)[:, :tile]
            for k in range(nk)
        ],
        axis=1,
    ).astype(bf16)

    owner = lax.broadcasted_iota(jnp.int32, (tokens, chans), 1) // head_width

    def one(s, carry):
        full = nn_dot(w, v_ref[s])
        for e in range(2):
            cut = slice(e * chans, (e + 1) * chans)
            mean = jnp.zeros((tokens, chans), f32)
            for h in range(heads):
                mean = jnp.where(owner == h, full[h * tokens : (h + 1) * tokens, cut], mean)
            at = pl.ds(pl.multiple_of((e * half + s) * tokens, tokens), tokens)
            gated_ref[at, :] = (gate_ref[at, :] * mean).astype(bf16)
        return carry

    lax.fori_loop(0, half, one, 0, unroll=8)
    out_ref[...] = (x_ref[...].astype(f32) + nt_dot(gated_ref[...], wf_ref[...])).astype(bf16)


def on_device(
    counts,
    alignment_input,
    pair_input,
    token_valid_mask,
    first_factor_weights,
    second_factor_weights,
    content_weights_grid,
    sigmoid_weights_grid,
    outer_matrix,
    score_matrix,
    final_mixing_weights,
    adjoint_of_rowset,
):
    nq, nr, nk = counts
    row_index = lax.axis_index("row")
    col_index = lax.axis_index("col")
    seqs, tokens, width = alignment_input.shape
    tile_i, tile_j, z = pair_input.shape
    fc = first_factor_weights.shape[1]
    fd = second_factor_weights.shape[1]
    heads = score_matrix.shape[1]
    chans = content_weights_grid.shape[1]
    groups = tile_i // pack
    lanes = pack * tile_j
    sds = jax.ShapeDtypeStruct

    mask = token_valid_mask.reshape(1, -1)
    own_start = ((row_index * nk + col_index) * tokens).astype(jnp.int32).reshape(1)
    seq_index = lax.axis_index("seq")
    place = tuple(x.astype(jnp.int32).reshape(1) for x in (row_index, col_index, seq_index))
    col_scalar = col_index.astype(jnp.int32).reshape(1)
    half = seqs // 2

    l_rows = tokens // pack * fc
    r_rows = fd * tokens // 128 * seqs
    n_rows = half * tokens
    shard, rows, own_left, normed, weights = call(
        prepare_kernel,
        (
            sds((l_rows + 2 * n_rows + r_rows, 128), bf16),
            sds((l_rows + 2 * n_rows, 128), bf16),
            sds((l_rows, 128), bf16),
            sds((n_rows, 128), bf16),
            sds((width, 3 * chans), bf16),
        ),
        scratch=(
            pltpu.VMEM((tokens, seqs, width), f32),
            pltpu.VMEM((fd * tokens // 128, seqs, 128), f32),
        ),
        smem=1,
        vmem=60 * 1024 * 1024,
    )(
        own_start,
        alignment_input,
        adjoint_of_rowset,
        first_factor_weights.T,
        second_factor_weights.T,
        mask,
        content_weights_grid,
        sigmoid_weights_grid,
        final_mixing_weights.T,
    )

    def exchange(x, bit):
        return lax.ppermute(x, "col", [(c, c ^ bit) for c in range(nk)])

    other = exchange(shard, 1)
    across = exchange(rows, 2)
    pair = jnp.concatenate([x[l_rows + n_rows :] for x in (shard, other)], axis=0)
    all_cols = [
        lax.ppermute(
            pair,
            ("row", "col"),
            [(r * nk + c, (c ^ flip) * nk + r) for r in range(nr) for c in range(nk)],
        )
        for flip in (0, 2)
    ]

    def over_seq(x):
        if nq == 2:
            return lax.ppermute(x, "seq", [(0, 1), (1, 0)])
        return lax.all_gather(x, "seq", axis=0, tiled=True)

    lefts = [own_left, other, across, exchange(own_left, 3)]
    (left,) = call(join_left_kernel, (sds((nk * l_rows, 128), bf16),), smem=1)(place[1], *lefts)
    far_left = over_seq(left)
    across, far_left, *all_cols = lax.optimization_barrier((across, far_left, *all_cols))
    all_rows = [rows, other, across, exchange(across, 1)]

    (right,) = call(join_right_kernel, (sds((nk * r_rows, 128), bf16),), smem=1)(
        place[0], *all_cols
    )
    far_right = over_seq(right)

    head_lanes = seqs * chans // heads
    gw_own, block = call(
        weights_kernel,
        (
            sds((groups, heads, lanes), f32),
            sds((nk, half, tokens, 2 * width), bf16),
        ),
        scratch=(
            pltpu.VMEM((heads * tile_i, 2 * tile_j), f32),
            pltpu.VMEM((4 * width, 4 * chans), bf16),
            pltpu.VMEM((4 * width, 4 * chans), bf16),
            pltpu.VMEM((4 * width, 4 * chans), bf16),
            pltpu.VMEM((nk, 2, half, tokens, 2 * width), bf16),
            pltpu.VMEM((heads, tile_i, head_lanes), bf16),
            pltpu.VMEM((heads, 2 * tile_j, head_lanes), bf16),
        ),
        smem=2,
        flops=3_000_000_000,
        nbytes=3_000_000,
    )(*place[:2], *all_rows, *all_cols, weights)
    if nq == 2:
        gw_other = lax.ppermute(gw_own, "seq", [(0, 1), (1, 0)])
    else:
        gw_own, gw_other = lax.psum(gw_own, "seq"), jnp.zeros_like(gw_own)

    close, remote = exchange(block, 1), exchange(block, 2)

    pair_out, normal, inverse, logits = call(
        update_kernel,
        (
            sds((tile_i * tile_j, z), bf16),
            sds((groups, z, lanes), f32),
            sds((groups, 8, lanes), f32),
            sds((groups, heads, lanes), f32),
        ),
        scratch=(
            pltpu.VMEM((tile_i * tile_j, z), bf16),
            pltpu.SemaphoreType.DMA((groups // 4,)),
            pltpu.VMEM((nk, nq * r_rows, 128), bf16),
            pltpu.VMEM((fd, nq * seqs, 4 * tile_j), bf16),
            pltpu.VMEM((groups * fc, nq * pack * seqs), bf16),
            pltpu.VMEM((2 * z, fd * fc), bf16),
            pltpu.VMEM((groups // 4, fd * fc, 4 * lanes), bf16),
            pltpu.VMEM((groups // 4, fd * fc, 4 * lanes), bf16),
            pltpu.VMEM((z, 4 * lanes), f32),
            pltpu.VMEM((z, 4 * lanes), f32),
        ),
        smem=2,
        flops=14_000_000_000,
        nbytes=5_000_000,
        vmem=44 * 1024 * 1024,
        far=(6, 7, 8, 9),
        far_out=(0,),
    )(
        *place[1:],
        left,
        right,
        far_left,
        far_right,
        mask,
        outer_matrix,
        score_matrix.T,
        pair_input.reshape(tile_i * tile_j, z),
    )

    payload = sds((2 + groups // nk * (pack // 2), heads, 2 * tile_j), f32)
    gw, pay0, pay1, pay2, pay3 = call(
        softmax_kernel,
        (sds((groups, heads, lanes), f32), payload, payload, payload, payload),
        smem=1,
    )(col_scalar, logits, gw_own, gw_other, mask)

    got = [
        lax.ppermute(pay, "col", [(c, (c + shift) % nk) for c in range(nk)])
        for shift, pay in ((1, pay1), (2, pay2), (3, pay3))
    ]


    close, remote, pay0 = lax.optimization_barrier((close, remote, pay0))
    every = [block, close, remote, exchange(remote, 1)]
    values, gating = call(
        values_kernel,
        (sds((half, nr * nk * tokens, 2 * chans), bf16), sds((seqs * tokens, chans), f32)),
        scratch=(pltpu.VMEM((nr, nk, half, tokens, 2 * width), bf16),),
        smem=1,
        flops=4_000_000_000,
        nbytes=6_000_000,
    )(col_scalar, *every, content_weights_grid, normed, sigmoid_weights_grid)

    got, values, gating = lax.optimization_barrier((got, values, gating))

    (gradient,) = call(
        gradient_kernel,
        (sds((tile_i * tile_j, z), bf16),),
        scratch=(
            pltpu.VMEM((groups * heads, groups * heads), f32),
            pltpu.VMEM((tile_i * tile_j, z), bf16),
            pltpu.SemaphoreType.DMA((groups // 4,)),
        ),
        far_out=(0,),
        flops=4_000_000_000,
        nbytes=3_000_000,
    )(pay0, *got, logits, gw, normal, inverse, score_matrix.T)

    (aligned,) = call(
        alignment_kernel,
        (sds((seqs * tokens, width), bf16),),
        scratch=(
            pltpu.VMEM((nk, heads, tokens, 2 * tile_j), f32),
            pltpu.VMEM((seqs * tokens, chans), bf16),
        ),
        smem=1,
        flops=3_000_000_000,
        nbytes=5_000_000,
    )(
        col_scalar,
        pay0,
        *got,
        values,
        gating,
        alignment_input.reshape(seqs * tokens, width),
        final_mixing_weights.T,
    )
    return (
        aligned.reshape(seqs, tokens, width),
        pair_out.reshape(tile_i, tile_j, z),
        gradient.reshape(tile_i, tile_j, z),
    )


def solution(mesh):
    counts = (mesh.shape["seq"], mesh.shape["row"], mesh.shape["col"])
    in_specs = (
        P("seq", ("row", "col"), None),
        P("row", "col", None),
        P(),
        P(),
        P(),
        P(),
        P(),
        P(),
        P(),
        P(),
        P("seq", ("row", "col"), None),
    )
    out_specs = (P("seq", ("row", "col"), None), P("row", "col", None), P("row", "col", None))
    return jax.shard_map(
        functools.partial(on_device, counts),
        mesh=mesh,
        in_specs=in_specs,
        out_specs=out_specs,
        check_vma=False,
    )
```

```python
import functools

import jax
import jax.numpy as jnp
from jax import lax
from jax.experimental import pallas as pl
from jax.experimental.pallas import tpu as pltpu
from jax.sharding import PartitionSpec as P

epsilon = 1e-05
far_below = -1e30
vmem_bytes = 32 * 1024 * 1024
pack = 4

f32 = jnp.float32
bf16 = jnp.bfloat16


def nt_dot(a, b):
    return lax.dot_general(a, b, (((1,), (1,)), ((), ())), preferred_element_type=f32)


def nn_dot(a, b):
    return jnp.dot(a, b, preferred_element_type=f32)


def high_low(x):
    high = x.astype(bf16)
    return high, (x - high.astype(f32)).astype(bf16)


def call(
    kernel, out_shape, scratch=(), smem=0, flops=0, nbytes=0, vmem=vmem_bytes, far=(), far_out=()
):
    def run(*args):
        count = len(args)
        in_specs = [
            pl.BlockSpec(memory_space=pltpu.SMEM if n < smem else pltpu.VMEM) for n in range(count)
        ]
        for n in far:
            in_specs[n] = pl.BlockSpec(memory_space=pltpu.HBM)
        landing = [pltpu.VMEM(args[n].shape, args[n].dtype) for n in far]
        if far:
            landing.append(pltpu.SemaphoreType.DMA((len(far),)))

        def body(*refs):
            inputs = list(refs[:count])
            extra = refs[len(refs) - len(landing) :]
            rest = refs[count : len(refs) - len(landing)]
            copies = []
            for i, n in enumerate(far):
                copies.append(pltpu.make_async_copy(inputs[n], extra[i], extra[-1].at[i]))
                copies[-1].start()
                inputs[n] = extra[i]

            def ready():
                for copy in copies:
                    copy.wait()

            kernel(ready, *inputs, *rest)

        return pl.pallas_call(
            body,
            out_shape=out_shape,
            in_specs=in_specs,
            out_specs=[
                pl.BlockSpec(memory_space=pltpu.HBM if n in far_out else pltpu.VMEM)
                for n in range(len(out_shape))
            ],
            scratch_shapes=list(scratch) + landing,
            compiler_params=pltpu.CompilerParams(vmem_limit_bytes=vmem),
            cost_estimate=pl.CostEstimate(flops=flops, bytes_accessed=nbytes, transcendentals=0),
        )(*args)

    return run


def valid_count(mask_ref):
    return jnp.sum(mask_ref[...].astype(f32), axis=1, keepdims=True)


def column_mask(mask_ref, col, tile, copies):
    lane = lax.broadcasted_iota(jnp.int32, (1, copies * tile), 1)
    token = (lax.rem(lane, tile) + col * tile).astype(f32)
    return (token < valid_count(mask_ref)).astype(f32)


def twice(w):
    none = jnp.zeros_like(w)
    return jnp.concatenate(
        [jnp.concatenate([w, none], axis=1), jnp.concatenate([none, w], axis=1)], axis=0
    )


def prepare_kernel(
    ready,
    own_ref,
    x_ref,
    adj_ref,
    w1_ref,
    w2_ref,
    mask_ref,
    wv_ref,
    wg_ref,
    wf_ref,
    shard_ref,
    rows_ref,
    left_ref,
    norm_ref,
    weights_ref,
    turn_ref,
    place_ref,
):
    chans = wv_ref.shape[1]
    weights_ref[:, :chans] = wv_ref[...]
    weights_ref[:, chans : 2 * chans] = wg_ref[...]
    weights_ref[:, 2 * chans :] = wf_ref[...]
    seqs, tokens, width = x_ref.shape
    half = seqs // 2
    fd = w2_ref.shape[0]
    x = x_ref[...].astype(f32)
    center = x - jnp.mean(x, axis=-1, keepdims=True)
    inverse = lax.rsqrt(jnp.mean(center * center, axis=-1, keepdims=True) + epsilon)
    normed = center * inverse
    rows = half * tokens
    adj = adj_ref[...].astype(f32)

    def two(x):
        x = jnp.concatenate([x[:half], x[half:]], axis=-1)
        return x.reshape(rows, 2 * width).astype(bf16)

    packed = two(normed)
    norm_ref[...] = packed
    base = tokens // pack * w1_ref.shape[0]
    shard_ref[base : base + rows, :] = two(adj)
    shard_ref[base + rows : base + 2 * rows, :] = packed
    token = lax.broadcasted_iota(jnp.int32, (seqs, tokens, width), 1) + own_ref[0]
    count = valid_count(mask_ref).reshape(1, 1, 1)
    real = jnp.where(token.astype(f32) < count, normed, 0.0)
    for s in range(seqs):
        turn_ref[:, s, :] = real[s]
    turned = turn_ref[...].astype(bf16).reshape(tokens * seqs, width)
    left = nt_dot(w1_ref[...], turned).astype(bf16)
    fc = w1_ref.shape[0]
    wk = pack * seqs
    for g in range(tokens // pack):
        shard_ref[g * fc : (g + 1) * fc, :] = left[:, g * wk : (g + 1) * wk]
    size = 128 // tokens
    real = real.astype(bf16)
    w2 = w2_ref[...]
    d = lax.broadcasted_iota(jnp.int32, (fd, 128), 0)
    lane = lax.broadcasted_iota(jnp.int32, (fd, 128), 1)
    mine = lax.rem(d, size) == lane // tokens
    for s in range(seqs):
        res = nt_dot(w2, jnp.concatenate([real[s]] * size, axis=0))
        res = jnp.where(mine, res, 0.0).reshape(fd // size, size, 128)
        place_ref[:, s, :] = jnp.sum(res, axis=1)
    right = place_ref[...].reshape(fd // size * seqs, 128).astype(bf16)
    rows_ref[...] = shard_ref[: base + 2 * rows, :]
    left_ref[...] = shard_ref[:base, :]
    shard_ref[base + 2 * rows :, :] = right


def join_left_kernel(ready, col_ref, rows0_ref, rows1_ref, rows2_ref, rows3_ref, out_ref):
    size = out_ref.shape[0] // 4
    for t, ref in enumerate((rows0_ref, rows1_ref, rows2_ref, rows3_ref)):
        at = pl.ds(pl.multiple_of(jnp.bitwise_xor(col_ref[0], t) * size, size), size)
        out_ref[at, :] = ref[:size, :]


def hand_on_kernel(ready, weights_ref, rows_ref, weights_out_ref, rows_out_ref):
    weights_out_ref[...] = weights_ref[...]
    rows_out_ref[...] = rows_ref[...]


def join_right_kernel(ready, row_ref, pair0_ref, pair1_ref, out_ref):
    size = out_ref.shape[0] // 4
    for t in range(4):
        ref = (pair0_ref, pair1_ref)[t // 2]
        at = pl.ds(pl.multiple_of(jnp.bitwise_xor(row_ref[0], t) * size, size), size)
        end = ref.shape[0] // 2 * (t % 2 + 1)
        out_ref[at, :] = ref[end - size : end, :]


def update_kernel(
    ready,
    col_ref,
    seq_ref,
    left_ref,
    right_ref,
    far_left_ref,
    far_right_ref,
    mask_ref,
    m_ref,
    score_ref,
    pair_ref,
    pout_hbm,
    normal_ref,
    inverse_ref,
    logits_ref,
    pout_ref,
    out_sem,
    rk_ref,
    rab_ref,
    lm_ref,
    mt_ref,
    oh_ref,
    ol_ref,
    update0_ref,
    update1_ref,
):
    nk = rk_ref.shape[0]
    width_d, pair_rows, _ = rab_ref.shape
    col, seq = col_ref[0], seq_ref[0]
    z = pair_ref.shape[1]
    groups, heads, lanes = logits_ref.shape
    tile_j = lanes // pack
    tokens = tile_j // nk
    fc = lm_ref.shape[0] // groups
    seqs = 128 // pack
    nq = pair_rows // seqs
    wk = pack * seqs

    r_rows = rk_ref.shape[1] // nq
    l_rows = groups * fc
    if nq == 2:
        sources = ((seq, 0, left_ref, right_ref), (1 - seq, 0, far_left_ref, far_right_ref))
    else:
        sources = tuple((q, q, far_left_ref, far_right_ref) for q in range(nq))
    for q, slot, from_left, from_right in sources:
        at = pl.ds(pl.multiple_of(q * r_rows, r_rows), r_rows)
        for k in range(nk):
            first = (slot * nk + k) * r_rows
            rk_ref[k, at, :] = from_right[first : first + r_rows, :]
        to = pl.ds(pl.multiple_of(q * wk, wk), wk)
        lm_ref[:, to] = from_left[slot * l_rows : (slot + 1) * l_rows, :]
    size = 128 // tokens
    right = jnp.concatenate([rk_ref[k] for k in range(nk)], axis=1)
    source = lax.broadcasted_iota(jnp.int32, (nk * 128, 4 * tile_j), 0)
    target = lax.broadcasted_iota(jnp.int32, (nk * 128, 4 * tile_j), 1)
    used = jnp.logical_or(target < tile_j, target >= 3 * tile_j)
    j = lax.rem(target, tile_j)
    offset = jnp.where(used, source - (j // tokens * 128 + lax.rem(j, tokens)), -1)
    blocks = width_d // size
    for e in range(size):
        pick = jnp.where(offset == e * tokens, 1.0, 0.0).astype(bf16)
        res = nn_dot(right, pick).astype(bf16)
        for q in range(nq):
            for n in range(blocks):
                at = (q * blocks + n) * seqs
                rab_ref[n * size + e, q * seqs : (q + 1) * seqs, :] = res[at : at + seqs]

    chunk = 8
    many = 4
    wide = oh_ref.shape[2] // lanes
    empty = jnp.zeros((seqs, 2 * tile_j), bf16)

    def block_of(d):
        rows = []
        for q in range(nq):
            both = rab_ref[d, q * seqs : (q + 1) * seqs, :]
            part = both[:, : 2 * tile_j], both[:, 2 * tile_j :]
            for i in range(pack):
                pieces = [empty] * (pack // 2)
                pieces[i // 2] = part[i % 2]
                rows.append(jnp.concatenate(pieces, axis=1))
        return jnp.concatenate(rows, axis=0)

    def outer_of(n, carry):
        block = jnp.concatenate([block_of(many * n + e) for e in range(many)], axis=1)
        for m in range(groups // chunk):
            out = nn_dot(lm_ref[m * chunk * fc : (m + 1) * chunk * fc, :], block)
            high, low = high_low(out)
            for e in range(many):
                at = pl.ds(pl.multiple_of((many * n + e) * fc, fc), fc)
                for g in range(chunk):
                    group = m * chunk + g
                    to = slice(group % wide * lanes, (group % wide + 1) * lanes)
                    cut = slice(g * fc, (g + 1) * fc), slice(e * lanes, (e + 1) * lanes)
                    oh_ref[group // wide, at, to] = high[cut]
                    ol_ref[group // wide, at, to] = low[cut]
        return carry

    lax.fori_loop(0, width_d // many, outer_of, 0, unroll=2)

    ready()
    some = z // fc
    for n in range(width_d // some):
        block = jnp.concatenate(
            [m_ref[pl.ds(n * some + e, fc, stride=width_d), :] for e in range(some)], axis=0
        ).T
        high, low = high_low(block)
        mt_ref[:z, n * z : (n + 1) * z] = high
        mt_ref[z:, n * z : (n + 1) * z] = low
    maskj = column_mask(mask_ref, col, tile_j, 2)

    maskl = jnp.concatenate([maskj] * (pack // 2), axis=1) > 0
    score = score_ref[...]
    s1 = score.astype(bf16).astype(f32)
    s2 = (score - s1).astype(bf16).astype(f32)
    s3 = score - s1 - s2
    none = jnp.zeros_like(s1)
    st = jnp.concatenate(
        [
            jnp.concatenate([s1, s2, s3, none], axis=0),
            jnp.concatenate([s1, s2, none, none], axis=0),
        ],
        axis=1,
    ).astype(bf16)

    def product(n):
        two = nn_dot(mt_ref[...], oh_ref[n])
        update_refs[n % 2][...] = two[:z] + two[z:] + nn_dot(mt_ref[:z, :], ol_ref[n])

    def finish(n):
        for e in range(wide):
            g = n * wide + e
            at = slice(g * lanes, (g + 1) * lanes)
            before = pair_ref[at, :].T.astype(f32)
            update = update_refs[n % 2][:, e * lanes : (e + 1) * lanes]
            result = (before + update).astype(bf16)
            x = result.astype(f32)
            pout_ref[at, :] = result.T
            center = x - jnp.mean(x, axis=0, keepdims=True)
            inverse = lax.rsqrt(jnp.mean(center * center, axis=0, keepdims=True) + epsilon)
            normal = center * inverse
            normal_ref[g] = normal
            inverse_ref[g] = jnp.broadcast_to(inverse, inverse_ref.shape[1:])
            high, low = high_low(normal)
            scores = nn_dot(st, jnp.concatenate([high, low], axis=0))
            logits = scores[:heads] + scores[heads : 2 * heads] + scores[2 * heads : 3 * heads]
            logits_ref[g] = jnp.where(maskl, logits, far_below)

    steps = groups // wide
    update_refs = (update0_ref, update1_ref)
    copies = []
    for n in range(steps + 1):
        if n < steps:
            product(n)
        if n > 0:
            finish(n - 1)
            at = pl.ds((n - 1) * wide * lanes, wide * lanes)
            part = pltpu.make_async_copy(pout_ref.at[at], pout_hbm.at[at], out_sem.at[n - 1])
            part.start()
            copies.append(part)
    for copy in copies:
        copy.wait()


def by_heads(w, heads, out_ref):
    width, chans = w.shape
    hw = chans // heads
    block = 4 * hw
    slot = lax.broadcasted_iota(jnp.int32, (width, block), 1) // hw
    w = w.astype(f32)
    for t in range(chans // block):
        part = w[:, t * block : (t + 1) * block]
        turns = [part] + [pltpu.roll(part, n * hw, 1) for n in range(1, 4)]
        for e in range(4):
            h = t * 4 + e
            for s in range(4):
                out_ref[s * width : (s + 1) * width, h * block : (h + 1) * block] = jnp.where(
                    slot == s, turns[(s - e) % 4], 0.0
                ).astype(bf16)


def weights_kernel(
    ready,
    row_ref,
    col_ref,
    side0_ref,
    side1_ref,
    side2_ref,
    side3_ref,
    cols0_ref,
    cols1_ref,
    weights_ref,
    gw_ref,
    cols_ref,
    acc_ref,
    bv_ref,
    bg_ref,
    bf_ref,
    rows_ref,
    gs_ref,
    vs_ref,
):
    nk, half, tokens, _ = cols_ref.shape
    tile = nk * tokens
    groups, heads, lanes = gw_ref.shape
    row, col = row_ref[0], col_ref[0]
    count = half * tokens
    size = side0_ref.shape[0] - 2 * count
    for t, ref in enumerate((side0_ref, side1_ref, side2_ref, side3_ref)):
        k = jnp.bitwise_xor(col, t)
        rows_ref[k] = ref[size : size + 2 * count, :].reshape(rows_ref.shape[1:])
    for t in range(nk):
        ref = (cols0_ref, cols1_ref)[t // 2]
        start = ref.shape[0] // 2 * (t % 2)
        part = ref[start : start + count, :]
        cols_ref[jnp.bitwise_xor(row, t)] = part.reshape(cols_ref.shape[1:])
    chans = weights_ref.shape[1] // 3
    by_heads(weights_ref[:, :chans], heads, bv_ref)
    by_heads(weights_ref[:, chans : 2 * chans], heads, bg_ref)
    by_heads(weights_ref[:, 2 * chans :], heads, bf_ref)
    block = bv_ref.shape[1] // heads

    def four(read, n):
        return jnp.concatenate(
            [
                jnp.concatenate(
                    [
                        jnp.concatenate([read(k, 2 * (2 * n + e) + p) for k in range(nk)], axis=0)
                        for p in range(2)
                    ],
                    axis=1,
                )
                for e in range(2)
            ],
            axis=0,
        )

    for hp in range(heads // 2):
        cut = slice(hp * 2 * block, (hp + 1) * 2 * block)
        for n in range(half // 4):
            v = nn_dot(four(lambda k, s: cols_ref[k, s], n), bv_ref[:, cut]).astype(bf16)
            gate = nn_dot(four(lambda k, s: rows_ref[k, 1, s], n), bg_ref[:, cut])
            grad = nn_dot(four(lambda k, s: rows_ref[k, 0, s], n), bf_ref[:, cut])
            g = (grad * jax.nn.sigmoid(gate)).astype(bf16)
            for e in range(2):
                to = slice((2 * n + e) * block, (2 * n + e + 1) * block)
                for o in range(2):
                    mine = slice(o * block, (o + 1) * block)
                    ve = v[e * tile : (e + 1) * tile, mine]
                    vs_ref[2 * hp + o, :tile, to] = ve
                    vs_ref[2 * hp + o, tile:, to] = ve
                    gs_ref[2 * hp + o, :, to] = g[e * tile : (e + 1) * tile, mine]
    for h in range(heads):
        acc_ref[h * tile : (h + 1) * tile, :] = nt_dot(gs_ref[h], vs_ref[h])

    first = lax.broadcasted_iota(jnp.int32, (groups, 2 * tile), 1) < tile
    for h in range(heads):
        for part in range(pack // 2):
            a = acc_ref[pl.ds(h * tile + 2 * part, groups, stride=pack), :]
            b = acc_ref[pl.ds(h * tile + 2 * part + 1, groups, stride=pack), :]
            gw_ref[:, h, part * 2 * tile : (part + 1) * 2 * tile] = jnp.where(first, a, b)


def softmax_kernel(
    ready,
    col_ref,
    logits_ref,
    gwa_ref,
    gwb_ref,
    mask_ref,
    gw_ref,
    own_ref,
    pay1_ref,
    pay2_ref,
    pay3_ref,
):
    groups, heads, lanes = logits_ref.shape
    tile = lanes // pack
    nk = 4
    rows = groups * heads
    col = col_ref[0]
    gw_ref[...] = gwa_ref[...] + gwb_ref[...]
    lane = lax.broadcasted_iota(jnp.int32, (rows, 2 * tile), 1)
    low = lane < tile
    maskj = column_mask(mask_ref, col, tile, 2)
    stats = jnp.zeros((rows, 2 * tile), f32)
    for part in range(pack // 2):
        cut = slice(part * 2 * tile, (part + 1) * 2 * tile)
        lg = logits_ref[:, :, cut].reshape(rows, 2 * tile)
        gw = gw_ref[:, :, cut].reshape(rows, 2 * tile)
        m0 = jnp.max(jnp.where(low, lg, far_below), axis=1, keepdims=True)
        m1 = jnp.max(jnp.where(low, far_below, lg), axis=1, keepdims=True)
        p = jnp.exp(lg - jnp.where(low, m0, m1)) * maskj
        pg = p * gw
        for e, m in ((0, m0), (1, m1)):
            mine = low if e == 0 else jnp.logical_not(low)
            i = 2 * part + e
            total = jnp.sum(jnp.where(mine, p, 0.0), axis=1, keepdims=True)
            inner = jnp.sum(jnp.where(mine, pg, 0.0), axis=1, keepdims=True)
            stats = jnp.where(lane == i, m, stats)
            stats = jnp.where(lane == pack + i, total, stats)
            stats = jnp.where(lane == 2 * pack + i, inner, stats)
    turned = stats.T[:16]
    per = groups // nk
    for shift, pay in enumerate((own_ref, pay1_ref, pay2_ref, pay3_ref)):
        dest = lax.rem(col + shift, nk)
        pay[0] = turned[:8]
        pay[1] = turned[8:]
        for g in range(per):
            piece = logits_ref[dest * per + g]
            for part in range(pack // 2):
                pay[2 + g * (pack // 2) + part] = piece[:, part * 2 * tile : (part + 1) * 2 * tile]


def values_kernel(
    ready, col_ref, ev0_ref, ev1_ref, ev2_ref, ev3_ref, wv_ref, norm_ref, wg_ref, v_ref, gate_ref, ev_ref
):
    nr, nk, half, tokens, wide = ev_ref.shape
    chans = wv_ref.shape[1]
    for t, ref in enumerate((ev0_ref, ev1_ref, ev2_ref, ev3_ref)):
        ev_ref[jnp.bitwise_xor(col_ref[0], t)] = ref[...]
    gate = jax.nn.sigmoid(nn_dot(norm_ref[...], twice(wg_ref[...])))
    gate_ref[: half * tokens] = gate[:, :chans]
    gate_ref[half * tokens :] = gate[:, chans:]
    wv = twice(wv_ref[...])
    for s in range(half):
        x = jnp.concatenate([ev_ref[r, k, s] for r in range(nr) for k in range(nk)], axis=0)
        v_ref[s] = nn_dot(x, wv).astype(bf16)


def gradient_kernel(
    ready,
    own_ref, r1_ref, r2_ref, r3_ref, logits_ref, gw_ref, normal_ref, inverse_ref, score_ref, out_hbm, stat_ref, out_ref, out_sem
):
    groups, heads, lanes = logits_ref.shape
    rows = groups * heads
    score = score_ref[...]
    z = score.shape[1]
    s1 = score.astype(bf16).astype(f32)
    s2 = (score - s1).astype(bf16).astype(f32)
    s3 = score - s1 - s2
    parts = [s1, s1, s1, s2, s2, s3, jnp.zeros((z - 6 * heads, z), f32)]
    sk = jnp.concatenate(parts, axis=0).T[:, : 6 * heads].astype(bf16)
    pays = (own_ref, r1_ref, r2_ref, r3_ref)
    ms = [p[0][:pack] for p in pays]
    ls = [p[0][pack : 2 * pack] for p in pays]
    ns = [p[1][:pack] for p in pays]
    top = functools.reduce(jnp.maximum, ms)
    scales = [jnp.exp(m - top) for m in ms]
    total = sum(a * b for a, b in zip(ls, scales))
    inner = sum(a * b for a, b in zip(ns, scales)) / total
    stacked = jnp.concatenate([top, total, inner, jnp.zeros((rows - 3 * pack, rows), f32)], axis=0)
    stat_ref[...] = stacked.T

    tile = lanes // pack
    low = lax.broadcasted_iota(jnp.int32, (heads, 2 * tile), 1) < tile

    def one(g):
        st = stat_ref[g * heads : (g + 1) * heads, :]

        def spread(base):
            halves = [
                jnp.where(
                    low,
                    st[:, base + 2 * half : base + 2 * half + 1],
                    st[:, base + 2 * half + 1 : base + 2 * half + 2],
                )
                for half in range(pack // 2)
            ]
            return jnp.concatenate(halves, axis=1)

        prob = jnp.exp(logits_ref[g] - spread(0)) / spread(pack)
        gl = prob * (gw_ref[g] - spread(2 * pack))
        g1 = gl.astype(bf16).astype(f32)
        g2 = (gl - g1).astype(bf16).astype(f32)
        g3 = gl - g1 - g2
        stack = jnp.concatenate([g1, g2, g3, g1, g2, g1], axis=0).astype(bf16)
        grad = nn_dot(sk, stack)
        normal = normal_ref[g]
        inverse = inverse_ref[g][:1]
        centered = grad - jnp.mean(grad, axis=0, keepdims=True)
        along = jnp.mean(grad * normal, axis=0, keepdims=True)
        result = inverse * (centered - normal * along)
        out_ref[g * lanes : (g + 1) * lanes, :] = result.astype(bf16).T

    many = 4

    copies = []
    for n in range(groups // many):
        for e in range(many):
            one(n * many + e)
        at = pl.ds(n * many * lanes, many * lanes)
        part = pltpu.make_async_copy(out_ref.at[at], out_hbm.at[at], out_sem.at[n])
        part.start()
        copies.append(part)
    for copy in copies:
        copy.wait()


def alignment_kernel(
    ready,
    col_ref,
    own_ref,
    r1_ref,
    r2_ref,
    r3_ref,
    v_ref,
    gate_ref,
    x_ref,
    wf_ref,
    out_ref,
    w_ref,
    gated_ref,
):
    pays = (own_ref, r1_ref, r2_ref, r3_ref)
    nk = len(pays)
    heads = own_ref.shape[1]
    wide = own_ref.shape[2]
    tile = wide // 2
    pieces = own_ref.shape[0] - 2
    rows = pieces * heads
    half, all_tokens, chans = v_ref.shape
    chans = chans // 2
    tokens = pieces * 2
    head_width = chans // heads
    col = col_ref[0]

    low = lax.broadcasted_iota(jnp.int32, (rows, wide), 1) < tile
    lgs = [p[2:].reshape(rows, wide) for p in pays]
    peak = functools.reduce(jnp.maximum, lgs)
    m0 = jnp.max(jnp.where(low, peak, far_below), axis=1, keepdims=True)
    m1 = jnp.max(jnp.where(low, far_below, peak), axis=1, keepdims=True)
    top = jnp.where(low, m0, m1)
    ps = [jnp.exp(lg - top) for lg in lgs]
    every = sum(ps)
    t0 = jnp.sum(jnp.where(low, every, 0.0), axis=1, keepdims=True)
    t1 = jnp.sum(jnp.where(low, 0.0, every), axis=1, keepdims=True)
    total = jnp.where(low, t0, t1)
    for shift, p in enumerate(ps):
        source = lax.rem(col + nk - shift, nk)
        weight = p / total
        rolled = pltpu.roll(weight, tile, 1)
        for n in range(pieces):
            w_ref[source, :, 2 * n, :] = weight[n * heads : (n + 1) * heads]
            w_ref[source, :, 2 * n + 1, :] = rolled[n * heads : (n + 1) * heads]
    w = jnp.concatenate(
        [
            w_ref[k].reshape(heads * tokens, wide)[:, :tile]
            for k in range(nk)
        ],
        axis=1,
    ).astype(bf16)

    owner = lax.broadcasted_iota(jnp.int32, (tokens, chans), 1) // head_width

    def one(s, carry):
        full = nn_dot(w, v_ref[s])
        for e in range(2):
            cut = slice(e * chans, (e + 1) * chans)
            mean = jnp.zeros((tokens, chans), f32)
            for h in range(heads):
                mean = jnp.where(owner == h, full[h * tokens : (h + 1) * tokens, cut], mean)
            at = pl.ds(pl.multiple_of((e * half + s) * tokens, tokens), tokens)
            gated_ref[at, :] = (gate_ref[at, :] * mean).astype(bf16)
        return carry

    lax.fori_loop(0, half, one, 0, unroll=8)
    out_ref[...] = (x_ref[...].astype(f32) + nt_dot(gated_ref[...], wf_ref[...])).astype(bf16)


def on_device(
    counts,
    alignment_input,
    pair_input,
    token_valid_mask,
    first_factor_weights,
    second_factor_weights,
    content_weights_grid,
    sigmoid_weights_grid,
    outer_matrix,
    score_matrix,
    final_mixing_weights,
    adjoint_of_rowset,
):
    nq, nr, nk = counts
    row_index = lax.axis_index("row")
    col_index = lax.axis_index("col")
    seqs, tokens, width = alignment_input.shape
    tile_i, tile_j, z = pair_input.shape
    fc = first_factor_weights.shape[1]
    fd = second_factor_weights.shape[1]
    heads = score_matrix.shape[1]
    chans = content_weights_grid.shape[1]
    groups = tile_i // pack
    lanes = pack * tile_j
    sds = jax.ShapeDtypeStruct

    mask = token_valid_mask.reshape(1, -1)
    own_start = ((row_index * nk + col_index) * tokens).astype(jnp.int32).reshape(1)
    seq_index = lax.axis_index("seq")
    place = tuple(x.astype(jnp.int32).reshape(1) for x in (row_index, col_index, seq_index))
    col_scalar = col_index.astype(jnp.int32).reshape(1)
    half = seqs // 2

    l_rows = tokens // pack * fc
    r_rows = fd * tokens // 128 * seqs
    n_rows = half * tokens
    shard, rows, own_left, normed, weights = call(
        prepare_kernel,
        (
            sds((l_rows + 2 * n_rows + r_rows, 128), bf16),
            sds((l_rows + 2 * n_rows, 128), bf16),
            sds((l_rows, 128), bf16),
            sds((n_rows, 128), bf16),
            sds((width, 3 * chans), bf16),
        ),
        scratch=(
            pltpu.VMEM((tokens, seqs, width), f32),
            pltpu.VMEM((fd * tokens // 128, seqs, 128), f32),
        ),
        smem=1,
        vmem=60 * 1024 * 1024,
    )(
        own_start,
        alignment_input,
        adjoint_of_rowset,
        first_factor_weights.T,
        second_factor_weights.T,
        mask,
        content_weights_grid,
        sigmoid_weights_grid,
        final_mixing_weights.T,
    )

    def exchange(x, bit):
        return lax.ppermute(x, "col", [(c, c ^ bit) for c in range(nk)])

    other = exchange(shard, 1)
    across = exchange(rows, 2)
    pair = jnp.concatenate([x[l_rows + n_rows :] for x in (shard, other)], axis=0)
    all_cols = [
        lax.ppermute(
            pair,
            ("row", "col"),
            [(r * nk + c, (c ^ flip) * nk + r) for r in range(nr) for c in range(nk)],
        )
        for flip in (0, 2)
    ]

    def over_seq(x):
        if nq == 2:
            return lax.ppermute(x, "seq", [(0, 1), (1, 0)])
        return lax.all_gather(x, "seq", axis=0, tiled=True)

    lefts = [own_left, other, across, exchange(own_left, 3)]
    (left,) = call(join_left_kernel, (sds((nk * l_rows, 128), bf16),), smem=1)(place[1], *lefts)
    far_left = over_seq(left)
    weights, own = call(hand_on_kernel, (sds(weights.shape, bf16), sds(rows.shape, bf16)))(
        weights, rows
    )
    across, far_left, weights, own, *all_cols = lax.optimization_barrier(
        (across, far_left, weights, own, *all_cols)
    )
    all_rows = [own, other, across, exchange(across, 1)]

    (right,) = call(join_right_kernel, (sds((nk * r_rows, 128), bf16),), smem=1)(
        place[0], *all_cols
    )
    far_right = over_seq(right)

    head_lanes = seqs * chans // heads
    gw_own, block = call(
        weights_kernel,
        (
            sds((groups, heads, lanes), f32),
            sds((nk, half, tokens, 2 * width), bf16),
        ),
        scratch=(
            pltpu.VMEM((heads * tile_i, 2 * tile_j), f32),
            pltpu.VMEM((4 * width, 4 * chans), bf16),
            pltpu.VMEM((4 * width, 4 * chans), bf16),
            pltpu.VMEM((4 * width, 4 * chans), bf16),
            pltpu.VMEM((nk, 2, half, tokens, 2 * width), bf16),
            pltpu.VMEM((heads, tile_i, head_lanes), bf16),
            pltpu.VMEM((heads, 2 * tile_j, head_lanes), bf16),
        ),
        smem=2,
        flops=3_000_000_000,
        nbytes=3_000_000,
    )(*place[:2], *all_rows, *all_cols, weights)
    if nq == 2:
        gw_other = lax.ppermute(gw_own, "seq", [(0, 1), (1, 0)])
    else:
        gw_own, gw_other = lax.psum(gw_own, "seq"), jnp.zeros_like(gw_own)

    close, remote = exchange(block, 1), exchange(block, 2)

    pair_out, normal, inverse, logits = call(
        update_kernel,
        (
            sds((tile_i * tile_j, z), bf16),
            sds((groups, z, lanes), f32),
            sds((groups, 8, lanes), f32),
            sds((groups, heads, lanes), f32),
        ),
        scratch=(
            pltpu.VMEM((tile_i * tile_j, z), bf16),
            pltpu.SemaphoreType.DMA((groups // 4,)),
            pltpu.VMEM((nk, nq * r_rows, 128), bf16),
            pltpu.VMEM((fd, nq * seqs, 4 * tile_j), bf16),
            pltpu.VMEM((groups * fc, nq * pack * seqs), bf16),
            pltpu.VMEM((2 * z, fd * fc), bf16),
            pltpu.VMEM((groups // 4, fd * fc, 4 * lanes), bf16),
            pltpu.VMEM((groups // 4, fd * fc, 4 * lanes), bf16),
            pltpu.VMEM((z, 4 * lanes), f32),
            pltpu.VMEM((z, 4 * lanes), f32),
        ),
        smem=2,
        flops=14_000_000_000,
        nbytes=5_000_000,
        vmem=44 * 1024 * 1024,
        far=(6, 7, 8, 9),
        far_out=(0,),
    )(
        *place[1:],
        left,
        right,
        far_left,
        far_right,
        mask,
        outer_matrix,
        score_matrix.T,
        pair_input.reshape(tile_i * tile_j, z),
    )

    payload = sds((2 + groups // nk * (pack // 2), heads, 2 * tile_j), f32)
    gw, pay0, pay1, pay2, pay3 = call(
        softmax_kernel,
        (sds((groups, heads, lanes), f32), payload, payload, payload, payload),
        smem=1,
    )(col_scalar, logits, gw_own, gw_other, mask)

    got = [
        lax.ppermute(pay, "col", [(c, (c + shift) % nk) for c in range(nk)])
        for shift, pay in ((1, pay1), (2, pay2), (3, pay3))
    ]


    close, remote, pay0 = lax.optimization_barrier((close, remote, pay0))
    every = [block, close, remote, exchange(remote, 1)]
    values, gating = call(
        values_kernel,
        (sds((half, nr * nk * tokens, 2 * chans), bf16), sds((seqs * tokens, chans), f32)),
        scratch=(pltpu.VMEM((nr, nk, half, tokens, 2 * width), bf16),),
        smem=1,
        flops=4_000_000_000,
        nbytes=6_000_000,
    )(col_scalar, *every, content_weights_grid, normed, sigmoid_weights_grid)

    got, values, gating = lax.optimization_barrier((got, values, gating))

    (gradient,) = call(
        gradient_kernel,
        (sds((tile_i * tile_j, z), bf16),),
        scratch=(
            pltpu.VMEM((groups * heads, groups * heads), f32),
            pltpu.VMEM((tile_i * tile_j, z), bf16),
            pltpu.SemaphoreType.DMA((groups // 4,)),
        ),
        far_out=(0,),
        flops=4_000_000_000,
        nbytes=3_000_000,
    )(pay0, *got, logits, gw, normal, inverse, score_matrix.T)

    (aligned,) = call(
        alignment_kernel,
        (sds((seqs * tokens, width), bf16),),
        scratch=(
            pltpu.VMEM((nk, heads, tokens, 2 * tile_j), f32),
            pltpu.VMEM((seqs * tokens, chans), bf16),
        ),
        smem=1,
        flops=3_000_000_000,
        nbytes=5_000_000,
    )(
        col_scalar,
        pay0,
        *got,
        values,
        gating,
        alignment_input.reshape(seqs * tokens, width),
        final_mixing_weights.T,
    )
    return (
        aligned.reshape(seqs, tokens, width),
        pair_out.reshape(tile_i, tile_j, z),
        gradient.reshape(tile_i, tile_j, z),
    )


def solution(mesh):
    counts = (mesh.shape["seq"], mesh.shape["row"], mesh.shape["col"])
    in_specs = (
        P("seq", ("row", "col"), None),
        P("row", "col", None),
        P(),
        P(),
        P(),
        P(),
        P(),
        P(),
        P(),
        P(),
        P("seq", ("row", "col"), None),
    )
    out_specs = (P("seq", ("row", "col"), None), P("row", "col", None), P("row", "col", None))
    return jax.shard_map(
        functools.partial(on_device, counts),
        mesh=mesh,
        in_specs=in_specs,
        out_specs=out_specs,
        check_vma=False,
    )
```

```python
import functools

import jax
import jax.numpy as jnp
from jax import lax
from jax.experimental import pallas as pl
from jax.experimental.pallas import tpu as pltpu
from jax.sharding import PartitionSpec as P

epsilon = 1e-05
far_below = -1e30
vmem_bytes = 32 * 1024 * 1024
pack = 4

f32 = jnp.float32
bf16 = jnp.bfloat16


def nt_dot(a, b):
    return lax.dot_general(a, b, (((1,), (1,)), ((), ())), preferred_element_type=f32)


def nn_dot(a, b):
    return jnp.dot(a, b, preferred_element_type=f32)


def high_low(x):
    high = x.astype(bf16)
    return high, (x - high.astype(f32)).astype(bf16)


def call(
    kernel, out_shape, scratch=(), smem=0, flops=0, nbytes=0, vmem=vmem_bytes, far=(), far_out=()
):
    def run(*args):
        count = len(args)
        in_specs = [
            pl.BlockSpec(memory_space=pltpu.SMEM if n < smem else pltpu.VMEM) for n in range(count)
        ]
        for n in far:
            in_specs[n] = pl.BlockSpec(memory_space=pltpu.HBM)
        landing = [pltpu.VMEM(args[n].shape, args[n].dtype) for n in far]
        if far:
            landing.append(pltpu.SemaphoreType.DMA((len(far),)))

        def body(*refs):
            inputs = list(refs[:count])
            extra = refs[len(refs) - len(landing) :]
            rest = refs[count : len(refs) - len(landing)]
            copies = []
            for i, n in enumerate(far):
                copies.append(pltpu.make_async_copy(inputs[n], extra[i], extra[-1].at[i]))
                copies[-1].start()
                inputs[n] = extra[i]

            def ready():
                for copy in copies:
                    copy.wait()

            kernel(ready, *inputs, *rest)

        return pl.pallas_call(
            body,
            out_shape=out_shape,
            in_specs=in_specs,
            out_specs=[
                pl.BlockSpec(memory_space=pltpu.HBM if n in far_out else pltpu.VMEM)
                for n in range(len(out_shape))
            ],
            scratch_shapes=list(scratch) + landing,
            compiler_params=pltpu.CompilerParams(vmem_limit_bytes=vmem),
            cost_estimate=pl.CostEstimate(flops=flops, bytes_accessed=nbytes, transcendentals=0),
        )(*args)

    return run


def valid_count(mask_ref):
    return jnp.sum(mask_ref[...].astype(f32), axis=1, keepdims=True)


def column_mask(mask_ref, col, tile, copies):
    lane = lax.broadcasted_iota(jnp.int32, (1, copies * tile), 1)
    token = (lax.rem(lane, tile) + col * tile).astype(f32)
    return (token < valid_count(mask_ref)).astype(f32)


def twice(w):
    none = jnp.zeros_like(w)
    return jnp.concatenate(
        [jnp.concatenate([w, none], axis=1), jnp.concatenate([none, w], axis=1)], axis=0
    )


def prepare_kernel(
    ready,
    own_ref,
    x_ref,
    adj_ref,
    w1_ref,
    w2_ref,
    mask_ref,
    wv_ref,
    wg_ref,
    wf_ref,
    shard_ref,
    rows_ref,
    mine_ref,
    left_ref,
    norm_ref,
    weights_ref,
    turn_ref,
    place_ref,
):
    chans = wv_ref.shape[1]
    weights_ref[:, :chans] = wv_ref[...]
    weights_ref[:, chans : 2 * chans] = wg_ref[...]
    weights_ref[:, 2 * chans :] = wf_ref[...]
    seqs, tokens, width = x_ref.shape
    half = seqs // 2
    fd = w2_ref.shape[0]
    x = x_ref[...].astype(f32)
    center = x - jnp.mean(x, axis=-1, keepdims=True)
    inverse = lax.rsqrt(jnp.mean(center * center, axis=-1, keepdims=True) + epsilon)
    normed = center * inverse
    rows = half * tokens
    adj = adj_ref[...].astype(f32)

    def two(x):
        x = jnp.concatenate([x[:half], x[half:]], axis=-1)
        return x.reshape(rows, 2 * width).astype(bf16)

    packed = two(normed)
    norm_ref[...] = packed
    base = tokens // pack * w1_ref.shape[0]
    shard_ref[base : base + rows, :] = two(adj)
    shard_ref[base + rows : base + 2 * rows, :] = packed
    token = lax.broadcasted_iota(jnp.int32, (seqs, tokens, width), 1) + own_ref[0]
    count = valid_count(mask_ref).reshape(1, 1, 1)
    real = jnp.where(token.astype(f32) < count, normed, 0.0)
    for s in range(seqs):
        turn_ref[:, s, :] = real[s]
    turned = turn_ref[...].astype(bf16).reshape(tokens * seqs, width)
    left = nt_dot(w1_ref[...], turned).astype(bf16)
    fc = w1_ref.shape[0]
    wk = pack * seqs
    for g in range(tokens // pack):
        shard_ref[g * fc : (g + 1) * fc, :] = left[:, g * wk : (g + 1) * wk]
    size = 128 // tokens
    real = real.astype(bf16)
    w2 = w2_ref[...]
    d = lax.broadcasted_iota(jnp.int32, (fd, 128), 0)
    lane = lax.broadcasted_iota(jnp.int32, (fd, 128), 1)
    mine = lax.rem(d, size) == lane // tokens
    for s in range(seqs):
        res = nt_dot(w2, jnp.concatenate([real[s]] * size, axis=0))
        res = jnp.where(mine, res, 0.0).reshape(fd // size, size, 128)
        place_ref[:, s, :] = jnp.sum(res, axis=1)
    right = place_ref[...].reshape(fd // size * seqs, 128).astype(bf16)
    rows_ref[...] = shard_ref[: base + 2 * rows, :]
    left_ref[...] = shard_ref[:base, :]
    shard_ref[base + 2 * rows :, :] = right
    mine_ref[...] = shard_ref[base + rows :, :]


def join_left_kernel(ready, col_ref, rows0_ref, rows1_ref, rows2_ref, rows3_ref, out_ref):
    size = out_ref.shape[0] // 4
    for t, ref in enumerate((rows0_ref, rows1_ref, rows2_ref, rows3_ref)):
        at = pl.ds(pl.multiple_of(jnp.bitwise_xor(col_ref[0], t) * size, size), size)
        out_ref[at, :] = ref[:size, :]


def hand_on_kernel(ready, weights_ref, rows_ref, weights_out_ref, rows_out_ref):
    weights_out_ref[...] = weights_ref[...]
    rows_out_ref[...] = rows_ref[...]


def join_right_kernel(ready, row_ref, pair0_ref, pair1_ref, out_ref):
    size = out_ref.shape[0] // 4
    for t in range(4):
        ref = (pair0_ref, pair1_ref)[t // 2]
        at = pl.ds(pl.multiple_of(jnp.bitwise_xor(row_ref[0], t) * size, size), size)
        end = ref.shape[0] // 2 * (t % 2 + 1)
        out_ref[at, :] = ref[end - size : end, :]


def update_kernel(
    ready,
    col_ref,
    seq_ref,
    left_ref,
    right_ref,
    far_left_ref,
    far_right_ref,
    mask_ref,
    m_ref,
    score_ref,
    pair_ref,
    pout_hbm,
    normal_ref,
    inverse_ref,
    logits_ref,
    pout_ref,
    out_sem,
    rk_ref,
    rab_ref,
    lm_ref,
    mt_ref,
    oh_ref,
    ol_ref,
    update0_ref,
    update1_ref,
):
    nk = rk_ref.shape[0]
    width_d, pair_rows, _ = rab_ref.shape
    col, seq = col_ref[0], seq_ref[0]
    z = pair_ref.shape[1]
    groups, heads, lanes = logits_ref.shape
    tile_j = lanes // pack
    tokens = tile_j // nk
    fc = lm_ref.shape[0] // groups
    seqs = 128 // pack
    nq = pair_rows // seqs
    wk = pack * seqs

    r_rows = rk_ref.shape[1] // nq
    l_rows = groups * fc
    if nq == 2:
        sources = ((seq, 0, left_ref, right_ref), (1 - seq, 0, far_left_ref, far_right_ref))
    else:
        sources = tuple((q, q, far_left_ref, far_right_ref) for q in range(nq))
    for q, slot, from_left, from_right in sources:
        at = pl.ds(pl.multiple_of(q * r_rows, r_rows), r_rows)
        for k in range(nk):
            first = (slot * nk + k) * r_rows
            rk_ref[k, at, :] = from_right[first : first + r_rows, :]
        to = pl.ds(pl.multiple_of(q * wk, wk), wk)
        lm_ref[:, to] = from_left[slot * l_rows : (slot + 1) * l_rows, :]
    size = 128 // tokens
    right = jnp.concatenate([rk_ref[k] for k in range(nk)], axis=1)
    source = lax.broadcasted_iota(jnp.int32, (nk * 128, 4 * tile_j), 0)
    target = lax.broadcasted_iota(jnp.int32, (nk * 128, 4 * tile_j), 1)
    used = jnp.logical_or(target < tile_j, target >= 3 * tile_j)
    j = lax.rem(target, tile_j)
    offset = jnp.where(used, source - (j // tokens * 128 + lax.rem(j, tokens)), -1)
    blocks = width_d // size
    for e in range(size):
        pick = jnp.where(offset == e * tokens, 1.0, 0.0).astype(bf16)
        res = nn_dot(right, pick).astype(bf16)
        for q in range(nq):
            for n in range(blocks):
                at = (q * blocks + n) * seqs
                rab_ref[n * size + e, q * seqs : (q + 1) * seqs, :] = res[at : at + seqs]

    chunk = 8
    many = 4
    wide = oh_ref.shape[2] // lanes
    empty = jnp.zeros((seqs, 2 * tile_j), bf16)

    def block_of(d):
        rows = []
        for q in range(nq):
            both = rab_ref[d, q * seqs : (q + 1) * seqs, :]
            part = both[:, : 2 * tile_j], both[:, 2 * tile_j :]
            for i in range(pack):
                pieces = [empty] * (pack // 2)
                pieces[i // 2] = part[i % 2]
                rows.append(jnp.concatenate(pieces, axis=1))
        return jnp.concatenate(rows, axis=0)

    def outer_of(n):
        block = jnp.concatenate([block_of(many * n + e) for e in range(many)], axis=1)
        for m in range(groups // chunk):
            out = nn_dot(lm_ref[m * chunk * fc : (m + 1) * chunk * fc, :], block)
            high, low = high_low(out)
            for e in range(many):
                at = slice((many * n + e) * fc, (many * n + e + 1) * fc)
                for g in range(chunk):
                    group = m * chunk + g
                    to = slice(group % wide * lanes, (group % wide + 1) * lanes)
                    cut = slice(g * fc, (g + 1) * fc), slice(e * lanes, (e + 1) * lanes)
                    oh_ref[group // wide, at, to] = high[cut]
                    ol_ref[group // wide, at, to] = low[cut]

    for n in range(width_d // many):
        outer_of(n)

    ready()
    some = z // fc
    for n in range(width_d // some):
        block = jnp.concatenate(
            [m_ref[pl.ds(n * some + e, fc, stride=width_d), :] for e in range(some)], axis=0
        ).T
        high, low = high_low(block)
        mt_ref[:z, n * z : (n + 1) * z] = high
        mt_ref[z:, n * z : (n + 1) * z] = low
    maskj = column_mask(mask_ref, col, tile_j, 2)

    maskl = jnp.concatenate([maskj] * (pack // 2), axis=1) > 0
    score = score_ref[...]
    s1 = score.astype(bf16).astype(f32)
    s2 = (score - s1).astype(bf16).astype(f32)
    s3 = score - s1 - s2
    none = jnp.zeros_like(s1)
    st = jnp.concatenate(
        [
            jnp.concatenate([s1, s2, s3, none], axis=0),
            jnp.concatenate([s1, s2, none, none], axis=0),
        ],
        axis=1,
    ).astype(bf16)

    def product(n):
        two = nn_dot(mt_ref[...], oh_ref[n])
        update_refs[n % 2][...] = two[:z] + two[z:] + nn_dot(mt_ref[:z, :], ol_ref[n])

    def finish(n):
        for e in range(wide):
            g = n * wide + e
            at = slice(g * lanes, (g + 1) * lanes)
            before = pair_ref[at, :].T.astype(f32)
            update = update_refs[n % 2][:, e * lanes : (e + 1) * lanes]
            result = (before + update).astype(bf16)
            x = result.astype(f32)
            pout_ref[at, :] = result.T
            center = x - jnp.mean(x, axis=0, keepdims=True)
            inverse = lax.rsqrt(jnp.mean(center * center, axis=0, keepdims=True) + epsilon)
            normal = center * inverse
            normal_ref[g] = normal
            inverse_ref[g] = jnp.broadcast_to(inverse, inverse_ref.shape[1:])
            high, low = high_low(normal)
            scores = nn_dot(st, jnp.concatenate([high, low], axis=0))
            logits = scores[:heads] + scores[heads : 2 * heads] + scores[2 * heads : 3 * heads]
            logits_ref[g] = jnp.where(maskl, logits, far_below)

    steps = groups // wide
    update_refs = (update0_ref, update1_ref)
    copies = []
    for n in range(steps + 1):
        if n < steps:
            product(n)
        if n > 0:
            finish(n - 1)
            at = pl.ds((n - 1) * wide * lanes, wide * lanes)
            part = pltpu.make_async_copy(pout_ref.at[at], pout_hbm.at[at], out_sem.at[n - 1])
            part.start()
            copies.append(part)
    for copy in copies:
        copy.wait()


def by_heads(w, heads, out_ref):
    width, chans = w.shape
    hw = chans // heads
    block = 4 * hw
    slot = lax.broadcasted_iota(jnp.int32, (width, block), 1) // hw
    w = w.astype(f32)
    for t in range(chans // block):
        part = w[:, t * block : (t + 1) * block]
        turns = [part] + [pltpu.roll(part, n * hw, 1) for n in range(1, 4)]
        for e in range(4):
            h = t * 4 + e
            for s in range(4):
                out_ref[s * width : (s + 1) * width, h * block : (h + 1) * block] = jnp.where(
                    slot == s, turns[(s - e) % 4], 0.0
                ).astype(bf16)


def weights_kernel(
    ready,
    row_ref,
    col_ref,
    side0_ref,
    side1_ref,
    side2_ref,
    side3_ref,
    cols0_ref,
    cols1_ref,
    weights_ref,
    gw_ref,
    cols_ref,
    acc_ref,
    bv_ref,
    bg_ref,
    bf_ref,
    rows_ref,
    gs_ref,
    vs_ref,
):
    nk, half, tokens, _ = cols_ref.shape
    tile = nk * tokens
    groups, heads, lanes = gw_ref.shape
    row, col = row_ref[0], col_ref[0]
    count = half * tokens
    size = side0_ref.shape[0] - 2 * count
    for t, ref in enumerate((side0_ref, side1_ref, side2_ref, side3_ref)):
        k = jnp.bitwise_xor(col, t)
        rows_ref[k] = ref[size : size + 2 * count, :].reshape(rows_ref.shape[1:])
    for t in range(nk):
        ref = (cols0_ref, cols1_ref)[t // 2]
        start = ref.shape[0] // 2 * (t % 2)
        part = ref[start : start + count, :]
        cols_ref[jnp.bitwise_xor(row, t)] = part.reshape(cols_ref.shape[1:])
    chans = weights_ref.shape[1] // 3
    by_heads(weights_ref[:, :chans], heads, bv_ref)
    by_heads(weights_ref[:, chans : 2 * chans], heads, bg_ref)
    by_heads(weights_ref[:, 2 * chans :], heads, bf_ref)
    block = bv_ref.shape[1] // heads

    def four(read, n):
        return jnp.concatenate(
            [
                jnp.concatenate(
                    [
                        jnp.concatenate([read(k, 2 * (2 * n + e) + p) for k in range(nk)], axis=0)
                        for p in range(2)
                    ],
                    axis=1,
                )
                for e in range(2)
            ],
            axis=0,
        )

    for hp in range(heads // 2):
        cut = slice(hp * 2 * block, (hp + 1) * 2 * block)
        for n in range(half // 4):
            v = nn_dot(four(lambda k, s: cols_ref[k, s], n), bv_ref[:, cut]).astype(bf16)
            gate = nn_dot(four(lambda k, s: rows_ref[k, 1, s], n), bg_ref[:, cut])
            grad = nn_dot(four(lambda k, s: rows_ref[k, 0, s], n), bf_ref[:, cut])
            g = (grad * jax.nn.sigmoid(gate)).astype(bf16)
            for e in range(2):
                to = slice((2 * n + e) * block, (2 * n + e + 1) * block)
                for o in range(2):
                    mine = slice(o * block, (o + 1) * block)
                    ve = v[e * tile : (e + 1) * tile, mine]
                    vs_ref[2 * hp + o, :tile, to] = ve
                    vs_ref[2 * hp + o, tile:, to] = ve
                    gs_ref[2 * hp + o, :, to] = g[e * tile : (e + 1) * tile, mine]
    for h in range(heads):
        acc_ref[h * tile : (h + 1) * tile, :] = nt_dot(gs_ref[h], vs_ref[h])

    first = lax.broadcasted_iota(jnp.int32, (groups, 2 * tile), 1) < tile
    for h in range(heads):
        for part in range(pack // 2):
            a = acc_ref[pl.ds(h * tile + 2 * part, groups, stride=pack), :]
            b = acc_ref[pl.ds(h * tile + 2 * part + 1, groups, stride=pack), :]
            gw_ref[:, h, part * 2 * tile : (part + 1) * 2 * tile] = jnp.where(first, a, b)


def softmax_kernel(
    ready,
    col_ref,
    logits_ref,
    gwa_ref,
    gwb_ref,
    mask_ref,
    gw_ref,
    own_ref,
    pay1_ref,
    pay2_ref,
    pay3_ref,
):
    groups, heads, lanes = logits_ref.shape
    tile = lanes // pack
    nk = 4
    rows = groups * heads
    col = col_ref[0]
    gw_ref[...] = gwa_ref[...] + gwb_ref[...]
    lane = lax.broadcasted_iota(jnp.int32, (rows, 2 * tile), 1)
    low = lane < tile
    maskj = column_mask(mask_ref, col, tile, 2)
    stats = jnp.zeros((rows, 2 * tile), f32)
    for part in range(pack // 2):
        cut = slice(part * 2 * tile, (part + 1) * 2 * tile)
        lg = logits_ref[:, :, cut].reshape(rows, 2 * tile)
        gw = gw_ref[:, :, cut].reshape(rows, 2 * tile)
        m0 = jnp.max(jnp.where(low, lg, far_below), axis=1, keepdims=True)
        m1 = jnp.max(jnp.where(low, far_below, lg), axis=1, keepdims=True)
        p = jnp.exp(lg - jnp.where(low, m0, m1)) * maskj
        pg = p * gw
        for e, m in ((0, m0), (1, m1)):
            mine = low if e == 0 else jnp.logical_not(low)
            i = 2 * part + e
            total = jnp.sum(jnp.where(mine, p, 0.0), axis=1, keepdims=True)
            inner = jnp.sum(jnp.where(mine, pg, 0.0), axis=1, keepdims=True)
            stats = jnp.where(lane == i, m, stats)
            stats = jnp.where(lane == pack + i, total, stats)
            stats = jnp.where(lane == 2 * pack + i, inner, stats)
    turned = stats.T[:16]
    per = groups // nk
    for shift, pay in enumerate((own_ref, pay1_ref, pay2_ref, pay3_ref)):
        dest = lax.rem(col + shift, nk)
        pay[0] = turned[:8]
        pay[1] = turned[8:]
        for g in range(per):
            piece = logits_ref[dest * per + g]
            for part in range(pack // 2):
                pay[2 + g * (pack // 2) + part] = piece[:, part * 2 * tile : (part + 1) * 2 * tile]


def values_kernel(
    ready, col_ref, ev0_ref, ev1_ref, ev2_ref, ev3_ref, wv_ref, norm_ref, wg_ref, v_ref, gate_ref, ev_ref
):
    nr, nk, half, tokens, wide = ev_ref.shape
    chans = wv_ref.shape[1]
    for t, ref in enumerate((ev0_ref, ev1_ref, ev2_ref, ev3_ref)):
        ev_ref[jnp.bitwise_xor(col_ref[0], t)] = ref[...]
    gate = jax.nn.sigmoid(nn_dot(norm_ref[...], twice(wg_ref[...])))
    gate_ref[: half * tokens] = gate[:, :chans]
    gate_ref[half * tokens :] = gate[:, chans:]
    wv = twice(wv_ref[...])
    for s in range(half):
        x = jnp.concatenate([ev_ref[r, k, s] for r in range(nr) for k in range(nk)], axis=0)
        v_ref[s] = nn_dot(x, wv).astype(bf16)


def gradient_kernel(
    ready,
    own_ref, r1_ref, r2_ref, r3_ref, logits_ref, gw_ref, normal_ref, inverse_ref, score_ref, out_hbm, stat_ref, out_ref, out_sem
):
    groups, heads, lanes = logits_ref.shape
    rows = groups * heads
    score = score_ref[...]
    z = score.shape[1]
    s1 = score.astype(bf16).astype(f32)
    s2 = (score - s1).astype(bf16).astype(f32)
    s3 = score - s1 - s2
    parts = [s1, s1, s1, s2, s2, s3, jnp.zeros((z - 6 * heads, z), f32)]
    sk = jnp.concatenate(parts, axis=0).T[:, : 6 * heads].astype(bf16)
    pays = (own_ref, r1_ref, r2_ref, r3_ref)
    ms = [p[0][:pack] for p in pays]
    ls = [p[0][pack : 2 * pack] for p in pays]
    ns = [p[1][:pack] for p in pays]
    top = functools.reduce(jnp.maximum, ms)
    scales = [jnp.exp(m - top) for m in ms]
    total = sum(a * b for a, b in zip(ls, scales))
    inner = sum(a * b for a, b in zip(ns, scales)) / total
    stacked = jnp.concatenate([top, total, inner, jnp.zeros((rows - 3 * pack, rows), f32)], axis=0)
    stat_ref[...] = stacked.T

    tile = lanes // pack
    low = lax.broadcasted_iota(jnp.int32, (heads, 2 * tile), 1) < tile

    def one(g):
        st = stat_ref[g * heads : (g + 1) * heads, :]

        def spread(base):
            halves = [
                jnp.where(
                    low,
                    st[:, base + 2 * half : base + 2 * half + 1],
                    st[:, base + 2 * half + 1 : base + 2 * half + 2],
                )
                for half in range(pack // 2)
            ]
            return jnp.concatenate(halves, axis=1)

        prob = jnp.exp(logits_ref[g] - spread(0)) / spread(pack)
        gl = prob * (gw_ref[g] - spread(2 * pack))
        g1 = gl.astype(bf16).astype(f32)
        g2 = (gl - g1).astype(bf16).astype(f32)
        g3 = gl - g1 - g2
        stack = jnp.concatenate([g1, g2, g3, g1, g2, g1], axis=0).astype(bf16)
        grad = nn_dot(sk, stack)
        normal = normal_ref[g]
        inverse = inverse_ref[g][:1]
        centered = grad - jnp.mean(grad, axis=0, keepdims=True)
        along = jnp.mean(grad * normal, axis=0, keepdims=True)
        result = inverse * (centered - normal * along)
        out_ref[g * lanes : (g + 1) * lanes, :] = result.astype(bf16).T

    many = 4

    copies = []
    for n in range(groups // many):
        for e in range(many):
            one(n * many + e)
        at = pl.ds(n * many * lanes, many * lanes)
        part = pltpu.make_async_copy(out_ref.at[at], out_hbm.at[at], out_sem.at[n])
        part.start()
        copies.append(part)
    for copy in copies:
        copy.wait()


def alignment_kernel(
    ready,
    col_ref,
    own_ref,
    r1_ref,
    r2_ref,
    r3_ref,
    v_ref,
    gate_ref,
    x_ref,
    wf_ref,
    out_ref,
    w_ref,
    gated_ref,
):
    pays = (own_ref, r1_ref, r2_ref, r3_ref)
    nk = len(pays)
    heads = own_ref.shape[1]
    wide = own_ref.shape[2]
    tile = wide // 2
    pieces = own_ref.shape[0] - 2
    rows = pieces * heads
    half, all_tokens, chans = v_ref.shape
    chans = chans // 2
    tokens = pieces * 2
    head_width = chans // heads
    col = col_ref[0]

    low = lax.broadcasted_iota(jnp.int32, (rows, wide), 1) < tile
    lgs = [p[2:].reshape(rows, wide) for p in pays]
    peak = functools.reduce(jnp.maximum, lgs)
    m0 = jnp.max(jnp.where(low, peak, far_below), axis=1, keepdims=True)
    m1 = jnp.max(jnp.where(low, far_below, peak), axis=1, keepdims=True)
    top = jnp.where(low, m0, m1)
    ps = [jnp.exp(lg - top) for lg in lgs]
    every = sum(ps)
    t0 = jnp.sum(jnp.where(low, every, 0.0), axis=1, keepdims=True)
    t1 = jnp.sum(jnp.where(low, 0.0, every), axis=1, keepdims=True)
    total = jnp.where(low, t0, t1)
    for shift, p in enumerate(ps):
        source = lax.rem(col + nk - shift, nk)
        weight = p / total
        rolled = pltpu.roll(weight, tile, 1)
        for n in range(pieces):
            w_ref[source, :, 2 * n, :] = weight[n * heads : (n + 1) * heads]
            w_ref[source, :, 2 * n + 1, :] = rolled[n * heads : (n + 1) * heads]
    w = jnp.concatenate(
        [
            w_ref[k].reshape(heads * tokens, wide)[:, :tile]
            for k in range(nk)
        ],
        axis=1,
    ).astype(bf16)

    owner = lax.broadcasted_iota(jnp.int32, (tokens, chans), 1) // head_width

    def one(s, carry):
        full = nn_dot(w, v_ref[s])
        for e in range(2):
            cut = slice(e * chans, (e + 1) * chans)
            mean = jnp.zeros((tokens, chans), f32)
            for h in range(heads):
                mean = jnp.where(owner == h, full[h * tokens : (h + 1) * tokens, cut], mean)
            at = pl.ds(pl.multiple_of((e * half + s) * tokens, tokens), tokens)
            gated_ref[at, :] = (gate_ref[at, :] * mean).astype(bf16)
        return carry

    lax.fori_loop(0, half, one, 0, unroll=8)
    out_ref[...] = (x_ref[...].astype(f32) + nt_dot(gated_ref[...], wf_ref[...])).astype(bf16)


def on_device(
    counts,
    alignment_input,
    pair_input,
    token_valid_mask,
    first_factor_weights,
    second_factor_weights,
    content_weights_grid,
    sigmoid_weights_grid,
    outer_matrix,
    score_matrix,
    final_mixing_weights,
    adjoint_of_rowset,
):
    nq, nr, nk = counts
    row_index = lax.axis_index("row")
    col_index = lax.axis_index("col")
    seqs, tokens, width = alignment_input.shape
    tile_i, tile_j, z = pair_input.shape
    fc = first_factor_weights.shape[1]
    fd = second_factor_weights.shape[1]
    heads = score_matrix.shape[1]
    chans = content_weights_grid.shape[1]
    groups = tile_i // pack
    lanes = pack * tile_j
    sds = jax.ShapeDtypeStruct

    mask = token_valid_mask.reshape(1, -1)
    own_start = ((row_index * nk + col_index) * tokens).astype(jnp.int32).reshape(1)
    seq_index = lax.axis_index("seq")
    place = tuple(x.astype(jnp.int32).reshape(1) for x in (row_index, col_index, seq_index))
    col_scalar = col_index.astype(jnp.int32).reshape(1)
    half = seqs // 2

    l_rows = tokens // pack * fc
    r_rows = fd * tokens // 128 * seqs
    n_rows = half * tokens
    shard, rows, mine, own_left, normed, weights = call(
        prepare_kernel,
        (
            sds((l_rows + 2 * n_rows + r_rows, 128), bf16),
            sds((l_rows + 2 * n_rows, 128), bf16),
            sds((n_rows + r_rows, 128), bf16),
            sds((l_rows, 128), bf16),
            sds((n_rows, 128), bf16),
            sds((width, 3 * chans), bf16),
        ),
        scratch=(
            pltpu.VMEM((tokens, seqs, width), f32),
            pltpu.VMEM((fd * tokens // 128, seqs, 128), f32),
        ),
        smem=1,
        vmem=60 * 1024 * 1024,
    )(
        own_start,
        alignment_input,
        adjoint_of_rowset,
        first_factor_weights.T,
        second_factor_weights.T,
        mask,
        content_weights_grid,
        sigmoid_weights_grid,
        final_mixing_weights.T,
    )

    def exchange(x, bit):
        return lax.ppermute(x, "col", [(c, c ^ bit) for c in range(nk)])

    other = exchange(shard, 1)
    across = exchange(rows, 2)
    pair = jnp.concatenate([mine, other[l_rows + n_rows :]], axis=0)
    all_cols = [
        lax.ppermute(
            pair,
            ("row", "col"),
            [(r * nk + c, (c ^ flip) * nk + r) for r in range(nr) for c in range(nk)],
        )
        for flip in (0, 2)
    ]

    def over_seq(x):
        if nq == 2:
            return lax.ppermute(x, "seq", [(0, 1), (1, 0)])
        return lax.all_gather(x, "seq", axis=0, tiled=True)

    lefts = [own_left, other, across, exchange(own_left, 3)]
    (left,) = call(join_left_kernel, (sds((nk * l_rows, 128), bf16),), smem=1)(place[1], *lefts)
    far_left = over_seq(left)
    weights, own = call(hand_on_kernel, (sds(weights.shape, bf16), sds(rows.shape, bf16)))(
        weights, rows
    )
    across, far_left, weights, own, *all_cols = lax.optimization_barrier(
        (across, far_left, weights, own, *all_cols)
    )
    all_rows = [own, other, across, exchange(across, 1)]

    (right,) = call(join_right_kernel, (sds((nk * r_rows, 128), bf16),), smem=1)(
        place[0], *all_cols
    )
    far_right = over_seq(right)

    head_lanes = seqs * chans // heads
    gw_own, block = call(
        weights_kernel,
        (
            sds((groups, heads, lanes), f32),
            sds((nk, half, tokens, 2 * width), bf16),
        ),
        scratch=(
            pltpu.VMEM((heads * tile_i, 2 * tile_j), f32),
            pltpu.VMEM((4 * width, 4 * chans), bf16),
            pltpu.VMEM((4 * width, 4 * chans), bf16),
            pltpu.VMEM((4 * width, 4 * chans), bf16),
            pltpu.VMEM((nk, 2, half, tokens, 2 * width), bf16),
            pltpu.VMEM((heads, tile_i, head_lanes), bf16),
            pltpu.VMEM((heads, 2 * tile_j, head_lanes), bf16),
        ),
        smem=2,
        flops=3_000_000_000,
        nbytes=3_000_000,
    )(*place[:2], *all_rows, *all_cols, weights)
    if nq == 2:
        gw_other = lax.ppermute(gw_own, "seq", [(0, 1), (1, 0)])
    else:
        gw_own, gw_other = lax.psum(gw_own, "seq"), jnp.zeros_like(gw_own)

    close, remote = exchange(block, 1), exchange(block, 2)

    pair_out, normal, inverse, logits = call(
        update_kernel,
        (
            sds((tile_i * tile_j, z), bf16),
            sds((groups, z, lanes), f32),
            sds((groups, 8, lanes), f32),
            sds((groups, heads, lanes), f32),
        ),
        scratch=(
            pltpu.VMEM((tile_i * tile_j, z), bf16),
            pltpu.SemaphoreType.DMA((groups // 4,)),
            pltpu.VMEM((nk, nq * r_rows, 128), bf16),
            pltpu.VMEM((fd, nq * seqs, 4 * tile_j), bf16),
            pltpu.VMEM((groups * fc, nq * pack * seqs), bf16),
            pltpu.VMEM((2 * z, fd * fc), bf16),
            pltpu.VMEM((groups // 4, fd * fc, 4 * lanes), bf16),
            pltpu.VMEM((groups // 4, fd * fc, 4 * lanes), bf16),
            pltpu.VMEM((z, 4 * lanes), f32),
            pltpu.VMEM((z, 4 * lanes), f32),
        ),
        smem=2,
        flops=14_000_000_000,
        nbytes=5_000_000,
        vmem=44 * 1024 * 1024,
        far=(6, 7, 8, 9),
        far_out=(0,),
    )(
        *place[1:],
        left,
        right,
        far_left,
        far_right,
        mask,
        outer_matrix,
        score_matrix.T,
        pair_input.reshape(tile_i * tile_j, z),
    )

    payload = sds((2 + groups // nk * (pack // 2), heads, 2 * tile_j), f32)
    gw, pay0, pay1, pay2, pay3 = call(
        softmax_kernel,
        (sds((groups, heads, lanes), f32), payload, payload, payload, payload),
        smem=1,
    )(col_scalar, logits, gw_own, gw_other, mask)

    got = [
        lax.ppermute(pay, "col", [(c, (c + shift) % nk) for c in range(nk)])
        for shift, pay in ((1, pay1), (2, pay2), (3, pay3))
    ]


    close, remote, pay0 = lax.optimization_barrier((close, remote, pay0))
    every = [block, close, remote, exchange(remote, 1)]
    values, gating = call(
        values_kernel,
        (sds((half, nr * nk * tokens, 2 * chans), bf16), sds((seqs * tokens, chans), f32)),
        scratch=(pltpu.VMEM((nr, nk, half, tokens, 2 * width), bf16),),
        smem=1,
        flops=4_000_000_000,
        nbytes=6_000_000,
    )(col_scalar, *every, content_weights_grid, normed, sigmoid_weights_grid)

    got, values, gating = lax.optimization_barrier((got, values, gating))

    (gradient,) = call(
        gradient_kernel,
        (sds((tile_i * tile_j, z), bf16),),
        scratch=(
            pltpu.VMEM((groups * heads, groups * heads), f32),
            pltpu.VMEM((tile_i * tile_j, z), bf16),
            pltpu.SemaphoreType.DMA((groups // 4,)),
        ),
        far_out=(0,),
        flops=4_000_000_000,
        nbytes=3_000_000,
    )(pay0, *got, logits, gw, normal, inverse, score_matrix.T)

    (aligned,) = call(
        alignment_kernel,
        (sds((seqs * tokens, width), bf16),),
        scratch=(
            pltpu.VMEM((nk, heads, tokens, 2 * tile_j), f32),
            pltpu.VMEM((seqs * tokens, chans), bf16),
        ),
        smem=1,
        flops=3_000_000_000,
        nbytes=5_000_000,
    )(
        col_scalar,
        pay0,
        *got,
        values,
        gating,
        alignment_input.reshape(seqs * tokens, width),
        final_mixing_weights.T,
    )
    return (
        aligned.reshape(seqs, tokens, width),
        pair_out.reshape(tile_i, tile_j, z),
        gradient.reshape(tile_i, tile_j, z),
    )


def solution(mesh):
    counts = (mesh.shape["seq"], mesh.shape["row"], mesh.shape["col"])
    in_specs = (
        P("seq", ("row", "col"), None),
        P("row", "col", None),
        P(),
        P(),
        P(),
        P(),
        P(),
        P(),
        P(),
        P(),
        P("seq", ("row", "col"), None),
    )
    out_specs = (P("seq", ("row", "col"), None), P("row", "col", None), P("row", "col", None))
    return jax.shard_map(
        functools.partial(on_device, counts),
        mesh=mesh,
        in_specs=in_specs,
        out_specs=out_specs,
        check_vma=False,
    )
```

```python
import functools

import jax
import jax.numpy as jnp
from jax import lax
from jax.experimental import pallas as pl
from jax.experimental.pallas import tpu as pltpu
from jax.sharding import PartitionSpec as P

epsilon = 1e-05
far_below = -1e30
vmem_bytes = 32 * 1024 * 1024
pack = 4

f32 = jnp.float32
bf16 = jnp.bfloat16


def nt_dot(a, b):
    return lax.dot_general(a, b, (((1,), (1,)), ((), ())), preferred_element_type=f32)


def nn_dot(a, b):
    return jnp.dot(a, b, preferred_element_type=f32)


def high_low(x):
    high = x.astype(bf16)
    return high, (x - high.astype(f32)).astype(bf16)


def call(
    kernel, out_shape, scratch=(), smem=0, flops=0, nbytes=0, vmem=vmem_bytes, far=(), far_out=()
):
    def run(*args):
        count = len(args)
        in_specs = [
            pl.BlockSpec(memory_space=pltpu.SMEM if n < smem else pltpu.VMEM) for n in range(count)
        ]
        for n in far:
            in_specs[n] = pl.BlockSpec(memory_space=pltpu.HBM)
        landing = [pltpu.VMEM(args[n].shape, args[n].dtype) for n in far]
        if far:
            landing.append(pltpu.SemaphoreType.DMA((len(far),)))

        def body(*refs):
            inputs = list(refs[:count])
            extra = refs[len(refs) - len(landing) :]
            rest = refs[count : len(refs) - len(landing)]
            copies = []
            for i, n in enumerate(far):
                copies.append(pltpu.make_async_copy(inputs[n], extra[i], extra[-1].at[i]))
                copies[-1].start()
                inputs[n] = extra[i]

            def ready():
                for copy in copies:
                    copy.wait()

            kernel(ready, *inputs, *rest)

        return pl.pallas_call(
            body,
            out_shape=out_shape,
            in_specs=in_specs,
            out_specs=[
                pl.BlockSpec(memory_space=pltpu.HBM if n in far_out else pltpu.VMEM)
                for n in range(len(out_shape))
            ],
            scratch_shapes=list(scratch) + landing,
            compiler_params=pltpu.CompilerParams(vmem_limit_bytes=vmem),
            cost_estimate=pl.CostEstimate(flops=flops, bytes_accessed=nbytes, transcendentals=0),
        )(*args)

    return run


def valid_count(mask_ref):
    return jnp.sum(mask_ref[...].astype(f32), axis=1, keepdims=True)


def column_mask(mask_ref, col, tile, copies):
    lane = lax.broadcasted_iota(jnp.int32, (1, copies * tile), 1)
    token = (lax.rem(lane, tile) + col * tile).astype(f32)
    return (token < valid_count(mask_ref)).astype(f32)


def twice(w):
    none = jnp.zeros_like(w)
    return jnp.concatenate(
        [jnp.concatenate([w, none], axis=1), jnp.concatenate([none, w], axis=1)], axis=0
    )


def prepare_kernel(
    ready,
    own_ref,
    x_ref,
    adj_ref,
    w1_ref,
    w2_ref,
    mask_ref,
    wv_ref,
    wg_ref,
    wf_ref,
    shard_ref,
    rows_ref,
    left_ref,
    norm_ref,
    weights_ref,
    turn_ref,
    place_ref,
):
    chans = wv_ref.shape[1]
    weights_ref[:, :chans] = wv_ref[...]
    weights_ref[:, chans : 2 * chans] = wg_ref[...]
    weights_ref[:, 2 * chans :] = wf_ref[...]
    seqs, tokens, width = x_ref.shape
    half = seqs // 2
    fd = w2_ref.shape[0]
    x = x_ref[...].astype(f32)
    center = x - jnp.mean(x, axis=-1, keepdims=True)
    inverse = lax.rsqrt(jnp.mean(center * center, axis=-1, keepdims=True) + epsilon)
    normed = center * inverse
    rows = half * tokens
    adj = adj_ref[...].astype(f32)

    def two(x):
        x = jnp.concatenate([x[:half], x[half:]], axis=-1)
        return x.reshape(rows, 2 * width).astype(bf16)

    packed = two(normed)
    norm_ref[...] = packed
    base = tokens // pack * w1_ref.shape[0]
    shard_ref[base : base + rows, :] = two(adj)
    shard_ref[base + rows : base + 2 * rows, :] = packed
    token = lax.broadcasted_iota(jnp.int32, (seqs, tokens, width), 1) + own_ref[0]
    count = valid_count(mask_ref).reshape(1, 1, 1)
    real = jnp.where(token.astype(f32) < count, normed, 0.0)
    for s in range(seqs):
        turn_ref[:, s, :] = real[s]
    turned = turn_ref[...].astype(bf16).reshape(tokens * seqs, width)
    left = nt_dot(w1_ref[...], turned).astype(bf16)
    fc = w1_ref.shape[0]
    wk = pack * seqs
    for g in range(tokens // pack):
        shard_ref[g * fc : (g + 1) * fc, :] = left[:, g * wk : (g + 1) * wk]
    size = 128 // tokens
    real = real.astype(bf16)
    w2 = w2_ref[...]
    d = lax.broadcasted_iota(jnp.int32, (fd, 128), 0)
    lane = lax.broadcasted_iota(jnp.int32, (fd, 128), 1)
    mine = lax.rem(d, size) == lane // tokens
    for s in range(seqs):
        res = nt_dot(w2, jnp.concatenate([real[s]] * size, axis=0))
        res = jnp.where(mine, res, 0.0).reshape(fd // size, size, 128)
        place_ref[:, s, :] = jnp.sum(res, axis=1)
    right = place_ref[...].reshape(fd // size * seqs, 128).astype(bf16)
    rows_ref[...] = shard_ref[: base + 2 * rows, :]
    left_ref[...] = shard_ref[:base, :]
    shard_ref[base + 2 * rows :, :] = right


def join_left_kernel(ready, col_ref, rows0_ref, rows1_ref, rows2_ref, rows3_ref, out_ref):
    size = out_ref.shape[0] // 4
    for t, ref in enumerate((rows0_ref, rows1_ref, rows2_ref, rows3_ref)):
        at = pl.ds(pl.multiple_of(jnp.bitwise_xor(col_ref[0], t) * size, size), size)
        out_ref[at, :] = ref[:size, :]


def hand_on_kernel(ready, weights_ref, rows_ref, weights_out_ref, rows_out_ref):
    weights_out_ref[...] = weights_ref[...]
    rows_out_ref[...] = rows_ref[...]


def join_right_kernel(ready, row_ref, pair0_ref, pair1_ref, out_ref):
    size = out_ref.shape[0] // 4
    for t in range(4):
        ref = (pair0_ref, pair1_ref)[t // 2]
        at = pl.ds(pl.multiple_of(jnp.bitwise_xor(row_ref[0], t) * size, size), size)
        end = ref.shape[0] // 2 * (t % 2 + 1)
        out_ref[at, :] = ref[end - size : end, :]


def update_kernel(
    ready,
    col_ref,
    seq_ref,
    left_ref,
    right_ref,
    far_left_ref,
    far_right_ref,
    mask_ref,
    m_ref,
    score_ref,
    pair_ref,
    pout_hbm,
    normal_ref,
    inverse_ref,
    logits_ref,
    pout_ref,
    out_sem,
    rk_ref,
    rab_ref,
    lm_ref,
    mt_ref,
    oh_ref,
    ol_ref,
    update0_ref,
    update1_ref,
):
    nk = rk_ref.shape[0]
    width_d, pair_rows, _ = rab_ref.shape
    col, seq = col_ref[0], seq_ref[0]
    z = pair_ref.shape[1]
    groups, heads, lanes = logits_ref.shape
    tile_j = lanes // pack
    tokens = tile_j // nk
    fc = lm_ref.shape[0] // groups
    seqs = 128 // pack
    nq = pair_rows // seqs
    wk = pack * seqs

    r_rows = rk_ref.shape[1] // nq
    l_rows = groups * fc
    if nq == 2:
        sources = ((seq, 0, left_ref, right_ref), (1 - seq, 0, far_left_ref, far_right_ref))
    else:
        sources = tuple((q, q, far_left_ref, far_right_ref) for q in range(nq))
    for q, slot, from_left, from_right in sources:
        at = pl.ds(pl.multiple_of(q * r_rows, r_rows), r_rows)
        for k in range(nk):
            first = (slot * nk + k) * r_rows
            rk_ref[k, at, :] = from_right[first : first + r_rows, :]
        to = pl.ds(pl.multiple_of(q * wk, wk), wk)
        lm_ref[:, to] = from_left[slot * l_rows : (slot + 1) * l_rows, :]
    size = 128 // tokens
    right = jnp.concatenate([rk_ref[k] for k in range(nk)], axis=1)
    source = lax.broadcasted_iota(jnp.int32, (nk * 128, 4 * tile_j), 0)
    target = lax.broadcasted_iota(jnp.int32, (nk * 128, 4 * tile_j), 1)
    used = jnp.logical_or(target < tile_j, target >= 3 * tile_j)
    j = lax.rem(target, tile_j)
    offset = jnp.where(used, source - (j // tokens * 128 + lax.rem(j, tokens)), -1)
    blocks = width_d // size
    for e in range(size):
        pick = jnp.where(offset == e * tokens, 1.0, 0.0).astype(bf16)
        res = nn_dot(right, pick).astype(bf16)
        for q in range(nq):
            for n in range(blocks):
                at = (q * blocks + n) * seqs
                rab_ref[n * size + e, q * seqs : (q + 1) * seqs, :] = res[at : at + seqs]

    chunk = 8
    many = 4
    wide = oh_ref.shape[2] // lanes
    empty = jnp.zeros((seqs, 2 * tile_j), bf16)

    def block_of(d):
        rows = []
        for q in range(nq):
            both = rab_ref[d, q * seqs : (q + 1) * seqs, :]
            part = both[:, : 2 * tile_j], both[:, 2 * tile_j :]
            for i in range(pack):
                pieces = [empty] * (pack // 2)
                pieces[i // 2] = part[i % 2]
                rows.append(jnp.concatenate(pieces, axis=1))
        return jnp.concatenate(rows, axis=0)

    def outer_of(n):
        block = jnp.concatenate([block_of(many * n + e) for e in range(many)], axis=1)
        for m in range(groups // chunk):
            out = nn_dot(lm_ref[m * chunk * fc : (m + 1) * chunk * fc, :], block)
            high, low = high_low(out)
            for e in range(many):
                at = slice((many * n + e) * fc, (many * n + e + 1) * fc)
                for g in range(chunk):
                    group = m * chunk + g
                    to = slice(group % wide * lanes, (group % wide + 1) * lanes)
                    cut = slice(g * fc, (g + 1) * fc), slice(e * lanes, (e + 1) * lanes)
                    oh_ref[group // wide, at, to] = high[cut]
                    ol_ref[group // wide, at, to] = low[cut]

    for n in range(width_d // many):
        outer_of(n)

    ready()
    some = z // fc
    for n in range(width_d // some):
        block = jnp.concatenate(
            [m_ref[pl.ds(n * some + e, fc, stride=width_d), :] for e in range(some)], axis=0
        ).T
        high, low = high_low(block)
        mt_ref[:z, n * z : (n + 1) * z] = high
        mt_ref[z:, n * z : (n + 1) * z] = low
    maskj = column_mask(mask_ref, col, tile_j, 2)

    maskl = jnp.concatenate([maskj] * (pack // 2), axis=1) > 0
    score = score_ref[...]
    s1 = score.astype(bf16).astype(f32)
    s2 = (score - s1).astype(bf16).astype(f32)
    s3 = score - s1 - s2
    none = jnp.zeros_like(s1)
    st = jnp.concatenate(
        [
            jnp.concatenate([s1, s2, s3, none], axis=0),
            jnp.concatenate([s1, s2, none, none], axis=0),
        ],
        axis=1,
    ).astype(bf16)

    def product(n):
        two = nn_dot(mt_ref[...], oh_ref[n])
        update_refs[n % 2][...] = two[:z] + two[z:] + nn_dot(mt_ref[:z, :], ol_ref[n])

    def finish(n):
        for e in range(wide):
            g = n * wide + e
            at = slice(g * lanes, (g + 1) * lanes)
            before = pair_ref[at, :].T.astype(f32)
            update = update_refs[n % 2][:, e * lanes : (e + 1) * lanes]
            result = (before + update).astype(bf16)
            x = result.astype(f32)
            pout_ref[at, :] = result.T
            center = x - jnp.mean(x, axis=0, keepdims=True)
            inverse = lax.rsqrt(jnp.mean(center * center, axis=0, keepdims=True) + epsilon)
            normal = center * inverse
            normal_ref[g] = normal
            inverse_ref[g] = jnp.broadcast_to(inverse, inverse_ref.shape[1:])
            high, low = high_low(normal)
            scores = nn_dot(st, jnp.concatenate([high, low], axis=0))
            logits = scores[:heads] + scores[heads : 2 * heads] + scores[2 * heads : 3 * heads]
            logits_ref[g] = jnp.where(maskl, logits, far_below)

    steps = groups // wide
    update_refs = (update0_ref, update1_ref)
    copies = []
    for n in range(steps + 1):
        if n < steps:
            product(n)
        if n > 0:
            finish(n - 1)
            at = pl.ds((n - 1) * wide * lanes, wide * lanes)
            part = pltpu.make_async_copy(pout_ref.at[at], pout_hbm.at[at], out_sem.at[n - 1])
            part.start()
            copies.append(part)
    for copy in copies:
        copy.wait()


def by_heads(w, heads, out_ref):
    width, chans = w.shape
    hw = chans // heads
    block = 4 * hw
    slot = lax.broadcasted_iota(jnp.int32, (width, block), 1) // hw
    w = w.astype(f32)
    for t in range(chans // block):
        part = w[:, t * block : (t + 1) * block]
        turns = [part] + [pltpu.roll(part, n * hw, 1) for n in range(1, 4)]
        for e in range(4):
            h = t * 4 + e
            for s in range(4):
                out_ref[s * width : (s + 1) * width, h * block : (h + 1) * block] = jnp.where(
                    slot == s, turns[(s - e) % 4], 0.0
                ).astype(bf16)


def weights_kernel(
    ready,
    row_ref,
    col_ref,
    side0_ref,
    side1_ref,
    side2_ref,
    side3_ref,
    cols0_ref,
    cols1_ref,
    weights_ref,
    gw_ref,
    cols_ref,
    acc_ref,
    bv_ref,
    bg_ref,
    bf_ref,
    rows_ref,
    gs_ref,
    vs_ref,
):
    nk, half, tokens, _ = cols_ref.shape
    tile = nk * tokens
    groups, heads, lanes = gw_ref.shape
    row, col = row_ref[0], col_ref[0]
    count = half * tokens
    size = side0_ref.shape[0] - 2 * count
    for t, ref in enumerate((side0_ref, side1_ref, side2_ref, side3_ref)):
        k = jnp.bitwise_xor(col, t)
        rows_ref[k] = ref[size : size + 2 * count, :].reshape(rows_ref.shape[1:])
    for t in range(nk):
        ref = (cols0_ref, cols1_ref)[t // 2]
        start = ref.shape[0] // 2 * (t % 2)
        part = ref[start : start + count, :]
        cols_ref[jnp.bitwise_xor(row, t)] = part.reshape(cols_ref.shape[1:])
    chans = weights_ref.shape[1] // 3
    by_heads(weights_ref[:, :chans], heads, bv_ref)
    by_heads(weights_ref[:, chans : 2 * chans], heads, bg_ref)
    by_heads(weights_ref[:, 2 * chans :], heads, bf_ref)
    block = bv_ref.shape[1] // heads

    def four(read, n):
        return jnp.concatenate(
            [
                jnp.concatenate(
                    [
                        jnp.concatenate([read(k, 2 * (2 * n + e) + p) for k in range(nk)], axis=0)
                        for p in range(2)
                    ],
                    axis=1,
                )
                for e in range(2)
            ],
            axis=0,
        )

    for hp in range(heads // 2):
        cut = slice(hp * 2 * block, (hp + 1) * 2 * block)
        for n in range(half // 4):
            v = nn_dot(four(lambda k, s: cols_ref[k, s], n), bv_ref[:, cut]).astype(bf16)
            gate = nn_dot(four(lambda k, s: rows_ref[k, 1, s], n), bg_ref[:, cut])
            grad = nn_dot(four(lambda k, s: rows_ref[k, 0, s], n), bf_ref[:, cut])
            g = (grad * jax.nn.sigmoid(gate)).astype(bf16)
            for e in range(2):
                to = slice((2 * n + e) * block, (2 * n + e + 1) * block)
                for o in range(2):
                    mine = slice(o * block, (o + 1) * block)
                    ve = v[e * tile : (e + 1) * tile, mine]
                    vs_ref[2 * hp + o, :tile, to] = ve
                    vs_ref[2 * hp + o, tile:, to] = ve
                    gs_ref[2 * hp + o, :, to] = g[e * tile : (e + 1) * tile, mine]
    for h in range(heads):
        acc_ref[h * tile : (h + 1) * tile, :] = nt_dot(gs_ref[h], vs_ref[h])

    first = lax.broadcasted_iota(jnp.int32, (groups, 2 * tile), 1) < tile
    for h in range(heads):
        for part in range(pack // 2):
            a = acc_ref[pl.ds(h * tile + 2 * part, groups, stride=pack), :]
            b = acc_ref[pl.ds(h * tile + 2 * part + 1, groups, stride=pack), :]
            gw_ref[:, h, part * 2 * tile : (part + 1) * 2 * tile] = jnp.where(first, a, b)


def softmax_kernel(
    ready,
    col_ref,
    logits_ref,
    gwa_ref,
    gwb_ref,
    mask_ref,
    gw_ref,
    own_ref,
    pay1_ref,
    pay2_ref,
    pay3_ref,
):
    groups, heads, lanes = logits_ref.shape
    tile = lanes // pack
    nk = 4
    rows = groups * heads
    col = col_ref[0]
    gw_ref[...] = gwa_ref[...] + gwb_ref[...]
    lane = lax.broadcasted_iota(jnp.int32, (rows, 2 * tile), 1)
    low = lane < tile
    maskj = column_mask(mask_ref, col, tile, 2)
    stats = jnp.zeros((rows, 2 * tile), f32)
    for part in range(pack // 2):
        cut = slice(part * 2 * tile, (part + 1) * 2 * tile)
        lg = logits_ref[:, :, cut].reshape(rows, 2 * tile)
        gw = gw_ref[:, :, cut].reshape(rows, 2 * tile)
        m0 = jnp.max(jnp.where(low, lg, far_below), axis=1, keepdims=True)
        m1 = jnp.max(jnp.where(low, far_below, lg), axis=1, keepdims=True)
        p = jnp.exp(lg - jnp.where(low, m0, m1)) * maskj
        pg = p * gw
        for e, m in ((0, m0), (1, m1)):
            mine = low if e == 0 else jnp.logical_not(low)
            i = 2 * part + e
            total = jnp.sum(jnp.where(mine, p, 0.0), axis=1, keepdims=True)
            inner = jnp.sum(jnp.where(mine, pg, 0.0), axis=1, keepdims=True)
            stats = jnp.where(lane == i, m, stats)
            stats = jnp.where(lane == pack + i, total, stats)
            stats = jnp.where(lane == 2 * pack + i, inner, stats)
    turned = stats.T[:16]
    per = groups // nk
    for shift, pay in enumerate((own_ref, pay1_ref, pay2_ref, pay3_ref)):
        dest = lax.rem(col + shift, nk)
        pay[0] = turned[:8]
        pay[1] = turned[8:]
        for g in range(per):
            piece = logits_ref[dest * per + g]
            for part in range(pack // 2):
                pay[2 + g * (pack // 2) + part] = piece[:, part * 2 * tile : (part + 1) * 2 * tile]


def values_kernel(
    ready, col_ref, ev0_ref, ev1_ref, ev2_ref, ev3_ref, wv_ref, norm_ref, wg_ref, v_ref, gate_ref, ev_ref
):
    nr, nk, half, tokens, wide = ev_ref.shape
    chans = wv_ref.shape[1]
    for t, ref in enumerate((ev0_ref, ev1_ref, ev2_ref, ev3_ref)):
        ev_ref[jnp.bitwise_xor(col_ref[0], t)] = ref[...]
    gate = jax.nn.sigmoid(nn_dot(norm_ref[...], twice(wg_ref[...])))
    gate_ref[: half * tokens] = gate[:, :chans]
    gate_ref[half * tokens :] = gate[:, chans:]
    wv = twice(wv_ref[...])
    for s in range(half):
        x = jnp.concatenate([ev_ref[r, k, s] for r in range(nr) for k in range(nk)], axis=0)
        v_ref[s] = nn_dot(x, wv).astype(bf16)


def gradient_kernel(
    ready,
    own_ref, r1_ref, r2_ref, r3_ref, logits_ref, gw_ref, normal_ref, inverse_ref, score_ref, out_hbm, stat_ref, out_ref, out_sem
):
    groups, heads, lanes = logits_ref.shape
    rows = groups * heads
    score = score_ref[...]
    z = score.shape[1]
    s1 = score.astype(bf16).astype(f32)
    s2 = (score - s1).astype(bf16).astype(f32)
    s3 = score - s1 - s2
    parts = [s1, s1, s1, s2, s2, s3, jnp.zeros((z - 6 * heads, z), f32)]
    sk = jnp.concatenate(parts, axis=0).T[:, : 6 * heads].astype(bf16)
    pays = (own_ref, r1_ref, r2_ref, r3_ref)
    ms = [p[0][:pack] for p in pays]
    ls = [p[0][pack : 2 * pack] for p in pays]
    ns = [p[1][:pack] for p in pays]
    top = functools.reduce(jnp.maximum, ms)
    scales = [jnp.exp(m - top) for m in ms]
    total = sum(a * b for a, b in zip(ls, scales))
    inner = sum(a * b for a, b in zip(ns, scales)) / total
    stacked = jnp.concatenate([top, total, inner, jnp.zeros((rows - 3 * pack, rows), f32)], axis=0)
    stat_ref[...] = stacked.T

    tile = lanes // pack
    low = lax.broadcasted_iota(jnp.int32, (heads, 2 * tile), 1) < tile

    def one(g):
        st = stat_ref[g * heads : (g + 1) * heads, :]

        def spread(base):
            halves = [
                jnp.where(
                    low,
                    st[:, base + 2 * half : base + 2 * half + 1],
                    st[:, base + 2 * half + 1 : base + 2 * half + 2],
                )
                for half in range(pack // 2)
            ]
            return jnp.concatenate(halves, axis=1)

        prob = jnp.exp(logits_ref[g] - spread(0)) / spread(pack)
        gl = prob * (gw_ref[g] - spread(2 * pack))
        g1 = gl.astype(bf16).astype(f32)
        g2 = (gl - g1).astype(bf16).astype(f32)
        g3 = gl - g1 - g2
        stack = jnp.concatenate([g1, g2, g3, g1, g2, g1], axis=0).astype(bf16)
        grad = nn_dot(sk, stack)
        normal = normal_ref[g]
        inverse = inverse_ref[g][:1]
        centered = grad - jnp.mean(grad, axis=0, keepdims=True)
        along = jnp.mean(grad * normal, axis=0, keepdims=True)
        result = inverse * (centered - normal * along)
        out_ref[g * lanes : (g + 1) * lanes, :] = result.astype(bf16).T

    many = 4

    copies = []
    for n in range(groups // many):
        for e in range(many):
            one(n * many + e)
        at = pl.ds(n * many * lanes, many * lanes)
        part = pltpu.make_async_copy(out_ref.at[at], out_hbm.at[at], out_sem.at[n])
        part.start()
        copies.append(part)
    for copy in copies:
        copy.wait()


def alignment_kernel(
    ready,
    col_ref,
    own_ref,
    r1_ref,
    r2_ref,
    r3_ref,
    v_ref,
    gate_ref,
    x_ref,
    wf_ref,
    out_ref,
    w_ref,
    gated_ref,
):
    pays = (own_ref, r1_ref, r2_ref, r3_ref)
    nk = len(pays)
    heads = own_ref.shape[1]
    wide = own_ref.shape[2]
    tile = wide // 2
    pieces = own_ref.shape[0] - 2
    rows = pieces * heads
    half, all_tokens, chans = v_ref.shape
    chans = chans // 2
    tokens = pieces * 2
    head_width = chans // heads
    col = col_ref[0]

    low = lax.broadcasted_iota(jnp.int32, (rows, wide), 1) < tile
    lgs = [p[2:].reshape(rows, wide) for p in pays]
    peak = functools.reduce(jnp.maximum, lgs)
    m0 = jnp.max(jnp.where(low, peak, far_below), axis=1, keepdims=True)
    m1 = jnp.max(jnp.where(low, far_below, peak), axis=1, keepdims=True)
    top = jnp.where(low, m0, m1)
    ps = [jnp.exp(lg - top) for lg in lgs]
    every = sum(ps)
    t0 = jnp.sum(jnp.where(low, every, 0.0), axis=1, keepdims=True)
    t1 = jnp.sum(jnp.where(low, 0.0, every), axis=1, keepdims=True)
    total = jnp.where(low, t0, t1)
    for shift, p in enumerate(ps):
        source = lax.rem(col + nk - shift, nk)
        weight = p / total
        rolled = pltpu.roll(weight, tile, 1)
        for n in range(pieces):
            w_ref[source, :, 2 * n, :] = weight[n * heads : (n + 1) * heads]
            w_ref[source, :, 2 * n + 1, :] = rolled[n * heads : (n + 1) * heads]
    w = jnp.concatenate(
        [
            w_ref[k].reshape(heads * tokens, wide)[:, :tile]
            for k in range(nk)
        ],
        axis=1,
    ).astype(bf16)

    owner = lax.broadcasted_iota(jnp.int32, (tokens, chans), 1) // head_width

    def one(s, carry):
        full = nn_dot(w, v_ref[s])
        for e in range(2):
            cut = slice(e * chans, (e + 1) * chans)
            mean = jnp.zeros((tokens, chans), f32)
            for h in range(heads):
                mean = jnp.where(owner == h, full[h * tokens : (h + 1) * tokens, cut], mean)
            at = pl.ds(pl.multiple_of((e * half + s) * tokens, tokens), tokens)
            gated_ref[at, :] = (gate_ref[at, :] * mean).astype(bf16)
        return carry

    lax.fori_loop(0, half, one, 0, unroll=8)
    out_ref[...] = (x_ref[...].astype(f32) + nt_dot(gated_ref[...], wf_ref[...])).astype(bf16)


def on_device(
    counts,
    alignment_input,
    pair_input,
    token_valid_mask,
    first_factor_weights,
    second_factor_weights,
    content_weights_grid,
    sigmoid_weights_grid,
    outer_matrix,
    score_matrix,
    final_mixing_weights,
    adjoint_of_rowset,
):
    nq, nr, nk = counts
    row_index = lax.axis_index("row")
    col_index = lax.axis_index("col")
    seqs, tokens, width = alignment_input.shape
    tile_i, tile_j, z = pair_input.shape
    fc = first_factor_weights.shape[1]
    fd = second_factor_weights.shape[1]
    heads = score_matrix.shape[1]
    chans = content_weights_grid.shape[1]
    groups = tile_i // pack
    lanes = pack * tile_j
    sds = jax.ShapeDtypeStruct

    mask = token_valid_mask.reshape(1, -1)
    own_start = ((row_index * nk + col_index) * tokens).astype(jnp.int32).reshape(1)
    seq_index = lax.axis_index("seq")
    place = tuple(x.astype(jnp.int32).reshape(1) for x in (row_index, col_index, seq_index))
    col_scalar = col_index.astype(jnp.int32).reshape(1)
    half = seqs // 2

    l_rows = tokens // pack * fc
    r_rows = fd * tokens // 128 * seqs
    n_rows = half * tokens
    shard, rows, own_left, normed, weights = call(
        prepare_kernel,
        (
            sds((l_rows + 2 * n_rows + r_rows, 128), bf16),
            sds((l_rows + 2 * n_rows, 128), bf16),
            sds((l_rows, 128), bf16),
            sds((n_rows, 128), bf16),
            sds((width, 3 * chans), bf16),
        ),
        scratch=(
            pltpu.VMEM((tokens, seqs, width), f32),
            pltpu.VMEM((fd * tokens // 128, seqs, 128), f32),
        ),
        smem=1,
        vmem=60 * 1024 * 1024,
    )(
        own_start,
        alignment_input,
        adjoint_of_rowset,
        first_factor_weights.T,
        second_factor_weights.T,
        mask,
        content_weights_grid,
        sigmoid_weights_grid,
        final_mixing_weights.T,
    )

    def exchange(x, bit):
        return lax.ppermute(x, "col", [(c, c ^ bit) for c in range(nk)])

    other = exchange(shard, 1)
    across = exchange(rows, 2)
    pair = jnp.concatenate([x[l_rows + n_rows :] for x in (shard, other)], axis=0)
    all_cols = [
        lax.ppermute(
            pair,
            ("row", "col"),
            [(r * nk + c, (c ^ flip) * nk + r) for r in range(nr) for c in range(nk)],
        )
        for flip in (0, 2)
    ]

    def over_seq(x):
        if nq == 2:
            return lax.ppermute(x, "seq", [(0, 1), (1, 0)])
        return lax.all_gather(x, "seq", axis=0, tiled=True)

    lefts = [own_left, other, across, exchange(own_left, 3)]
    (left,) = call(join_left_kernel, (sds((nk * l_rows, 128), bf16),), smem=1)(place[1], *lefts)
    far_left = over_seq(left)
    weights, own = call(hand_on_kernel, (sds(weights.shape, bf16), sds(rows.shape, bf16)))(
        weights, rows
    )
    across, far_left, weights, own, *all_cols = lax.optimization_barrier(
        (across, far_left, weights, own, *all_cols)
    )
    all_rows = [own, other, across, exchange(across, 1)]

    (right,) = call(join_right_kernel, (sds((nk * r_rows, 128), bf16),), smem=1)(
        place[0], *all_cols
    )
    far_right = over_seq(right)

    head_lanes = seqs * chans // heads
    gw_own, block = call(
        weights_kernel,
        (
            sds((groups, heads, lanes), f32),
            sds((nk, half, tokens, 2 * width), bf16),
        ),
        scratch=(
            pltpu.VMEM((heads * tile_i, 2 * tile_j), f32),
            pltpu.VMEM((4 * width, 4 * chans), bf16),
            pltpu.VMEM((4 * width, 4 * chans), bf16),
            pltpu.VMEM((4 * width, 4 * chans), bf16),
            pltpu.VMEM((nk, 2, half, tokens, 2 * width), bf16),
            pltpu.VMEM((heads, tile_i, head_lanes), bf16),
            pltpu.VMEM((heads, 2 * tile_j, head_lanes), bf16),
        ),
        smem=2,
        flops=3_000_000_000,
        nbytes=3_000_000,
    )(*place[:2], *all_rows, *all_cols, weights)
    if nq == 2:
        gw_other = lax.ppermute(gw_own, "seq", [(0, 1), (1, 0)])
    else:
        gw_own, gw_other = lax.psum(gw_own, "seq"), jnp.zeros_like(gw_own)

    close, remote = exchange(block, 1), exchange(block, 2)

    pair_out, normal, inverse, logits = call(
        update_kernel,
        (
            sds((tile_i * tile_j, z), bf16),
            sds((groups, z, lanes), f32),
            sds((groups, 8, lanes), f32),
            sds((groups, heads, lanes), f32),
        ),
        scratch=(
            pltpu.VMEM((tile_i * tile_j, z), bf16),
            pltpu.SemaphoreType.DMA((groups // 4,)),
            pltpu.VMEM((nk, nq * r_rows, 128), bf16),
            pltpu.VMEM((fd, nq * seqs, 4 * tile_j), bf16),
            pltpu.VMEM((groups * fc, nq * pack * seqs), bf16),
            pltpu.VMEM((2 * z, fd * fc), bf16),
            pltpu.VMEM((groups // 4, fd * fc, 4 * lanes), bf16),
            pltpu.VMEM((groups // 4, fd * fc, 4 * lanes), bf16),
            pltpu.VMEM((z, 4 * lanes), f32),
            pltpu.VMEM((z, 4 * lanes), f32),
        ),
        smem=2,
        flops=14_000_000_000,
        nbytes=5_000_000,
        vmem=44 * 1024 * 1024,
        far=(6, 7, 8, 9),
        far_out=(0,),
    )(
        *place[1:],
        left,
        right,
        far_left,
        far_right,
        mask,
        outer_matrix,
        score_matrix.T,
        pair_input.reshape(tile_i * tile_j, z),
    )

    payload = sds((2 + groups // nk * (pack // 2), heads, 2 * tile_j), f32)
    gw, pay0, pay1, pay2, pay3 = call(
        softmax_kernel,
        (sds((groups, heads, lanes), f32), payload, payload, payload, payload),
        smem=1,
    )(col_scalar, logits, gw_own, gw_other, mask)

    got = [
        lax.ppermute(pay, "col", [(c, (c + shift) % nk) for c in range(nk)])
        for shift, pay in ((1, pay1), (2, pay2), (3, pay3))
    ]


    close, remote, pay0 = lax.optimization_barrier((close, remote, pay0))
    every = [block, close, remote, exchange(remote, 1)]
    values, gating = call(
        values_kernel,
        (sds((half, nr * nk * tokens, 2 * chans), bf16), sds((seqs * tokens, chans), f32)),
        scratch=(pltpu.VMEM((nr, nk, half, tokens, 2 * width), bf16),),
        smem=1,
        flops=4_000_000_000,
        nbytes=6_000_000,
    )(col_scalar, *every, content_weights_grid, normed, sigmoid_weights_grid)

    got, values, gating = lax.optimization_barrier((got, values, gating))

    (gradient,) = call(
        gradient_kernel,
        (sds((tile_i * tile_j, z), bf16),),
        scratch=(
            pltpu.VMEM((groups * heads, groups * heads), f32),
            pltpu.VMEM((tile_i * tile_j, z), bf16),
            pltpu.SemaphoreType.DMA((groups // 4,)),
        ),
        far_out=(0,),
        flops=4_000_000_000,
        nbytes=3_000_000,
    )(pay0, *got, logits, gw, normal, inverse, score_matrix.T)

    (aligned,) = call(
        alignment_kernel,
        (sds((seqs * tokens, width), bf16),),
        scratch=(
            pltpu.VMEM((nk, heads, tokens, 2 * tile_j), f32),
            pltpu.VMEM((seqs * tokens, chans), bf16),
        ),
        smem=1,
        flops=3_000_000_000,
        nbytes=5_000_000,
    )(
        col_scalar,
        pay0,
        *got,
        values,
        gating,
        alignment_input.reshape(seqs * tokens, width),
        final_mixing_weights.T,
    )
    return (
        aligned.reshape(seqs, tokens, width),
        pair_out.reshape(tile_i, tile_j, z),
        gradient.reshape(tile_i, tile_j, z),
    )


def solution(mesh):
    counts = (mesh.shape["seq"], mesh.shape["row"], mesh.shape["col"])
    in_specs = (
        P("seq", ("row", "col"), None),
        P("row", "col", None),
        P(),
        P(),
        P(),
        P(),
        P(),
        P(),
        P(),
        P(),
        P("seq", ("row", "col"), None),
    )
    out_specs = (P("seq", ("row", "col"), None), P("row", "col", None), P("row", "col", None))
    return jax.shard_map(
        functools.partial(on_device, counts),
        mesh=mesh,
        in_specs=in_specs,
        out_specs=out_specs,
        check_vma=False,
    )
```

```python
import functools

import jax
import jax.numpy as jnp
from jax import lax
from jax.experimental import pallas as pl
from jax.experimental.pallas import tpu as pltpu
from jax.sharding import PartitionSpec as P

epsilon = 1e-05
far_below = -1e30
vmem_bytes = 32 * 1024 * 1024
pack = 4

f32 = jnp.float32
bf16 = jnp.bfloat16


def nt_dot(a, b):
    return lax.dot_general(a, b, (((1,), (1,)), ((), ())), preferred_element_type=f32)


def nn_dot(a, b):
    return jnp.dot(a, b, preferred_element_type=f32)


def high_low(x):
    high = x.astype(bf16)
    return high, (x - high.astype(f32)).astype(bf16)


def call(
    kernel, out_shape, scratch=(), smem=0, flops=0, nbytes=0, vmem=vmem_bytes, far=(), far_out=()
):
    def run(*args):
        count = len(args)
        in_specs = [
            pl.BlockSpec(memory_space=pltpu.SMEM if n < smem else pltpu.VMEM) for n in range(count)
        ]
        for n in far:
            in_specs[n] = pl.BlockSpec(memory_space=pltpu.HBM)
        landing = [pltpu.VMEM(args[n].shape, args[n].dtype) for n in far]
        if far:
            landing.append(pltpu.SemaphoreType.DMA((len(far),)))

        def body(*refs):
            inputs = list(refs[:count])
            extra = refs[len(refs) - len(landing) :]
            rest = refs[count : len(refs) - len(landing)]
            copies = []
            for i, n in enumerate(far):
                copies.append(pltpu.make_async_copy(inputs[n], extra[i], extra[-1].at[i]))
                copies[-1].start()
                inputs[n] = extra[i]

            def ready():
                for copy in copies:
                    copy.wait()

            kernel(ready, *inputs, *rest)

        return pl.pallas_call(
            body,
            out_shape=out_shape,
            in_specs=in_specs,
            out_specs=[
                pl.BlockSpec(memory_space=pltpu.HBM if n in far_out else pltpu.VMEM)
                for n in range(len(out_shape))
            ],
            scratch_shapes=list(scratch) + landing,
            compiler_params=pltpu.CompilerParams(vmem_limit_bytes=vmem),
            cost_estimate=pl.CostEstimate(flops=flops, bytes_accessed=nbytes, transcendentals=0),
        )(*args)

    return run


def valid_count(mask_ref):
    return jnp.sum(mask_ref[...].astype(f32), axis=1, keepdims=True)


def column_mask(mask_ref, col, tile, copies):
    lane = lax.broadcasted_iota(jnp.int32, (1, copies * tile), 1)
    token = (lax.rem(lane, tile) + col * tile).astype(f32)
    return (token < valid_count(mask_ref)).astype(f32)


def twice(w):
    none = jnp.zeros_like(w)
    return jnp.concatenate(
        [jnp.concatenate([w, none], axis=1), jnp.concatenate([none, w], axis=1)], axis=0
    )


def prepare_kernel(
    ready,
    own_ref,
    x_ref,
    adj_ref,
    w1_ref,
    w2_ref,
    mask_ref,
    wv_ref,
    wg_ref,
    wf_ref,
    shard_ref,
    rows_ref,
    left_ref,
    norm_ref,
    weights_ref,
    turn_ref,
    place_ref,
):
    chans = wv_ref.shape[1]
    weights_ref[:, :chans] = wv_ref[...]
    weights_ref[:, chans : 2 * chans] = wg_ref[...]
    weights_ref[:, 2 * chans :] = wf_ref[...]
    seqs, tokens, width = x_ref.shape
    half = seqs // 2
    fd = w2_ref.shape[0]
    x = x_ref[...].astype(f32)
    center = x - jnp.mean(x, axis=-1, keepdims=True)
    inverse = lax.rsqrt(jnp.mean(center * center, axis=-1, keepdims=True) + epsilon)
    normed = center * inverse
    rows = half * tokens
    adj = adj_ref[...].astype(f32)

    def two(x):
        x = jnp.concatenate([x[:half], x[half:]], axis=-1)
        return x.reshape(rows, 2 * width).astype(bf16)

    packed = two(normed)
    norm_ref[...] = packed
    base = tokens // pack * w1_ref.shape[0]
    shard_ref[base : base + rows, :] = two(adj)
    shard_ref[base + rows : base + 2 * rows, :] = packed
    token = lax.broadcasted_iota(jnp.int32, (seqs, tokens, width), 1) + own_ref[0]
    count = valid_count(mask_ref).reshape(1, 1, 1)
    real = jnp.where(token.astype(f32) < count, normed, 0.0)
    for s in range(seqs):
        turn_ref[:, s, :] = real[s]
    turned = turn_ref[...].astype(bf16).reshape(tokens * seqs, width)
    left = nt_dot(w1_ref[...], turned).astype(bf16)
    fc = w1_ref.shape[0]
    wk = pack * seqs
    for g in range(tokens // pack):
        shard_ref[g * fc : (g + 1) * fc, :] = left[:, g * wk : (g + 1) * wk]
    size = 128 // tokens
    real = real.astype(bf16)
    w2 = w2_ref[...]
    d = lax.broadcasted_iota(jnp.int32, (fd, 128), 0)
    lane = lax.broadcasted_iota(jnp.int32, (fd, 128), 1)
    mine = lax.rem(d, size) == lane // tokens
    for s in range(seqs):
        res = nt_dot(w2, jnp.concatenate([real[s]] * size, axis=0))
        res = jnp.where(mine, res, 0.0).reshape(fd // size, size, 128)
        place_ref[:, s, :] = jnp.sum(res, axis=1)
    right = place_ref[...].reshape(fd // size * seqs, 128).astype(bf16)
    rows_ref[...] = shard_ref[: base + 2 * rows, :]
    left_ref[...] = shard_ref[:base, :]
    shard_ref[base + 2 * rows :, :] = right


def join_left_kernel(ready, col_ref, rows0_ref, rows1_ref, rows2_ref, rows3_ref, out_ref):
    size = out_ref.shape[0] // 4
    for t, ref in enumerate((rows0_ref, rows1_ref, rows2_ref, rows3_ref)):
        at = pl.ds(pl.multiple_of(jnp.bitwise_xor(col_ref[0], t) * size, size), size)
        out_ref[at, :] = ref[:size, :]


def hand_on_kernel(ready, weights_ref, rows_ref, weights_out_ref, rows_out_ref):
    weights_out_ref[...] = weights_ref[...]
    rows_out_ref[...] = rows_ref[...]


def join_right_kernel(ready, row_ref, pair0_ref, pair1_ref, out_ref):
    size = out_ref.shape[0] // 4
    for t in range(4):
        ref = (pair0_ref, pair1_ref)[t // 2]
        at = pl.ds(pl.multiple_of(jnp.bitwise_xor(row_ref[0], t) * size, size), size)
        end = ref.shape[0] // 2 * (t % 2 + 1)
        out_ref[at, :] = ref[end - size : end, :]


def update_kernel(
    ready,
    col_ref,
    seq_ref,
    left_ref,
    right_ref,
    far_left_ref,
    far_right_ref,
    mask_ref,
    m_ref,
    score_ref,
    pair_ref,
    pout_hbm,
    normal_ref,
    inverse_ref,
    logits_ref,
    pout_ref,
    out_sem,
    rk_ref,
    rab_ref,
    lm_ref,
    mt_ref,
    oh_ref,
    ol_ref,
    update0_ref,
    update1_ref,
):
    nk = rk_ref.shape[0]
    width_d, pair_rows, _ = rab_ref.shape
    col, seq = col_ref[0], seq_ref[0]
    z = pair_ref.shape[1]
    groups, heads, lanes = logits_ref.shape
    tile_j = lanes // pack
    tokens = tile_j // nk
    fc = lm_ref.shape[0] // groups
    seqs = 128 // pack
    nq = pair_rows // seqs
    wk = pack * seqs

    r_rows = rk_ref.shape[1] // nq
    l_rows = groups * fc
    if nq == 2:
        sources = ((seq, 0, left_ref, right_ref), (1 - seq, 0, far_left_ref, far_right_ref))
    else:
        sources = tuple((q, q, far_left_ref, far_right_ref) for q in range(nq))
    for q, slot, from_left, from_right in sources:
        at = pl.ds(pl.multiple_of(q * r_rows, r_rows), r_rows)
        for k in range(nk):
            first = (slot * nk + k) * r_rows
            rk_ref[k, at, :] = from_right[first : first + r_rows, :]
        to = pl.ds(pl.multiple_of(q * wk, wk), wk)
        lm_ref[:, to] = from_left[slot * l_rows : (slot + 1) * l_rows, :]
    size = 128 // tokens
    right = jnp.concatenate([rk_ref[k] for k in range(nk)], axis=1)
    source = lax.broadcasted_iota(jnp.int32, (nk * 128, 4 * tile_j), 0)
    target = lax.broadcasted_iota(jnp.int32, (nk * 128, 4 * tile_j), 1)
    used = jnp.logical_or(target < tile_j, target >= 3 * tile_j)
    j = lax.rem(target, tile_j)
    offset = jnp.where(used, source - (j // tokens * 128 + lax.rem(j, tokens)), -1)
    blocks = width_d // size
    for e in range(size):
        pick = jnp.where(offset == e * tokens, 1.0, 0.0).astype(bf16)
        res = nn_dot(right, pick).astype(bf16)
        for q in range(nq):
            for n in range(blocks):
                at = (q * blocks + n) * seqs
                rab_ref[n * size + e, q * seqs : (q + 1) * seqs, :] = res[at : at + seqs]

    chunk = 4
    many = 4
    wide = oh_ref.shape[2] // lanes
    empty = jnp.zeros((seqs, 2 * tile_j), bf16)

    def block_of(d):
        rows = []
        for q in range(nq):
            both = rab_ref[d, q * seqs : (q + 1) * seqs, :]
            part = both[:, : 2 * tile_j], both[:, 2 * tile_j :]
            for i in range(pack):
                pieces = [empty] * (pack // 2)
                pieces[i // 2] = part[i % 2]
                rows.append(jnp.concatenate(pieces, axis=1))
        return jnp.concatenate(rows, axis=0)

    def outer_of(n):
        block = jnp.concatenate([block_of(many * n + e) for e in range(many)], axis=1)
        for m in range(groups // chunk):
            out = nn_dot(lm_ref[m * chunk * fc : (m + 1) * chunk * fc, :], block)
            high, low = high_low(out)
            for e in range(many):
                at = slice((many * n + e) * fc, (many * n + e + 1) * fc)
                for g in range(chunk):
                    group = m * chunk + g
                    to = slice(group % wide * lanes, (group % wide + 1) * lanes)
                    cut = slice(g * fc, (g + 1) * fc), slice(e * lanes, (e + 1) * lanes)
                    oh_ref[group // wide, at, to] = high[cut]
                    ol_ref[group // wide, at, to] = low[cut]

    for n in range(width_d // many):
        outer_of(n)

    ready()
    some = z // fc
    for n in range(width_d // some):
        block = jnp.concatenate(
            [m_ref[pl.ds(n * some + e, fc, stride=width_d), :] for e in range(some)], axis=0
        ).T
        high, low = high_low(block)
        mt_ref[:z, n * z : (n + 1) * z] = high
        mt_ref[z:, n * z : (n + 1) * z] = low
    maskj = column_mask(mask_ref, col, tile_j, 2)

    maskl = jnp.concatenate([maskj] * (pack // 2), axis=1) > 0
    score = score_ref[...]
    s1 = score.astype(bf16).astype(f32)
    s2 = (score - s1).astype(bf16).astype(f32)
    s3 = score - s1 - s2
    none = jnp.zeros_like(s1)
    st = jnp.concatenate(
        [
            jnp.concatenate([s1, s2, s3, none], axis=0),
            jnp.concatenate([s1, s2, none, none], axis=0),
        ],
        axis=1,
    ).astype(bf16)

    def product(n):
        two = nn_dot(mt_ref[...], oh_ref[n])
        update_refs[n % 2][...] = two[:z] + two[z:] + nn_dot(mt_ref[:z, :], ol_ref[n])

    def finish(n):
        for e in range(wide):
            g = n * wide + e
            at = slice(g * lanes, (g + 1) * lanes)
            before = pair_ref[at, :].T.astype(f32)
            update = update_refs[n % 2][:, e * lanes : (e + 1) * lanes]
            result = (before + update).astype(bf16)
            x = result.astype(f32)
            pout_ref[at, :] = result.T
            center = x - jnp.mean(x, axis=0, keepdims=True)
            inverse = lax.rsqrt(jnp.mean(center * center, axis=0, keepdims=True) + epsilon)
            normal = center * inverse
            normal_ref[g] = normal
            inverse_ref[g] = jnp.broadcast_to(inverse, inverse_ref.shape[1:])
            high, low = high_low(normal)
            scores = nn_dot(st, jnp.concatenate([high, low], axis=0))
            logits = scores[:heads] + scores[heads : 2 * heads] + scores[2 * heads : 3 * heads]
            logits_ref[g] = jnp.where(maskl, logits, far_below)

    steps = groups // wide
    update_refs = (update0_ref, update1_ref)
    copies = []
    for n in range(steps + 1):
        if n < steps:
            product(n)
        if n > 0:
            finish(n - 1)
            at = pl.ds((n - 1) * wide * lanes, wide * lanes)
            part = pltpu.make_async_copy(pout_ref.at[at], pout_hbm.at[at], out_sem.at[n - 1])
            part.start()
            copies.append(part)
    for copy in copies:
        copy.wait()


def by_heads(w, heads, out_ref):
    width, chans = w.shape
    hw = chans // heads
    block = 4 * hw
    slot = lax.broadcasted_iota(jnp.int32, (width, block), 1) // hw
    w = w.astype(f32)
    for t in range(chans // block):
        part = w[:, t * block : (t + 1) * block]
        turns = [part] + [pltpu.roll(part, n * hw, 1) for n in range(1, 4)]
        for e in range(4):
            h = t * 4 + e
            for s in range(4):
                out_ref[s * width : (s + 1) * width, h * block : (h + 1) * block] = jnp.where(
                    slot == s, turns[(s - e) % 4], 0.0
                ).astype(bf16)


def weights_kernel(
    ready,
    row_ref,
    col_ref,
    side0_ref,
    side1_ref,
    side2_ref,
    side3_ref,
    cols0_ref,
    cols1_ref,
    weights_ref,
    gw_ref,
    cols_ref,
    acc_ref,
    bv_ref,
    bg_ref,
    bf_ref,
    rows_ref,
    gs_ref,
    vs_ref,
):
    nk, half, tokens, _ = cols_ref.shape
    tile = nk * tokens
    groups, heads, lanes = gw_ref.shape
    row, col = row_ref[0], col_ref[0]
    count = half * tokens
    size = side0_ref.shape[0] - 2 * count
    for t, ref in enumerate((side0_ref, side1_ref, side2_ref, side3_ref)):
        k = jnp.bitwise_xor(col, t)
        rows_ref[k] = ref[size : size + 2 * count, :].reshape(rows_ref.shape[1:])
    for t in range(nk):
        ref = (cols0_ref, cols1_ref)[t // 2]
        start = ref.shape[0] // 2 * (t % 2)
        part = ref[start : start + count, :]
        cols_ref[jnp.bitwise_xor(row, t)] = part.reshape(cols_ref.shape[1:])
    chans = weights_ref.shape[1] // 3
    by_heads(weights_ref[:, :chans], heads, bv_ref)
    by_heads(weights_ref[:, chans : 2 * chans], heads, bg_ref)
    by_heads(weights_ref[:, 2 * chans :], heads, bf_ref)
    block = bv_ref.shape[1] // heads

    def four(read, n):
        return jnp.concatenate(
            [
                jnp.concatenate(
                    [
                        jnp.concatenate([read(k, 2 * (2 * n + e) + p) for k in range(nk)], axis=0)
                        for p in range(2)
                    ],
                    axis=1,
                )
                for e in range(2)
            ],
            axis=0,
        )

    for hp in range(heads // 2):
        cut = slice(hp * 2 * block, (hp + 1) * 2 * block)
        for n in range(half // 4):
            v = nn_dot(four(lambda k, s: cols_ref[k, s], n), bv_ref[:, cut]).astype(bf16)
            gate = nn_dot(four(lambda k, s: rows_ref[k, 1, s], n), bg_ref[:, cut])
            grad = nn_dot(four(lambda k, s: rows_ref[k, 0, s], n), bf_ref[:, cut])
            g = (grad * jax.nn.sigmoid(gate)).astype(bf16)
            for e in range(2):
                to = slice((2 * n + e) * block, (2 * n + e + 1) * block)
                for o in range(2):
                    mine = slice(o * block, (o + 1) * block)
                    ve = v[e * tile : (e + 1) * tile, mine]
                    vs_ref[2 * hp + o, :tile, to] = ve
                    vs_ref[2 * hp + o, tile:, to] = ve
                    gs_ref[2 * hp + o, :, to] = g[e * tile : (e + 1) * tile, mine]
    for h in range(heads):
        acc_ref[h * tile : (h + 1) * tile, :] = nt_dot(gs_ref[h], vs_ref[h])

    first = lax.broadcasted_iota(jnp.int32, (groups, 2 * tile), 1) < tile
    for h in range(heads):
        for part in range(pack // 2):
            a = acc_ref[pl.ds(h * tile + 2 * part, groups, stride=pack), :]
            b = acc_ref[pl.ds(h * tile + 2 * part + 1, groups, stride=pack), :]
            gw_ref[:, h, part * 2 * tile : (part + 1) * 2 * tile] = jnp.where(first, a, b)


def softmax_kernel(
    ready,
    col_ref,
    logits_ref,
    gwa_ref,
    gwb_ref,
    mask_ref,
    gw_ref,
    own_ref,
    pay1_ref,
    pay2_ref,
    pay3_ref,
):
    groups, heads, lanes = logits_ref.shape
    tile = lanes // pack
    nk = 4
    rows = groups * heads
    col = col_ref[0]
    gw_ref[...] = gwa_ref[...] + gwb_ref[...]
    lane = lax.broadcasted_iota(jnp.int32, (rows, 2 * tile), 1)
    low = lane < tile
    maskj = column_mask(mask_ref, col, tile, 2)
    stats = jnp.zeros((rows, 2 * tile), f32)
    for part in range(pack // 2):
        cut = slice(part * 2 * tile, (part + 1) * 2 * tile)
        lg = logits_ref[:, :, cut].reshape(rows, 2 * tile)
        gw = gw_ref[:, :, cut].reshape(rows, 2 * tile)
        m0 = jnp.max(jnp.where(low, lg, far_below), axis=1, keepdims=True)
        m1 = jnp.max(jnp.where(low, far_below, lg), axis=1, keepdims=True)
        p = jnp.exp(lg - jnp.where(low, m0, m1)) * maskj
        pg = p * gw
        for e, m in ((0, m0), (1, m1)):
            mine = low if e == 0 else jnp.logical_not(low)
            i = 2 * part + e
            total = jnp.sum(jnp.where(mine, p, 0.0), axis=1, keepdims=True)
            inner = jnp.sum(jnp.where(mine, pg, 0.0), axis=1, keepdims=True)
            stats = jnp.where(lane == i, m, stats)
            stats = jnp.where(lane == pack + i, total, stats)
            stats = jnp.where(lane == 2 * pack + i, inner, stats)
    turned = stats.T[:16]
    per = groups // nk
    for shift, pay in enumerate((own_ref, pay1_ref, pay2_ref, pay3_ref)):
        dest = lax.rem(col + shift, nk)
        pay[0] = turned[:8]
        pay[1] = turned[8:]
        for g in range(per):
            piece = logits_ref[dest * per + g]
            for part in range(pack // 2):
                pay[2 + g * (pack // 2) + part] = piece[:, part * 2 * tile : (part + 1) * 2 * tile]


def values_kernel(
    ready, col_ref, ev0_ref, ev1_ref, ev2_ref, ev3_ref, wv_ref, norm_ref, wg_ref, v_ref, gate_ref, ev_ref
):
    nr, nk, half, tokens, wide = ev_ref.shape
    chans = wv_ref.shape[1]
    for t, ref in enumerate((ev0_ref, ev1_ref, ev2_ref, ev3_ref)):
        ev_ref[jnp.bitwise_xor(col_ref[0], t)] = ref[...]
    gate = jax.nn.sigmoid(nn_dot(norm_ref[...], twice(wg_ref[...])))
    gate_ref[: half * tokens] = gate[:, :chans]
    gate_ref[half * tokens :] = gate[:, chans:]
    wv = twice(wv_ref[...])
    for s in range(half):
        x = jnp.concatenate([ev_ref[r, k, s] for r in range(nr) for k in range(nk)], axis=0)
        v_ref[s] = nn_dot(x, wv).astype(bf16)


def gradient_kernel(
    ready,
    own_ref, r1_ref, r2_ref, r3_ref, logits_ref, gw_ref, normal_ref, inverse_ref, score_ref, out_hbm, stat_ref, out_ref, out_sem
):
    groups, heads, lanes = logits_ref.shape
    rows = groups * heads
    score = score_ref[...]
    z = score.shape[1]
    s1 = score.astype(bf16).astype(f32)
    s2 = (score - s1).astype(bf16).astype(f32)
    s3 = score - s1 - s2
    parts = [s1, s1, s1, s2, s2, s3, jnp.zeros((z - 6 * heads, z), f32)]
    sk = jnp.concatenate(parts, axis=0).T[:, : 6 * heads].astype(bf16)
    pays = (own_ref, r1_ref, r2_ref, r3_ref)
    ms = [p[0][:pack] for p in pays]
    ls = [p[0][pack : 2 * pack] for p in pays]
    ns = [p[1][:pack] for p in pays]
    top = functools.reduce(jnp.maximum, ms)
    scales = [jnp.exp(m - top) for m in ms]
    total = sum(a * b for a, b in zip(ls, scales))
    inner = sum(a * b for a, b in zip(ns, scales)) / total
    stacked = jnp.concatenate([top, total, inner, jnp.zeros((rows - 3 * pack, rows), f32)], axis=0)
    stat_ref[...] = stacked.T

    tile = lanes // pack
    low = lax.broadcasted_iota(jnp.int32, (heads, 2 * tile), 1) < tile

    def one(g):
        st = stat_ref[g * heads : (g + 1) * heads, :]

        def spread(base):
            halves = [
                jnp.where(
                    low,
                    st[:, base + 2 * half : base + 2 * half + 1],
                    st[:, base + 2 * half + 1 : base + 2 * half + 2],
                )
                for half in range(pack // 2)
            ]
            return jnp.concatenate(halves, axis=1)

        prob = jnp.exp(logits_ref[g] - spread(0)) / spread(pack)
        gl = prob * (gw_ref[g] - spread(2 * pack))
        g1 = gl.astype(bf16).astype(f32)
        g2 = (gl - g1).astype(bf16).astype(f32)
        g3 = gl - g1 - g2
        stack = jnp.concatenate([g1, g2, g3, g1, g2, g1], axis=0).astype(bf16)
        grad = nn_dot(sk, stack)
        normal = normal_ref[g]
        inverse = inverse_ref[g][:1]
        centered = grad - jnp.mean(grad, axis=0, keepdims=True)
        along = jnp.mean(grad * normal, axis=0, keepdims=True)
        result = inverse * (centered - normal * along)
        out_ref[g * lanes : (g + 1) * lanes, :] = result.astype(bf16).T

    many = 4

    copies = []
    for n in range(groups // many):
        for e in range(many):
            one(n * many + e)
        at = pl.ds(n * many * lanes, many * lanes)
        part = pltpu.make_async_copy(out_ref.at[at], out_hbm.at[at], out_sem.at[n])
        part.start()
        copies.append(part)
    for copy in copies:
        copy.wait()


def alignment_kernel(
    ready,
    col_ref,
    own_ref,
    r1_ref,
    r2_ref,
    r3_ref,
    v_ref,
    gate_ref,
    x_ref,
    wf_ref,
    out_ref,
    w_ref,
    gated_ref,
):
    pays = (own_ref, r1_ref, r2_ref, r3_ref)
    nk = len(pays)
    heads = own_ref.shape[1]
    wide = own_ref.shape[2]
    tile = wide // 2
    pieces = own_ref.shape[0] - 2
    rows = pieces * heads
    half, all_tokens, chans = v_ref.shape
    chans = chans // 2
    tokens = pieces * 2
    head_width = chans // heads
    col = col_ref[0]

    low = lax.broadcasted_iota(jnp.int32, (rows, wide), 1) < tile
    lgs = [p[2:].reshape(rows, wide) for p in pays]
    peak = functools.reduce(jnp.maximum, lgs)
    m0 = jnp.max(jnp.where(low, peak, far_below), axis=1, keepdims=True)
    m1 = jnp.max(jnp.where(low, far_below, peak), axis=1, keepdims=True)
    top = jnp.where(low, m0, m1)
    ps = [jnp.exp(lg - top) for lg in lgs]
    every = sum(ps)
    t0 = jnp.sum(jnp.where(low, every, 0.0), axis=1, keepdims=True)
    t1 = jnp.sum(jnp.where(low, 0.0, every), axis=1, keepdims=True)
    total = jnp.where(low, t0, t1)
    for shift, p in enumerate(ps):
        source = lax.rem(col + nk - shift, nk)
        weight = p / total
        rolled = pltpu.roll(weight, tile, 1)
        for n in range(pieces):
            w_ref[source, :, 2 * n, :] = weight[n * heads : (n + 1) * heads]
            w_ref[source, :, 2 * n + 1, :] = rolled[n * heads : (n + 1) * heads]
    w = jnp.concatenate(
        [
            w_ref[k].reshape(heads * tokens, wide)[:, :tile]
            for k in range(nk)
        ],
        axis=1,
    ).astype(bf16)

    owner = lax.broadcasted_iota(jnp.int32, (tokens, chans), 1) // head_width

    def one(s, carry):
        full = nn_dot(w, v_ref[s])
        for e in range(2):
            cut = slice(e * chans, (e + 1) * chans)
            mean = jnp.zeros((tokens, chans), f32)
            for h in range(heads):
                mean = jnp.where(owner == h, full[h * tokens : (h + 1) * tokens, cut], mean)
            at = pl.ds(pl.multiple_of((e * half + s) * tokens, tokens), tokens)
            gated_ref[at, :] = (gate_ref[at, :] * mean).astype(bf16)
        return carry

    lax.fori_loop(0, half, one, 0, unroll=8)
    out_ref[...] = (x_ref[...].astype(f32) + nt_dot(gated_ref[...], wf_ref[...])).astype(bf16)


def on_device(
    counts,
    alignment_input,
    pair_input,
    token_valid_mask,
    first_factor_weights,
    second_factor_weights,
    content_weights_grid,
    sigmoid_weights_grid,
    outer_matrix,
    score_matrix,
    final_mixing_weights,
    adjoint_of_rowset,
):
    nq, nr, nk = counts
    row_index = lax.axis_index("row")
    col_index = lax.axis_index("col")
    seqs, tokens, width = alignment_input.shape
    tile_i, tile_j, z = pair_input.shape
    fc = first_factor_weights.shape[1]
    fd = second_factor_weights.shape[1]
    heads = score_matrix.shape[1]
    chans = content_weights_grid.shape[1]
    groups = tile_i // pack
    lanes = pack * tile_j
    sds = jax.ShapeDtypeStruct

    mask = token_valid_mask.reshape(1, -1)
    own_start = ((row_index * nk + col_index) * tokens).astype(jnp.int32).reshape(1)
    seq_index = lax.axis_index("seq")
    place = tuple(x.astype(jnp.int32).reshape(1) for x in (row_index, col_index, seq_index))
    col_scalar = col_index.astype(jnp.int32).reshape(1)
    half = seqs // 2

    l_rows = tokens // pack * fc
    r_rows = fd * tokens // 128 * seqs
    n_rows = half * tokens
    shard, rows, own_left, normed, weights = call(
        prepare_kernel,
        (
            sds((l_rows + 2 * n_rows + r_rows, 128), bf16),
            sds((l_rows + 2 * n_rows, 128), bf16),
            sds((l_rows, 128), bf16),
            sds((n_rows, 128), bf16),
            sds((width, 3 * chans), bf16),
        ),
        scratch=(
            pltpu.VMEM((tokens, seqs, width), f32),
            pltpu.VMEM((fd * tokens // 128, seqs, 128), f32),
        ),
        smem=1,
        vmem=60 * 1024 * 1024,
    )(
        own_start,
        alignment_input,
        adjoint_of_rowset,
        first_factor_weights.T,
        second_factor_weights.T,
        mask,
        content_weights_grid,
        sigmoid_weights_grid,
        final_mixing_weights.T,
    )

    def exchange(x, bit):
        return lax.ppermute(x, "col", [(c, c ^ bit) for c in range(nk)])

    other = exchange(shard, 1)
    across = exchange(rows, 2)
    pair = jnp.concatenate([x[l_rows + n_rows :] for x in (shard, other)], axis=0)
    all_cols = [
        lax.ppermute(
            pair,
            ("row", "col"),
            [(r * nk + c, (c ^ flip) * nk + r) for r in range(nr) for c in range(nk)],
        )
        for flip in (0, 2)
    ]

    def over_seq(x):
        if nq == 2:
            return lax.ppermute(x, "seq", [(0, 1), (1, 0)])
        return lax.all_gather(x, "seq", axis=0, tiled=True)

    lefts = [own_left, other, across, exchange(own_left, 3)]
    (left,) = call(join_left_kernel, (sds((nk * l_rows, 128), bf16),), smem=1)(place[1], *lefts)
    far_left = over_seq(left)
    weights, own = call(hand_on_kernel, (sds(weights.shape, bf16), sds(rows.shape, bf16)))(
        weights, rows
    )
    across, far_left, weights, own, *all_cols = lax.optimization_barrier(
        (across, far_left, weights, own, *all_cols)
    )
    all_rows = [own, other, across, exchange(across, 1)]

    (right,) = call(join_right_kernel, (sds((nk * r_rows, 128), bf16),), smem=1)(
        place[0], *all_cols
    )
    far_right = over_seq(right)

    head_lanes = seqs * chans // heads
    gw_own, block = call(
        weights_kernel,
        (
            sds((groups, heads, lanes), f32),
            sds((nk, half, tokens, 2 * width), bf16),
        ),
        scratch=(
            pltpu.VMEM((heads * tile_i, 2 * tile_j), f32),
            pltpu.VMEM((4 * width, 4 * chans), bf16),
            pltpu.VMEM((4 * width, 4 * chans), bf16),
            pltpu.VMEM((4 * width, 4 * chans), bf16),
            pltpu.VMEM((nk, 2, half, tokens, 2 * width), bf16),
            pltpu.VMEM((heads, tile_i, head_lanes), bf16),
            pltpu.VMEM((heads, 2 * tile_j, head_lanes), bf16),
        ),
        smem=2,
        flops=3_000_000_000,
        nbytes=3_000_000,
    )(*place[:2], *all_rows, *all_cols, weights)
    if nq == 2:
        gw_other = lax.ppermute(gw_own, "seq", [(0, 1), (1, 0)])
    else:
        gw_own, gw_other = lax.psum(gw_own, "seq"), jnp.zeros_like(gw_own)

    close, remote = exchange(block, 1), exchange(block, 2)

    pair_out, normal, inverse, logits = call(
        update_kernel,
        (
            sds((tile_i * tile_j, z), bf16),
            sds((groups, z, lanes), f32),
            sds((groups, 8, lanes), f32),
            sds((groups, heads, lanes), f32),
        ),
        scratch=(
            pltpu.VMEM((tile_i * tile_j, z), bf16),
            pltpu.SemaphoreType.DMA((groups // 4,)),
            pltpu.VMEM((nk, nq * r_rows, 128), bf16),
            pltpu.VMEM((fd, nq * seqs, 4 * tile_j), bf16),
            pltpu.VMEM((groups * fc, nq * pack * seqs), bf16),
            pltpu.VMEM((2 * z, fd * fc), bf16),
            pltpu.VMEM((groups // 4, fd * fc, 4 * lanes), bf16),
            pltpu.VMEM((groups // 4, fd * fc, 4 * lanes), bf16),
            pltpu.VMEM((z, 4 * lanes), f32),
            pltpu.VMEM((z, 4 * lanes), f32),
        ),
        smem=2,
        flops=14_000_000_000,
        nbytes=5_000_000,
        vmem=44 * 1024 * 1024,
        far=(6, 7, 8, 9),
        far_out=(0,),
    )(
        *place[1:],
        left,
        right,
        far_left,
        far_right,
        mask,
        outer_matrix,
        score_matrix.T,
        pair_input.reshape(tile_i * tile_j, z),
    )

    payload = sds((2 + groups // nk * (pack // 2), heads, 2 * tile_j), f32)
    gw, pay0, pay1, pay2, pay3 = call(
        softmax_kernel,
        (sds((groups, heads, lanes), f32), payload, payload, payload, payload),
        smem=1,
    )(col_scalar, logits, gw_own, gw_other, mask)

    got = [
        lax.ppermute(pay, "col", [(c, (c + shift) % nk) for c in range(nk)])
        for shift, pay in ((1, pay1), (2, pay2), (3, pay3))
    ]


    close, remote, pay0 = lax.optimization_barrier((close, remote, pay0))
    every = [block, close, remote, exchange(remote, 1)]
    values, gating = call(
        values_kernel,
        (sds((half, nr * nk * tokens, 2 * chans), bf16), sds((seqs * tokens, chans), f32)),
        scratch=(pltpu.VMEM((nr, nk, half, tokens, 2 * width), bf16),),
        smem=1,
        flops=4_000_000_000,
        nbytes=6_000_000,
    )(col_scalar, *every, content_weights_grid, normed, sigmoid_weights_grid)

    got, values, gating = lax.optimization_barrier((got, values, gating))

    (gradient,) = call(
        gradient_kernel,
        (sds((tile_i * tile_j, z), bf16),),
        scratch=(
            pltpu.VMEM((groups * heads, groups * heads), f32),
            pltpu.VMEM((tile_i * tile_j, z), bf16),
            pltpu.SemaphoreType.DMA((groups // 4,)),
        ),
        far_out=(0,),
        flops=4_000_000_000,
        nbytes=3_000_000,
    )(pay0, *got, logits, gw, normal, inverse, score_matrix.T)

    (aligned,) = call(
        alignment_kernel,
        (sds((seqs * tokens, width), bf16),),
        scratch=(
            pltpu.VMEM((nk, heads, tokens, 2 * tile_j), f32),
            pltpu.VMEM((seqs * tokens, chans), bf16),
        ),
        smem=1,
        flops=3_000_000_000,
        nbytes=5_000_000,
    )(
        col_scalar,
        pay0,
        *got,
        values,
        gating,
        alignment_input.reshape(seqs * tokens, width),
        final_mixing_weights.T,
    )
    return (
        aligned.reshape(seqs, tokens, width),
        pair_out.reshape(tile_i, tile_j, z),
        gradient.reshape(tile_i, tile_j, z),
    )


def solution(mesh):
    counts = (mesh.shape["seq"], mesh.shape["row"], mesh.shape["col"])
    in_specs = (
        P("seq", ("row", "col"), None),
        P("row", "col", None),
        P(),
        P(),
        P(),
        P(),
        P(),
        P(),
        P(),
        P(),
        P("seq", ("row", "col"), None),
    )
    out_specs = (P("seq", ("row", "col"), None), P("row", "col", None), P("row", "col", None))
    return jax.shard_map(
        functools.partial(on_device, counts),
        mesh=mesh,
        in_specs=in_specs,
        out_specs=out_specs,
        check_vma=False,
    )
```
